32 devices in a mesh: ctx: 4 (over y, core), fsdp: 4 (over z), tp: 2 (over x).
Axes of the slice: x: 2, y: 2, z: 4, core: 2. Of those that a mesh axis runs over, the one named last changes fastest.
Arguments:
- hidden_in: bfloat16 [4, 1024, 2048], P('fsdp', 'ctx'), may hold values from -6 to 6
- teacher: bfloat16 [4, 1024, 2048], P('fsdp', ('ctx', 'tp')), may hold values from -6 to 6
- lengths: int32 [4], replicated, may hold values from 256 to 1024, as said below
- routes: int32 [4, 1024, 8], P('fsdp', ('ctx', 'tp')), may hold values from 0 to 31, all different within a row; in each aligned block of 128 rows (0 to 127, 128 to 255, ..., all dimensions but the last counted through in order) at most 48 rows name the same one
- attn_gain: float32 [2048], replicated, may hold values from 0.25 to 1.75
- w_query: bfloat16 [2048, 4096], P('fsdp', 'tp'), may hold values from -0.125 to 0.125
- w_key: bfloat16 [2048, 512], P('fsdp', 'tp'), may hold values from -0.125 to 0.125
- w_value: bfloat16 [2048, 512], P('fsdp', 'tp'), may hold values from -0.125 to 0.125
- w_output: bfloat16 [4096, 2048], P('tp', 'fsdp'), may hold values from -1.5 to 1.5
- query_gain: float32 [128], replicated, may hold values from 0.25 to 1.75
- key_gain: float32 [128], replicated, may hold values from 0.25 to 1.75
- ffn_gain: float32 [2048], replicated, may hold values from 0.25 to 1.75
- w_router: bfloat16 [2048, 32], P('fsdp'), may hold values from -0.0625 to 0.0625
- w_expert_in: bfloat16 [32, 2048, 1536], P(('ctx', 'fsdp', 'tp')), may hold values from -0.125 to 0.125
- w_expert_out: bfloat16 [32, 768, 2048], P(('ctx', 'fsdp', 'tp')), may hold values from -1.25 to 1.25
Outputs:
- output: bfloat16 [4, 1024, 2048], P('fsdp', ('ctx', 'tp'))
- loss_value: float32 [], replicated
- grad_input: float32 [4, 1024, 2048], P('fsdp', ('ctx', 'tp'))
- grad_attn_gain: float32 [2048], replicated
- grad_query: float32 [2048, 4096], P('fsdp', 'tp')
- grad_key: float32 [2048, 512], P('fsdp', 'tp')
- grad_value: float32 [2048, 512], P('fsdp', 'tp')
- grad_w_output: float32 [4096, 2048], P('tp', 'fsdp')
- grad_query_gain: float32 [128], replicated
- grad_key_gain: float32 [128], replicated
- grad_ffn_gain: float32 [2048], replicated
- grad_router: float32 [2048, 32], P('fsdp')
- grad_expert_in: float32 [32, 2048, 1536], P(('ctx', 'fsdp', 'tp'))
- grad_expert_out: float32 [32, 768, 2048], P(('ctx', 'fsdp', 'tp'))
The draws below stay inside these ranges and needn't reach their ends.
Inputs may be any that keep to these rules, and one draw needn't show every extreme that they name: `lengths`: one sequence, which one drawn from the seed, has all 1024 slots valid; valid slots are the first ones of a sequence. `routes`: A row names 8 different experts. In every aligned block of 128 rows (flattened in order), no expert is named by more than 48 rows; in some blocks one expert is named by exactly 48.
All inputs are finite; a program needn't handle non-finite values.
Results may differ from the reference program's by a relative error of at most 0.012.
The reference program's roundings to bfloat16 on the way count: a program that leaves them out, or rounds other values in their place, can miss the bound.
Values may be sent and summed in bfloat16 or wider, within the bound.
A program may use at most 256 MiB of HBM per device.

```python
import math
import jax
import jax.numpy as jnp
import numpy as np
from jax import lax

D = 2048
HEADS = 32
KV_HEADS = 4
HEAD = 128
FF = 768
TOPK = 8
SEQS = 4
LEN = 1024
TOKENS = 4096
HALF = 128
EXPERTS = 32
MOST = 48


def draw_lengths(key, part):
    key = jax.random.fold_in(key, 11)
    first_key, second_key = jax.random.split(key)
    spans = jax.random.randint(first_key, (SEQS,), LEN // 4, LEN + 1)
    chosen = jax.random.randint(second_key, (), 0, SEQS)
    return jnp.where(jnp.arange(SEQS) == chosen, LEN, spans).astype(jnp.int32)


def block_levels(own_key, shape, cuts, least, largest):
    gain = 1.0
    for position, parts in cuts:
        heights = jax.random.uniform(jax.random.fold_in(jax.random.fold_in(own_key, 6), position), (parts,), jnp.float32, least / len(cuts), largest / len(cuts))
        gain = gain * jnp.repeat(jnp.exp(heights), shape[position] // parts).reshape((-1,) + (1,) * (len(shape) - 1 - position))
    return gain


def deal_out(key, own, number, rows, count, top, most, slope):
    order = jax.random.permutation(key, count)
    packed, common = shares(count, rows * top, most, slope, True), shares(count, rows * top, most, slope, False)
    places = jnp.arange(count)

    def named(sizes, turn):
        used = int((sizes > 0).sum())
        fixed = max(1, used // 4)
        passed = fixed + (places - fixed + turn * (used - fixed)) % max(1, count - fixed)
        return jnp.zeros((count,), jnp.int32).at[order[jnp.where(places < fixed, places, passed)]].set(jnp.asarray(sizes, jnp.int32))

    sizes = jnp.where(number % 4 == 0, named(packed, number // 4), named(common, number - number // 4 - 1))
    mixed = jax.random.permutation(jax.random.fold_in(own, 3), count)
    donor, taker = mixed[0:count // 2 * 2:2], mixed[1:count // 2 * 2:2]
    slack = jnp.minimum(sizes[donor] - 1, most - sizes[taker]) // 2
    slack = jnp.where((donor == order[0]) | (taker == order[0]) | (sizes[taker] == 0), 0, jnp.maximum(slack, 0))
    passed = jax.random.randint(jax.random.fold_in(own, 4), (count // 2,), 0, 1 << 20) % (slack + 1)
    sizes = sizes.at[donor].add(-passed).at[taker].add(passed)
    labels = jnp.searchsorted(jnp.cumsum(sizes), jnp.arange(rows * top), side="right").astype(jnp.int32)
    table = labels.reshape(top, rows).T
    table = table[jax.random.permutation(jax.random.fold_in(own, 1), rows)]
    turn = jax.random.randint(jax.random.fold_in(own, 2), (rows, 1), 0, top)
    return jnp.take_along_axis(table, (jnp.arange(top)[None, :] + turn) % top, axis=1)


def shares(amount, total, most, skew, full):
    portions = [(1 << 20) // math.isqrt(rank ** skew) + 1 for rank in range(1, amount + 1)]
    largest = most if full else min(most, max(-(-total // amount), total * portions[0] // sum(portions)))
    least = 1 if total - largest >= amount - 1 else 0
    given, rest = [largest] + [least] * (amount - 1), total - largest - least * (amount - 1)
    while rest > 0:
        free = [i for i in range(1, amount) if given[i] < largest] or [i for i in range(1, amount) if given[i] < most]
        whole, left = sum([portions[i] for i in free]), rest
        for i in free:
            more = min(most - given[i], max(1, left * portions[i] // whole), rest)
            given[i] = given[i] + more
            rest = rest - more
    return np.array(given)


def bell_draw(stream_key, dims, deviation, most, cuts=(), kind=jnp.bfloat16):
    array = jax.random.normal(stream_key, dims, jnp.float32) * deviation
    if len(cuts) > 0:
        array = block_levels(stream_key, dims, cuts, -0.22, 0.18) * array
    return jnp.clip(array, min=-most, max=most).astype(kind)


def setup_inputs(seed: int = 0) -> dict:
    key_of = jax.random.split(jax.random.key(seed), 16)
    hidden_in = bell_draw(key_of[0], (SEQS, LEN, D), 1.0, 6.0, ((0, 4), (1, 4)))
    teacher = bell_draw(key_of[1], (SEQS, LEN, D), 1.0, 6.0, ((0, 4), (1, 8)))
    lengths = draw_lengths(jax.random.fold_in(key_of[15], 71), 0)
    routes_keys = jax.random.split(jax.random.fold_in(key_of[3], 1), SEQS * LEN // HALF)
    routes_turns = jax.random.permutation(jax.random.fold_in(key_of[3], 3), SEQS * LEN // HALF)
    routes = jax.vmap(lambda own, number: deal_out(jax.random.fold_in(key_of[3], 2), own, number, HALF, EXPERTS, TOPK, MOST, 1))(routes_keys, routes_turns).reshape((SEQS, LEN, TOPK))
    attn_gain = jnp.clip(1.0 + 0.15 * jax.random.normal(key_of[4], (D,), jnp.float32), 0.25, 1.75)
    w_query = bell_draw(key_of[5], (D, HEADS * HEAD), D ** -0.5, 0.125, ((0, 4), (1, 2)))
    w_key = bell_draw(key_of[6], (D, KV_HEADS * HEAD), D ** -0.5, 0.125, ((0, 4), (1, 2)))
    w_value = bell_draw(key_of[7], (D, KV_HEADS * HEAD), D ** -0.5, 0.125, ((0, 4), (1, 2)))
    w_output = bell_draw(key_of[8], (HEADS * HEAD, D), (max(4, HEADS * HEAD // 256)) ** -0.5, 1.5, ((0, 2), (1, 4)))
    query_gain = jnp.clip(1.0 + 0.15 * jax.random.normal(key_of[9], (HEAD,), jnp.float32), 0.25, 1.75)
    key_gain = jnp.clip(1.0 + 0.15 * jax.random.normal(key_of[10], (HEAD,), jnp.float32), 0.25, 1.75)
    ffn_gain = jnp.clip(1.0 + 0.15 * jax.random.normal(key_of[11], (D,), jnp.float32), 0.25, 1.75)
    w_router = bell_draw(key_of[12], (D, EXPERTS), (4 * D) ** -0.5, 0.0625, ((0, 4),))
    w_expert_in = bell_draw(key_of[13], (EXPERTS, D, 2 * FF), D ** -0.5, 0.125, ((0, 32),))
    w_expert_out = bell_draw(key_of[14], (EXPERTS, FF, D), (max(4, FF // 32)) ** -0.5, 1.25, ((0, 32),))
    return {"hidden_in": hidden_in, "teacher": teacher, "lengths": lengths, "routes": routes, "attn_gain": attn_gain, "w_query": w_query, "w_key": w_key, "w_value": w_value, "w_output": w_output, "query_gain": query_gain, "key_gain": key_gain, "ffn_gain": ffn_gain, "w_router": w_router, "w_expert_in": w_expert_in, "w_expert_out": w_expert_out}


EPS = 1e-06
ROPE_BASE = 1000000.0
MASKED = -1e+30

@jax.custom_vjp
def low(v):
    return lax.optimization_barrier(v.astype(jnp.bfloat16)).astype(jnp.float32)

@jax.custom_vjp
def low_back(v):
    return v

def low_keep(v):
    return (low(v), None)

def low_pass(kept, grad):
    return (grad,)

def back_keep(v):
    return (v, None)

def back_low(kept, grad):
    return (low(grad),)
low.defvjp(low_keep, low_pass)
low_back.defvjp(back_keep, back_low)

def matmul(left, right):
    return jnp.dot(left, right, precision=lax.Precision.HIGHEST, preferred_element_type=jnp.float32)

def rms_rows(values, gain_vec):
    return values * lax.rsqrt(lax.optimization_barrier(jnp.mean(values * values, axis=-1, keepdims=True)) + EPS) * gain_vec

def rope_tables(positions, head_size):
    half_size = head_size // 2
    frequency = jnp.power(ROPE_BASE, -jnp.arange(half_size, dtype=jnp.float32) * (2.0 / head_size))
    angles = positions.astype(jnp.float32)[:, None] * frequency[None, :]
    return (jnp.cos(angles), jnp.sin(angles))

def rotate(values, cosine, sine_tab):
    half_size = values.shape[-1] // 2
    front_half = values[..., :half_size]
    back_half = values[..., half_size:]
    cos_rows = cosine[:, None, :]
    sin_rows = sine_tab[:, None, :]
    return jnp.concatenate([front_half * cos_rows - back_half * sin_rows, back_half * cos_rows + front_half * sin_rows], axis=-1)

def attend(queries, keys, values, length):
    group_size = HEADS // KV_HEADS
    query_block = min(512, LEN)
    key_pos = jnp.arange(LEN, dtype=jnp.int32)
    inv_root = HEAD ** (-0.5)

    def one_block(offset):
        query_rows = lax.dynamic_slice_in_dim(queries, offset, query_block, 2)
        raw_scores = jnp.einsum('kgqd,kjd->kgqj', query_rows, keys, precision=lax.Precision.HIGHEST)
        scores = low_back(raw_scores * inv_root)
        query_pos = offset + jnp.arange(query_block, dtype=jnp.int32)
        allowed = (key_pos[None, :] <= query_pos[:, None]) & (key_pos[None, :] < length)
        scores = jnp.where(allowed, scores, MASKED)
        row_peak = lax.optimization_barrier(jnp.max(scores, axis=-1, keepdims=True))
        exponent = jnp.where(allowed, jnp.exp(scores - row_peak), 0.0)
        probabilities = exponent / lax.optimization_barrier(jnp.sum(exponent, axis=-1, keepdims=True))
        return jnp.einsum('kgqj,kjd->kgqd', low(probabilities), values, precision=lax.Precision.HIGHEST)
    offsets = jnp.arange(0, LEN, query_block, dtype=jnp.int32)
    pieces = lax.map(jax.checkpoint(one_block), offsets)
    return jnp.transpose(pieces, (1, 2, 0, 3, 4)).reshape(KV_HEADS, group_size, LEN, HEAD)

def reference(hidden_in, teacher, lengths, routes, attn_gain, w_query, w_key, w_value, w_output, query_gain, key_gain, ffn_gain, w_router, w_expert_in, w_expert_out):
    group_size = HEADS // KV_HEADS
    positions = jnp.tile(jnp.arange(LEN, dtype=jnp.int32), SEQS)
    valid = (positions.reshape(SEQS, LEN) < lengths[:, None]).reshape(TOKENS)
    count = jnp.sum(lengths).astype(jnp.float32)
    route_ids = routes.reshape(TOKENS, TOPK)
    flat_routes = route_ids.reshape(-1)
    assigned = TOKENS * TOPK
    order = jnp.argsort(flat_routes, stable=True).astype(jnp.int32)
    expert_ids = jnp.arange(EXPERTS, dtype=jnp.int32)
    loads = lax.optimization_barrier(jnp.sum((flat_routes[:, None] == expert_ids[None, :]).astype(jnp.int32), axis=0)).astype(jnp.int32)
    firsts = (jnp.cumsum(loads) - loads).astype(jnp.int32)
    buffer_rows = TOKENS // HALF * MOST
    teacher_rows = teacher.reshape(TOKENS, D).astype(jnp.float32)
    cosine, sine_tab = rope_tables(positions, HEAD)

    def forward(inputs, gain_attn, query_w, key_w, value_w, output_w, gain_query, gain_key, gain_ffn, router_w, expert_in, expert_out):
        flat_in = inputs.reshape(TOKENS, D)
        normed = low(rms_rows(flat_in, gain_attn))
        q_raw = low_back(matmul(normed, query_w)).reshape(TOKENS, HEADS, HEAD)
        k_raw = low_back(matmul(normed, key_w)).reshape(TOKENS, KV_HEADS, HEAD)
        v_all = low(low_back(matmul(normed, value_w))).reshape(TOKENS, KV_HEADS, HEAD)
        q_rot = low(rotate(rms_rows(q_raw, gain_query), cosine, sine_tab))
        k_rot = low(rotate(rms_rows(k_raw, gain_key), cosine, sine_tab))
        q_seq = jnp.transpose(q_rot.reshape(SEQS, LEN, KV_HEADS, group_size, HEAD), (0, 2, 3, 1, 4))
        k_seq = jnp.transpose(k_rot.reshape(SEQS, LEN, KV_HEADS, HEAD), (0, 2, 1, 3))
        v_seq = jnp.transpose(v_all.reshape(SEQS, LEN, KV_HEADS, HEAD), (0, 2, 1, 3))
        attended = lax.map(lambda bundle: attend(bundle[0], bundle[1], bundle[2], bundle[3]), (q_seq, k_seq, v_seq, lengths))
        heads_all = jnp.transpose(attended, (0, 3, 1, 2, 4)).reshape(TOKENS, HEADS * HEAD)
        heads_all = low(low_back(heads_all))
        residual = flat_in + low_back(matmul(heads_all, output_w))
        ffn_in = low(rms_rows(residual, gain_ffn))
        logits = low_back(matmul(ffn_in, router_w))
        chosen = jnp.take_along_axis(logits, route_ids, axis=1)
        shifted = jnp.exp(chosen - lax.optimization_barrier(jnp.max(chosen, axis=-1, keepdims=True)))
        gates = shifted / lax.optimization_barrier(jnp.sum(shifted, axis=-1, keepdims=True))
        gate_flat = gates.reshape(-1)

        def expert_term(weights_in, weights_out, first_slot, load_count):
            slot_ids = jnp.arange(buffer_rows, dtype=jnp.int32)
            live_slot = slot_ids < load_count
            picked = order[jnp.minimum(first_slot + slot_ids, assigned - 1)]
            token_ids = (picked // TOPK).astype(jnp.int32)
            rows_in = low_back(ffn_in[token_ids])
            both_pre = low_back(matmul(rows_in, weights_in))
            gate_pre = both_pre[:, :FF]
            up_pre = both_pre[:, FF:]
            mixed = low(gate_pre * jax.nn.sigmoid(gate_pre) * up_pre)
            expert_y = low(low_back(matmul(mixed, weights_out)))
            weight = jnp.where(live_slot, gate_flat[picked], 0.0)
            return (expert_y * weight[:, None], token_ids)

        def add_expert(running, bundle):
            term, token_ids = jax.checkpoint(expert_term)(bundle[0], bundle[1], bundle[2], bundle[3])
            return (running.at[token_ids].add(term), None)
        mixture, _ = lax.scan(add_expert, jnp.zeros((TOKENS, D), jnp.float32), (expert_in, expert_out, firsts, loads))
        output_f = residual + mixture
        error = jnp.where(valid[:, None], output_f - teacher_rows, 0.0)
        loss_value = jnp.sum(error * error) / (count * D)
        return (loss_value, output_f)
    params = (hidden_in.astype(jnp.float32), attn_gain.astype(jnp.float32), w_query.astype(jnp.float32), w_key.astype(jnp.float32), w_value.astype(jnp.float32), w_output.astype(jnp.float32), query_gain.astype(jnp.float32), key_gain.astype(jnp.float32), ffn_gain.astype(jnp.float32), w_router.astype(jnp.float32), w_expert_in.astype(jnp.float32), w_expert_out.astype(jnp.float32))
    (loss_value, output_f), pullback = jax.vjp(forward, *params)
    grads = pullback((jnp.asarray(TOKENS * D / 2.0, dtype=jnp.float32), jnp.zeros_like(output_f)))
    return (output_f.reshape(SEQS, LEN, D).astype(jnp.bfloat16), loss_value, grads[0], grads[1], grads[2], grads[3], grads[4], grads[5], grads[6], grads[7], grads[8], grads[9], grads[10], grads[11])
```

```python
import functools

import jax
import jax.numpy as jnp
from jax import lax
from jax.experimental import pallas as pl
from jax.experimental.pallas import tpu as pltpu
from jax.sharding import PartitionSpec as P

EPS = 1e-06
ROPE_BASE = 1000000.0
MASKED = -1e30
AXES = ("ctx", "fsdp", "tp")
MESH = pl.DeviceIdType.MESH
ANY = pl.BlockSpec(memory_space=pl.ANY)
VMEM = pl.BlockSpec(memory_space=pltpu.VMEM)
BF = jnp.bfloat16
FL = jnp.float32
MIB = 1024 * 1024


def norm_rows(values, gain_vec):
    factor = lax.rsqrt(jnp.mean(values * values, axis=-1, keepdims=True) + EPS)
    return (values * factor * gain_vec, factor)


def norm_back(values, factor, gain_vec, upstream):
    weighted = upstream * gain_vec
    inner_mean = jnp.mean(values * weighted, axis=-1, keepdims=True)
    return (
        factor * weighted - values * (factor * factor * factor) * inner_mean,
        upstream * values * factor,
    )


def rope_tables(positions, head_size):
    half_size = head_size // 2
    frequency = jnp.power(ROPE_BASE, -jnp.arange(half_size, dtype=jnp.float32) * (2.0 / head_size))
    angles = positions.astype(jnp.float32)[:, None] * frequency[None, :]
    return (jnp.cos(angles), jnp.sin(angles))


def rotate(values, cosine, sine_tab):
    half_size = values.shape[-1] // 2
    front_half = values[..., :half_size]
    back_half = values[..., half_size:]
    cos_rows = cosine[:, None, :]
    sin_rows = sine_tab[:, None, :]
    return jnp.concatenate(
        [
            front_half * cos_rows - back_half * sin_rows,
            back_half * cos_rows + front_half * sin_rows,
        ],
        axis=-1,
    )


def inner_rows(left, right):
    return lax.dot_general(
        left, right, (((0,), (0,)), ((), ())), preferred_element_type=jnp.float32
    )


def outer_cols(left, right):
    return lax.dot_general(
        left, right, (((1,), (1,)), ((), ())), preferred_element_type=jnp.float32
    )


def block_scores(queries, key_rows, offset, positions, length, inv_root):
    block_len = key_rows.shape[1]
    raw_scores = (
        jnp.einsum("kgqd,kjd->kgqj", queries, key_rows, preferred_element_type=jnp.float32)
        * inv_root
    )
    key_pos = offset + jnp.arange(block_len, dtype=jnp.int32)
    allowed = (key_pos[None, :] <= positions[:, None]) & (key_pos[None, :] < length)
    return (jnp.where(allowed, raw_scores, MASKED), allowed)


def place():
    return tuple(lax.axis_index(axis) for axis in AXES)


def remote(source, target, sent, got, device):
    return pltpu.make_async_remote_copy(
        src_ref=source, dst_ref=target, send_sem=sent, recv_sem=got,
        device_id=device, device_id_type=MESH,
    )


def greet(devices):
    barrier = pltpu.get_barrier_semaphore()
    for device in devices:
        pl.semaphore_signal(barrier, inc=1, device_id=device, device_id_type=MESH)
    pl.semaphore_wait(barrier, len(devices))


def params(identity, mebibytes):
    return pltpu.CompilerParams(
        collective_id=identity, has_side_effects=True, vmem_limit_bytes=int(mebibytes * MIB)
    )


def gather_body(C, F, wa, wo, tab, fa, fo, ftab, loc, zs, zr, ys, yr, ks, kr, ts, tr):
    c, f, t = place()
    core, chip = lax.rem(c, 2), lax.div(c, 2)
    chips = C // 2
    sib = c + 1 - 2 * core
    ra, (ro, co) = wa.shape[0], wo.shape
    pa, po = ra // C, ro // C

    def spot(arr, b, p):
        if arr == 0:
            return fa.at[pl.ds(pl.multiple_of(b * ra + p * pa, pa), pa)]
        return fo.at[pl.ds(pl.multiple_of(p * po, po), po), pl.ds(pl.multiple_of(b * co, co), co)]

    def own(arr):
        if arr == 0:
            return wa.at[pl.ds(pl.multiple_of(c * pa, pa), pa)]
        return wo.at[pl.ds(pl.multiple_of(c * po, po), po)]

    peers = [(c, lax.rem(f + k, F), t) for k in range(1, F)]
    peers += [(lax.rem(chip + k, chips) * 2 + core, f, t) for k in range(1, chips)]
    peers += [(sib, f, t)]
    greet(peers)

    def z_copy(arr, s, d):
        b = f - (s - 1) if d == 0 else f + (s - 1)
        source = own(arr) if s == 1 else spot(arr, b, c)
        return remote(
            source, spot(arr, b, c), zs.at[d, s, arr], zr.at[d, s, arr],
            (c, f + 1 if d == 0 else f - 1, t),
        )

    def z_sends(s, d):
        b = f - (s - 1) if d == 0 else f + (s - 1)
        return (f + 1 < F) & (b >= 0) if d == 0 else (f > 0) & (b < F)

    def z_gets(s, d):
        return f - s >= 0 if d == 0 else f + s < F

    def came(s, d):
        return f - s if d == 0 else f + s

    def z_arrival(arr, s, d):
        b = came(s, d)
        here = spot(arr, b, c)
        return remote(here, here, zs.at[d, s, arr], zr.at[d, s, arr], (c, f, t))

    def y_copy(arr, s, d, k):
        here = spot(arr, came(s, d), c)
        there = (lax.rem(chip + k, chips) * 2 + core, f, t)
        return remote(here, here, ys.at[d, s, k, arr], yr.at[d, s, k, arr], there)

    def k_copy(arr, s, d, k, side):
        p = lax.rem(chip + chips - k, chips) * 2 + side
        here = spot(arr, came(s, d), p)
        return remote(here, here, ks.at[d, s, k, arr], kr.at[d, s, k, arr], (sib, f, t))

    def y_arrival(arr, s, d, k):
        p = lax.rem(chip + chips - k, chips) * 2 + core
        here = spot(arr, came(s, d), p)
        return remote(here, here, ys.at[d, s, k, arr], yr.at[d, s, k, arr], (sib, f, t))

    tabs = [
        remote(tab, ftab.at[f], ts.at[k], tr.at[k], (c, lax.rem(f + k, F), t)) for k in range(1, F)
    ]
    for copy in tabs:
        copy.start()
    for d in range(2):

        @pl.when(z_sends(1, d))
        def _():
            for arr in range(2):
                z_copy(arr, 1, d).start()

    locals_ = [
        pltpu.make_async_copy(tab, ftab.at[f], loc.at[0]),
        pltpu.make_async_copy(wa, fa.at[pl.ds(pl.multiple_of(f * ra, ra), ra)], loc.at[1]),
        pltpu.make_async_copy(wo, fo.at[:, pl.ds(pl.multiple_of(f * co, co), co)], loc.at[2]),
    ]
    for copy in locals_:
        copy.start()

    def pass_on(s, d):
        for arr in range(2):
            for k in range(1, chips):
                y_arrival(arr, s, d, k).wait_recv()
                k_copy(arr, s, d, k, core).start()

    for s in range(1, F):
        for d in range(2):

            @pl.when(z_gets(s, d))
            def _():
                for arr in range(2):
                    z_arrival(arr, s, d).wait_recv()
                    if s + 1 < F:

                        @pl.when(z_sends(s + 1, d))
                        def _():
                            z_copy(arr, s + 1, d).start()

                    for k in range(1, chips):
                        y_copy(arr, s, d, k).start()
                    k_copy(arr, s, d, 0, core).start()

        if s > 1:
            for d in range(2):
                pl.when(z_gets(s - 1, d))(functools.partial(pass_on, s - 1, d))
    for d in range(2):
        pl.when(z_gets(F - 1, d))(functools.partial(pass_on, F - 1, d))
    for copy in tabs:
        copy.wait()
    for copy in locals_:
        copy.wait()
    for s in range(1, F):
        for d in range(2):

            @pl.when(z_sends(s, d))
            def _():
                for arr in range(2):
                    z_copy(arr, s, d).wait_send()

            @pl.when(z_gets(s, d))
            def _():
                for arr in range(2):
                    for k in range(1, chips):
                        y_copy(arr, s, d, k).wait_send()
                    for k in range(chips):
                        k_copy(arr, s, d, k, core).wait_send()
                        k_copy(arr, s, d, k, 1 - core).wait_recv()


def gather_weights(C, F, wa, wo, tab):
    ra, ca = wa.shape
    ro, co = wo.shape
    chips = C // 2
    dma = pltpu.SemaphoreType.DMA
    return pl.pallas_call(
        functools.partial(gather_body, C, F),
        out_shape=(
            jax.ShapeDtypeStruct((F * ra, ca), wa.dtype),
            jax.ShapeDtypeStruct((ro, F * co), wo.dtype),
            jax.ShapeDtypeStruct((F,) + tab.shape, tab.dtype),
        ),
        in_specs=[ANY] * 3,
        out_specs=[ANY] * 3,
        scratch_shapes=[
            dma((3,)), dma((2, F, 2)), dma((2, F, 2)),
            dma((2, F, chips, 2)), dma((2, F, chips, 2)),
            dma((2, F, chips, 2)), dma((2, F, chips, 2)),
            dma((F,)), dma((F,)),
        ],
        compiler_params=params(1, 16),
    )(wa, wo, tab)


def slab_place(C, T):
    c, f, t = place()
    return c, f, t, c * T + t


def slab_device(index, f, T):
    return (lax.div(index, T), f, lax.rem(index, T))


def dispatch_body(C, F, T, tabbed, rows, select, *refs):
    if tabbed:
        tab, out, zbuf, ftab, stage, loc, zs, zr, ss, sr, ts, tr = refs
    else:
        out, zbuf, stage, loc, zs, zr, ss, sr = refs
    c, f, t, me = slab_place(C, T)
    S = C * T
    K = select.shape[2]
    copies = select.shape[3] // rows.shape[0]
    columns = [(c, lax.rem(f + k, F), t) for k in range(1, F)]
    greet(columns + [slab_device(lax.rem(me + j, S), f, T) for j in range(1, S)])
    sends = [
        remote(rows, zbuf.at[f], zs.at[k], zr.at[k], columns[k - 1]) for k in range(1, F)
    ]
    if tabbed:
        tabs = [remote(tab, ftab.at[f], ts.at[k], tr.at[k], columns[k - 1]) for k in range(1, F)]
        for copy in tabs:
            copy.start()
        ftab[f] = tab[...]
    for copy in sends:
        copy.start()
    zbuf[f] = rows[...]

    def slab_copy(k, j):
        b = lax.rem(f + F - k, F)
        e = lax.rem(me + j, S)
        return remote(
            stage.at[e, b], out.at[me, b], ss.at[k, j], sr.at[k, j], slab_device(e, f, T)
        )

    def slab_arrival(k, j):
        b = lax.rem(f + F - k, F)
        e = lax.rem(me + S - j, S)
        return remote(
            stage.at[e, b], out.at[e, b], ss.at[k, j], sr.at[k, j], slab_device(e, f, T)
        )

    def own_copy(k):
        b = lax.rem(f + F - k, F)
        return pltpu.make_async_copy(stage.at[me, b], out.at[me, b], loc.at[k])

    for k in range(F):
        b = lax.rem(f + F - k, F)
        if k > 0:
            remote(rows, zbuf.at[b], zs.at[k], zr.at[k], columns[k - 1]).wait_recv()

        def pick(j):
            e = lax.rem(me + j, S)
            block = zbuf[b]
            if copies > 1:
                block = jnp.concatenate([block] * copies, axis=0)
            stage[e, b] = jnp.dot(
                select[b, e], block, preferred_element_type=FL
            ).astype(BF)

        if S <= 8:
            for j in range(1, S):
                pick(j)
                slab_copy(k, j).start()
        else:

            def step(j, carry):
                pick(j)
                slab_copy(k, j).start()
                return carry

            lax.fori_loop(1, S, step, 0)
        pick(0)
        own_copy(k).start()
    if tabbed:
        for copy in tabs:
            copy.wait()
    for copy in sends:
        copy.wait_send()
    for k in range(F):
        own_copy(k).wait()

        def settle(j, carry):
            slab_copy(k, j).wait_send()
            slab_arrival(k, j).wait_recv()
            return carry

        lax.fori_loop(1, S, settle, 0)


def dispatch(identity, C, F, T, rows, select, tab=None):
    S = C * T
    K = select.shape[2]
    R, W = rows.shape
    dma = pltpu.SemaphoreType.DMA
    tabbed = tab is not None
    outs = [jax.ShapeDtypeStruct((S, F, K, W), BF), jax.ShapeDtypeStruct((F, R, W), BF)]
    out_specs = [ANY, VMEM]
    ins = [rows, select]
    scratch = [
        pltpu.VMEM((S, F, K, W), BF), dma((F,)), dma((F,)), dma((F,)), dma((F, S)), dma((F, S)),
    ]
    if tabbed:
        outs.append(jax.ShapeDtypeStruct((F,) + tab.shape, tab.dtype))
        out_specs.append(VMEM)
        ins.append(tab)
        scratch += [dma((F,)), dma((F,))]
    return pl.pallas_call(
        functools.partial(dispatch_body, C, F, T, tabbed),
        out_shape=tuple(outs),
        in_specs=[VMEM] * len(ins),
        out_specs=out_specs,
        scratch_shapes=scratch,
        compiler_params=params(identity, 32),
    )(*ins)


def combine_body(C, F, T, tabbed, rows, weigh, *refs):
    if tabbed:
        tab, got, part, ftab, stage, loc, zs, zr, ss, sr, ts, tr = refs
    else:
        got, part, stage, loc, zs, zr, ss, sr = refs
    c, f, t, me = slab_place(C, T)
    S = C * T
    K, W = got.shape[2], got.shape[3]
    n = weigh.shape[1]
    columns = [(c, lax.rem(f + k, F), t) for k in range(1, F)]
    greet(columns + [slab_device(lax.rem(me + j, S), f, T) for j in range(1, S)])

    def slab_copy(k, j):
        b = lax.rem(f + k, F)
        e = lax.rem(me + j, S)
        return remote(
            rows.at[e, b], got.at[b, me], ss.at[k, j], sr.at[k, j], slab_device(e, f, T)
        )

    def slab_arrival(k, j):
        b = lax.rem(f + k, F)
        e = lax.rem(me + S - j, S)
        return remote(
            rows.at[e, b], got.at[b, e], ss.at[k, j], sr.at[k, j], slab_device(e, f, T)
        )

    def own_copy(k):
        b = lax.rem(f + k, F)
        return pltpu.make_async_copy(rows.at[me, b], got.at[b, me], loc.at[k])

    order = list(range(1, F)) + [0]
    for k in order:

        def begin(j, carry):
            slab_copy(k, j).start()
            return carry

        lax.fori_loop(1, S, begin, 0)
        own_copy(k).start()
    if tabbed:
        tabs = [
            remote(tab.at[lax.rem(f + k, F)], ftab.at[f], ts.at[k], tr.at[k], columns[k - 1])
            for k in range(1, F)
        ]
        for copy in tabs:
            copy.start()
        ftab[f] = tab[f]

    def z_copy(k):
        b = lax.rem(f + k, F)
        return remote(stage.at[b], part.at[f], zs.at[k], zr.at[k], columns[k - 1])

    def z_arrival(k):
        b = lax.rem(f + F - k, F)
        return remote(stage.at[b], part.at[b], zs.at[k], zr.at[k], columns[k - 1])

    step = min(W, 512)
    for k in order:
        b = lax.rem(f + k, F)
        own_copy(k).wait()

        def settle(j, carry):
            slab_arrival(k, j).wait_recv()
            return carry

        lax.fori_loop(1, S, settle, 0)
        target = part if k == 0 else stage

        def add(i, carry):
            columns_ = pl.ds(pl.multiple_of(i * step, step), step)
            block = got[b, :, :, columns_].reshape(S * K, step)
            total = jnp.dot(weigh[b, 0], block, preferred_element_type=FL)
            for m in range(1, n):
                total += jnp.dot(weigh[b, m], block, preferred_element_type=FL)
            target[b, :, columns_] = total.astype(BF)
            return carry

        lax.fori_loop(0, W // step, add, 0)
        if k > 0:
            z_copy(k).start()
    for k in range(1, F):
        z_copy(k).wait_send()
        z_arrival(k).wait_recv()
    for k in range(F):

        def leave(j, carry):
            slab_copy(k, j).wait_send()
            return carry

        lax.fori_loop(1, S, leave, 0)
    if tabbed:
        for copy in tabs:
            copy.wait()


def combine(identity, C, F, T, rows, weigh, tab=None):
    S, _, K, W = rows.shape
    R = weigh.shape[2]
    dma = pltpu.SemaphoreType.DMA
    tabbed = tab is not None
    outs = [jax.ShapeDtypeStruct((F, S, K, W), BF), jax.ShapeDtypeStruct((F, R, W), BF)]
    ins = [rows, weigh]
    scratch = [
        pltpu.VMEM((F, R, W), BF), dma((F,)), dma((F,)), dma((F,)), dma((F, S)), dma((F, S)),
    ]
    if tabbed:
        outs.append(jax.ShapeDtypeStruct(tab.shape, tab.dtype))
        ins.append(tab)
        scratch += [dma((F,)), dma((F,))]
    return pl.pallas_call(
        functools.partial(combine_body, C, F, T, tabbed),
        out_shape=tuple(outs),
        in_specs=[ANY] + [VMEM] * (len(ins) - 1),
        out_specs=[VMEM] * len(outs),
        scratch_shapes=scratch,
        compiler_params=params(identity, 32),
    )(*ins)


def ctx_sum_body(C, x, out, got, ss, sr):
    c, f, t = place()
    peers = [(lax.rem(c + k, C), f, t) for k in range(1, C)]
    greet(peers)

    def copy(k):
        p = lax.rem(c + k, C)
        return remote(x.at[p], got.at[c], ss.at[k], sr.at[k], (p, f, t))

    def arrival(k):
        p = lax.rem(c + C - k, C)
        return remote(x.at[p], got.at[p], ss.at[k], sr.at[k], (p, f, t))

    for k in range(1, C):
        copy(k).start()
    got[c] = x[c]
    for k in range(1, C):
        arrival(k).wait_recv()
    total = got[0].astype(FL)
    for p in range(1, C):
        total += got[p].astype(FL)
    out[...] = total
    for k in range(1, C):
        copy(k).wait_send()


def ctx_sum(identity, C, x):
    dma = pltpu.SemaphoreType.DMA
    return pl.pallas_call(
        functools.partial(ctx_sum_body, C),
        out_shape=jax.ShapeDtypeStruct(x.shape[1:], FL),
        in_specs=[VMEM],
        out_specs=VMEM,
        scratch_shapes=[pltpu.VMEM(x.shape, x.dtype), dma((C,)), dma((C,))],
        compiler_params=params(identity, 24),
    )(x)


def small_body(C, F, T, x, out, zgot, mid, sgot, zs, zr, ss, sr):
    c, f, t, me = slab_place(C, T)
    S = C * T
    columns = [(c, lax.rem(f + k, F), t) for k in range(1, F)]
    greet(columns + [slab_device(lax.rem(me + j, S), f, T) for j in range(1, S)])

    def z_copy(k):
        return remote(x.at[lax.rem(f + k, F)], zgot.at[f], zs.at[k], zr.at[k], columns[k - 1])

    def z_arrival(k):
        b = lax.rem(f + F - k, F)
        return remote(x.at[b], zgot.at[b], zs.at[k], zr.at[k], columns[k - 1])

    for k in range(1, F):
        z_copy(k).start()
    zgot[f] = x[f]
    for k in range(1, F):
        z_arrival(k).wait_recv()
    total = zgot[0]
    for b in range(1, F):
        total += zgot[b]
    mid[...] = total
    sgot[me] = total

    def s_copy(j):
        return remote(
            mid, sgot.at[me], ss.at[j], sr.at[j], slab_device(lax.rem(me + j, S), f, T)
        )

    def s_arrival(j):
        e = lax.rem(me + S - j, S)
        return remote(mid, sgot.at[e], ss.at[j], sr.at[j], slab_device(e, f, T))

    for j in range(1, S):
        s_copy(j).start()
    for j in range(1, S):
        s_arrival(j).wait_recv()
    total = sgot[0]
    for e in range(1, S):
        total += sgot[e]
    out[...] = total
    for k in range(1, F):
        z_copy(k).wait_send()
    for j in range(1, S):
        s_copy(j).wait_send()


def small_sum(identity, C, F, T, x):
    dma = pltpu.SemaphoreType.DMA
    S = C * T
    one = x.shape[1:]
    return pl.pallas_call(
        functools.partial(small_body, C, F, T),
        out_shape=jax.ShapeDtypeStruct(one, FL),
        in_specs=[VMEM],
        out_specs=VMEM,
        scratch_shapes=[
            pltpu.VMEM((F,) + one, FL), pltpu.VMEM(one, FL), pltpu.VMEM((S,) + one, FL),
            dma((F,)), dma((F,)), dma((S,)), dma((S,)),
        ],
        compiler_params=params(identity, 24),
    )(x)


def far_first(F):
    table = []
    for f in range(F):
        order = []
        for i in range(F):
            ends = [F - 1 - i, i] if f * 2 < F else [i, F - 1 - i]
            for b in ends:
                if ((b > f and b == F - 1 - i) or (b < f and b == i)) and b not in order:
                    order.append(b)
        table.append(order + [f])
    return table


def grads_body(
    C, F, xt, da, ht, dt, outa, outo,
    ska, sko, rka, rko, sya, syo, rya, ryo, rza, rzo, sza, szo,
    k_s, k_r, y_s, y_r, z_s, z_r, g_s, g_r, h_s, h_r,
):
    c, f, t = place()
    core, chip = lax.rem(c, 2), lax.div(c, 2)
    chips = C // 2
    sib = c + 1 - 2 * core
    pa, po, co = outa.shape[1], outo.shape[1], outo.shape[2]
    ra = pa * C
    table = far_first(F)

    def block(q):
        value = jnp.int32(table[0][q])
        for g in range(1, F):
            value = jnp.where(f == g, table[g][q], value)
        return value

    blocks = [block(q) for q in range(F)]
    ends = [(c, lax.rem(f + 1, F), t), (c, lax.rem(f + F - 1, F), t)]
    mates = [(lax.rem(chip + k, chips) * 2 + core, f, t) for k in range(1, chips)]
    greet(ends + mates + [(sib, f, t)])

    def piece_a(b, p):
        rows = pl.ds(pl.multiple_of(b * ra + p * pa, pa), pa)
        return jnp.dot(xt[rows, :], da[...], preferred_element_type=FL)

    def piece_o(b, p):
        rows = pl.ds(pl.multiple_of(p * po, po), po)
        cols = pl.ds(pl.multiple_of(b * co, co), co)
        return jnp.dot(ht[rows, :], dt[:, cols], preferred_element_type=FL)

    def core_copies(q, k):
        b = blocks[q]
        return [
            remote(ska.at[b, k], rka.at[b, k], k_s.at[q, k, 0], k_r.at[q, k, 0], (sib, f, t)),
            remote(sko.at[b, k], rko.at[b, k], k_s.at[q, k, 1], k_r.at[q, k, 1], (sib, f, t)),
        ]

    for q in range(F):
        b = blocks[q]
        for k in [*range(1, chips), 0]:
            p = lax.rem(chip + k, chips) * 2 + 1 - core
            ska[b, k] = piece_a(b, p).astype(BF)
            sko[b, k] = piece_o(b, p).astype(BF)
            for copy in core_copies(q, k):
                copy.start()

    def chip_copies(q, k):
        b = blocks[q]
        there = mates[k - 1]
        return [
            remote(sya.at[b, k - 1], rya.at[b, k - 1], y_s.at[q, k, 0], y_r.at[q, k, 0], there),
            remote(syo.at[b, k - 1], ryo.at[b, k - 1], y_s.at[q, k, 1], y_r.at[q, k, 1], there),
        ]

    for q in range(F):
        b = blocks[q]
        for k in range(1, chips):
            p = lax.rem(chip + k, chips) * 2 + core
            for copy in core_copies(q, k):
                copy.wait_recv()
            sya[b, k - 1] = (piece_a(b, p) + rka[b, k].astype(FL)).astype(BF)
            syo[b, k - 1] = (piece_o(b, p) + rko[b, k].astype(FL)).astype(BF)
            for copy in chip_copies(q, k):
                copy.start()

    def z_copies(q, b, slot, there):
        return [
            remote(sza.at[b], rza.at[slot], z_s.at[q, 0], z_r.at[slot, 0], there),
            remote(szo.at[b], rzo.at[slot], z_s.at[q, 1], z_r.at[slot, 1], there),
        ]

    def z_wait(slot):
        for copy in z_copies(0, 0, slot, ends[0]):
            copy.wait_recv()

    for q in range(F):
        b = blocks[q]
        for copy in core_copies(q, 0):
            copy.wait_recv()
        for k in range(1, chips):
            for copy in chip_copies(q, k):
                copy.wait_recv()
        total_a = piece_a(b, c) + rka[b, 0].astype(FL)
        total_o = piece_o(b, c) + rko[b, 0].astype(FL)
        for k in range(1, chips):
            total_a += rya[b, k - 1].astype(FL)
            total_o += ryo[b, k - 1].astype(FL)
        if q < F - 1:
            up = b > f
            first = jnp.where(up, f == 0, f == F - 1)

            @pl.when(first)
            def _():
                sza[b] = total_a.astype(BF)
                szo[b] = total_o.astype(BF)

            @pl.when(jnp.logical_not(first))
            def _():
                z_wait(b)
                sza[b] = (total_a + rza[b].astype(FL)).astype(BF)
                szo[b] = (total_o + rzo[b].astype(FL)).astype(BF)

            @pl.when(up)
            def _():
                for copy in z_copies(q, b, b, (c, f + 1, t)):
                    copy.start()

            @pl.when(jnp.logical_not(up))
            def _():
                slot = jnp.where(b == f - 1, F, b)
                for copy in z_copies(q, b, slot, (c, f - 1, t)):
                    copy.start()

        else:
            sza[f] = total_a.astype(BF)
            szo[f] = total_o.astype(BF)

            @pl.when(f > 0)
            def _():
                z_wait(f)
                sza[f] = (total_a + rza[f].astype(FL)).astype(BF)
                szo[f] = (total_o + rzo[f].astype(FL)).astype(BF)

            @pl.when(f < F - 1)
            def _():
                z_wait(F)
                outa[c] = (sza[f].astype(FL) + rza[F].astype(FL)).astype(BF)
                outo[c] = (szo[f].astype(FL) + rzo[F].astype(FL)).astype(BF)

            @pl.when(f == F - 1)
            def _():
                outa[c] = sza[f]
                outo[c] = szo[f]

    def spread(k):
        there = mates[k - 1]
        return [
            remote(outa.at[c], outa.at[c], g_s.at[k, 0], g_r.at[k, 0], there),
            remote(outo.at[c], outo.at[c], g_s.at[k, 1], g_r.at[k, 1], there),
        ]

    def hand(k, side):
        p = lax.rem(chip + chips - k, chips) * 2 + side
        return [
            remote(outa.at[p], outa.at[p], h_s.at[k, 0], h_r.at[k, 0], (sib, f, t)),
            remote(outo.at[p], outo.at[p], h_s.at[k, 1], h_r.at[k, 1], (sib, f, t)),
        ]

    def spread_arrival(k):
        p = lax.rem(chip + chips - k, chips) * 2 + core
        return [
            remote(outa.at[p], outa.at[p], g_s.at[k, 0], g_r.at[k, 0], mates[k - 1]),
            remote(outo.at[p], outo.at[p], g_s.at[k, 1], g_r.at[k, 1], mates[k - 1]),
        ]

    for k in range(1, chips):
        for copy in spread(k):
            copy.start()
    for copy in hand(0, core):
        copy.start()
    for k in range(1, chips):
        for copy in spread_arrival(k):
            copy.wait_recv()
        for copy in hand(k, core):
            copy.start()
    for k in range(chips):
        for copy in hand(k, 1 - core):
            copy.wait_recv()
        for copy in hand(k, core):
            copy.wait_send()
    for k in range(1, chips):
        for copy in spread(k):
            copy.wait_send()
    for q in range(F):
        for k in range(chips):
            for copy in core_copies(q, k):
                copy.wait_send()
        for k in range(1, chips):
            for copy in chip_copies(q, k):
                copy.wait_send()
        if q < F - 1:
            for copy in z_copies(q, 0, 0, ends[0]):
                copy.wait_send()


def weight_grads(identity, C, F, xt, da, ht, dt):
    D, R = xt.shape
    pa, na = D // F // C, da.shape[1]
    po, no = ht.shape[0] // C, dt.shape[1] // F
    chips = C // 2
    dma = pltpu.SemaphoreType.DMA

    def pair(*lead):
        return [pltpu.VMEM(lead + (pa, na), BF), pltpu.VMEM(lead + (po, no), BF)]

    return pl.pallas_call(
        functools.partial(grads_body, C, F),
        out_shape=(
            jax.ShapeDtypeStruct((C, pa, na), BF),
            jax.ShapeDtypeStruct((C, po, no), BF),
        ),
        in_specs=[VMEM] * 4,
        out_specs=[VMEM] * 2,
        scratch_shapes=[
            *pair(F, chips), *pair(F, chips), *pair(F, chips - 1), *pair(F, chips - 1),
            *pair(F + 1), *pair(F),
            dma((F, chips, 2)), dma((F, chips, 2)), dma((F, chips, 2)), dma((F, chips, 2)),
            dma((F, 2)), dma((F + 1, 2)), dma((chips, 2)), dma((chips, 2)),
            dma((chips, 2)), dma((chips, 2)),
        ],
        compiler_params=params(identity, 60),
    )(xt, da, ht, dt)


def split_low(values):
    high = lax.reduce_precision(values, 8, 7)
    return high.astype(BF), (values - high).astype(BF)


def local(
    hidden_in,
    teacher,
    lengths,
    routes,
    attn_gain,
    w_query,
    w_key,
    w_value,
    w_output,
    query_gain,
    key_gain,
    ffn_gain,
    w_router,
    w_expert_in,
    w_expert_out,
):
    c, f, t = place()
    C, F, T = (lax.axis_size(axis) for axis in AXES)
    S = C * T
    row_count = hidden_in.shape[1]
    width = hidden_in.shape[2]
    half_rows = row_count // T
    head_size = query_gain.shape[0]
    inv_root = head_size ** (-0.5)
    bf_type = BF
    fl_type = FL

    expert_count = S * F
    lanes = -(-expert_count // 128) * 128
    route_ids = routes[0]
    top_count = route_ids.shape[1]
    capacity = max(2, half_rows * top_count * 3 // (2 * expert_count))
    cap = -(-capacity // 16) * 16
    expert_ids = jnp.arange(lanes, dtype=jnp.int32)
    named = jnp.any(route_ids[:, :, None] == expert_ids[None, None, :], axis=1)
    row_ids = jnp.arange(half_rows, dtype=jnp.int32)
    below = (row_ids[None, :] < row_ids[:, None]).astype(bf_type)
    earlier = jnp.dot(below, named.astype(bf_type), preferred_element_type=fl_type)
    rank_tab = jnp.where(named, earlier, -1.0)

    q_cols, kv_cols = w_query.shape[1], w_key.shape[1]
    w_all = jnp.concatenate(
        [w_query, w_key, w_value, jnp.pad(w_router, ((0, 0), (0, lanes - expert_count)))], axis=1
    )
    full_all, full_o, rank_z = gather_weights(C, F, w_all, w_output, rank_tab)
    proj_cols = q_cols + 2 * kv_cols
    full_qkv = full_all[:, :proj_cols]
    full_router = full_all[:, proj_cols : proj_cols + expert_count]

    def of_slab(table):
        picked = table[:, :, :expert_count].reshape(F, half_rows, C, F, T)
        return lax.dynamic_index_in_dim(picked, f, 3, keepdims=False).reshape(F, half_rows, S)

    rank_slab = of_slab(rank_z)
    slot_ids = jnp.arange(cap, dtype=fl_type)
    chosen_rows = rank_slab[:, :, :, None] == slot_ids
    chosen_slots = (
        jnp.transpose(rank_slab, (0, 2, 1))[:, :, None, :] == slot_ids[:, None]
    )

    q_heads = q_cols // head_size
    kv_heads = kv_cols // head_size
    group_size = q_heads // kv_heads
    inputs = hidden_in[0].astype(fl_type)
    normed, norm_factor = norm_rows(inputs, attn_gain)
    normed_low = normed.astype(bf_type)
    raw = jnp.dot(normed_low, full_qkv, preferred_element_type=fl_type)
    q_raw = raw[:, :q_cols].reshape(row_count, q_heads, head_size)
    k_raw = raw[:, q_cols : q_cols + kv_cols].reshape(row_count, kv_heads, head_size)
    values_low = raw[:, q_cols + kv_cols :].astype(bf_type).reshape(row_count, kv_heads, head_size)
    q_normed, q_factor = norm_rows(q_raw, query_gain)
    k_normed, k_factor = norm_rows(k_raw, key_gain)
    positions = c * row_count + jnp.arange(row_count, dtype=jnp.int32)
    cosine, sine_tab = rope_tables(positions, head_size)
    q_rot = rotate(q_normed, cosine, sine_tab).astype(bf_type)
    k_rot = rotate(k_normed, cosine, sine_tab).astype(bf_type)
    queries = jnp.transpose(q_rot.reshape(row_count, kv_heads, group_size, head_size), (1, 2, 0, 3))
    both = jnp.transpose(jnp.concatenate([k_rot, values_low], axis=1), (1, 0, 2))
    all_both = lax.all_gather(both, "ctx", axis=1, tiled=True)
    all_keys, all_values = all_both[:kv_heads], all_both[kv_heads:]
    total_len = all_keys.shape[1]
    block_len = min(1024, total_len)
    offsets = jnp.arange(total_len // block_len, dtype=jnp.int32) * block_len
    length = jnp.take(lengths, f)
    stat_shape = (kv_heads, group_size, row_count)

    def lse_step(carry, offset):
        running_max, running_sum = carry
        key_rows = lax.dynamic_slice_in_dim(all_keys, offset, block_len, 1)
        scores, allowed = block_scores(queries, key_rows, offset, positions, length, inv_root)
        new_max = jnp.maximum(running_max, jnp.max(scores, axis=-1))
        exponent = jnp.where(allowed, jnp.exp(scores - new_max[..., None]), 0.0)
        return (
            (new_max, running_sum * jnp.exp(running_max - new_max) + jnp.sum(exponent, axis=-1)),
            None,
        )

    (row_max, row_sum), _ = lax.scan(
        lse_step, (jnp.full(stat_shape, MASKED, fl_type), jnp.zeros(stat_shape, fl_type)), offsets
    )
    log_total = row_max + jnp.log(row_sum)

    def probs_of(offset):
        key_rows = lax.dynamic_slice_in_dim(all_keys, offset, block_len, 1)
        value_rows = lax.dynamic_slice_in_dim(all_values, offset, block_len, 1)
        scores, allowed = block_scores(queries, key_rows, offset, positions, length, inv_root)
        return (
            jnp.where(allowed, jnp.exp(scores - log_total[..., None]), 0.0),
            key_rows,
            value_rows,
        )

    def out_step(running, offset):
        probabilities, key_rows, value_rows = probs_of(offset)
        return (
            running
            + jnp.einsum(
                "kgqj,kjd->kgqd",
                probabilities.astype(bf_type),
                value_rows,
                preferred_element_type=fl_type,
            ),
            None,
        )

    attn_acc, _ = lax.scan(
        out_step, jnp.zeros((kv_heads, group_size, row_count, head_size), fl_type), offsets
    )
    heads_low = (
        jnp.transpose(attn_acc, (2, 0, 1, 3))
        .reshape(row_count, q_heads * head_size)
        .astype(bf_type)
    )
    swap = [(i, 1 - i) for i in range(T)]
    row_start = t * half_rows
    other_start = (1 - t) * half_rows
    heads_other = lax.dynamic_slice_in_dim(heads_low, other_start, half_rows, 0)
    heads_own = lax.dynamic_slice_in_dim(heads_low, row_start, half_rows, 0)
    theirs = jnp.dot(heads_other, full_o, preferred_element_type=fl_type).astype(bf_type)
    ours = lax.ppermute(theirs, "tp", swap)
    attn_rows = jnp.dot(heads_own, full_o, preferred_element_type=fl_type) + ours.astype(fl_type)
    own_inputs = lax.dynamic_slice_in_dim(inputs, row_start, half_rows, 0)
    own_factor = lax.dynamic_slice_in_dim(norm_factor, row_start, half_rows, 0)
    own_positions = lax.dynamic_slice_in_dim(positions, row_start, half_rows, 0)
    residual = own_inputs + attn_rows
    ffn_in, ffn_factor = norm_rows(residual, ffn_gain)
    ffn_low = ffn_in.astype(bf_type)
    logits = jnp.dot(ffn_low, full_router, preferred_element_type=fl_type)
    is_named = named[:, :expert_count]
    masked = jnp.where(is_named, logits, MASKED)
    shifted = jnp.where(is_named, jnp.exp(masked - jnp.max(masked, axis=-1, keepdims=True)), 0.0)
    gates = shifted / jnp.sum(shifted, axis=-1, keepdims=True)
    gate_tab = jnp.pad(gates, ((0, 0), (0, lanes - expert_count)))

    select = chosen_slots.astype(bf_type)
    received, _, gate_z = dispatch(2, C, F, T, ffn_low, select, gate_tab)
    expert_rows = received.reshape(-1, width)
    both_pre = jnp.dot(expert_rows, w_expert_in[0], preferred_element_type=fl_type)
    ff_width = w_expert_out.shape[1]
    gate_pre = both_pre[:, :ff_width]
    up_pre = both_pre[:, ff_width:]
    sigmoid_gate = jax.nn.sigmoid(gate_pre)
    silu_gate = gate_pre * sigmoid_gate
    mixed_low = (silu_gate * up_pre).astype(bf_type)
    expert_out = (
        jnp.dot(mixed_low, w_expert_out[0], preferred_element_type=fl_type)
        .astype(bf_type)
        .reshape(S, F, cap, width)
    )
    gate_slab = of_slab(gate_z)
    weigh = jnp.where(chosen_rows, gate_slab[..., None], 0.0).reshape(F, 1, half_rows, S * cap)
    weigh = jnp.concatenate(split_low(weigh), axis=1)
    returned, parts = combine(3, C, F, T, expert_out, weigh)
    output_f = residual + jnp.sum(parts.astype(fl_type), axis=0)
    count = jnp.sum(lengths).astype(fl_type)
    tokens_total = lengths.shape[0] * row_count * C
    valid = own_positions < length
    error = jnp.where(valid[:, None], output_f - teacher[0].astype(fl_type), 0.0)
    loss_part = jnp.sum(error * error)
    grad_out = error * (tokens_total / count)

    select_gates = jnp.where(
        chosen_slots, jnp.transpose(gate_slab, (0, 2, 1))[:, :, None, :], 0.0
    )
    select_gates = jnp.concatenate(split_low(select_gates), axis=-1)
    grad_recv, grad_out_z = dispatch(4, C, F, T, grad_out.astype(bf_type), select_gates)
    slot_grads = jnp.einsum("zskr,zrd->zskd", select, grad_out_z, preferred_element_type=fl_type)
    slot_gate = jnp.sum(slot_grads * returned.astype(fl_type), axis=-1)
    gate_grads = jnp.sum(jnp.where(chosen_rows, slot_gate[:, None, :, :], 0.0), axis=-1)
    gate_grads = jnp.pad(gate_grads, ((0, 0), (0, 0), (0, -S % 128)))

    grad_recv = grad_recv.reshape(-1, width)
    grad_mixed = outer_cols(grad_recv, w_expert_out[0])
    grad_expert_out = inner_rows(mixed_low, grad_recv)
    grad_gate_pre = grad_mixed * up_pre * (sigmoid_gate * (1.0 + gate_pre * (1.0 - sigmoid_gate)))
    grad_up_pre = grad_mixed * silu_gate
    grad_pre = jnp.concatenate([grad_gate_pre, grad_up_pre], axis=1).astype(bf_type)
    grad_expert_in = inner_rows(expert_rows, grad_pre)
    grad_rows = (
        outer_cols(grad_pre, w_expert_in[0]).astype(bf_type).reshape(S, F, cap, width)
    )
    weigh_one = chosen_rows.astype(bf_type).reshape(F, 1, half_rows, S * cap)
    _, grad_parts, gate_back = combine(5, C, F, T, grad_rows, weigh_one, gate_grads)
    grad_gate = jnp.transpose(
        gate_back[:, :, :S].reshape(F, half_rows, C, T), (1, 2, 0, 3)
    ).reshape(half_rows, expert_count)
    grad_logits = (
        gates * (grad_gate - jnp.sum(gates * grad_gate, axis=-1, keepdims=True))
    ).astype(bf_type)
    grad_ffn = jnp.sum(grad_parts.astype(fl_type), axis=0) + outer_cols(grad_logits, full_router)
    router_part = inner_rows(ffn_low, grad_logits)
    grad_resid_norm, ffn_gain_terms = norm_back(residual, ffn_factor, ffn_gain, grad_ffn)
    grad_residual = grad_out + grad_resid_norm
    grad_own = grad_residual.astype(bf_type)
    grad_other = lax.ppermute(grad_own, "tp", swap)
    grad_attn = jnp.where(
        t == 0,
        jnp.concatenate([grad_own, grad_other], axis=0),
        jnp.concatenate([grad_other, grad_own], axis=0),
    )
    grad_heads = jnp.transpose(
        outer_cols(grad_attn, full_o)
        .astype(bf_type)
        .reshape(row_count, kv_heads, group_size, head_size),
        (1, 2, 0, 3),
    )

    def delta_step(running, offset):
        probabilities, key_rows, value_rows = probs_of(offset)
        grad_weights = jnp.einsum(
            "kgqd,kjd->kgqj", grad_heads, value_rows, preferred_element_type=fl_type
        )
        return (running + jnp.sum(probabilities * grad_weights, axis=-1), None)

    delta, _ = lax.scan(delta_step, jnp.zeros(stat_shape, fl_type), offsets)

    def grad_step(running, offset):
        probabilities, key_rows, value_rows = probs_of(offset)
        grad_weights = jnp.einsum(
            "kgqd,kjd->kgqj", grad_heads, value_rows, preferred_element_type=fl_type
        )
        grad_scores = (probabilities * (grad_weights - delta[..., None])).astype(bf_type)
        running = (
            running
            + jnp.einsum("kgqj,kjd->kgqd", grad_scores, key_rows, preferred_element_type=fl_type)
            * inv_root
        )
        key_part = (
            jnp.einsum("kgqj,kgqd->kjd", grad_scores, queries, preferred_element_type=fl_type)
            * inv_root
        )
        value_part = jnp.einsum(
            "kgqj,kgqd->kjd",
            probabilities.astype(bf_type),
            grad_heads,
            preferred_element_type=fl_type,
        )
        return (running, (key_part, value_part))

    grad_qrot, (key_blocks, value_blocks) = lax.scan(
        grad_step, jnp.zeros((kv_heads, group_size, row_count, head_size), fl_type), offsets
    )
    both_grads = jnp.concatenate([key_blocks, value_blocks], axis=1).astype(bf_type)
    both_grads = jnp.transpose(both_grads, (0, 2, 1, 3)).reshape(C, row_count, 2 * kv_cols)
    both_sum = ctx_sum(6, C, both_grads)
    grad_krot = both_sum[:, :kv_cols].reshape(row_count, kv_heads, head_size)
    grad_values_low = both_sum[:, kv_cols:].astype(bf_type)
    grad_qrot = jnp.transpose(grad_qrot, (2, 0, 1, 3)).reshape(row_count, q_heads, head_size)
    grad_qraw, query_gain_terms = norm_back(
        q_raw, q_factor, query_gain, rotate(grad_qrot, cosine, -sine_tab)
    )
    grad_kraw, key_gain_terms = norm_back(
        k_raw, k_factor, key_gain, rotate(grad_krot, cosine, -sine_tab)
    )
    grad_raw = jnp.concatenate(
        [
            grad_qraw.astype(bf_type).reshape(row_count, -1),
            grad_kraw.astype(bf_type).reshape(row_count, -1),
            grad_values_low,
        ],
        axis=1,
    )
    raw_other = lax.dynamic_slice_in_dim(grad_raw, other_start, half_rows, 0)
    raw_own = lax.dynamic_slice_in_dim(grad_raw, row_start, half_rows, 0)
    norm_theirs = outer_cols(raw_other, full_qkv).astype(bf_type)
    norm_ours = lax.ppermute(norm_theirs, "tp", swap)
    grad_normed = outer_cols(raw_own, full_qkv) + norm_ours.astype(fl_type)
    grad_input_norm, attn_gain_terms = norm_back(own_inputs, own_factor, attn_gain, grad_normed)
    grad_input = grad_residual + grad_input_norm

    total_a, total_o = weight_grads(
        7, C, F, normed_low.T, grad_raw, heads_low.T, grad_attn
    )
    total_a = total_a.reshape(-1, proj_cols).astype(fl_type)
    grad_query = total_a[:, :q_cols]
    grad_key = total_a[:, q_cols : q_cols + kv_cols]
    grad_value = total_a[:, q_cols + kv_cols :]
    grad_output_w = total_o.reshape(w_output.shape).astype(fl_type)

    vector = jnp.concatenate(
        [
            jnp.sum(attn_gain_terms, axis=0),
            jnp.sum(ffn_gain_terms, axis=0),
            jnp.sum(query_gain_terms, axis=(0, 1)),
            jnp.sum(key_gain_terms, axis=(0, 1)),
            loss_part[None],
        ]
    )
    vector = jnp.pad(vector, (0, -vector.shape[0] % 1024)).reshape(-1, 128)
    router_rows = router_part.reshape(F, -1, 128)
    small = jnp.concatenate(
        [router_rows, jnp.broadcast_to(vector[None], (F,) + vector.shape)], axis=1
    )
    summed = small_sum(8, C, F, T, small)
    router_len = router_rows.shape[1]
    grad_router = summed[:router_len].reshape(w_router.shape)
    flat = summed[router_len:].reshape(-1)
    head_at = 2 * width
    loss_value = flat[head_at + 2 * head_size] / (count * width)
    return (
        output_f.astype(bf_type)[None],
        loss_value,
        grad_input[None],
        flat[:width],
        grad_query,
        grad_key,
        grad_value,
        grad_output_w,
        flat[head_at : head_at + head_size],
        flat[head_at + head_size : head_at + 2 * head_size],
        flat[width:head_at],
        grad_router,
        grad_expert_in[None],
        grad_expert_out[None],
    )


def solution(mesh):
    return jax.shard_map(
        local,
        mesh=mesh,
        in_specs=(
            P("fsdp", "ctx", None),
            P("fsdp", ("ctx", "tp"), None),
            P(),
            P("fsdp", ("ctx", "tp"), None),
            P(),
            P("fsdp", "tp"),
            P("fsdp", "tp"),
            P("fsdp", "tp"),
            P("tp", "fsdp"),
            P(),
            P(),
            P(),
            P("fsdp", None),
            P(("ctx", "fsdp", "tp"), None, None),
            P(("ctx", "fsdp", "tp"), None, None),
        ),
        out_specs=(
            P("fsdp", ("ctx", "tp"), None),
            P(),
            P("fsdp", ("ctx", "tp"), None),
            P(),
            P("fsdp", "tp"),
            P("fsdp", "tp"),
            P("fsdp", "tp"),
            P("tp", "fsdp"),
            P(),
            P(),
            P(),
            P("fsdp", None),
            P(("ctx", "fsdp", "tp"), None, None),
            P(("ctx", "fsdp", "tp"), None, None),
        ),
        check_vma=False,
    )
```

```python
import functools

import jax
import jax.numpy as jnp
from jax import lax
from jax.experimental import pallas as pl
from jax.experimental.pallas import tpu as pltpu
from jax.sharding import PartitionSpec as P

EPS = 1e-06
ROPE_BASE = 1000000.0
MASKED = -1e30
AXES = ("ctx", "fsdp", "tp")
MESH = pl.DeviceIdType.MESH
ANY = pl.BlockSpec(memory_space=pl.ANY)
VMEM = pl.BlockSpec(memory_space=pltpu.VMEM)
BF = jnp.bfloat16
FL = jnp.float32
MIB = 1024 * 1024


def norm_rows(values, gain_vec):
    factor = lax.rsqrt(jnp.mean(values * values, axis=-1, keepdims=True) + EPS)
    return (values * factor * gain_vec, factor)


def norm_back(values, factor, gain_vec, upstream):
    weighted = upstream * gain_vec
    inner_mean = jnp.mean(values * weighted, axis=-1, keepdims=True)
    return (
        factor * weighted - values * (factor * factor * factor) * inner_mean,
        upstream * values * factor,
    )


def rope_tables(positions, head_size):
    half_size = head_size // 2
    frequency = jnp.power(ROPE_BASE, -jnp.arange(half_size, dtype=jnp.float32) * (2.0 / head_size))
    angles = positions.astype(jnp.float32)[:, None] * frequency[None, :]
    return (jnp.cos(angles), jnp.sin(angles))


def rotate(values, cosine, sine_tab):
    half_size = values.shape[-1] // 2
    front_half = values[..., :half_size]
    back_half = values[..., half_size:]
    cos_rows = cosine[:, None, :]
    sin_rows = sine_tab[:, None, :]
    return jnp.concatenate(
        [
            front_half * cos_rows - back_half * sin_rows,
            back_half * cos_rows + front_half * sin_rows,
        ],
        axis=-1,
    )


def inner_rows(left, right):
    return lax.dot_general(
        left, right, (((0,), (0,)), ((), ())), preferred_element_type=jnp.float32
    )


def outer_cols(left, right):
    return lax.dot_general(
        left, right, (((1,), (1,)), ((), ())), preferred_element_type=jnp.float32
    )


def block_scores(queries, key_rows, offset, positions, length, inv_root):
    block_len = key_rows.shape[1]
    raw_scores = (
        jnp.einsum("kgqd,kjd->kgqj", queries, key_rows, preferred_element_type=jnp.float32)
        * inv_root
    )
    key_pos = offset + jnp.arange(block_len, dtype=jnp.int32)
    allowed = (key_pos[None, :] <= positions[:, None]) & (key_pos[None, :] < length)
    return (jnp.where(allowed, raw_scores, MASKED), allowed)


def place():
    return tuple(lax.axis_index(axis) for axis in AXES)


def remote(source, target, sent, got, device):
    return pltpu.make_async_remote_copy(
        src_ref=source, dst_ref=target, send_sem=sent, recv_sem=got,
        device_id=device, device_id_type=MESH,
    )


def greet(devices):
    barrier = pltpu.get_barrier_semaphore()
    for device in devices:
        pl.semaphore_signal(barrier, inc=1, device_id=device, device_id_type=MESH)
    pl.semaphore_wait(barrier, len(devices))


def params(identity, mebibytes):
    return pltpu.CompilerParams(
        collective_id=identity, has_side_effects=True, vmem_limit_bytes=int(mebibytes * MIB)
    )


def gather_body(C, F, wa, wo, tab, fa, fo, ftab, loc, zs, zr, ys, yr, ks, kr, ts, tr):
    c, f, t = place()
    core, chip = lax.rem(c, 2), lax.div(c, 2)
    chips = C // 2
    sib = c + 1 - 2 * core
    ra, (ro, co) = wa.shape[0], wo.shape
    pa, po = ra // C, ro // C

    def spot(arr, b, p):
        if arr == 0:
            return fa.at[pl.ds(pl.multiple_of(b * ra + p * pa, pa), pa)]
        return fo.at[pl.ds(pl.multiple_of(p * po, po), po), pl.ds(pl.multiple_of(b * co, co), co)]

    def own(arr):
        if arr == 0:
            return wa.at[pl.ds(pl.multiple_of(c * pa, pa), pa)]
        return wo.at[pl.ds(pl.multiple_of(c * po, po), po)]

    peers = [(c, lax.rem(f + k, F), t) for k in range(1, F)]
    peers += [(lax.rem(chip + k, chips) * 2 + core, f, t) for k in range(1, chips)]
    peers += [(sib, f, t)]
    greet(peers)

    def z_copy(arr, s, d):
        b = f - (s - 1) if d == 0 else f + (s - 1)
        source = own(arr) if s == 1 else spot(arr, b, c)
        return remote(
            source, spot(arr, b, c), zs.at[d, s, arr], zr.at[d, s, arr],
            (c, f + 1 if d == 0 else f - 1, t),
        )

    def z_sends(s, d):
        b = f - (s - 1) if d == 0 else f + (s - 1)
        return (f + 1 < F) & (b >= 0) if d == 0 else (f > 0) & (b < F)

    def z_gets(s, d):
        return f - s >= 0 if d == 0 else f + s < F

    def came(s, d):
        return f - s if d == 0 else f + s

    def z_arrival(arr, s, d):
        b = came(s, d)
        here = spot(arr, b, c)
        return remote(here, here, zs.at[d, s, arr], zr.at[d, s, arr], (c, f, t))

    def y_copy(arr, s, d, k):
        here = spot(arr, came(s, d), c)
        there = (lax.rem(chip + k, chips) * 2 + core, f, t)
        return remote(here, here, ys.at[d, s, k, arr], yr.at[d, s, k, arr], there)

    def k_copy(arr, s, d, k, side):
        p = lax.rem(chip + chips - k, chips) * 2 + side
        here = spot(arr, came(s, d), p)
        return remote(here, here, ks.at[d, s, k, arr], kr.at[d, s, k, arr], (sib, f, t))

    def y_arrival(arr, s, d, k):
        p = lax.rem(chip + chips - k, chips) * 2 + core
        here = spot(arr, came(s, d), p)
        return remote(here, here, ys.at[d, s, k, arr], yr.at[d, s, k, arr], (sib, f, t))

    tabs = [
        remote(tab, ftab.at[f], ts.at[k], tr.at[k], (c, lax.rem(f + k, F), t)) for k in range(1, F)
    ]
    for copy in tabs:
        copy.start()
    for d in range(2):

        @pl.when(z_sends(1, d))
        def _():
            for arr in range(2):
                z_copy(arr, 1, d).start()

    locals_ = [
        pltpu.make_async_copy(tab, ftab.at[f], loc.at[0]),
        pltpu.make_async_copy(wa, fa.at[pl.ds(pl.multiple_of(f * ra, ra), ra)], loc.at[1]),
        pltpu.make_async_copy(wo, fo.at[:, pl.ds(pl.multiple_of(f * co, co), co)], loc.at[2]),
    ]
    for copy in locals_:
        copy.start()

    def pass_on(s, d):
        for arr in range(2):
            for k in range(1, chips):
                y_arrival(arr, s, d, k).wait_recv()
                k_copy(arr, s, d, k, core).start()

    for s in range(1, F):
        for d in range(2):

            @pl.when(z_gets(s, d))
            def _():
                for arr in range(2):
                    z_arrival(arr, s, d).wait_recv()
                    if s + 1 < F:

                        @pl.when(z_sends(s + 1, d))
                        def _():
                            z_copy(arr, s + 1, d).start()

                    for k in range(1, chips):
                        y_copy(arr, s, d, k).start()
                    k_copy(arr, s, d, 0, core).start()

        if s > 1:
            for d in range(2):
                pl.when(z_gets(s - 1, d))(functools.partial(pass_on, s - 1, d))
    for d in range(2):
        pl.when(z_gets(F - 1, d))(functools.partial(pass_on, F - 1, d))
    for copy in tabs:
        copy.wait()
    for copy in locals_:
        copy.wait()
    for s in range(1, F):
        for d in range(2):

            @pl.when(z_sends(s, d))
            def _():
                for arr in range(2):
                    z_copy(arr, s, d).wait_send()

            @pl.when(z_gets(s, d))
            def _():
                for arr in range(2):
                    for k in range(1, chips):
                        y_copy(arr, s, d, k).wait_send()
                    for k in range(chips):
                        k_copy(arr, s, d, k, core).wait_send()
                        k_copy(arr, s, d, k, 1 - core).wait_recv()


def gather_weights(C, F, wa, wo, tab):
    ra, ca = wa.shape
    ro, co = wo.shape
    chips = C // 2
    dma = pltpu.SemaphoreType.DMA
    return pl.pallas_call(
        functools.partial(gather_body, C, F),
        out_shape=(
            jax.ShapeDtypeStruct((F * ra, ca), wa.dtype),
            jax.ShapeDtypeStruct((ro, F * co), wo.dtype),
            jax.ShapeDtypeStruct((F,) + tab.shape, tab.dtype),
        ),
        in_specs=[ANY] * 3,
        out_specs=[ANY] * 3,
        scratch_shapes=[
            dma((3,)), dma((2, F, 2)), dma((2, F, 2)),
            dma((2, F, chips, 2)), dma((2, F, chips, 2)),
            dma((2, F, chips, 2)), dma((2, F, chips, 2)),
            dma((F,)), dma((F,)),
        ],
        compiler_params=params(1, 16),
    )(wa, wo, tab)


def slab_place(C, T):
    c, f, t = place()
    return c, f, t, c * T + t


def slab_device(index, f, T):
    return (lax.div(index, T), f, lax.rem(index, T))


def dispatch_body(C, F, T, tabbed, rows, select, *refs):
    if tabbed:
        tab, out, zbuf, ftab, stage, loc, zs, zr, ss, sr, ts, tr = refs
    else:
        out, zbuf, stage, loc, zs, zr, ss, sr = refs
    c, f, t, me = slab_place(C, T)
    S = C * T
    K = select.shape[2]
    copies = select.shape[3] // rows.shape[0]
    columns = [(c, lax.rem(f + k, F), t) for k in range(1, F)]
    greet(columns + [slab_device(lax.rem(me + j, S), f, T) for j in range(1, S)])
    sends = [
        remote(rows, zbuf.at[f], zs.at[k], zr.at[k], columns[k - 1]) for k in range(1, F)
    ]
    if tabbed:
        tabs = [remote(tab, ftab.at[f], ts.at[k], tr.at[k], columns[k - 1]) for k in range(1, F)]
        for copy in tabs:
            copy.start()
        ftab[f] = tab[...]
    for copy in sends:
        copy.start()
    zbuf[f] = rows[...]

    def slab_copy(k, j):
        b = lax.rem(f + F - k, F)
        e = lax.rem(me + j, S)
        return remote(
            stage.at[e, b], out.at[me, b], ss.at[k, j], sr.at[k, j], slab_device(e, f, T)
        )

    def slab_arrival(k, j):
        b = lax.rem(f + F - k, F)
        e = lax.rem(me + S - j, S)
        return remote(
            stage.at[e, b], out.at[e, b], ss.at[k, j], sr.at[k, j], slab_device(e, f, T)
        )

    def own_copy(k):
        b = lax.rem(f + F - k, F)
        return pltpu.make_async_copy(stage.at[me, b], out.at[me, b], loc.at[k])

    for k in range(F):
        b = lax.rem(f + F - k, F)
        if k > 0:
            remote(rows, zbuf.at[b], zs.at[k], zr.at[k], columns[k - 1]).wait_recv()

        def pick(j):
            e = lax.rem(me + j, S)
            block = zbuf[b]
            if copies > 1:
                block = jnp.concatenate([block] * copies, axis=0)
            stage[e, b] = jnp.dot(
                select[b, e], block, preferred_element_type=FL
            ).astype(BF)

        if S <= 8:
            for j in range(1, S):
                pick(j)
                slab_copy(k, j).start()
        else:

            def step(j, carry):
                pick(j)
                slab_copy(k, j).start()
                return carry

            lax.fori_loop(1, S, step, 0)
        pick(0)
        own_copy(k).start()
    if tabbed:
        for copy in tabs:
            copy.wait()
    for copy in sends:
        copy.wait_send()
    for k in range(F):
        own_copy(k).wait()

        def settle(j, carry):
            slab_copy(k, j).wait_send()
            slab_arrival(k, j).wait_recv()
            return carry

        lax.fori_loop(1, S, settle, 0)


def dispatch(identity, C, F, T, rows, select, tab=None):
    S = C * T
    K = select.shape[2]
    R, W = rows.shape
    dma = pltpu.SemaphoreType.DMA
    tabbed = tab is not None
    outs = [jax.ShapeDtypeStruct((S, F, K, W), BF), jax.ShapeDtypeStruct((F, R, W), BF)]
    out_specs = [ANY, VMEM]
    ins = [rows, select]
    scratch = [
        pltpu.VMEM((S, F, K, W), BF), dma((F,)), dma((F,)), dma((F,)), dma((F, S)), dma((F, S)),
    ]
    if tabbed:
        outs.append(jax.ShapeDtypeStruct((F,) + tab.shape, tab.dtype))
        out_specs.append(VMEM)
        ins.append(tab)
        scratch += [dma((F,)), dma((F,))]
    return pl.pallas_call(
        functools.partial(dispatch_body, C, F, T, tabbed),
        out_shape=tuple(outs),
        in_specs=[VMEM] * len(ins),
        out_specs=out_specs,
        scratch_shapes=scratch,
        compiler_params=params(identity, 32),
    )(*ins)


def combine_body(C, F, T, tabbed, rows, weigh, *refs):
    if tabbed:
        tab, got, part, ftab, stage, loc, zs, zr, ss, sr, ts, tr = refs
    else:
        got, part, stage, loc, zs, zr, ss, sr = refs
    c, f, t, me = slab_place(C, T)
    S = C * T
    K, W = got.shape[2], got.shape[3]
    n = weigh.shape[1]
    columns = [(c, lax.rem(f + k, F), t) for k in range(1, F)]
    greet(columns + [slab_device(lax.rem(me + j, S), f, T) for j in range(1, S)])

    def slab_copy(k, j):
        b = lax.rem(f + k, F)
        e = lax.rem(me + j, S)
        return remote(
            rows.at[e, b], got.at[b, me], ss.at[k, j], sr.at[k, j], slab_device(e, f, T)
        )

    def slab_arrival(k, j):
        b = lax.rem(f + k, F)
        e = lax.rem(me + S - j, S)
        return remote(
            rows.at[e, b], got.at[b, e], ss.at[k, j], sr.at[k, j], slab_device(e, f, T)
        )

    def own_copy(k):
        b = lax.rem(f + k, F)
        return pltpu.make_async_copy(rows.at[me, b], got.at[b, me], loc.at[k])

    order = list(range(1, F)) + [0]
    for k in order:

        def begin(j, carry):
            slab_copy(k, j).start()
            return carry

        lax.fori_loop(1, S, begin, 0)
        own_copy(k).start()
    if tabbed:
        tabs = [
            remote(tab.at[lax.rem(f + k, F)], ftab.at[f], ts.at[k], tr.at[k], columns[k - 1])
            for k in range(1, F)
        ]
        for copy in tabs:
            copy.start()
        ftab[f] = tab[f]

    def z_copy(k):
        b = lax.rem(f + k, F)
        return remote(stage.at[b], part.at[f], zs.at[k], zr.at[k], columns[k - 1])

    def z_arrival(k):
        b = lax.rem(f + F - k, F)
        return remote(stage.at[b], part.at[b], zs.at[k], zr.at[k], columns[k - 1])

    step = min(W, 512)
    for k in order:
        b = lax.rem(f + k, F)
        own_copy(k).wait()

        def settle(j, carry):
            slab_arrival(k, j).wait_recv()
            return carry

        lax.fori_loop(1, S, settle, 0)
        target = part if k == 0 else stage

        def add(i, carry):
            columns_ = pl.ds(pl.multiple_of(i * step, step), step)
            block = got[b, :, :, columns_].reshape(S * K, step)
            total = jnp.dot(weigh[b, 0], block, preferred_element_type=FL)
            for m in range(1, n):
                total += jnp.dot(weigh[b, m], block, preferred_element_type=FL)
            target[b, :, columns_] = total.astype(BF)
            return carry

        lax.fori_loop(0, W // step, add, 0)
        if k > 0:
            z_copy(k).start()
    for k in range(1, F):
        z_copy(k).wait_send()
        z_arrival(k).wait_recv()
    for k in range(F):

        def leave(j, carry):
            slab_copy(k, j).wait_send()
            return carry

        lax.fori_loop(1, S, leave, 0)
    if tabbed:
        for copy in tabs:
            copy.wait()


def combine(identity, C, F, T, rows, weigh, tab=None):
    S, _, K, W = rows.shape
    R = weigh.shape[2]
    dma = pltpu.SemaphoreType.DMA
    tabbed = tab is not None
    outs = [jax.ShapeDtypeStruct((F, S, K, W), BF), jax.ShapeDtypeStruct((F, R, W), BF)]
    ins = [rows, weigh]
    scratch = [
        pltpu.VMEM((F, R, W), BF), dma((F,)), dma((F,)), dma((F,)), dma((F, S)), dma((F, S)),
    ]
    if tabbed:
        outs.append(jax.ShapeDtypeStruct(tab.shape, tab.dtype))
        ins.append(tab)
        scratch += [dma((F,)), dma((F,))]
    return pl.pallas_call(
        functools.partial(combine_body, C, F, T, tabbed),
        out_shape=tuple(outs),
        in_specs=[ANY] + [VMEM] * (len(ins) - 1),
        out_specs=[VMEM] * len(outs),
        scratch_shapes=scratch,
        compiler_params=params(identity, 32),
    )(*ins)


def ctx_sum_body(C, x, out, got, ss, sr):
    c, f, t = place()
    peers = [(lax.rem(c + k, C), f, t) for k in range(1, C)]
    greet(peers)

    def copy(k):
        p = lax.rem(c + k, C)
        return remote(x.at[p], got.at[c], ss.at[k], sr.at[k], (p, f, t))

    def arrival(k):
        p = lax.rem(c + C - k, C)
        return remote(x.at[p], got.at[p], ss.at[k], sr.at[k], (p, f, t))

    for k in range(1, C):
        copy(k).start()
    got[c] = x[c]
    for k in range(1, C):
        arrival(k).wait_recv()
    total = got[0].astype(FL)
    for p in range(1, C):
        total += got[p].astype(FL)
    out[...] = total
    for k in range(1, C):
        copy(k).wait_send()


def ctx_sum(identity, C, x):
    dma = pltpu.SemaphoreType.DMA
    return pl.pallas_call(
        functools.partial(ctx_sum_body, C),
        out_shape=jax.ShapeDtypeStruct(x.shape[1:], FL),
        in_specs=[VMEM],
        out_specs=VMEM,
        scratch_shapes=[pltpu.VMEM(x.shape, x.dtype), dma((C,)), dma((C,))],
        compiler_params=params(identity, 24),
    )(x)


def small_body(C, F, T, x, out, zgot, mid, sgot, zs, zr, ss, sr):
    c, f, t, me = slab_place(C, T)
    S = C * T
    columns = [(c, lax.rem(f + k, F), t) for k in range(1, F)]
    greet(columns + [slab_device(lax.rem(me + j, S), f, T) for j in range(1, S)])

    def z_copy(k):
        return remote(x.at[lax.rem(f + k, F)], zgot.at[f], zs.at[k], zr.at[k], columns[k - 1])

    def z_arrival(k):
        b = lax.rem(f + F - k, F)
        return remote(x.at[b], zgot.at[b], zs.at[k], zr.at[k], columns[k - 1])

    for k in range(1, F):
        z_copy(k).start()
    zgot[f] = x[f]
    for k in range(1, F):
        z_arrival(k).wait_recv()
    total = zgot[0]
    for b in range(1, F):
        total += zgot[b]
    mid[...] = total
    sgot[me] = total

    def s_copy(j):
        return remote(
            mid, sgot.at[me], ss.at[j], sr.at[j], slab_device(lax.rem(me + j, S), f, T)
        )

    def s_arrival(j):
        e = lax.rem(me + S - j, S)
        return remote(mid, sgot.at[e], ss.at[j], sr.at[j], slab_device(e, f, T))

    for j in range(1, S):
        s_copy(j).start()
    for j in range(1, S):
        s_arrival(j).wait_recv()
    total = sgot[0]
    for e in range(1, S):
        total += sgot[e]
    out[...] = total
    for k in range(1, F):
        z_copy(k).wait_send()
    for j in range(1, S):
        s_copy(j).wait_send()


def small_sum(identity, C, F, T, x):
    dma = pltpu.SemaphoreType.DMA
    S = C * T
    one = x.shape[1:]
    return pl.pallas_call(
        functools.partial(small_body, C, F, T),
        out_shape=jax.ShapeDtypeStruct(one, FL),
        in_specs=[VMEM],
        out_specs=VMEM,
        scratch_shapes=[
            pltpu.VMEM((F,) + one, FL), pltpu.VMEM(one, FL), pltpu.VMEM((S,) + one, FL),
            dma((F,)), dma((F,)), dma((S,)), dma((S,)),
        ],
        compiler_params=params(identity, 24),
    )(x)


def far_first(F):
    table = []
    for f in range(F):
        order = []
        for i in range(F):
            ends = [F - 1 - i, i] if f * 2 < F else [i, F - 1 - i]
            for b in ends:
                if ((b > f and b == F - 1 - i) or (b < f and b == i)) and b not in order:
                    order.append(b)
        table.append(order + [f])
    return table


def grads_body(
    C, F, xt, da, ht, dt, outa, outo,
    ska, sko, rka, rko, sya, syo, rya, ryo, rza, rzo, sza, szo,
    k_s, k_r, y_s, y_r, z_s, z_r, g_s, g_r, h_s, h_r,
):
    c, f, t = place()
    core, chip = lax.rem(c, 2), lax.div(c, 2)
    chips = C // 2
    sib = c + 1 - 2 * core
    pa, po, co = outa.shape[1], outo.shape[1], outo.shape[2]
    ra = pa * C
    table = far_first(F)

    def block(q):
        value = jnp.int32(table[0][q])
        for g in range(1, F):
            value = jnp.where(f == g, table[g][q], value)
        return value

    blocks = [block(q) for q in range(F)]
    ends = [(c, lax.rem(f + 1, F), t), (c, lax.rem(f + F - 1, F), t)]
    mates = [(lax.rem(chip + k, chips) * 2 + core, f, t) for k in range(1, chips)]
    greet(ends + mates + [(sib, f, t)])

    def piece_a(b, p):
        rows = pl.ds(pl.multiple_of(b * ra + p * pa, pa), pa)
        return jnp.dot(xt[rows, :], da[...], preferred_element_type=FL)

    def piece_o(b, p):
        rows = pl.ds(pl.multiple_of(p * po, po), po)
        cols = pl.ds(pl.multiple_of(b * co, co), co)
        return jnp.dot(ht[rows, :], dt[:, cols], preferred_element_type=FL)

    def core_copies(q, k):
        b = blocks[q]
        return [
            remote(ska.at[b, k], rka.at[b, k], k_s.at[q, k, 0], k_r.at[q, k, 0], (sib, f, t)),
            remote(sko.at[b, k], rko.at[b, k], k_s.at[q, k, 1], k_r.at[q, k, 1], (sib, f, t)),
        ]

    for q in range(F):
        b = blocks[q]
        for k in [*range(1, chips), 0]:
            p = lax.rem(chip + k, chips) * 2 + 1 - core
            ska[b, k] = piece_a(b, p).astype(BF)
            sko[b, k] = piece_o(b, p).astype(BF)
            for copy in core_copies(q, k):
                copy.start()

    def chip_copies(q, k):
        b = blocks[q]
        there = mates[k - 1]
        return [
            remote(sya.at[b, k - 1], rya.at[b, k - 1], y_s.at[q, k, 0], y_r.at[q, k, 0], there),
            remote(syo.at[b, k - 1], ryo.at[b, k - 1], y_s.at[q, k, 1], y_r.at[q, k, 1], there),
        ]

    for q in range(F):
        b = blocks[q]
        for k in range(1, chips):
            p = lax.rem(chip + k, chips) * 2 + core
            for copy in core_copies(q, k):
                copy.wait_recv()
            sya[b, k - 1] = (piece_a(b, p) + rka[b, k].astype(FL)).astype(BF)
            syo[b, k - 1] = (piece_o(b, p) + rko[b, k].astype(FL)).astype(BF)
            for copy in chip_copies(q, k):
                copy.start()

    def z_copies(q, b, slot, there):
        return [
            remote(sza.at[b], rza.at[slot], z_s.at[q, 0], z_r.at[slot, 0], there),
            remote(szo.at[b], rzo.at[slot], z_s.at[q, 1], z_r.at[slot, 1], there),
        ]

    def z_wait(slot):
        for copy in z_copies(0, 0, slot, ends[0]):
            copy.wait_recv()

    for q in range(F):
        b = blocks[q]
        for copy in core_copies(q, 0):
            copy.wait_recv()
        for k in range(1, chips):
            for copy in chip_copies(q, k):
                copy.wait_recv()
        total_a = piece_a(b, c) + rka[b, 0].astype(FL)
        total_o = piece_o(b, c) + rko[b, 0].astype(FL)
        for k in range(1, chips):
            total_a += rya[b, k - 1].astype(FL)
            total_o += ryo[b, k - 1].astype(FL)
        if q < F - 1:
            up = b > f
            first = jnp.where(up, f == 0, f == F - 1)

            @pl.when(first)
            def _():
                sza[b] = total_a.astype(BF)
                szo[b] = total_o.astype(BF)

            @pl.when(jnp.logical_not(first))
            def _():
                z_wait(b)
                sza[b] = (total_a + rza[b].astype(FL)).astype(BF)
                szo[b] = (total_o + rzo[b].astype(FL)).astype(BF)

            @pl.when(up)
            def _():
                for copy in z_copies(q, b, b, (c, f + 1, t)):
                    copy.start()

            @pl.when(jnp.logical_not(up))
            def _():
                slot = jnp.where(b == f - 1, F, b)
                for copy in z_copies(q, b, slot, (c, f - 1, t)):
                    copy.start()

        else:
            sza[f] = total_a.astype(BF)
            szo[f] = total_o.astype(BF)

            @pl.when(f > 0)
            def _():
                z_wait(f)
                sza[f] = (total_a + rza[f].astype(FL)).astype(BF)
                szo[f] = (total_o + rzo[f].astype(FL)).astype(BF)

            @pl.when(f < F - 1)
            def _():
                z_wait(F)
                outa[c] = (sza[f].astype(FL) + rza[F].astype(FL)).astype(BF)
                outo[c] = (szo[f].astype(FL) + rzo[F].astype(FL)).astype(BF)

            @pl.when(f == F - 1)
            def _():
                outa[c] = sza[f]
                outo[c] = szo[f]

    def spread(k):
        there = mates[k - 1]
        return [
            remote(outa.at[c], outa.at[c], g_s.at[k, 0], g_r.at[k, 0], there),
            remote(outo.at[c], outo.at[c], g_s.at[k, 1], g_r.at[k, 1], there),
        ]

    def hand(k, side):
        p = lax.rem(chip + chips - k, chips) * 2 + side
        return [
            remote(outa.at[p], outa.at[p], h_s.at[k, 0], h_r.at[k, 0], (sib, f, t)),
            remote(outo.at[p], outo.at[p], h_s.at[k, 1], h_r.at[k, 1], (sib, f, t)),
        ]

    def spread_arrival(k):
        p = lax.rem(chip + chips - k, chips) * 2 + core
        return [
            remote(outa.at[p], outa.at[p], g_s.at[k, 0], g_r.at[k, 0], mates[k - 1]),
            remote(outo.at[p], outo.at[p], g_s.at[k, 1], g_r.at[k, 1], mates[k - 1]),
        ]

    for k in range(1, chips):
        for copy in spread(k):
            copy.start()
    for copy in hand(0, core):
        copy.start()
    for k in range(1, chips):
        for copy in spread_arrival(k):
            copy.wait_recv()
        for copy in hand(k, core):
            copy.start()
    for k in range(chips):
        for copy in hand(k, 1 - core):
            copy.wait_recv()
        for copy in hand(k, core):
            copy.wait_send()
    for k in range(1, chips):
        for copy in spread(k):
            copy.wait_send()
    for q in range(F):
        for k in range(chips):
            for copy in core_copies(q, k):
                copy.wait_send()
        for k in range(1, chips):
            for copy in chip_copies(q, k):
                copy.wait_send()
        if q < F - 1:
            for copy in z_copies(q, 0, 0, ends[0]):
                copy.wait_send()


def weight_grads(identity, C, F, xt, da, ht, dt):
    D, R = xt.shape
    pa, na = D // F // C, da.shape[1]
    po, no = ht.shape[0] // C, dt.shape[1] // F
    chips = C // 2
    dma = pltpu.SemaphoreType.DMA

    def pair(*lead):
        return [pltpu.VMEM(lead + (pa, na), BF), pltpu.VMEM(lead + (po, no), BF)]

    return pl.pallas_call(
        functools.partial(grads_body, C, F),
        out_shape=(
            jax.ShapeDtypeStruct((C, pa, na), BF),
            jax.ShapeDtypeStruct((C, po, no), BF),
        ),
        in_specs=[VMEM] * 4,
        out_specs=[VMEM] * 2,
        scratch_shapes=[
            *pair(F, chips), *pair(F, chips), *pair(F, chips - 1), *pair(F, chips - 1),
            *pair(F + 1), *pair(F),
            dma((F, chips, 2)), dma((F, chips, 2)), dma((F, chips, 2)), dma((F, chips, 2)),
            dma((F, 2)), dma((F + 1, 2)), dma((chips, 2)), dma((chips, 2)),
            dma((chips, 2)), dma((chips, 2)),
        ],
        compiler_params=params(identity, 60),
    )(xt, da, ht, dt)


def tail_body(
    C, F, T, KH,
    grad_own, heads, normed, qrot, kv, keys_t, raw, lse, bias, cosf, sins, qgain, kgain, again,
    own_in, resid_in, router, vec_in, fo, fall,
    gin, outa, outo, small,
    wbuf, dall, nall, hq, rq, dheads, draw, dk, dv, ksend, kgot, gains, nsend, ngot, nown,
    sza, szo, rza, rzo, smx, zgot, mid, sgot,
    wsem, xs, xr, as_, ar, hs, hr, ds_, dr, rs, rr, z_s, z_r, ts, tr, us, ur,
):
    c, f, t, me = slab_place(C, T)
    S = C * T
    R, QC = heads.shape
    W = normed.shape[1]
    PC = raw.shape[1]
    L = kv.shape[1]
    HS = qgain.shape[1]
    QH = QC // HS
    G = QH // KH
    Rh = grad_own.shape[0]
    KC = KH * HS
    pa = rq.shape[2]
    po = hq.shape[2]
    rows_a, cols_o = outa.shape[1], outo.shape[2]
    root = HS ** (-0.5)
    core = lax.rem(c, 2)
    sib = c + 1 - 2 * core
    mate = lax.rem(c + 2, C)
    mate_sib = lax.rem(sib + 2, C)
    table = far_first(F)

    def block(q):
        value = jnp.int32(table[0][q])
        for g in range(1, F):
            value = jnp.where(f == g, table[g][q], value)
        return value

    blocks = [block(q) for q in range(F)]
    columns = [(c, lax.rem(f + k, F), t) for k in range(1, F)]
    greet(columns + [slab_device(lax.rem(me + j, S), f, T) for j in range(1, S)])
    at_t = pl.ds(pl.multiple_of(t * Rh, Rh), Rh)
    at_u = pl.ds(pl.multiple_of((1 - t) * Rh, Rh), Rh)
    beside = (c, f, 1 - t)

    load_o = pltpu.make_async_copy(fo, wbuf.at[:, pl.ds(0, W)], wsem.at[0])
    load_o.start()

    swap_d = remote(grad_own, dall.at[c, at_t], xs.at[0], xr.at[0], beside)
    swap_d_in = remote(grad_own, dall.at[c, at_u], xs.at[0], xr.at[0], beside)
    swap_n = remote(nsend, ngot, xs.at[1], xr.at[1], beside)

    def spread(buf, n, i):
        here = buf.at[mate] if i == 2 else buf.at[c]
        there = (mate if i == 0 else sib, f, t)
        return remote(here, here, as_.at[n, i], ar.at[n, i], there)

    def spread_in(buf, n, i):
        here = buf.at[(mate, sib, mate_sib)[i]]
        return remote(here, here, as_.at[n, i], ar.at[n, i], (sib, f, t))

    def spread_start(buf, n):
        spread(buf, n, 0).start()
        spread(buf, n, 1).start()

    def spread_pass(buf, n):
        spread_in(buf, n, 0).wait_recv()
        spread(buf, n, 2).start()

    def spread_end(buf, n):
        spread_in(buf, n, 1).wait_recv()
        spread_in(buf, n, 2).wait_recv()

    def spread_sent(buf, n):
        for i in range(3):
            spread(buf, n, i).wait_send()

    def chunk_copies(source, target, ss, sr):
        out, come = [], []
        for k in range(1, C):
            p, o = lax.rem(c + k, C), lax.rem(c + C - k, C)
            out.append(remote(source(p), target(c), ss.at[k], sr.at[k], (p, f, t)))
            come.append(remote(source(o), target(o), ss.at[k], sr.at[k], (o, f, t)))
        return out, come

    def lane(p, n):
        return pl.ds(pl.multiple_of(p * n, n), n)

    heads_out, heads_come = chunk_copies(
        lambda p: heads.at[:, lane(p, po)], lambda o: hq.at[o], hs, hr
    )
    kv_moves = [
        chunk_copies(lambda p, g=g: ksend.at[g, p], lambda o, g=g: kgot.at[g, o], ds_.at[g], dr.at[g])
        for g in range(KH)
    ]
    raw_out, raw_come = chunk_copies(
        lambda p: draw.at[:, lane(p, pa)], lambda o: rq.at[o], rs, rr
    )

    swap_d.start()
    for copy in heads_out:
        copy.start()
    dall[c, at_t] = grad_own[...]
    nall[c] = normed[...]
    spread_start(nall, 0)
    hq[c] = heads[:, lane(c, po)]
    swap_d_in.wait_recv()
    spread_start(dall, 1)

    load_o.wait()
    step = min(512, QC)

    def head_grads(i, carry):
        at = lane(i, step)
        dheads[:, at] = outer_cols(dall[c], wbuf[at, pl.ds(0, W)]).astype(BF)
        return carry

    lax.fori_loop(0, QC // step, head_grads, 0)
    load_w = pltpu.make_async_copy(fall.at[:, pl.ds(0, PC)], wbuf, wsem.at[1])
    load_w.start()

    def unturn(values):
        return values * cosf[...] - pltpu.roll(values, HS // 2, 1) * sins[...]

    def norm_grads(values, gain_vec, upstream):
        factor = lax.rsqrt(jnp.mean(values * values, axis=-1, keepdims=True) + EPS)
        out, terms = norm_back(values, factor, gain_vec, upstream)
        return out, jnp.sum(terms, axis=0, keepdims=True)

    gains[...] = jnp.zeros_like(gains)
    key_step = min(L, 512)
    for g in range(KH):
        dk[...] = jnp.zeros_like(dk)
        dv[...] = jnp.zeros_like(dv)

        def one_head(i, carry):
            h = g * G + i
            at = lane(h, HS)
            q_head, o_grad = qrot[:, at], dheads[:, at]
            product = o_grad.astype(FL) * heads[:, at].astype(FL)
            delta = jnp.sum(product.T, axis=0, keepdims=True)
            row = lse[pl.ds(h, 1), :]
            q_grad = jnp.zeros((HS, R), FL)
            for j in range(L // key_step):
                ks = pl.ds(j * key_step, key_step)
                scores = outer_cols(kv[g, ks, :], q_head) * root
                probs = jnp.exp(scores + bias[ks, :] - row)
                d_probs = outer_cols(kv[KH + g, ks, :], o_grad)
                d_scores = (probs * (d_probs - delta)).astype(BF)
                dv[ks, :] += jnp.dot(probs.astype(BF), o_grad, preferred_element_type=FL)
                dk[ks, :] += jnp.dot(d_scores, q_head, preferred_element_type=FL)
                q_grad += jnp.dot(keys_t[g, :, ks], d_scores, preferred_element_type=FL)
            q_back, terms = norm_grads(raw[:, at], qgain[...], unturn(q_grad.T * root))
            draw[:, at] = q_back.astype(BF)
            gains[0:1, :] += terms
            return carry

        lax.fori_loop(0, G, one_head, 0)
        for p in range(C):
            at = pl.ds(p * R, R)
            ksend[g, p, :, 0:HS] = (dk[at, :] * root).astype(BF)
            ksend[g, p, :, HS : 2 * HS] = dv[at, :].astype(BF)
        for copy in kv_moves[g][0]:
            copy.start()
        kgot[g, c] = ksend[g, c]
        if g == 0:
            spread_pass(nall, 0)
            spread_pass(dall, 1)
    if KH == 0:
        spread_pass(nall, 0)

    for copy in heads_come:
        copy.wait_recv()
    spread_end(dall, 1)

    def piece_o(b):
        return inner_rows(
            hq[...].reshape(C * R, po), dall[:, :, lane(b, cols_o)].reshape(C * R, cols_o)
        )

    def piece_a(b):
        return inner_rows(
            nall[:, :, lane(b, rows_a)].reshape(C * R, rows_a), rq[...].reshape(C * R, pa)
        )

    pieces = ((piece_o, szo, rzo, outo), (piece_a, sza, rza, outa))
    end = (f == 0) | (f == F - 1)

    def z_out(n, q):
        b = blocks[q]
        _, send, got, _ = pieces[n]
        return remote(send.at[b], got.at[b], z_s.at[n, q], z_r.at[n, b], (c, f + 1, t))

    def z_down(n, q):
        b = blocks[q]
        slot = jnp.where(b == f - 1, F, b)
        _, send, got, _ = pieces[n]
        return remote(send.at[b], got.at[slot], z_s.at[n, q], z_r.at[n, slot], (c, f - 1, t))

    def z_wait(n, slot):
        _, send, got, _ = pieces[n]
        remote(send.at[0], got.at[slot], z_s.at[n, 0], z_r.at[n, slot], (c, f, t)).wait_recv()

    def z_send(n, q):
        up = blocks[q] > f

        @pl.when(up)
        def _():
            z_out(n, q).start()

        @pl.when(jnp.logical_not(up))
        def _():
            z_down(n, q).start()

    def z_first(n):
        fn, send, _, _ = pieces[n]

        @pl.when(end)
        def _():
            for q in range(F - 1):
                send[blocks[q]] = fn(blocks[q]).astype(BF)
                z_send(n, q)

    def z_relay(n, q):
        fn, send, got, _ = pieces[n]

        @pl.when(jnp.logical_not(end))
        def _():
            b = blocks[q]
            z_wait(n, b)
            send[b] = (fn(b) + got[b].astype(FL)).astype(BF)
            z_send(n, q)

    def z_last(n):
        fn, send, got, out = pieces[n]
        send[f] = fn(f).astype(BF)

        @pl.when(f > 0)
        def _():
            z_wait(n, f)
            send[f] = (send[f].astype(FL) + got[f].astype(FL)).astype(BF)

        @pl.when(f < F - 1)
        def _():
            z_wait(n, F)
            out[c] = (send[f].astype(FL) + got[F].astype(FL)).astype(BF)

        @pl.when(f == F - 1)
        def _():
            out[c] = send[f]

    z_first(0)

    for g in range(KH):
        for copy in kv_moves[g][1]:
            copy.wait_recv()
        total = kgot[g, 0].astype(FL)
        for p in range(1, C):
            total += kgot[g, p].astype(FL)
        k_cols = slice(QC + g * HS, QC + (g + 1) * HS)
        k_back, terms = norm_grads(raw[:, k_cols], kgain[...], unturn(total[:, :HS]))
        draw[:, k_cols] = k_back.astype(BF)
        draw[:, QC + KC + g * HS : QC + KC + (g + 1) * HS] = total[:, HS:].astype(BF)
        gains[1:2, :] += terms
    for copy in raw_out:
        copy.start()
    rq[c] = draw[:, lane(c, pa)]
    load_w.wait()
    width_step = min(512, W)

    def norm_theirs(i, carry):
        at = lane(i, width_step)
        nsend[:, at] = outer_cols(draw[at_u, :], wbuf[at, :]).astype(BF)
        return carry

    lax.fori_loop(0, W // width_step, norm_theirs, 0)
    swap_n.start()

    def norm_ours(i, carry):
        at = lane(i, width_step)
        nown[:, at] = outer_cols(draw[at_t, :], wbuf[at, :])
        return carry

    lax.fori_loop(0, W // width_step, norm_ours, 0)

    spread_end(nall, 0)
    for copy in raw_come:
        copy.wait_recv()
    z_first(1)
    z_relay(0, 0)
    z_relay(1, 0)

    swap_n.wait_recv()
    upstream = nown[...] + ngot[...].astype(FL)
    values = own_in[...]
    factor = lax.rsqrt(jnp.mean(values * values, axis=-1, keepdims=True) + EPS)
    back, terms = norm_back(values, factor, again[...], upstream)
    gin[...] = resid_in[...] + back
    for b in range(F):
        smx[b, 0 : router.shape[1]] = router[b]
        at = router.shape[1]
        smx[b, at : at + 8] = vec_in[...]
        smx[b, at : at + 1] = jnp.sum(terms, axis=0, keepdims=True)
        smx[b, at + 2 : at + 3, 0:HS] = gains[0:1, :]
        smx[b, at + 2 : at + 3, HS : 2 * HS] = gains[1:2, :]

    def t_copy(k):
        return remote(smx.at[lax.rem(f + k, F)], zgot.at[f], ts.at[k], tr.at[k], columns[k - 1])

    def t_arrival(k):
        b = lax.rem(f + F - k, F)
        return remote(smx.at[b], zgot.at[b], ts.at[k], tr.at[k], columns[k - 1])

    for k in range(1, F):
        t_copy(k).start()
    zgot[f] = smx[f]
    for q in range(1, F - 1):
        z_relay(0, q)
        z_relay(1, q)
    for k in range(1, F):
        t_arrival(k).wait_recv()
    total = zgot[0]
    for b in range(1, F):
        total += zgot[b]
    mid[...] = total
    sgot[me] = total

    def u_copy(j):
        return remote(
            mid, sgot.at[me], us.at[j], ur.at[j], slab_device(lax.rem(me + j, S), f, T)
        )

    def u_arrival(j):
        e = lax.rem(me + S - j, S)
        return remote(mid, sgot.at[e], us.at[j], ur.at[j], slab_device(e, f, T))

    for j in range(1, S):
        u_copy(j).start()
    z_last(0)
    spread_start(outo, 2)
    z_last(1)
    spread_start(outa, 3)
    for j in range(1, S):
        u_arrival(j).wait_recv()
    total = sgot[0]
    for e in range(1, S):
        total += sgot[e]
    small[...] = total
    spread_pass(outo, 2)
    spread_pass(outa, 3)
    spread_end(outo, 2)
    spread_end(outa, 3)

    for buf, n in ((nall, 0), (dall, 1), (outo, 2), (outa, 3)):
        spread_sent(buf, n)
    swap_d.wait_send()
    swap_n.wait_send()
    for copy in heads_out + raw_out:
        copy.wait_send()
    for g in range(KH):
        for copy in kv_moves[g][0]:
            copy.wait_send()
    for n in range(2):
        for q in range(F - 1):
            z_out(n, q).wait_send()
    for k in range(1, F):
        t_copy(k).wait_send()
    for j in range(1, S):
        u_copy(j).wait_send()


def tail(identity, C, F, T, KH, args, D, po):
    grad_own, heads, normed, qrot, kv, keys_t, raw, lse, bias = args[:9]
    qgain = args[11]
    router, fall = args[16], args[19]
    R, QC = heads.shape
    W = normed.shape[1]
    PC = raw.shape[1]
    L = kv.shape[1]
    HS = qgain.shape[1]
    Rh = grad_own.shape[0]
    S = C * T
    pa = PC // C
    rows_a, cols_o = W // F, W // F
    small_shape = (router.shape[1] + 8, W)
    dma = pltpu.SemaphoreType.DMA
    V = pltpu.VMEM
    return pl.pallas_call(
        functools.partial(tail_body, C, F, T, KH),
        out_shape=(
            jax.ShapeDtypeStruct((Rh, W), FL),
            jax.ShapeDtypeStruct((C, rows_a, pa), BF),
            jax.ShapeDtypeStruct((C, po, cols_o), BF),
            jax.ShapeDtypeStruct(small_shape, FL),
        ),
        in_specs=[VMEM] * 18 + [ANY] * 2,
        out_specs=[VMEM] * 4,
        scratch_shapes=[
            V((W, PC), BF), V((C, R, W), BF), V((C, R, W), BF), V((C, R, po), BF),
            V((C, R, pa), BF), V((R, QC), BF), V((R, PC), BF), V((L, HS), FL), V((L, HS), FL),
            V((KH, C, R, 2 * HS), BF), V((KH, C, R, 2 * HS), BF), V((8, HS), FL),
            V((Rh, W), BF), V((Rh, W), BF), V((Rh, W), FL),
            V((F, rows_a, pa), BF), V((F, po, cols_o), BF),
            V((F + 1, rows_a, pa), BF), V((F + 1, po, cols_o), BF),
            V((F,) + small_shape, FL), V((F,) + small_shape, FL), V(small_shape, FL),
            V((S,) + small_shape, FL),
            dma((2,)), dma((2,)), dma((2,)), dma((4, 3)), dma((4, 3)), dma((C,)), dma((C,)),
            dma((KH, C)), dma((KH, C)), dma((C,)), dma((C,)),
            dma((2, F)), dma((2, F + 1)), dma((F,)), dma((F,)), dma((S,)), dma((S,)),
        ],
        compiler_params=params(identity, 62),
    )(*args)


def split_low(values):
    high = lax.reduce_precision(values, 8, 7)
    return high.astype(BF), (values - high).astype(BF)


def local(
    hidden_in,
    teacher,
    lengths,
    routes,
    attn_gain,
    w_query,
    w_key,
    w_value,
    w_output,
    query_gain,
    key_gain,
    ffn_gain,
    w_router,
    w_expert_in,
    w_expert_out,
):
    c, f, t = place()
    C, F, T = (lax.axis_size(axis) for axis in AXES)
    S = C * T
    row_count = hidden_in.shape[1]
    width = hidden_in.shape[2]
    half_rows = row_count // T
    head_size = query_gain.shape[0]
    inv_root = head_size ** (-0.5)
    bf_type = BF
    fl_type = FL

    expert_count = S * F
    lanes = -(-expert_count // 128) * 128
    route_ids = routes[0]
    top_count = route_ids.shape[1]
    capacity = max(2, half_rows * top_count * 3 // (2 * expert_count))
    cap = -(-capacity // 16) * 16
    expert_ids = jnp.arange(lanes, dtype=jnp.int32)
    named = jnp.any(route_ids[:, :, None] == expert_ids[None, None, :], axis=1)
    row_ids = jnp.arange(half_rows, dtype=jnp.int32)
    below = (row_ids[None, :] < row_ids[:, None]).astype(bf_type)
    earlier = jnp.dot(below, named.astype(bf_type), preferred_element_type=fl_type)
    rank_tab = jnp.where(named, earlier, -1.0)

    q_cols, kv_cols = w_query.shape[1], w_key.shape[1]
    w_all = jnp.concatenate(
        [w_query, w_key, w_value, jnp.pad(w_router, ((0, 0), (0, lanes - expert_count)))], axis=1
    )
    full_all, full_o, rank_z = gather_weights(C, F, w_all, w_output, rank_tab)
    proj_cols = q_cols + 2 * kv_cols
    full_qkv = full_all[:, :proj_cols]
    full_router = full_all[:, proj_cols : proj_cols + expert_count]

    def of_slab(table):
        picked = table[:, :, :expert_count].reshape(F, half_rows, C, F, T)
        return lax.dynamic_index_in_dim(picked, f, 3, keepdims=False).reshape(F, half_rows, S)

    rank_slab = of_slab(rank_z)
    slot_ids = jnp.arange(cap, dtype=fl_type)
    chosen_rows = rank_slab[:, :, :, None] == slot_ids
    chosen_slots = (
        jnp.transpose(rank_slab, (0, 2, 1))[:, :, None, :] == slot_ids[:, None]
    )

    q_heads = q_cols // head_size
    kv_heads = kv_cols // head_size
    group_size = q_heads // kv_heads
    inputs = hidden_in[0].astype(fl_type)
    normed, norm_factor = norm_rows(inputs, attn_gain)
    normed_low = normed.astype(bf_type)
    raw = jnp.dot(normed_low, full_qkv, preferred_element_type=fl_type)
    q_raw = raw[:, :q_cols].reshape(row_count, q_heads, head_size)
    k_raw = raw[:, q_cols : q_cols + kv_cols].reshape(row_count, kv_heads, head_size)
    values_low = raw[:, q_cols + kv_cols :].astype(bf_type).reshape(row_count, kv_heads, head_size)
    q_normed, q_factor = norm_rows(q_raw, query_gain)
    k_normed, k_factor = norm_rows(k_raw, key_gain)
    positions = c * row_count + jnp.arange(row_count, dtype=jnp.int32)
    cosine, sine_tab = rope_tables(positions, head_size)
    q_rot = rotate(q_normed, cosine, sine_tab).astype(bf_type)
    k_rot = rotate(k_normed, cosine, sine_tab).astype(bf_type)
    queries = jnp.transpose(q_rot.reshape(row_count, kv_heads, group_size, head_size), (1, 2, 0, 3))
    both = jnp.transpose(jnp.concatenate([k_rot, values_low], axis=1), (1, 0, 2))
    all_both = lax.all_gather(both, "ctx", axis=1, tiled=True)
    all_keys, all_values = all_both[:kv_heads], all_both[kv_heads:]
    total_len = all_keys.shape[1]
    block_len = min(1024, total_len)
    offsets = jnp.arange(total_len // block_len, dtype=jnp.int32) * block_len
    length = jnp.take(lengths, f)
    stat_shape = (kv_heads, group_size, row_count)

    def lse_step(carry, offset):
        running_max, running_sum = carry
        key_rows = lax.dynamic_slice_in_dim(all_keys, offset, block_len, 1)
        scores, allowed = block_scores(queries, key_rows, offset, positions, length, inv_root)
        new_max = jnp.maximum(running_max, jnp.max(scores, axis=-1))
        exponent = jnp.where(allowed, jnp.exp(scores - new_max[..., None]), 0.0)
        return (
            (new_max, running_sum * jnp.exp(running_max - new_max) + jnp.sum(exponent, axis=-1)),
            None,
        )

    (row_max, row_sum), _ = lax.scan(
        lse_step, (jnp.full(stat_shape, MASKED, fl_type), jnp.zeros(stat_shape, fl_type)), offsets
    )
    log_total = row_max + jnp.log(row_sum)

    def probs_of(offset):
        key_rows = lax.dynamic_slice_in_dim(all_keys, offset, block_len, 1)
        value_rows = lax.dynamic_slice_in_dim(all_values, offset, block_len, 1)
        scores, allowed = block_scores(queries, key_rows, offset, positions, length, inv_root)
        return (
            jnp.where(allowed, jnp.exp(scores - log_total[..., None]), 0.0),
            key_rows,
            value_rows,
        )

    def out_step(running, offset):
        probabilities, key_rows, value_rows = probs_of(offset)
        return (
            running
            + jnp.einsum(
                "kgqj,kjd->kgqd",
                probabilities.astype(bf_type),
                value_rows,
                preferred_element_type=fl_type,
            ),
            None,
        )

    attn_acc, _ = lax.scan(
        out_step, jnp.zeros((kv_heads, group_size, row_count, head_size), fl_type), offsets
    )
    heads_low = (
        jnp.transpose(attn_acc, (2, 0, 1, 3))
        .reshape(row_count, q_heads * head_size)
        .astype(bf_type)
    )
    swap = [(i, 1 - i) for i in range(T)]
    row_start = t * half_rows
    other_start = (1 - t) * half_rows
    heads_other = lax.dynamic_slice_in_dim(heads_low, other_start, half_rows, 0)
    heads_own = lax.dynamic_slice_in_dim(heads_low, row_start, half_rows, 0)
    theirs = jnp.dot(heads_other, full_o, preferred_element_type=fl_type).astype(bf_type)
    ours = lax.ppermute(theirs, "tp", swap)
    attn_rows = jnp.dot(heads_own, full_o, preferred_element_type=fl_type) + ours.astype(fl_type)
    own_inputs = lax.dynamic_slice_in_dim(inputs, row_start, half_rows, 0)
    own_factor = lax.dynamic_slice_in_dim(norm_factor, row_start, half_rows, 0)
    own_positions = lax.dynamic_slice_in_dim(positions, row_start, half_rows, 0)
    residual = own_inputs + attn_rows
    ffn_in, ffn_factor = norm_rows(residual, ffn_gain)
    ffn_low = ffn_in.astype(bf_type)
    logits = jnp.dot(ffn_low, full_router, preferred_element_type=fl_type)
    is_named = named[:, :expert_count]
    masked = jnp.where(is_named, logits, MASKED)
    shifted = jnp.where(is_named, jnp.exp(masked - jnp.max(masked, axis=-1, keepdims=True)), 0.0)
    gates = shifted / jnp.sum(shifted, axis=-1, keepdims=True)
    gate_tab = jnp.pad(gates, ((0, 0), (0, lanes - expert_count)))

    select = chosen_slots.astype(bf_type)
    received, _, gate_z = dispatch(2, C, F, T, ffn_low, select, gate_tab)
    expert_rows = received.reshape(-1, width)
    both_pre = jnp.dot(expert_rows, w_expert_in[0], preferred_element_type=fl_type)
    ff_width = w_expert_out.shape[1]
    gate_pre = both_pre[:, :ff_width]
    up_pre = both_pre[:, ff_width:]
    sigmoid_gate = jax.nn.sigmoid(gate_pre)
    silu_gate = gate_pre * sigmoid_gate
    mixed_low = (silu_gate * up_pre).astype(bf_type)
    expert_out = (
        jnp.dot(mixed_low, w_expert_out[0], preferred_element_type=fl_type)
        .astype(bf_type)
        .reshape(S, F, cap, width)
    )
    gate_slab = of_slab(gate_z)
    weigh = jnp.where(chosen_rows, gate_slab[..., None], 0.0).reshape(F, 1, half_rows, S * cap)
    weigh = jnp.concatenate(split_low(weigh), axis=1)
    returned, parts = combine(3, C, F, T, expert_out, weigh)
    output_f = residual + jnp.sum(parts.astype(fl_type), axis=0)
    count = jnp.sum(lengths).astype(fl_type)
    tokens_total = lengths.shape[0] * row_count * C
    valid = own_positions < length
    error = jnp.where(valid[:, None], output_f - teacher[0].astype(fl_type), 0.0)
    loss_part = jnp.sum(error * error)
    grad_out = error * (tokens_total / count)

    select_gates = jnp.where(
        chosen_slots, jnp.transpose(gate_slab, (0, 2, 1))[:, :, None, :], 0.0
    )
    select_gates = jnp.concatenate(split_low(select_gates), axis=-1)
    grad_recv, grad_out_z = dispatch(4, C, F, T, grad_out.astype(bf_type), select_gates)
    slot_grads = jnp.einsum("zskr,zrd->zskd", select, grad_out_z, preferred_element_type=fl_type)
    slot_gate = jnp.sum(slot_grads * returned.astype(fl_type), axis=-1)
    gate_grads = jnp.sum(jnp.where(chosen_rows, slot_gate[:, None, :, :], 0.0), axis=-1)
    gate_grads = jnp.pad(gate_grads, ((0, 0), (0, 0), (0, -S % 128)))

    grad_recv = grad_recv.reshape(-1, width)
    grad_mixed = outer_cols(grad_recv, w_expert_out[0])
    grad_expert_out = inner_rows(mixed_low, grad_recv)
    grad_gate_pre = grad_mixed * up_pre * (sigmoid_gate * (1.0 + gate_pre * (1.0 - sigmoid_gate)))
    grad_up_pre = grad_mixed * silu_gate
    grad_pre = jnp.concatenate([grad_gate_pre, grad_up_pre], axis=1).astype(bf_type)
    grad_expert_in = inner_rows(expert_rows, grad_pre)
    grad_rows = (
        outer_cols(grad_pre, w_expert_in[0]).astype(bf_type).reshape(S, F, cap, width)
    )
    weigh_one = chosen_rows.astype(bf_type).reshape(F, 1, half_rows, S * cap)
    _, grad_parts, gate_back = combine(5, C, F, T, grad_rows, weigh_one, gate_grads)
    grad_gate = jnp.transpose(
        gate_back[:, :, :S].reshape(F, half_rows, C, T), (1, 2, 0, 3)
    ).reshape(half_rows, expert_count)
    grad_logits = (
        gates * (grad_gate - jnp.sum(gates * grad_gate, axis=-1, keepdims=True))
    ).astype(bf_type)
    grad_ffn = jnp.sum(grad_parts.astype(fl_type), axis=0) + outer_cols(grad_logits, full_router)
    router_part = inner_rows(ffn_low, grad_logits)
    grad_resid_norm, ffn_gain_terms = norm_back(residual, ffn_factor, ffn_gain, grad_ffn)
    grad_residual = grad_out + grad_resid_norm
    grad_own = grad_residual.astype(bf_type)
    if C == 4 and T == 2:
        cos_full = jnp.concatenate([cosine, cosine], axis=1)
        sin_signed = jnp.concatenate([-sine_tab, sine_tab], axis=1)
        key_pos = jnp.arange(total_len, dtype=jnp.int32)[:, None]
        bias = jnp.where((key_pos <= positions[None, :]) & (key_pos < length), 0.0, MASKED)
        vec_in = jnp.zeros((8, width), fl_type)
        vec_in = vec_in.at[1].set(jnp.sum(ffn_gain_terms, axis=0))
        vec_in = vec_in.at[2, 2 * head_size].set(loss_part)
        router_rows = router_part.reshape(F, -1, width)
        grad_input, total_a, total_o, summed = tail(
            9, C, F, T, kv_heads,
            (
                grad_own, heads_low, normed_low, q_rot.reshape(row_count, q_cols), all_both,
                jnp.swapaxes(all_keys, 1, 2), raw, log_total.reshape(q_heads, row_count), bias,
                cos_full, sin_signed, query_gain[None], key_gain[None], attn_gain[None],
                own_inputs, grad_residual, router_rows, vec_in, full_o, full_all,
            ),
            width, q_cols // C,
        )
        total_a = jnp.swapaxes(total_a, 0, 1).reshape(-1, proj_cols).astype(fl_type)
        grad_query = total_a[:, :q_cols]
        grad_key = total_a[:, q_cols : q_cols + kv_cols]
        grad_value = total_a[:, q_cols + kv_cols :]
        grad_output_w = total_o.reshape(w_output.shape).astype(fl_type)
        router_len = router_rows.shape[1]
        grad_router = summed[:router_len].reshape(w_router.shape)
        sum_attn, sum_ffn = summed[router_len], summed[router_len + 1]
        sum_query = summed[router_len + 2, :head_size]
        sum_key = summed[router_len + 2, head_size : 2 * head_size]
        loss_total = summed[router_len + 2, 2 * head_size]
    else:
        grad_other = lax.ppermute(grad_own, "tp", swap)
        grad_attn = jnp.where(
            t == 0,
            jnp.concatenate([grad_own, grad_other], axis=0),
            jnp.concatenate([grad_other, grad_own], axis=0),
        )
        grad_heads = jnp.transpose(
            outer_cols(grad_attn, full_o)
            .astype(bf_type)
            .reshape(row_count, kv_heads, group_size, head_size),
            (1, 2, 0, 3),
        )

        def delta_step(running, offset):
            probabilities, key_rows, value_rows = probs_of(offset)
            grad_weights = jnp.einsum(
                "kgqd,kjd->kgqj", grad_heads, value_rows, preferred_element_type=fl_type
            )
            return (running + jnp.sum(probabilities * grad_weights, axis=-1), None)

        delta, _ = lax.scan(delta_step, jnp.zeros(stat_shape, fl_type), offsets)

        def grad_step(running, offset):
            probabilities, key_rows, value_rows = probs_of(offset)
            grad_weights = jnp.einsum(
                "kgqd,kjd->kgqj", grad_heads, value_rows, preferred_element_type=fl_type
            )
            grad_scores = (probabilities * (grad_weights - delta[..., None])).astype(bf_type)
            running = (
                running
                + jnp.einsum("kgqj,kjd->kgqd", grad_scores, key_rows, preferred_element_type=fl_type)
                * inv_root
            )
            key_part = (
                jnp.einsum("kgqj,kgqd->kjd", grad_scores, queries, preferred_element_type=fl_type)
                * inv_root
            )
            value_part = jnp.einsum(
                "kgqj,kgqd->kjd",
                probabilities.astype(bf_type),
                grad_heads,
                preferred_element_type=fl_type,
            )
            return (running, (key_part, value_part))

        grad_qrot, (key_blocks, value_blocks) = lax.scan(
            grad_step, jnp.zeros((kv_heads, group_size, row_count, head_size), fl_type), offsets
        )
        both_grads = jnp.concatenate([key_blocks, value_blocks], axis=1).astype(bf_type)
        both_grads = jnp.transpose(both_grads, (0, 2, 1, 3)).reshape(C, row_count, 2 * kv_cols)
        both_sum = ctx_sum(6, C, both_grads)
        grad_krot = both_sum[:, :kv_cols].reshape(row_count, kv_heads, head_size)
        grad_values_low = both_sum[:, kv_cols:].astype(bf_type)
        grad_qrot = jnp.transpose(grad_qrot, (2, 0, 1, 3)).reshape(row_count, q_heads, head_size)
        grad_qraw, query_gain_terms = norm_back(
            q_raw, q_factor, query_gain, rotate(grad_qrot, cosine, -sine_tab)
        )
        grad_kraw, key_gain_terms = norm_back(
            k_raw, k_factor, key_gain, rotate(grad_krot, cosine, -sine_tab)
        )
        grad_raw = jnp.concatenate(
            [
                grad_qraw.astype(bf_type).reshape(row_count, -1),
                grad_kraw.astype(bf_type).reshape(row_count, -1),
                grad_values_low,
            ],
            axis=1,
        )
        raw_other = lax.dynamic_slice_in_dim(grad_raw, other_start, half_rows, 0)
        raw_own = lax.dynamic_slice_in_dim(grad_raw, row_start, half_rows, 0)
        norm_theirs = outer_cols(raw_other, full_qkv).astype(bf_type)
        norm_ours = lax.ppermute(norm_theirs, "tp", swap)
        grad_normed = outer_cols(raw_own, full_qkv) + norm_ours.astype(fl_type)
        grad_input_norm, attn_gain_terms = norm_back(own_inputs, own_factor, attn_gain, grad_normed)
        grad_input = grad_residual + grad_input_norm

        total_a, total_o = weight_grads(
            7, C, F, normed_low.T, grad_raw, heads_low.T, grad_attn
        )
        total_a = total_a.reshape(-1, proj_cols).astype(fl_type)
        grad_query = total_a[:, :q_cols]
        grad_key = total_a[:, q_cols : q_cols + kv_cols]
        grad_value = total_a[:, q_cols + kv_cols :]
        grad_output_w = total_o.reshape(w_output.shape).astype(fl_type)

        vector = jnp.concatenate(
            [
                jnp.sum(attn_gain_terms, axis=0),
                jnp.sum(ffn_gain_terms, axis=0),
                jnp.sum(query_gain_terms, axis=(0, 1)),
                jnp.sum(key_gain_terms, axis=(0, 1)),
                loss_part[None],
            ]
        )
        vector = jnp.pad(vector, (0, -vector.shape[0] % 1024)).reshape(-1, 128)
        router_rows = router_part.reshape(F, -1, 128)
        small = jnp.concatenate(
            [router_rows, jnp.broadcast_to(vector[None], (F,) + vector.shape)], axis=1
        )
        summed = small_sum(8, C, F, T, small)
        router_len = router_rows.shape[1]
        grad_router = summed[:router_len].reshape(w_router.shape)
        flat = summed[router_len:].reshape(-1)
        head_at = 2 * width
        sum_attn, sum_ffn = flat[:width], flat[width:head_at]
        sum_query = flat[head_at : head_at + head_size]
        sum_key = flat[head_at + head_size : head_at + 2 * head_size]
        loss_total = flat[head_at + 2 * head_size]
    loss_value = loss_total / (count * width)
    return (
        output_f.astype(bf_type)[None],
        loss_value,
        grad_input[None],
        sum_attn,
        grad_query,
        grad_key,
        grad_value,
        grad_output_w,
        sum_query,
        sum_key,
        sum_ffn,
        grad_router,
        grad_expert_in[None],
        grad_expert_out[None],
    )


def solution(mesh):
    return jax.shard_map(
        local,
        mesh=mesh,
        in_specs=(
            P("fsdp", "ctx", None),
            P("fsdp", ("ctx", "tp"), None),
            P(),
            P("fsdp", ("ctx", "tp"), None),
            P(),
            P("fsdp", "tp"),
            P("fsdp", "tp"),
            P("fsdp", "tp"),
            P("tp", "fsdp"),
            P(),
            P(),
            P(),
            P("fsdp", None),
            P(("ctx", "fsdp", "tp"), None, None),
            P(("ctx", "fsdp", "tp"), None, None),
        ),
        out_specs=(
            P("fsdp", ("ctx", "tp"), None),
            P(),
            P("fsdp", ("ctx", "tp"), None),
            P(),
            P("fsdp", "tp"),
            P("fsdp", "tp"),
            P("fsdp", "tp"),
            P("tp", "fsdp"),
            P(),
            P(),
            P(),
            P("fsdp", None),
            P(("ctx", "fsdp", "tp"), None, None),
            P(("ctx", "fsdp", "tp"), None, None),
        ),
        check_vma=False,
    )
```

```python
import functools

import jax
import jax.numpy as jnp
from jax import lax
from jax.experimental import pallas as pl
from jax.experimental.pallas import tpu as pltpu
from jax.sharding import PartitionSpec as P

EPS = 1e-06
ROPE_BASE = 1000000.0
MASKED = -1e30
AXES = ("ctx", "fsdp", "tp")
MESH = pl.DeviceIdType.MESH
ANY = pl.BlockSpec(memory_space=pl.ANY)
VMEM = pl.BlockSpec(memory_space=pltpu.VMEM)
BF = jnp.bfloat16
FL = jnp.float32
MIB = 1024 * 1024


def norm_rows(values, gain_vec):
    factor = lax.rsqrt(jnp.mean(values * values, axis=-1, keepdims=True) + EPS)
    return (values * factor * gain_vec, factor)


def norm_back(values, factor, gain_vec, upstream):
    weighted = upstream * gain_vec
    inner_mean = jnp.mean(values * weighted, axis=-1, keepdims=True)
    return (
        factor * weighted - values * (factor * factor * factor) * inner_mean,
        upstream * values * factor,
    )


def rope_tables(positions, head_size):
    half_size = head_size // 2
    frequency = jnp.power(ROPE_BASE, -jnp.arange(half_size, dtype=jnp.float32) * (2.0 / head_size))
    angles = positions.astype(jnp.float32)[:, None] * frequency[None, :]
    return (jnp.cos(angles), jnp.sin(angles))


def rotate(values, cosine, sine_tab):
    half_size = values.shape[-1] // 2
    front_half = values[..., :half_size]
    back_half = values[..., half_size:]
    cos_rows = cosine[:, None, :]
    sin_rows = sine_tab[:, None, :]
    return jnp.concatenate(
        [
            front_half * cos_rows - back_half * sin_rows,
            back_half * cos_rows + front_half * sin_rows,
        ],
        axis=-1,
    )


def inner_rows(left, right):
    return lax.dot_general(
        left, right, (((0,), (0,)), ((), ())), preferred_element_type=jnp.float32
    )


def outer_cols(left, right):
    return lax.dot_general(
        left, right, (((1,), (1,)), ((), ())), preferred_element_type=jnp.float32
    )


def block_scores(queries, key_rows, offset, positions, length, inv_root):
    block_len = key_rows.shape[1]
    raw_scores = (
        jnp.einsum("kgqd,kjd->kgqj", queries, key_rows, preferred_element_type=jnp.float32)
        * inv_root
    )
    key_pos = offset + jnp.arange(block_len, dtype=jnp.int32)
    allowed = (key_pos[None, :] <= positions[:, None]) & (key_pos[None, :] < length)
    return (jnp.where(allowed, raw_scores, MASKED), allowed)


def place():
    return tuple(lax.axis_index(axis) for axis in AXES)


def remote(source, target, sent, got, device):
    return pltpu.make_async_remote_copy(
        src_ref=source, dst_ref=target, send_sem=sent, recv_sem=got,
        device_id=device, device_id_type=MESH,
    )


def greet(devices):
    barrier = pltpu.get_barrier_semaphore()
    for device in devices:
        pl.semaphore_signal(barrier, inc=1, device_id=device, device_id_type=MESH)
    pl.semaphore_wait(barrier, len(devices))


def params(identity, mebibytes):
    return pltpu.CompilerParams(
        collective_id=identity, has_side_effects=True, vmem_limit_bytes=int(mebibytes * MIB)
    )


def gather_body(C, F, wa, wo, tab, fa, fo, ftab, loc, zs, zr, ys, yr, ks, kr, ts, tr):
    c, f, t = place()
    core, chip = lax.rem(c, 2), lax.div(c, 2)
    chips = C // 2
    sib = c + 1 - 2 * core
    ra, (ro, co) = wa.shape[0], wo.shape
    pa, po = ra // C, ro // C

    def spot(arr, b, p):
        if arr == 0:
            return fa.at[pl.ds(pl.multiple_of(b * ra + p * pa, pa), pa)]
        return fo.at[pl.ds(pl.multiple_of(p * po, po), po), pl.ds(pl.multiple_of(b * co, co), co)]

    def own(arr):
        if arr == 0:
            return wa.at[pl.ds(pl.multiple_of(c * pa, pa), pa)]
        return wo.at[pl.ds(pl.multiple_of(c * po, po), po)]

    peers = [(c, lax.rem(f + k, F), t) for k in range(1, F)]
    peers += [(lax.rem(chip + k, chips) * 2 + core, f, t) for k in range(1, chips)]
    peers += [(sib, f, t)]
    greet(peers)

    def z_copy(arr, s, d):
        b = f - (s - 1) if d == 0 else f + (s - 1)
        source = own(arr) if s == 1 else spot(arr, b, c)
        return remote(
            source, spot(arr, b, c), zs.at[d, s, arr], zr.at[d, s, arr],
            (c, f + 1 if d == 0 else f - 1, t),
        )

    def z_sends(s, d):
        b = f - (s - 1) if d == 0 else f + (s - 1)
        return (f + 1 < F) & (b >= 0) if d == 0 else (f > 0) & (b < F)

    def z_gets(s, d):
        return f - s >= 0 if d == 0 else f + s < F

    def came(s, d):
        return f - s if d == 0 else f + s

    def z_arrival(arr, s, d):
        b = came(s, d)
        here = spot(arr, b, c)
        return remote(here, here, zs.at[d, s, arr], zr.at[d, s, arr], (c, f, t))

    def y_copy(arr, s, d, k):
        here = spot(arr, came(s, d), c)
        there = (lax.rem(chip + k, chips) * 2 + core, f, t)
        return remote(here, here, ys.at[d, s, k, arr], yr.at[d, s, k, arr], there)

    def k_copy(arr, s, d, k, side):
        p = lax.rem(chip + chips - k, chips) * 2 + side
        here = spot(arr, came(s, d), p)
        return remote(here, here, ks.at[d, s, k, arr], kr.at[d, s, k, arr], (sib, f, t))

    def y_arrival(arr, s, d, k):
        p = lax.rem(chip + chips - k, chips) * 2 + core
        here = spot(arr, came(s, d), p)
        return remote(here, here, ys.at[d, s, k, arr], yr.at[d, s, k, arr], (sib, f, t))

    tabs = [
        remote(tab, ftab.at[f], ts.at[k], tr.at[k], (c, lax.rem(f + k, F), t)) for k in range(1, F)
    ]
    for copy in tabs:
        copy.start()
    for d in range(2):

        @pl.when(z_sends(1, d))
        def _():
            for arr in range(2):
                z_copy(arr, 1, d).start()

    locals_ = [
        pltpu.make_async_copy(tab, ftab.at[f], loc.at[0]),
        pltpu.make_async_copy(wa, fa.at[pl.ds(pl.multiple_of(f * ra, ra), ra)], loc.at[1]),
        pltpu.make_async_copy(wo, fo.at[:, pl.ds(pl.multiple_of(f * co, co), co)], loc.at[2]),
    ]
    for copy in locals_:
        copy.start()

    def pass_on(s, d):
        for arr in range(2):
            for k in range(1, chips):
                y_arrival(arr, s, d, k).wait_recv()
                k_copy(arr, s, d, k, core).start()

    for s in range(1, F):
        for d in range(2):

            @pl.when(z_gets(s, d))
            def _():
                for arr in range(2):
                    z_arrival(arr, s, d).wait_recv()
                    if s + 1 < F:

                        @pl.when(z_sends(s + 1, d))
                        def _():
                            z_copy(arr, s + 1, d).start()

                    for k in range(1, chips):
                        y_copy(arr, s, d, k).start()
                    k_copy(arr, s, d, 0, core).start()

        if s > 1:
            for d in range(2):
                pl.when(z_gets(s - 1, d))(functools.partial(pass_on, s - 1, d))
    for d in range(2):
        pl.when(z_gets(F - 1, d))(functools.partial(pass_on, F - 1, d))
    for copy in tabs:
        copy.wait()
    for copy in locals_:
        copy.wait()
    for s in range(1, F):
        for d in range(2):

            @pl.when(z_sends(s, d))
            def _():
                for arr in range(2):
                    z_copy(arr, s, d).wait_send()

            @pl.when(z_gets(s, d))
            def _():
                for arr in range(2):
                    for k in range(1, chips):
                        y_copy(arr, s, d, k).wait_send()
                    for k in range(chips):
                        k_copy(arr, s, d, k, core).wait_send()
                        k_copy(arr, s, d, k, 1 - core).wait_recv()


def gather_weights(C, F, wa, wo, tab):
    ra, ca = wa.shape
    ro, co = wo.shape
    chips = C // 2
    dma = pltpu.SemaphoreType.DMA
    return pl.pallas_call(
        functools.partial(gather_body, C, F),
        out_shape=(
            jax.ShapeDtypeStruct((F * ra, ca), wa.dtype),
            jax.ShapeDtypeStruct((ro, F * co), wo.dtype),
            jax.ShapeDtypeStruct((F,) + tab.shape, tab.dtype),
        ),
        in_specs=[ANY] * 3,
        out_specs=[ANY] * 3,
        scratch_shapes=[
            dma((3,)), dma((2, F, 2)), dma((2, F, 2)),
            dma((2, F, chips, 2)), dma((2, F, chips, 2)),
            dma((2, F, chips, 2)), dma((2, F, chips, 2)),
            dma((F,)), dma((F,)),
        ],
        compiler_params=params(1, 16),
    )(wa, wo, tab)


def slab_place(C, T):
    c, f, t = place()
    return c, f, t, c * T + t


def slab_device(index, f, T):
    return (lax.div(index, T), f, lax.rem(index, T))


def dispatch_body(C, F, T, tabbed, rows, select, *refs):
    if tabbed:
        tab, out, zbuf, ftab, stage, loc, zs, zr, ss, sr, ts, tr = refs
    else:
        out, zbuf, stage, loc, zs, zr, ss, sr = refs
    c, f, t, me = slab_place(C, T)
    S = C * T
    K = select.shape[2]
    copies = select.shape[3] // rows.shape[0]
    columns = [(c, lax.rem(f + k, F), t) for k in range(1, F)]
    greet(columns + [slab_device(lax.rem(me + j, S), f, T) for j in range(1, S)])
    sends = [
        remote(rows, zbuf.at[f], zs.at[k], zr.at[k], columns[k - 1]) for k in range(1, F)
    ]
    if tabbed:
        tabs = [remote(tab, ftab.at[f], ts.at[k], tr.at[k], columns[k - 1]) for k in range(1, F)]
        for copy in tabs:
            copy.start()
        ftab[f] = tab[...]
    for copy in sends:
        copy.start()
    zbuf[f] = rows[...]

    def slab_copy(k, j):
        b = lax.rem(f + F - k, F)
        e = lax.rem(me + j, S)
        return remote(
            stage.at[e, b], out.at[me, b], ss.at[k, j], sr.at[k, j], slab_device(e, f, T)
        )

    def slab_arrival(k, j):
        b = lax.rem(f + F - k, F)
        e = lax.rem(me + S - j, S)
        return remote(
            stage.at[e, b], out.at[e, b], ss.at[k, j], sr.at[k, j], slab_device(e, f, T)
        )

    def own_copy(k):
        b = lax.rem(f + F - k, F)
        return pltpu.make_async_copy(stage.at[me, b], out.at[me, b], loc.at[k])

    for k in range(F):
        b = lax.rem(f + F - k, F)
        if k > 0:
            remote(rows, zbuf.at[b], zs.at[k], zr.at[k], columns[k - 1]).wait_recv()

        def pick(j):
            e = lax.rem(me + j, S)
            block = zbuf[b]
            if copies > 1:
                block = jnp.concatenate([block] * copies, axis=0)
            stage[e, b] = jnp.dot(
                select[b, e], block, preferred_element_type=FL
            ).astype(BF)

        if S <= 8:
            for j in range(1, S):
                pick(j)
                slab_copy(k, j).start()
        else:

            def step(j, carry):
                pick(j)
                slab_copy(k, j).start()
                return carry

            lax.fori_loop(1, S, step, 0)
        pick(0)
        own_copy(k).start()
    if tabbed:
        for copy in tabs:
            copy.wait()
    for copy in sends:
        copy.wait_send()
    for k in range(F):
        own_copy(k).wait()

        def settle(j, carry):
            slab_copy(k, j).wait_send()
            slab_arrival(k, j).wait_recv()
            return carry

        lax.fori_loop(1, S, settle, 0)


def dispatch(identity, C, F, T, rows, select, tab=None):
    S = C * T
    K = select.shape[2]
    R, W = rows.shape
    dma = pltpu.SemaphoreType.DMA
    tabbed = tab is not None
    outs = [jax.ShapeDtypeStruct((S, F, K, W), BF), jax.ShapeDtypeStruct((F, R, W), BF)]
    out_specs = [ANY, VMEM]
    ins = [rows, select]
    scratch = [
        pltpu.VMEM((S, F, K, W), BF), dma((F,)), dma((F,)), dma((F,)), dma((F, S)), dma((F, S)),
    ]
    if tabbed:
        outs.append(jax.ShapeDtypeStruct((F,) + tab.shape, tab.dtype))
        out_specs.append(VMEM)
        ins.append(tab)
        scratch += [dma((F,)), dma((F,))]
    return pl.pallas_call(
        functools.partial(dispatch_body, C, F, T, tabbed),
        out_shape=tuple(outs),
        in_specs=[VMEM] * len(ins),
        out_specs=out_specs,
        scratch_shapes=scratch,
        compiler_params=params(identity, 32),
    )(*ins)


def combine_body(C, F, T, tabbed, rows, weigh, *refs):
    if tabbed:
        tab, got, part, ftab, stage, loc, zs, zr, ss, sr, ts, tr = refs
    else:
        got, part, stage, loc, zs, zr, ss, sr = refs
    c, f, t, me = slab_place(C, T)
    S = C * T
    K, W = got.shape[2], got.shape[3]
    n = weigh.shape[1]
    columns = [(c, lax.rem(f + k, F), t) for k in range(1, F)]
    greet(columns + [slab_device(lax.rem(me + j, S), f, T) for j in range(1, S)])

    def slab_copy(k, j):
        b = lax.rem(f + k, F)
        e = lax.rem(me + j, S)
        return remote(
            rows.at[e, b], got.at[b, me], ss.at[k, j], sr.at[k, j], slab_device(e, f, T)
        )

    def slab_arrival(k, j):
        b = lax.rem(f + k, F)
        e = lax.rem(me + S - j, S)
        return remote(
            rows.at[e, b], got.at[b, e], ss.at[k, j], sr.at[k, j], slab_device(e, f, T)
        )

    def own_copy(k):
        b = lax.rem(f + k, F)
        return pltpu.make_async_copy(rows.at[me, b], got.at[b, me], loc.at[k])

    order = list(range(1, F)) + [0]
    for k in order:

        def begin(j, carry):
            slab_copy(k, j).start()
            return carry

        lax.fori_loop(1, S, begin, 0)
        own_copy(k).start()
    if tabbed:
        tabs = [
            remote(tab.at[lax.rem(f + k, F)], ftab.at[f], ts.at[k], tr.at[k], columns[k - 1])
            for k in range(1, F)
        ]
        for copy in tabs:
            copy.start()
        ftab[f] = tab[f]

    def z_copy(k):
        b = lax.rem(f + k, F)
        return remote(stage.at[b], part.at[f], zs.at[k], zr.at[k], columns[k - 1])

    def z_arrival(k):
        b = lax.rem(f + F - k, F)
        return remote(stage.at[b], part.at[b], zs.at[k], zr.at[k], columns[k - 1])

    step = min(W, 512)
    for k in order:
        b = lax.rem(f + k, F)
        own_copy(k).wait()

        def settle(j, carry):
            slab_arrival(k, j).wait_recv()
            return carry

        lax.fori_loop(1, S, settle, 0)
        target = part if k == 0 else stage

        def add(i, carry):
            columns_ = pl.ds(pl.multiple_of(i * step, step), step)
            block = got[b, :, :, columns_].reshape(S * K, step)
            total = jnp.dot(weigh[b, 0], block, preferred_element_type=FL)
            for m in range(1, n):
                total += jnp.dot(weigh[b, m], block, preferred_element_type=FL)
            target[b, :, columns_] = total.astype(BF)
            return carry

        lax.fori_loop(0, W // step, add, 0)
        if k > 0:
            z_copy(k).start()
    for k in range(1, F):
        z_copy(k).wait_send()
        z_arrival(k).wait_recv()
    for k in range(F):

        def leave(j, carry):
            slab_copy(k, j).wait_send()
            return carry

        lax.fori_loop(1, S, leave, 0)
    if tabbed:
        for copy in tabs:
            copy.wait()


def combine(identity, C, F, T, rows, weigh, tab=None):
    S, _, K, W = rows.shape
    R = weigh.shape[2]
    dma = pltpu.SemaphoreType.DMA
    tabbed = tab is not None
    outs = [jax.ShapeDtypeStruct((F, S, K, W), BF), jax.ShapeDtypeStruct((F, R, W), BF)]
    ins = [rows, weigh]
    scratch = [
        pltpu.VMEM((F, R, W), BF), dma((F,)), dma((F,)), dma((F,)), dma((F, S)), dma((F, S)),
    ]
    if tabbed:
        outs.append(jax.ShapeDtypeStruct(tab.shape, tab.dtype))
        ins.append(tab)
        scratch += [dma((F,)), dma((F,))]
    return pl.pallas_call(
        functools.partial(combine_body, C, F, T, tabbed),
        out_shape=tuple(outs),
        in_specs=[ANY] + [VMEM] * (len(ins) - 1),
        out_specs=[VMEM] * len(outs),
        scratch_shapes=scratch,
        compiler_params=params(identity, 32),
    )(*ins)


def ctx_sum_body(C, x, out, got, ss, sr):
    c, f, t = place()
    peers = [(lax.rem(c + k, C), f, t) for k in range(1, C)]
    greet(peers)

    def copy(k):
        p = lax.rem(c + k, C)
        return remote(x.at[p], got.at[c], ss.at[k], sr.at[k], (p, f, t))

    def arrival(k):
        p = lax.rem(c + C - k, C)
        return remote(x.at[p], got.at[p], ss.at[k], sr.at[k], (p, f, t))

    for k in range(1, C):
        copy(k).start()
    got[c] = x[c]
    for k in range(1, C):
        arrival(k).wait_recv()
    total = got[0].astype(FL)
    for p in range(1, C):
        total += got[p].astype(FL)
    out[...] = total
    for k in range(1, C):
        copy(k).wait_send()


def ctx_sum(identity, C, x):
    dma = pltpu.SemaphoreType.DMA
    return pl.pallas_call(
        functools.partial(ctx_sum_body, C),
        out_shape=jax.ShapeDtypeStruct(x.shape[1:], FL),
        in_specs=[VMEM],
        out_specs=VMEM,
        scratch_shapes=[pltpu.VMEM(x.shape, x.dtype), dma((C,)), dma((C,))],
        compiler_params=params(identity, 24),
    )(x)


def small_body(C, F, T, x, out, zgot, mid, sgot, zs, zr, ss, sr):
    c, f, t, me = slab_place(C, T)
    S = C * T
    columns = [(c, lax.rem(f + k, F), t) for k in range(1, F)]
    greet(columns + [slab_device(lax.rem(me + j, S), f, T) for j in range(1, S)])

    def z_copy(k):
        return remote(x.at[lax.rem(f + k, F)], zgot.at[f], zs.at[k], zr.at[k], columns[k - 1])

    def z_arrival(k):
        b = lax.rem(f + F - k, F)
        return remote(x.at[b], zgot.at[b], zs.at[k], zr.at[k], columns[k - 1])

    for k in range(1, F):
        z_copy(k).start()
    zgot[f] = x[f]
    for k in range(1, F):
        z_arrival(k).wait_recv()
    total = zgot[0]
    for b in range(1, F):
        total += zgot[b]
    mid[...] = total
    sgot[me] = total

    def s_copy(j):
        return remote(
            mid, sgot.at[me], ss.at[j], sr.at[j], slab_device(lax.rem(me + j, S), f, T)
        )

    def s_arrival(j):
        e = lax.rem(me + S - j, S)
        return remote(mid, sgot.at[e], ss.at[j], sr.at[j], slab_device(e, f, T))

    for j in range(1, S):
        s_copy(j).start()
    for j in range(1, S):
        s_arrival(j).wait_recv()
    total = sgot[0]
    for e in range(1, S):
        total += sgot[e]
    out[...] = total
    for k in range(1, F):
        z_copy(k).wait_send()
    for j in range(1, S):
        s_copy(j).wait_send()


def small_sum(identity, C, F, T, x):
    dma = pltpu.SemaphoreType.DMA
    S = C * T
    one = x.shape[1:]
    return pl.pallas_call(
        functools.partial(small_body, C, F, T),
        out_shape=jax.ShapeDtypeStruct(one, FL),
        in_specs=[VMEM],
        out_specs=VMEM,
        scratch_shapes=[
            pltpu.VMEM((F,) + one, FL), pltpu.VMEM(one, FL), pltpu.VMEM((S,) + one, FL),
            dma((F,)), dma((F,)), dma((S,)), dma((S,)),
        ],
        compiler_params=params(identity, 24),
    )(x)


def far_first(F):
    table = []
    for f in range(F):
        order = []
        for i in range(F):
            ends = [F - 1 - i, i] if f * 2 < F else [i, F - 1 - i]
            for b in ends:
                if ((b > f and b == F - 1 - i) or (b < f and b == i)) and b not in order:
                    order.append(b)
        table.append(order + [f])
    return table


def grads_body(
    C, F, xt, da, ht, dt, outa, outo,
    ska, sko, rka, rko, sya, syo, rya, ryo, rza, rzo, sza, szo,
    k_s, k_r, y_s, y_r, z_s, z_r, g_s, g_r, h_s, h_r,
):
    c, f, t = place()
    core, chip = lax.rem(c, 2), lax.div(c, 2)
    chips = C // 2
    sib = c + 1 - 2 * core
    pa, po, co = outa.shape[1], outo.shape[1], outo.shape[2]
    ra = pa * C
    table = far_first(F)

    def block(q):
        value = jnp.int32(table[0][q])
        for g in range(1, F):
            value = jnp.where(f == g, table[g][q], value)
        return value

    blocks = [block(q) for q in range(F)]
    ends = [(c, lax.rem(f + 1, F), t), (c, lax.rem(f + F - 1, F), t)]
    mates = [(lax.rem(chip + k, chips) * 2 + core, f, t) for k in range(1, chips)]
    greet(ends + mates + [(sib, f, t)])

    def piece_a(b, p):
        rows = pl.ds(pl.multiple_of(b * ra + p * pa, pa), pa)
        return jnp.dot(xt[rows, :], da[...], preferred_element_type=FL)

    def piece_o(b, p):
        rows = pl.ds(pl.multiple_of(p * po, po), po)
        cols = pl.ds(pl.multiple_of(b * co, co), co)
        return jnp.dot(ht[rows, :], dt[:, cols], preferred_element_type=FL)

    def core_copies(q, k):
        b = blocks[q]
        return [
            remote(ska.at[b, k], rka.at[b, k], k_s.at[q, k, 0], k_r.at[q, k, 0], (sib, f, t)),
            remote(sko.at[b, k], rko.at[b, k], k_s.at[q, k, 1], k_r.at[q, k, 1], (sib, f, t)),
        ]

    for q in range(F):
        b = blocks[q]
        for k in [*range(1, chips), 0]:
            p = lax.rem(chip + k, chips) * 2 + 1 - core
            ska[b, k] = piece_a(b, p).astype(BF)
            sko[b, k] = piece_o(b, p).astype(BF)
            for copy in core_copies(q, k):
                copy.start()

    def chip_copies(q, k):
        b = blocks[q]
        there = mates[k - 1]
        return [
            remote(sya.at[b, k - 1], rya.at[b, k - 1], y_s.at[q, k, 0], y_r.at[q, k, 0], there),
            remote(syo.at[b, k - 1], ryo.at[b, k - 1], y_s.at[q, k, 1], y_r.at[q, k, 1], there),
        ]

    for q in range(F):
        b = blocks[q]
        for k in range(1, chips):
            p = lax.rem(chip + k, chips) * 2 + core
            for copy in core_copies(q, k):
                copy.wait_recv()
            sya[b, k - 1] = (piece_a(b, p) + rka[b, k].astype(FL)).astype(BF)
            syo[b, k - 1] = (piece_o(b, p) + rko[b, k].astype(FL)).astype(BF)
            for copy in chip_copies(q, k):
                copy.start()

    def z_copies(q, b, slot, there):
        return [
            remote(sza.at[b], rza.at[slot], z_s.at[q, 0], z_r.at[slot, 0], there),
            remote(szo.at[b], rzo.at[slot], z_s.at[q, 1], z_r.at[slot, 1], there),
        ]

    def z_wait(slot):
        for copy in z_copies(0, 0, slot, ends[0]):
            copy.wait_recv()

    for q in range(F):
        b = blocks[q]
        for copy in core_copies(q, 0):
            copy.wait_recv()
        for k in range(1, chips):
            for copy in chip_copies(q, k):
                copy.wait_recv()
        total_a = piece_a(b, c) + rka[b, 0].astype(FL)
        total_o = piece_o(b, c) + rko[b, 0].astype(FL)
        for k in range(1, chips):
            total_a += rya[b, k - 1].astype(FL)
            total_o += ryo[b, k - 1].astype(FL)
        if q < F - 1:
            up = b > f
            first = jnp.where(up, f == 0, f == F - 1)

            @pl.when(first)
            def _():
                sza[b] = total_a.astype(BF)
                szo[b] = total_o.astype(BF)

            @pl.when(jnp.logical_not(first))
            def _():
                z_wait(b)
                sza[b] = (total_a + rza[b].astype(FL)).astype(BF)
                szo[b] = (total_o + rzo[b].astype(FL)).astype(BF)

            @pl.when(up)
            def _():
                for copy in z_copies(q, b, b, (c, f + 1, t)):
                    copy.start()

            @pl.when(jnp.logical_not(up))
            def _():
                slot = jnp.where(b == f - 1, F, b)
                for copy in z_copies(q, b, slot, (c, f - 1, t)):
                    copy.start()

        else:
            sza[f] = total_a.astype(BF)
            szo[f] = total_o.astype(BF)

            @pl.when(f > 0)
            def _():
                z_wait(f)
                sza[f] = (total_a + rza[f].astype(FL)).astype(BF)
                szo[f] = (total_o + rzo[f].astype(FL)).astype(BF)

            @pl.when(f < F - 1)
            def _():
                z_wait(F)
                outa[c] = (sza[f].astype(FL) + rza[F].astype(FL)).astype(BF)
                outo[c] = (szo[f].astype(FL) + rzo[F].astype(FL)).astype(BF)

            @pl.when(f == F - 1)
            def _():
                outa[c] = sza[f]
                outo[c] = szo[f]

    def spread(k):
        there = mates[k - 1]
        return [
            remote(outa.at[c], outa.at[c], g_s.at[k, 0], g_r.at[k, 0], there),
            remote(outo.at[c], outo.at[c], g_s.at[k, 1], g_r.at[k, 1], there),
        ]

    def hand(k, side):
        p = lax.rem(chip + chips - k, chips) * 2 + side
        return [
            remote(outa.at[p], outa.at[p], h_s.at[k, 0], h_r.at[k, 0], (sib, f, t)),
            remote(outo.at[p], outo.at[p], h_s.at[k, 1], h_r.at[k, 1], (sib, f, t)),
        ]

    def spread_arrival(k):
        p = lax.rem(chip + chips - k, chips) * 2 + core
        return [
            remote(outa.at[p], outa.at[p], g_s.at[k, 0], g_r.at[k, 0], mates[k - 1]),
            remote(outo.at[p], outo.at[p], g_s.at[k, 1], g_r.at[k, 1], mates[k - 1]),
        ]

    for k in range(1, chips):
        for copy in spread(k):
            copy.start()
    for copy in hand(0, core):
        copy.start()
    for k in range(1, chips):
        for copy in spread_arrival(k):
            copy.wait_recv()
        for copy in hand(k, core):
            copy.start()
    for k in range(chips):
        for copy in hand(k, 1 - core):
            copy.wait_recv()
        for copy in hand(k, core):
            copy.wait_send()
    for k in range(1, chips):
        for copy in spread(k):
            copy.wait_send()
    for q in range(F):
        for k in range(chips):
            for copy in core_copies(q, k):
                copy.wait_send()
        for k in range(1, chips):
            for copy in chip_copies(q, k):
                copy.wait_send()
        if q < F - 1:
            for copy in z_copies(q, 0, 0, ends[0]):
                copy.wait_send()


def weight_grads(identity, C, F, xt, da, ht, dt):
    D, R = xt.shape
    pa, na = D // F // C, da.shape[1]
    po, no = ht.shape[0] // C, dt.shape[1] // F
    chips = C // 2
    dma = pltpu.SemaphoreType.DMA

    def pair(*lead):
        return [pltpu.VMEM(lead + (pa, na), BF), pltpu.VMEM(lead + (po, no), BF)]

    return pl.pallas_call(
        functools.partial(grads_body, C, F),
        out_shape=(
            jax.ShapeDtypeStruct((C, pa, na), BF),
            jax.ShapeDtypeStruct((C, po, no), BF),
        ),
        in_specs=[VMEM] * 4,
        out_specs=[VMEM] * 2,
        scratch_shapes=[
            *pair(F, chips), *pair(F, chips), *pair(F, chips - 1), *pair(F, chips - 1),
            *pair(F + 1), *pair(F),
            dma((F, chips, 2)), dma((F, chips, 2)), dma((F, chips, 2)), dma((F, chips, 2)),
            dma((F, 2)), dma((F + 1, 2)), dma((chips, 2)), dma((chips, 2)),
            dma((chips, 2)), dma((chips, 2)),
        ],
        compiler_params=params(identity, 60),
    )(xt, da, ht, dt)


def tail_body(
    C, F, T, KH,
    grad_own, heads, normed, qrot, kv, keys_t, raw, lse, bias, cosf, sins, qgain, kgain, again,
    own_in, resid_in, router, vec_in, fo, fall,
    gin, outa, outo, small,
    wbuf, dall, nall, hq, rq, dheads, draw, dk, dv, ksend, kgot, gains, nsend, ngot, nown,
    sza, szo, rza, rzo, smx, zgot, mid, sgot,
    wsem, xs, xr, as_, ar, hs, hr, ds_, dr, rs, rr, z_s, z_r, ts, tr, us, ur,
):
    c, f, t, me = slab_place(C, T)
    S = C * T
    R, QC = heads.shape
    W = normed.shape[1]
    PC = raw.shape[1]
    L = kv.shape[1]
    HS = qgain.shape[1]
    QH = QC // HS
    G = QH // KH
    Rh = grad_own.shape[0]
    KC = KH * HS
    pa = rq.shape[2]
    po = hq.shape[2]
    rows_a, cols_o = outa.shape[0], outo.shape[1]
    root = HS ** (-0.5)
    core = lax.rem(c, 2)
    sib = c + 1 - 2 * core
    mate = lax.rem(c + 2, C)
    mate_sib = lax.rem(sib + 2, C)
    table = far_first(F)

    def block(q):
        value = jnp.int32(table[0][q])
        for g in range(1, F):
            value = jnp.where(f == g, table[g][q], value)
        return value

    blocks = [block(q) for q in range(F)]
    columns = [(c, lax.rem(f + k, F), t) for k in range(1, F)]
    greet(columns + [slab_device(lax.rem(me + j, S), f, T) for j in range(1, S)])
    at_t = pl.ds(pl.multiple_of(t * Rh, Rh), Rh)
    at_u = pl.ds(pl.multiple_of((1 - t) * Rh, Rh), Rh)
    beside = (c, f, 1 - t)

    load_o = pltpu.make_async_copy(fo, wbuf.at[:, pl.ds(0, W)], wsem.at[0])
    load_o.start()

    swap_d = remote(grad_own, dall.at[c, at_t], xs.at[0], xr.at[0], beside)
    swap_d_in = remote(grad_own, dall.at[c, at_u], xs.at[0], xr.at[0], beside)
    swap_n = remote(nsend, ngot, xs.at[1], xr.at[1], beside)

    def spread(view, n, i):
        here = view(mate) if i == 2 else view(c)
        there = (mate if i == 0 else sib, f, t)
        return remote(here, here, as_.at[n, i], ar.at[n, i], there)

    def spread_in(view, n, i):
        here = view((mate, sib, mate_sib)[i])
        return remote(here, here, as_.at[n, i], ar.at[n, i], (sib, f, t))

    def spread_start(view, n):
        spread(view, n, 0).start()
        spread(view, n, 1).start()

    def spread_pass(view, n):
        spread_in(view, n, 0).wait_recv()
        spread(view, n, 2).start()

    def spread_end(view, n):
        spread_in(view, n, 1).wait_recv()
        spread_in(view, n, 2).wait_recv()

    def spread_sent(view, n):
        for i in range(3):
            spread(view, n, i).wait_send()

    def chunk_copies(source, target, ss, sr):
        out, come = [], []
        for k in range(1, C):
            p, o = lax.rem(c + k, C), lax.rem(c + C - k, C)
            out.append(remote(source(p), target(c), ss.at[k], sr.at[k], (p, f, t)))
            come.append(remote(source(o), target(o), ss.at[k], sr.at[k], (o, f, t)))
        return out, come

    def lane(p, n):
        return pl.ds(pl.multiple_of(p * n, n), n)

    heads_out, heads_come = chunk_copies(
        lambda p: heads.at[:, lane(p, po)], lambda o: hq.at[o], hs, hr
    )
    kv_moves = [
        chunk_copies(lambda p, g=g: ksend.at[g, p], lambda o, g=g: kgot.at[g, o], ds_.at[g], dr.at[g])
        for g in range(KH)
    ]
    def nall_of(p):
        return nall.at[p]

    def outo_of(p):
        return outo.at[lane(p, po)]

    def outa_of(p):
        return outa.at[:, lane(p, pa)]

    dall_of = [
        lambda p, q=q: dall.at[p, :, lane(blocks[q], cols_o)] for q in range(F)
    ]

    swap_d.start()
    for copy in heads_out:
        copy.start()
    dall[c, at_t] = grad_own[...]
    nall[c] = normed[...]
    hq[c] = heads[:, lane(c, po)]
    swap_d_in.wait_recv()
    for q in range(F):
        spread_start(dall_of[q], 3 + q)

    load_o.wait()
    step = min(512, QC)

    def head_grads(i, carry):
        at = lane(i, step)
        dheads[:, at] = outer_cols(dall[c], wbuf[at, pl.ds(0, W)]).astype(BF)
        return carry

    lax.fori_loop(0, QC // step, head_grads, 0)
    load_w = pltpu.make_async_copy(fall.at[:, pl.ds(0, PC)], wbuf, wsem.at[1])
    load_w.start()

    def unturn(values):
        return values * cosf[...] - pltpu.roll(values, HS // 2, 1) * sins[...]

    def norm_grads(values, gain_vec, upstream):
        factor = lax.rsqrt(jnp.mean(values * values, axis=-1, keepdims=True) + EPS)
        out, terms = norm_back(values, factor, gain_vec, upstream)
        return out, jnp.sum(terms, axis=0, keepdims=True)

    gains[...] = jnp.zeros_like(gains)
    def piece_o(b):
        return inner_rows(
            hq[...].reshape(C * R, po), dall[:, :, lane(b, cols_o)].reshape(C * R, cols_o)
        )

    def piece_a(b):
        return inner_rows(
            nall[:, :, lane(b, rows_a)].reshape(C * R, rows_a), rq[...].reshape(C * R, pa)
        )

    pieces = ((piece_o, szo, rzo, outo_of), (piece_a, sza, rza, outa_of))
    end = (f == 0) | (f == F - 1)

    def z_out(n, q):
        b = blocks[q]
        _, send, got, _ = pieces[n]
        return remote(send.at[b], got.at[b], z_s.at[n, q], z_r.at[n, b], (c, f + 1, t))

    def z_down(n, q):
        b = blocks[q]
        slot = jnp.where(b == f - 1, F, b)
        _, send, got, _ = pieces[n]
        return remote(send.at[b], got.at[slot], z_s.at[n, q], z_r.at[n, slot], (c, f - 1, t))

    def z_wait(n, slot):
        _, send, got, _ = pieces[n]
        remote(send.at[0], got.at[slot], z_s.at[n, 0], z_r.at[n, slot], (c, f, t)).wait_recv()

    def z_send(n, q):
        up = blocks[q] > f

        @pl.when(up)
        def _():
            z_out(n, q).start()

        @pl.when(jnp.logical_not(up))
        def _():
            z_down(n, q).start()

    def z_first(n, q):
        fn, send, _, _ = pieces[n]

        @pl.when(end)
        def _():
            send[blocks[q]] = fn(blocks[q]).astype(BF)
            z_send(n, q)

    def o_first(q):
        spread_end(dall_of[q], 3 + q)
        if q < F - 1:
            z_first(0, q)

    def z_relay(n, q):
        fn, send, got, _ = pieces[n]

        @pl.when(jnp.logical_not(end))
        def _():
            b = blocks[q]
            z_wait(n, b)
            send[b] = (fn(b) + got[b].astype(FL)).astype(BF)
            z_send(n, q)

    def z_last(n):
        fn, send, got, out = pieces[n]
        send[f] = fn(f).astype(BF)

        @pl.when(f > 0)
        def _():
            z_wait(n, f)
            send[f] = (send[f].astype(FL) + got[f].astype(FL)).astype(BF)

        @pl.when(f < F - 1)
        def _():
            z_wait(n, F)
            out(c)[...] = (send[f].astype(FL) + got[F].astype(FL)).astype(BF)

        @pl.when(f == F - 1)
        def _():
            out(c)[...] = send[f]


    key_step = min(L, 512)

    def one_head(g, h):
        at = lane(h, HS)
        q_head, o_grad = qrot[:, at], dheads[:, at]
        product = o_grad.astype(FL) * heads[:, at].astype(FL)
        delta = jnp.sum(product.T, axis=0, keepdims=True)
        row = lse[pl.ds(h, 1), :]
        q_grad = jnp.zeros((HS, R), FL)
        for j in range(L // key_step):
            ks = pl.ds(j * key_step, key_step)
            scores = outer_cols(kv[g, ks, :], q_head) * root
            probs = jnp.exp(scores + bias[ks, :] - row)
            d_probs = outer_cols(kv[KH + g, ks, :], o_grad)
            d_scores = (probs * (d_probs - delta)).astype(BF)
            dv[ks, :] += jnp.dot(probs.astype(BF), o_grad, preferred_element_type=FL)
            dk[ks, :] += jnp.dot(d_scores, q_head, preferred_element_type=FL)
            q_grad += jnp.dot(keys_t[g, :, ks], d_scores, preferred_element_type=FL)
        q_back, terms = norm_grads(raw[:, at], qgain[...], unturn(q_grad.T * root))
        draw[:, at] = q_back.astype(BF)
        gains[0:1, :] += terms

    def some_heads(g, first, count):
        def step_(i, carry):
            one_head(g, first + i)
            return carry

        lax.fori_loop(0, count, step_, 0)

    raw_due = [-(-min((p + 1) * pa, QC) // HS) for p in range(C)]
    raw_gone = []

    def raw_sends(done):
        for p in range(C):
            if p not in raw_gone and raw_due[p] <= done and (p + 1) * pa <= QC:
                raw_gone.append(p)
                raw_send(p)

    def raw_copy(p):
        return remote(draw.at[:, p * pa : (p + 1) * pa], rq.at[c], rs.at[p], rr.at[c], (p, f, t))

    def raw_come(o):
        return remote(draw.at[:, 0:pa], rq.at[o], rs.at[0], rr.at[o], (o, f, t))

    def raw_send(p):
        @pl.when(c != p)
        def _():
            raw_copy(p).start()

        @pl.when(c == p)
        def _():
            rq[c] = draw[:, p * pa : (p + 1) * pa]

    halves = 2
    part_heads = G // halves
    beat = 0
    for g in range(KH):
        dk[...] = jnp.zeros_like(dk)
        dv[...] = jnp.zeros_like(dv)
        for half in range(halves):
            some_heads(g, g * G + half * part_heads, part_heads)
            raw_sends(g * G + (half + 1) * part_heads)
            if half == halves - 1:
                for p in range(C):
                    at = pl.ds(p * R, R)
                    ksend[g, p, :, 0:HS] = (dk[at, :] * root).astype(BF)
                    ksend[g, p, :, HS : 2 * HS] = dv[at, :].astype(BF)
                for copy in kv_moves[g][0]:
                    copy.start()
                kgot[g, c] = ksend[g, c]
            if beat < F:
                spread_pass(dall_of[beat], 3 + beat)
            if beat == 0:
                for copy in heads_come:
                    copy.wait_recv()
            elif beat < F:
                o_first(beat - 1)
            beat += 1
    for q in range(beat, F):
        spread_pass(dall_of[q], 3 + q)
        o_first(q - 1)
    spread_start(nall_of, 0)

    o_first(F - 1)
    z_relay(0, 0)

    for g in range(KH):
        for copy in kv_moves[g][1]:
            copy.wait_recv()
        total = kgot[g, 0].astype(FL)
        for p in range(1, C):
            total += kgot[g, p].astype(FL)
        k_cols = slice(QC + g * HS, QC + (g + 1) * HS)
        k_back, terms = norm_grads(raw[:, k_cols], kgain[...], unturn(total[:, :HS]))
        draw[:, k_cols] = k_back.astype(BF)
        draw[:, QC + KC + g * HS : QC + KC + (g + 1) * HS] = total[:, HS:].astype(BF)
        gains[1:2, :] += terms
    for p in range(C):
        if p not in raw_gone:
            raw_send(p)
    z_relay(0, 1)
    load_w.wait()
    width_step = min(512, W)

    def norm_theirs(i, carry):
        at = lane(i, width_step)
        nsend[:, at] = outer_cols(draw[at_u, :], wbuf[at, :]).astype(BF)
        return carry

    lax.fori_loop(0, W // width_step, norm_theirs, 0)
    swap_n.start()

    def norm_ours(i, carry):
        at = lane(i, width_step)
        nown[:, at] = outer_cols(draw[at_t, :], wbuf[at, :])
        return carry

    lax.fori_loop(0, W // width_step, norm_ours, 0)

    spread_pass(nall_of, 0)
    for q in range(2, F - 1):
        z_relay(0, q)
    spread_end(nall_of, 0)
    for k in range(1, C):
        raw_come(lax.rem(c + k, C)).wait_recv()
    for q in range(F - 1):
        z_first(1, q)
    z_relay(1, 0)
    z_last(0)
    spread_start(outo_of, 1)

    swap_n.wait_recv()
    upstream = nown[...] + ngot[...].astype(FL)
    values = own_in[...]
    factor = lax.rsqrt(jnp.mean(values * values, axis=-1, keepdims=True) + EPS)
    back, terms = norm_back(values, factor, again[...], upstream)
    gin[...] = resid_in[...] + back
    for b in range(F):
        smx[b, 0 : router.shape[1]] = router[b]
        at = router.shape[1]
        smx[b, at : at + 8] = vec_in[...]
        smx[b, at : at + 1] = jnp.sum(terms, axis=0, keepdims=True)
        smx[b, at + 2 : at + 3, 0:HS] = gains[0:1, :]
        smx[b, at + 2 : at + 3, HS : 2 * HS] = gains[1:2, :]

    def t_copy(k):
        return remote(smx.at[lax.rem(f + k, F)], zgot.at[f], ts.at[k], tr.at[k], columns[k - 1])

    def t_arrival(k):
        b = lax.rem(f + F - k, F)
        return remote(smx.at[b], zgot.at[b], ts.at[k], tr.at[k], columns[k - 1])

    for k in range(1, F):
        t_copy(k).start()
    zgot[f] = smx[f]
    for q in range(1, F - 1):
        z_relay(1, q)
    spread_pass(outo_of, 1)
    for k in range(1, F):
        t_arrival(k).wait_recv()
    total = zgot[0]
    for b in range(1, F):
        total += zgot[b]
    mid[...] = total
    sgot[me] = total

    def u_copy(j):
        return remote(
            mid, sgot.at[me], us.at[j], ur.at[j], slab_device(lax.rem(me + j, S), f, T)
        )

    def u_arrival(j):
        e = lax.rem(me + S - j, S)
        return remote(mid, sgot.at[e], us.at[j], ur.at[j], slab_device(e, f, T))

    for j in range(1, S):
        u_copy(j).start()
    z_last(1)
    spread_start(outa_of, 2)
    for j in range(1, S):
        u_arrival(j).wait_recv()
    total = sgot[0]
    for e in range(1, S):
        total += sgot[e]
    small[...] = total
    spread_end(outo_of, 1)
    spread_pass(outa_of, 2)
    spread_end(outa_of, 2)

    for view, n in ((nall_of, 0), (outo_of, 1), (outa_of, 2)):
        spread_sent(view, n)
    for q in range(F):
        spread_sent(dall_of[q], 3 + q)
    swap_d.wait_send()
    swap_n.wait_send()
    for copy in heads_out:
        copy.wait_send()
    for p in range(C):

        @pl.when(c != p)
        def _():
            raw_copy(p).wait_send()

    for g in range(KH):
        for copy in kv_moves[g][0]:
            copy.wait_send()
    for n in range(2):
        for q in range(F - 1):
            z_out(n, q).wait_send()
    for k in range(1, F):
        t_copy(k).wait_send()
    for j in range(1, S):
        u_copy(j).wait_send()


def tail(identity, C, F, T, KH, args, D, po):
    grad_own, heads, normed, qrot, kv, keys_t, raw, lse, bias = args[:9]
    qgain = args[11]
    router, fall = args[16], args[19]
    R, QC = heads.shape
    W = normed.shape[1]
    PC = raw.shape[1]
    L = kv.shape[1]
    HS = qgain.shape[1]
    Rh = grad_own.shape[0]
    S = C * T
    pa = PC // C
    rows_a, cols_o = W // F, W // F
    small_shape = (router.shape[1] + 8, W)
    dma = pltpu.SemaphoreType.DMA
    V = pltpu.VMEM
    return pl.pallas_call(
        functools.partial(tail_body, C, F, T, KH),
        out_shape=(
            jax.ShapeDtypeStruct((Rh, W), FL),
            jax.ShapeDtypeStruct((rows_a, C * pa), BF),
            jax.ShapeDtypeStruct((C * po, cols_o), BF),
            jax.ShapeDtypeStruct(small_shape, FL),
        ),
        in_specs=[VMEM] * 18 + [ANY] * 2,
        out_specs=[VMEM] * 4,
        scratch_shapes=[
            V((W, PC), BF), V((C, R, W), BF), V((C, R, W), BF), V((C, R, po), BF),
            V((C, R, pa), BF), V((R, QC), BF), V((R, PC), BF), V((L, HS), FL), V((L, HS), FL),
            V((KH, C, R, 2 * HS), BF), V((KH, C, R, 2 * HS), BF), V((8, HS), FL),
            V((Rh, W), BF), V((Rh, W), BF), V((Rh, W), FL),
            V((F, rows_a, pa), BF), V((F, po, cols_o), BF),
            V((F + 1, rows_a, pa), BF), V((F + 1, po, cols_o), BF),
            V((F,) + small_shape, FL), V((F,) + small_shape, FL), V(small_shape, FL),
            V((S,) + small_shape, FL),
            dma((2,)), dma((2,)), dma((2,)), dma((3 + F, 3)), dma((3 + F, 3)), dma((C,)), dma((C,)),
            dma((KH, C)), dma((KH, C)), dma((C,)), dma((C,)),
            dma((2, F)), dma((2, F + 1)), dma((F,)), dma((F,)), dma((S,)), dma((S,)),
        ],
        compiler_params=params(identity, 62),
    )(*args)


def head_body(
    C, F, T, KH,
    hidden, tab, again, qgain, kgain, fgain, cosf, sins, bias, wa, wo,
    fall, full, ftab, raw, qrot, kv, keys_t, lse, heads, normed, resid, low, gates,
    fa, fo, vals_t, nsend, ngot, nown,
    loc, zs, zr, ys, yr, ks, kr, ts, tr, cs, cr, xs, xr,
):
    c, f, t, me = slab_place(C, T)
    S = C * T
    R, W = hidden.shape
    Rh = tab.shape[0]
    HS = qgain.shape[1]
    PC = raw.shape[1]
    QC = heads.shape[1]
    KC = KH * HS
    L = kv.shape[1]
    G = QC // HS // KH
    root = HS ** (-0.5)
    core = lax.rem(c, 2)
    sib = c + 1 - 2 * core
    mate = lax.rem(c + 2, C)
    mate_sib = lax.rem(sib + 2, C)
    ra, (ro, co) = wa.shape[0], wo.shape
    pa, po = ra // C, ro // C
    ha, ho = pa // 2, po // 2
    columns = [(c, lax.rem(f + k, F), t) for k in range(1, F)]
    greet(columns + [slab_device(lax.rem(me + j, S), f, T) for j in range(1, S)])

    def spot(arr, b, p):
        half = arr % 2
        if arr < 2:
            return fa.at[pl.ds(pl.multiple_of(b * ra + p * pa + half * ha, ha), ha)]
        rows = pl.ds(pl.multiple_of(p * po + half * ho, ho), ho)
        return fo.at[rows, pl.ds(pl.multiple_of(b * co, co), co)]

    def own(arr):
        half = arr % 2
        if arr < 2:
            return wa.at[pl.ds(pl.multiple_of(c * pa + half * ha, ha), ha)]
        return wo.at[pl.ds(pl.multiple_of(c * po + half * ho, ho), ho)]

    def z_copy(arr, s, d):
        b = f - (s - 1) if d == 0 else f + (s - 1)
        source = own(arr) if s == 1 else spot(arr, b, c)
        there = (c, f + 1 if d == 0 else f - 1, t)
        return remote(source, spot(arr, b, c), zs.at[d, s, arr], zr.at[d, s, arr], there)

    def z_sends(s, d):
        b = f - (s - 1) if d == 0 else f + (s - 1)
        return (f + 1 < F) & (b >= 0) if d == 0 else (f > 0) & (b < F)

    def z_gets(s, d):
        return f - s >= 0 if d == 0 else f + s < F

    def came(s, d):
        return f - s if d == 0 else f + s

    def move(arr, s, d, p, sent, got, i, device):
        here = spot(arr, came(s, d), p)
        return remote(here, here, sent.at[d, s, arr, i], got.at[d, s, arr, i], device)

    def z_begin(arr):
        for d in range(2):

            @pl.when(z_sends(1, d))
            def _():
                z_copy(arr, 1, d).start()

    def z_in(arr, s):
        for d in range(2):

            @pl.when(z_gets(s, d))
            def _():
                here = spot(arr, came(s, d), c)
                remote(here, here, zs.at[d, s, arr], zr.at[d, s, arr], (sib, f, t)).wait_recv()
                if s + 1 < F:

                    @pl.when(z_sends(s + 1, d))
                    def _():
                        z_copy(arr, s + 1, d).start()

                move(arr, s, d, c, ys, yr, 0, (mate, f, t)).start()
                move(arr, s, d, c, ks, kr, 0, (sib, f, t)).start()

    def y_in(arr, s):
        for d in range(2):

            @pl.when(z_gets(s, d))
            def _():
                move(arr, s, d, mate, ys, yr, 0, (mate, f, t)).wait_recv()
                move(arr, s, d, mate, ks, kr, 1, (sib, f, t)).start()

    def k_in(arr, s, d):
        move(arr, s, d, sib, ks, kr, 0, (sib, f, t)).wait_recv()
        move(arr, s, d, mate_sib, ks, kr, 1, (sib, f, t)).wait_recv()

    z_begin(0)
    z_begin(1)
    tabs = [
        remote(tab, ftab.at[f], ts.at[k], tr.at[k], columns[k - 1]) for k in range(1, F)
    ]
    for copy in tabs:
        copy.start()
    own_a = pltpu.make_async_copy(wa, fa.at[pl.ds(pl.multiple_of(f * ra, ra), ra)], loc.at[0])
    own_o = pltpu.make_async_copy(
        wo, fo.at[:, pl.ds(pl.multiple_of(f * co, co), co)], loc.at[1]
    )
    own_a.start()
    own_o.start()
    ftab[f] = tab[...]

    inputs = hidden[...].astype(FL)
    normed[...] = norm_rows(inputs, again[...])[0].astype(BF)
    wide = min(512, PC)

    def project(b, first):
        at = pl.ds(pl.multiple_of(b * ra, ra), ra)
        left = normed[:, at]

        def piece(i, carry):
            cols = pl.ds(pl.multiple_of(i * wide, wide), wide)
            part = jnp.dot(left, fa[at, cols], preferred_element_type=FL)
            if first:
                raw[:, cols] = part
            else:
                raw[:, cols] += part
            return carry

        lax.fori_loop(0, PC // wide, piece, 0)

    def project_in(s):
        for d in range(2):

            @pl.when(z_gets(s, d))
            def _():
                k_in(0, s, d)
                k_in(1, s, d)
                project(came(s, d), False)

    own_a.wait()
    project(f, True)
    z_in(0, 1)
    z_in(1, 1)
    for s in range(2, F):
        z_in(0, s)
        y_in(0, s - 1)
        z_in(1, s)
        y_in(1, s - 1)
        if s == F - 2:
            z_begin(2)
            z_begin(3)
        project_in(s - 1)
    y_in(0, F - 1)
    y_in(1, F - 1)
    project_in(F - 1)

    def turn(values):
        return values * cosf[...] + pltpu.roll(values, HS // 2, 1) * sins[...]

    at_c = pl.ds(pl.multiple_of(c * R, R), R)
    for g in range(KH):
        k_raw = raw[:, QC + g * HS : QC + (g + 1) * HS]
        kv[g, at_c, :] = turn(norm_rows(k_raw, kgain[...])[0]).astype(BF)
        kv[KH + g, at_c, :] = raw[:, QC + KC + g * HS : QC + KC + (g + 1) * HS].astype(BF)

    def kv_move(p, i, device):
        here = kv.at[:, pl.ds(pl.multiple_of(p * R, R), R), :]
        return remote(here, here, cs.at[i], cr.at[i], device)

    kv_move(c, 0, (mate, f, t)).start()
    kv_move(c, 1, (sib, f, t)).start()

    def query(i, carry):
        at = pl.ds(pl.multiple_of(i * HS, HS), HS)
        qrot[:, at] = turn(norm_rows(raw[:, at], qgain[...])[0]).astype(BF)
        return carry

    lax.fori_loop(0, QC // HS, query, 0)
    save_a = pltpu.make_async_copy(fa, fall, loc.at[2])
    save_a.start()
    z_in(2, 1)
    z_in(3, 1)
    kv_move(mate, 0, (mate, f, t)).wait_recv()
    kv_move(mate, 2, (sib, f, t)).start()
    kv_move(sib, 1, (sib, f, t)).wait_recv()
    kv_move(mate_sib, 2, (sib, f, t)).wait_recv()
    for g in range(KH):
        keys_t[g] = kv[g].astype(FL).T.astype(BF)
        vals_t[g] = kv[KH + g].astype(FL).T.astype(BF)

    def some_heads(g, first, count):
        def one_head(i, carry):
            h = first + i
            at = pl.ds(pl.multiple_of(h * HS, HS), HS)
            scores = outer_cols(kv[g], qrot[:, at]) * root + bias[...]
            peak = jnp.max(scores, axis=0, keepdims=True)
            weight = jnp.exp(scores - peak)
            total = jnp.sum(weight, axis=0, keepdims=True)
            lse[pl.ds(h, 1), :] = peak + jnp.log(total)
            probs = (weight / total).astype(BF)
            heads[:, at] = jnp.dot(vals_t[g], probs, preferred_element_type=FL).T.astype(BF)
            return carry

        lax.fori_loop(0, count, one_head, 0)

    o_events = []
    for s in range(2, F):
        o_events.append((z_in, 2, s, y_in, 2, s - 1))
        o_events.append((z_in, 3, s, y_in, 3, s - 1))
    half = G // 2
    for i in range(2 * KH):
        some_heads(i // 2, i * half, half)
        if i < len(o_events):
            za, arr_a, sa, ya, arr_b, sb = o_events[i]
            za(arr_a, sa)
            ya(arr_b, sb)
    for za, arr_a, sa, ya, arr_b, sb in o_events[2 * KH :]:
        za(arr_a, sa)
        ya(arr_b, sb)
    y_in(2, F - 1)
    y_in(3, F - 1)
    for s in range(1, F):
        for d in range(2):

            @pl.when(z_gets(s, d))
            def _():
                k_in(2, s, d)
                k_in(3, s, d)

    own_o.wait()
    save_o = pltpu.make_async_copy(fo, full, loc.at[3])
    save_o.start()
    at_t = pl.ds(pl.multiple_of(t * Rh, Rh), Rh)
    at_u = pl.ds(pl.multiple_of((1 - t) * Rh, Rh), Rh)
    step = min(512, W)

    def theirs(i, carry):
        cols = pl.ds(pl.multiple_of(i * step, step), step)
        nsend[:, cols] = jnp.dot(
            heads[at_u, :], fo[:, cols], preferred_element_type=FL
        ).astype(BF)
        return carry

    def ours(i, carry):
        cols = pl.ds(pl.multiple_of(i * step, step), step)
        nown[:, cols] = jnp.dot(heads[at_t, :], fo[:, cols], preferred_element_type=FL)
        return carry

    lax.fori_loop(0, W // step, theirs, 0)
    swap = remote(nsend, ngot, xs.at[0], xr.at[0], (c, f, 1 - t))
    swap.start()
    lax.fori_loop(0, W // step, ours, 0)
    swap.wait_recv()
    total = hidden[at_t, :].astype(FL) + (nown[...] + ngot[...].astype(FL))
    resid[...] = total
    ffn_low = norm_rows(total, fgain[...])[0].astype(BF)
    low[...] = ffn_low
    logits = jnp.dot(ffn_low, fa[:, PC:], preferred_element_type=FL)
    named = tab[...] >= 0.0
    masked = jnp.where(named, logits, MASKED)
    shifted = jnp.where(
        named, jnp.exp(masked - jnp.max(masked, axis=-1, keepdims=True)), 0.0
    )
    gates[...] = shifted / jnp.sum(shifted, axis=-1, keepdims=True)

    save_a.wait()
    save_o.wait()
    swap.wait_send()
    for copy in tabs:
        copy.wait()
    kv_move(c, 0, (mate, f, t)).wait_send()
    kv_move(c, 1, (sib, f, t)).wait_send()
    kv_move(mate, 2, (sib, f, t)).wait_send()
    for s in range(1, F):
        for d in range(2):

            @pl.when(z_sends(s, d))
            def _():
                for arr in range(4):
                    z_copy(arr, s, d).wait_send()

            @pl.when(z_gets(s, d))
            def _():
                for arr in range(4):
                    move(arr, s, d, c, ys, yr, 0, (mate, f, t)).wait_send()
                    move(arr, s, d, c, ks, kr, 0, (sib, f, t)).wait_send()
                    move(arr, s, d, mate, ks, kr, 1, (sib, f, t)).wait_send()


def head(identity, C, F, T, KH, PC, L, args):
    hidden, tab, qgain, wa, wo = args[0], args[1], args[3], args[9], args[10]
    R, W = hidden.shape
    Rh, lanes = tab.shape
    HS = qgain.shape[1]
    ra, ca = wa.shape
    QC, co = wo.shape
    dma = pltpu.SemaphoreType.DMA
    V = pltpu.VMEM
    shape = jax.ShapeDtypeStruct
    return pl.pallas_call(
        functools.partial(head_body, C, F, T, KH),
        out_shape=(
            shape((F * ra, ca), BF), shape((QC, F * co), BF), shape((F, Rh, lanes), FL),
            shape((R, PC), FL), shape((R, QC), BF), shape((2 * KH, L, HS), BF),
            shape((KH, HS, L), BF), shape((QC // HS, R), FL), shape((R, QC), BF),
            shape((R, W), BF), shape((Rh, W), FL), shape((Rh, W), BF), shape((Rh, lanes), FL),
        ),
        in_specs=[VMEM] * 9 + [ANY] * 2,
        out_specs=[ANY] * 2 + [VMEM] * 11,
        scratch_shapes=[
            V((F * ra, ca), BF), V((QC, F * co), BF), V((KH, HS, L), BF),
            V((Rh, W), BF), V((Rh, W), BF), V((Rh, W), FL),
            dma((4,)), dma((2, F, 4)), dma((2, F, 4)), dma((2, F, 4, 1)), dma((2, F, 4, 1)),
            dma((2, F, 4, 2)), dma((2, F, 4, 2)), dma((F,)), dma((F,)), dma((3,)), dma((3,)),
            dma((1,)), dma((1,)),
        ],
        compiler_params=params(identity, 58),
    )(*args)


def split_low(values):
    high = lax.reduce_precision(values, 8, 7)
    return high.astype(BF), (values - high).astype(BF)


def local(
    hidden_in,
    teacher,
    lengths,
    routes,
    attn_gain,
    w_query,
    w_key,
    w_value,
    w_output,
    query_gain,
    key_gain,
    ffn_gain,
    w_router,
    w_expert_in,
    w_expert_out,
):
    c, f, t = place()
    C, F, T = (lax.axis_size(axis) for axis in AXES)
    S = C * T
    row_count = hidden_in.shape[1]
    width = hidden_in.shape[2]
    half_rows = row_count // T
    head_size = query_gain.shape[0]
    inv_root = head_size ** (-0.5)
    bf_type = BF
    fl_type = FL

    expert_count = S * F
    lanes = -(-expert_count // 128) * 128
    route_ids = routes[0]
    top_count = route_ids.shape[1]
    capacity = max(2, half_rows * top_count * 3 // (2 * expert_count))
    cap = -(-capacity // 16) * 16
    expert_ids = jnp.arange(lanes, dtype=jnp.int32)
    named = jnp.any(route_ids[:, :, None] == expert_ids[None, None, :], axis=1)
    row_ids = jnp.arange(half_rows, dtype=jnp.int32)
    below = (row_ids[None, :] < row_ids[:, None]).astype(bf_type)
    earlier = jnp.dot(below, named.astype(bf_type), preferred_element_type=fl_type)
    rank_tab = jnp.where(named, earlier, -1.0)

    q_cols, kv_cols = w_query.shape[1], w_key.shape[1]
    w_all = jnp.concatenate(
        [w_query, w_key, w_value, jnp.pad(w_router, ((0, 0), (0, lanes - expert_count)))], axis=1
    )
    proj_cols = q_cols + 2 * kv_cols
    q_heads = q_cols // head_size
    kv_heads = kv_cols // head_size
    group_size = q_heads // kv_heads
    inputs = hidden_in[0].astype(fl_type)
    positions = c * row_count + jnp.arange(row_count, dtype=jnp.int32)
    cosine, sine_tab = rope_tables(positions, head_size)
    length = jnp.take(lengths, f)
    total_len = row_count * C
    row_start = t * half_rows
    other_start = (1 - t) * half_rows
    own_inputs = lax.dynamic_slice_in_dim(inputs, row_start, half_rows, 0)
    own_positions = lax.dynamic_slice_in_dim(positions, row_start, half_rows, 0)
    fused = C == 4 and T == 2
    swap = [(i, 1 - i) for i in range(T)]
    if fused:
        cos_full = jnp.concatenate([cosine, cosine], axis=1)
        sin_signed = jnp.concatenate([-sine_tab, sine_tab], axis=1)
        key_pos = jnp.arange(total_len, dtype=jnp.int32)[:, None]
        bias = jnp.where((key_pos <= positions[None, :]) & (key_pos < length), 0.0, MASKED)
        (
            full_all, full_o, rank_z, raw, q_rot, all_both, keys_t, log_total, heads_low,
            normed_low, residual, ffn_low, gate_tab,
        ) = head(
            1, C, F, T, kv_heads, proj_cols, total_len,
            (
                hidden_in[0], rank_tab, attn_gain[None], query_gain[None], key_gain[None],
                ffn_gain[None], cos_full, sin_signed, bias, w_all, w_output,
            ),
        )
        full_router = full_all[:, proj_cols : proj_cols + expert_count]
        gates = gate_tab[:, :expert_count]
        ffn_factor = lax.rsqrt(jnp.mean(residual * residual, axis=-1, keepdims=True) + EPS)
    else:
        full_all, full_o, rank_z = gather_weights(C, F, w_all, w_output, rank_tab)
        full_qkv = full_all[:, :proj_cols]
        full_router = full_all[:, proj_cols : proj_cols + expert_count]
        normed, norm_factor = norm_rows(inputs, attn_gain)
        normed_low = normed.astype(bf_type)
        raw = jnp.dot(normed_low, full_qkv, preferred_element_type=fl_type)
        q_raw = raw[:, :q_cols].reshape(row_count, q_heads, head_size)
        k_raw = raw[:, q_cols : q_cols + kv_cols].reshape(row_count, kv_heads, head_size)
        values_low = raw[:, q_cols + kv_cols :].astype(bf_type).reshape(row_count, kv_heads, head_size)
        q_normed, q_factor = norm_rows(q_raw, query_gain)
        k_normed, k_factor = norm_rows(k_raw, key_gain)
        q_rot = rotate(q_normed, cosine, sine_tab).astype(bf_type)
        k_rot = rotate(k_normed, cosine, sine_tab).astype(bf_type)
        queries = jnp.transpose(q_rot.reshape(row_count, kv_heads, group_size, head_size), (1, 2, 0, 3))
        both = jnp.transpose(jnp.concatenate([k_rot, values_low], axis=1), (1, 0, 2))
        all_both = lax.all_gather(both, "ctx", axis=1, tiled=True)
        all_keys, all_values = all_both[:kv_heads], all_both[kv_heads:]
        block_len = min(1024, total_len)
        offsets = jnp.arange(total_len // block_len, dtype=jnp.int32) * block_len
        stat_shape = (kv_heads, group_size, row_count)

        def lse_step(carry, offset):
            running_max, running_sum = carry
            key_rows = lax.dynamic_slice_in_dim(all_keys, offset, block_len, 1)
            scores, allowed = block_scores(queries, key_rows, offset, positions, length, inv_root)
            new_max = jnp.maximum(running_max, jnp.max(scores, axis=-1))
            exponent = jnp.where(allowed, jnp.exp(scores - new_max[..., None]), 0.0)
            return (
                (new_max, running_sum * jnp.exp(running_max - new_max) + jnp.sum(exponent, axis=-1)),
                None,
            )

        (row_max, row_sum), _ = lax.scan(
            lse_step, (jnp.full(stat_shape, MASKED, fl_type), jnp.zeros(stat_shape, fl_type)), offsets
        )
        log_total = row_max + jnp.log(row_sum)

        def probs_of(offset):
            key_rows = lax.dynamic_slice_in_dim(all_keys, offset, block_len, 1)
            value_rows = lax.dynamic_slice_in_dim(all_values, offset, block_len, 1)
            scores, allowed = block_scores(queries, key_rows, offset, positions, length, inv_root)
            return (
                jnp.where(allowed, jnp.exp(scores - log_total[..., None]), 0.0),
                key_rows,
                value_rows,
            )

        def out_step(running, offset):
            probabilities, key_rows, value_rows = probs_of(offset)
            return (
                running
                + jnp.einsum(
                    "kgqj,kjd->kgqd",
                    probabilities.astype(bf_type),
                    value_rows,
                    preferred_element_type=fl_type,
                ),
                None,
            )

        attn_acc, _ = lax.scan(
            out_step, jnp.zeros((kv_heads, group_size, row_count, head_size), fl_type), offsets
        )
        heads_low = (
            jnp.transpose(attn_acc, (2, 0, 1, 3))
            .reshape(row_count, q_heads * head_size)
            .astype(bf_type)
        )
        heads_other = lax.dynamic_slice_in_dim(heads_low, other_start, half_rows, 0)
        heads_own = lax.dynamic_slice_in_dim(heads_low, row_start, half_rows, 0)
        theirs = jnp.dot(heads_other, full_o, preferred_element_type=fl_type).astype(bf_type)
        ours = lax.ppermute(theirs, "tp", swap)
        attn_rows = jnp.dot(heads_own, full_o, preferred_element_type=fl_type) + ours.astype(fl_type)
        own_factor = lax.dynamic_slice_in_dim(norm_factor, row_start, half_rows, 0)
        residual = own_inputs + attn_rows
        ffn_in, ffn_factor = norm_rows(residual, ffn_gain)
        ffn_low = ffn_in.astype(bf_type)
        logits = jnp.dot(ffn_low, full_router, preferred_element_type=fl_type)
        is_named = named[:, :expert_count]
        masked = jnp.where(is_named, logits, MASKED)
        shifted = jnp.where(is_named, jnp.exp(masked - jnp.max(masked, axis=-1, keepdims=True)), 0.0)
        gates = shifted / jnp.sum(shifted, axis=-1, keepdims=True)
        gate_tab = jnp.pad(gates, ((0, 0), (0, lanes - expert_count)))

    def of_slab(table):
        picked = table[:, :, :expert_count].reshape(F, half_rows, C, F, T)
        return lax.dynamic_index_in_dim(picked, f, 3, keepdims=False).reshape(F, half_rows, S)

    rank_slab = of_slab(rank_z)
    slot_ids = jnp.arange(cap, dtype=fl_type)
    chosen_rows = rank_slab[:, :, :, None] == slot_ids
    chosen_slots = (
        jnp.transpose(rank_slab, (0, 2, 1))[:, :, None, :] == slot_ids[:, None]
    )

    select = chosen_slots.astype(bf_type)
    received, _, gate_z = dispatch(2, C, F, T, ffn_low, select, gate_tab)
    expert_rows = received.reshape(-1, width)
    both_pre = jnp.dot(expert_rows, w_expert_in[0], preferred_element_type=fl_type)
    ff_width = w_expert_out.shape[1]
    gate_pre = both_pre[:, :ff_width]
    up_pre = both_pre[:, ff_width:]
    sigmoid_gate = jax.nn.sigmoid(gate_pre)
    silu_gate = gate_pre * sigmoid_gate
    mixed_low = (silu_gate * up_pre).astype(bf_type)
    expert_out = (
        jnp.dot(mixed_low, w_expert_out[0], preferred_element_type=fl_type)
        .astype(bf_type)
        .reshape(S, F, cap, width)
    )
    gate_slab = of_slab(gate_z)
    weigh = jnp.where(chosen_rows, gate_slab[..., None], 0.0).reshape(F, 1, half_rows, S * cap)
    weigh = jnp.concatenate(split_low(weigh), axis=1)
    returned, parts = combine(3, C, F, T, expert_out, weigh)
    output_f = residual + jnp.sum(parts.astype(fl_type), axis=0)
    count = jnp.sum(lengths).astype(fl_type)
    tokens_total = lengths.shape[0] * row_count * C
    valid = own_positions < length
    error = jnp.where(valid[:, None], output_f - teacher[0].astype(fl_type), 0.0)
    loss_part = jnp.sum(error * error)
    grad_out = error * (tokens_total / count)

    select_gates = jnp.where(
        chosen_slots, jnp.transpose(gate_slab, (0, 2, 1))[:, :, None, :], 0.0
    )
    select_gates = jnp.concatenate(split_low(select_gates), axis=-1)
    grad_recv, grad_out_z = dispatch(4, C, F, T, grad_out.astype(bf_type), select_gates)
    slot_grads = jnp.einsum("zskr,zrd->zskd", select, grad_out_z, preferred_element_type=fl_type)
    slot_gate = jnp.sum(slot_grads * returned.astype(fl_type), axis=-1)
    gate_grads = jnp.sum(jnp.where(chosen_rows, slot_gate[:, None, :, :], 0.0), axis=-1)
    gate_grads = jnp.pad(gate_grads, ((0, 0), (0, 0), (0, -S % 128)))

    grad_recv = grad_recv.reshape(-1, width)
    grad_mixed = outer_cols(grad_recv, w_expert_out[0])
    grad_expert_out = inner_rows(mixed_low, grad_recv)
    grad_gate_pre = grad_mixed * up_pre * (sigmoid_gate * (1.0 + gate_pre * (1.0 - sigmoid_gate)))
    grad_up_pre = grad_mixed * silu_gate
    grad_pre = jnp.concatenate([grad_gate_pre, grad_up_pre], axis=1).astype(bf_type)
    grad_expert_in = inner_rows(expert_rows, grad_pre)
    grad_rows = (
        outer_cols(grad_pre, w_expert_in[0]).astype(bf_type).reshape(S, F, cap, width)
    )
    weigh_one = chosen_rows.astype(bf_type).reshape(F, 1, half_rows, S * cap)
    _, grad_parts, gate_back = combine(5, C, F, T, grad_rows, weigh_one, gate_grads)
    grad_gate = jnp.transpose(
        gate_back[:, :, :S].reshape(F, half_rows, C, T), (1, 2, 0, 3)
    ).reshape(half_rows, expert_count)
    grad_logits = (
        gates * (grad_gate - jnp.sum(gates * grad_gate, axis=-1, keepdims=True))
    ).astype(bf_type)
    grad_ffn = jnp.sum(grad_parts.astype(fl_type), axis=0) + outer_cols(grad_logits, full_router)
    router_part = inner_rows(ffn_low, grad_logits)
    grad_resid_norm, ffn_gain_terms = norm_back(residual, ffn_factor, ffn_gain, grad_ffn)
    grad_residual = grad_out + grad_resid_norm
    grad_own = grad_residual.astype(bf_type)
    if fused:
        vec_in = jnp.zeros((8, width), fl_type)
        vec_in = vec_in.at[1].set(jnp.sum(ffn_gain_terms, axis=0))
        vec_in = vec_in.at[2, 2 * head_size].set(loss_part)
        router_rows = router_part.reshape(F, -1, width)
        grad_input, total_a, total_o, summed = tail(
            9, C, F, T, kv_heads,
            (
                grad_own, heads_low, normed_low, q_rot, all_both, keys_t, raw, log_total, bias,
                cos_full, sin_signed, query_gain[None], key_gain[None], attn_gain[None],
                own_inputs, grad_residual, router_rows, vec_in, full_o, full_all,
            ),
            width, q_cols // C,
        )
        grad_query = total_a[:, :q_cols].astype(fl_type)
        grad_key = total_a[:, q_cols : q_cols + kv_cols].astype(fl_type)
        grad_value = total_a[:, q_cols + kv_cols :].astype(fl_type)
        grad_output_w = total_o.astype(fl_type)
        router_len = router_rows.shape[1]
        grad_router = summed[:router_len].reshape(w_router.shape)
        sum_attn, sum_ffn = summed[router_len], summed[router_len + 1]
        sum_query = summed[router_len + 2, :head_size]
        sum_key = summed[router_len + 2, head_size : 2 * head_size]
        loss_total = summed[router_len + 2, 2 * head_size]
    else:
        grad_other = lax.ppermute(grad_own, "tp", swap)
        grad_attn = jnp.where(
            t == 0,
            jnp.concatenate([grad_own, grad_other], axis=0),
            jnp.concatenate([grad_other, grad_own], axis=0),
        )
        grad_heads = jnp.transpose(
            outer_cols(grad_attn, full_o)
            .astype(bf_type)
            .reshape(row_count, kv_heads, group_size, head_size),
            (1, 2, 0, 3),
        )

        def delta_step(running, offset):
            probabilities, key_rows, value_rows = probs_of(offset)
            grad_weights = jnp.einsum(
                "kgqd,kjd->kgqj", grad_heads, value_rows, preferred_element_type=fl_type
            )
            return (running + jnp.sum(probabilities * grad_weights, axis=-1), None)

        delta, _ = lax.scan(delta_step, jnp.zeros(stat_shape, fl_type), offsets)

        def grad_step(running, offset):
            probabilities, key_rows, value_rows = probs_of(offset)
            grad_weights = jnp.einsum(
                "kgqd,kjd->kgqj", grad_heads, value_rows, preferred_element_type=fl_type
            )
            grad_scores = (probabilities * (grad_weights - delta[..., None])).astype(bf_type)
            running = (
                running
                + jnp.einsum("kgqj,kjd->kgqd", grad_scores, key_rows, preferred_element_type=fl_type)
                * inv_root
            )
            key_part = (
                jnp.einsum("kgqj,kgqd->kjd", grad_scores, queries, preferred_element_type=fl_type)
                * inv_root
            )
            value_part = jnp.einsum(
                "kgqj,kgqd->kjd",
                probabilities.astype(bf_type),
                grad_heads,
                preferred_element_type=fl_type,
            )
            return (running, (key_part, value_part))

        grad_qrot, (key_blocks, value_blocks) = lax.scan(
            grad_step, jnp.zeros((kv_heads, group_size, row_count, head_size), fl_type), offsets
        )
        both_grads = jnp.concatenate([key_blocks, value_blocks], axis=1).astype(bf_type)
        both_grads = jnp.transpose(both_grads, (0, 2, 1, 3)).reshape(C, row_count, 2 * kv_cols)
        both_sum = ctx_sum(6, C, both_grads)
        grad_krot = both_sum[:, :kv_cols].reshape(row_count, kv_heads, head_size)
        grad_values_low = both_sum[:, kv_cols:].astype(bf_type)
        grad_qrot = jnp.transpose(grad_qrot, (2, 0, 1, 3)).reshape(row_count, q_heads, head_size)
        grad_qraw, query_gain_terms = norm_back(
            q_raw, q_factor, query_gain, rotate(grad_qrot, cosine, -sine_tab)
        )
        grad_kraw, key_gain_terms = norm_back(
            k_raw, k_factor, key_gain, rotate(grad_krot, cosine, -sine_tab)
        )
        grad_raw = jnp.concatenate(
            [
                grad_qraw.astype(bf_type).reshape(row_count, -1),
                grad_kraw.astype(bf_type).reshape(row_count, -1),
                grad_values_low,
            ],
            axis=1,
        )
        raw_other = lax.dynamic_slice_in_dim(grad_raw, other_start, half_rows, 0)
        raw_own = lax.dynamic_slice_in_dim(grad_raw, row_start, half_rows, 0)
        norm_theirs = outer_cols(raw_other, full_qkv).astype(bf_type)
        norm_ours = lax.ppermute(norm_theirs, "tp", swap)
        grad_normed = outer_cols(raw_own, full_qkv) + norm_ours.astype(fl_type)
        grad_input_norm, attn_gain_terms = norm_back(own_inputs, own_factor, attn_gain, grad_normed)
        grad_input = grad_residual + grad_input_norm

        total_a, total_o = weight_grads(
            7, C, F, normed_low.T, grad_raw, heads_low.T, grad_attn
        )
        total_a = total_a.reshape(-1, proj_cols).astype(fl_type)
        grad_query = total_a[:, :q_cols]
        grad_key = total_a[:, q_cols : q_cols + kv_cols]
        grad_value = total_a[:, q_cols + kv_cols :]
        grad_output_w = total_o.reshape(w_output.shape).astype(fl_type)

        vector = jnp.concatenate(
            [
                jnp.sum(attn_gain_terms, axis=0),
                jnp.sum(ffn_gain_terms, axis=0),
                jnp.sum(query_gain_terms, axis=(0, 1)),
                jnp.sum(key_gain_terms, axis=(0, 1)),
                loss_part[None],
            ]
        )
        vector = jnp.pad(vector, (0, -vector.shape[0] % 1024)).reshape(-1, 128)
        router_rows = router_part.reshape(F, -1, 128)
        small = jnp.concatenate(
            [router_rows, jnp.broadcast_to(vector[None], (F,) + vector.shape)], axis=1
        )
        summed = small_sum(8, C, F, T, small)
        router_len = router_rows.shape[1]
        grad_router = summed[:router_len].reshape(w_router.shape)
        flat = summed[router_len:].reshape(-1)
        head_at = 2 * width
        sum_attn, sum_ffn = flat[:width], flat[width:head_at]
        sum_query = flat[head_at : head_at + head_size]
        sum_key = flat[head_at + head_size : head_at + 2 * head_size]
        loss_total = flat[head_at + 2 * head_size]
    loss_value = loss_total / (count * width)
    return (
        output_f.astype(bf_type)[None],
        loss_value,
        grad_input[None],
        sum_attn,
        grad_query,
        grad_key,
        grad_value,
        grad_output_w,
        sum_query,
        sum_key,
        sum_ffn,
        grad_router,
        grad_expert_in[None],
        grad_expert_out[None],
    )


def solution(mesh):
    return jax.shard_map(
        local,
        mesh=mesh,
        in_specs=(
            P("fsdp", "ctx", None),
            P("fsdp", ("ctx", "tp"), None),
            P(),
            P("fsdp", ("ctx", "tp"), None),
            P(),
            P("fsdp", "tp"),
            P("fsdp", "tp"),
            P("fsdp", "tp"),
            P("tp", "fsdp"),
            P(),
            P(),
            P(),
            P("fsdp", None),
            P(("ctx", "fsdp", "tp"), None, None),
            P(("ctx", "fsdp", "tp"), None, None),
        ),
        out_specs=(
            P("fsdp", ("ctx", "tp"), None),
            P(),
            P("fsdp", ("ctx", "tp"), None),
            P(),
            P("fsdp", "tp"),
            P("fsdp", "tp"),
            P("fsdp", "tp"),
            P("tp", "fsdp"),
            P(),
            P(),
            P(),
            P("fsdp", None),
            P(("ctx", "fsdp", "tp"), None, None),
            P(("ctx", "fsdp", "tp"), None, None),
        ),
        check_vma=False,
    )
```

```python
import functools

import jax
import jax.numpy as jnp
from jax import lax
from jax.experimental import pallas as pl
from jax.experimental.pallas import tpu as pltpu
from jax.sharding import PartitionSpec as P

EPS = 1e-06
ROPE_BASE = 1000000.0
MASKED = -1e30
AXES = ("ctx", "fsdp", "tp")
MESH = pl.DeviceIdType.MESH
ANY = pl.BlockSpec(memory_space=pl.ANY)
VMEM = pl.BlockSpec(memory_space=pltpu.VMEM)
BF = jnp.bfloat16
FL = jnp.float32
MIB = 1024 * 1024


def norm_rows(values, gain_vec):
    factor = lax.rsqrt(jnp.mean(values * values, axis=-1, keepdims=True) + EPS)
    return (values * factor * gain_vec, factor)


def norm_back(values, factor, gain_vec, upstream):
    weighted = upstream * gain_vec
    inner_mean = jnp.mean(values * weighted, axis=-1, keepdims=True)
    return (
        factor * weighted - values * (factor * factor * factor) * inner_mean,
        upstream * values * factor,
    )


def rope_tables(positions, head_size):
    half_size = head_size // 2
    frequency = jnp.power(ROPE_BASE, -jnp.arange(half_size, dtype=jnp.float32) * (2.0 / head_size))
    angles = positions.astype(jnp.float32)[:, None] * frequency[None, :]
    return (jnp.cos(angles), jnp.sin(angles))


def rotate(values, cosine, sine_tab):
    half_size = values.shape[-1] // 2
    front_half = values[..., :half_size]
    back_half = values[..., half_size:]
    cos_rows = cosine[:, None, :]
    sin_rows = sine_tab[:, None, :]
    return jnp.concatenate(
        [
            front_half * cos_rows - back_half * sin_rows,
            back_half * cos_rows + front_half * sin_rows,
        ],
        axis=-1,
    )


def inner_rows(left, right):
    return lax.dot_general(
        left, right, (((0,), (0,)), ((), ())), preferred_element_type=jnp.float32
    )


def outer_cols(left, right):
    return lax.dot_general(
        left, right, (((1,), (1,)), ((), ())), preferred_element_type=jnp.float32
    )


def block_scores(queries, key_rows, offset, positions, length, inv_root):
    block_len = key_rows.shape[1]
    raw_scores = (
        jnp.einsum("kgqd,kjd->kgqj", queries, key_rows, preferred_element_type=jnp.float32)
        * inv_root
    )
    key_pos = offset + jnp.arange(block_len, dtype=jnp.int32)
    allowed = (key_pos[None, :] <= positions[:, None]) & (key_pos[None, :] < length)
    return (jnp.where(allowed, raw_scores, MASKED), allowed)


def place():
    return tuple(lax.axis_index(axis) for axis in AXES)


def remote(source, target, sent, got, device):
    return pltpu.make_async_remote_copy(
        src_ref=source, dst_ref=target, send_sem=sent, recv_sem=got,
        device_id=device, device_id_type=MESH,
    )


def greet(devices):
    barrier = pltpu.get_barrier_semaphore()
    for device in devices:
        pl.semaphore_signal(barrier, inc=1, device_id=device, device_id_type=MESH)
    pl.semaphore_wait(barrier, len(devices))


def params(identity, mebibytes):
    return pltpu.CompilerParams(
        collective_id=identity, has_side_effects=True, vmem_limit_bytes=int(mebibytes * MIB)
    )


def gather_body(C, F, wa, wo, tab, fa, fo, ftab, loc, zs, zr, ys, yr, ks, kr, ts, tr):
    c, f, t = place()
    core, chip = lax.rem(c, 2), lax.div(c, 2)
    chips = C // 2
    sib = c + 1 - 2 * core
    ra, (ro, co) = wa.shape[0], wo.shape
    pa, po = ra // C, ro // C

    def spot(arr, b, p):
        if arr == 0:
            return fa.at[pl.ds(pl.multiple_of(b * ra + p * pa, pa), pa)]
        return fo.at[pl.ds(pl.multiple_of(p * po, po), po), pl.ds(pl.multiple_of(b * co, co), co)]

    def own(arr):
        if arr == 0:
            return wa.at[pl.ds(pl.multiple_of(c * pa, pa), pa)]
        return wo.at[pl.ds(pl.multiple_of(c * po, po), po)]

    peers = [(c, lax.rem(f + k, F), t) for k in range(1, F)]
    peers += [(lax.rem(chip + k, chips) * 2 + core, f, t) for k in range(1, chips)]
    peers += [(sib, f, t)]
    greet(peers)

    def z_copy(arr, s, d):
        b = f - (s - 1) if d == 0 else f + (s - 1)
        source = own(arr) if s == 1 else spot(arr, b, c)
        return remote(
            source, spot(arr, b, c), zs.at[d, s, arr], zr.at[d, s, arr],
            (c, f + 1 if d == 0 else f - 1, t),
        )

    def z_sends(s, d):
        b = f - (s - 1) if d == 0 else f + (s - 1)
        return (f + 1 < F) & (b >= 0) if d == 0 else (f > 0) & (b < F)

    def z_gets(s, d):
        return f - s >= 0 if d == 0 else f + s < F

    def came(s, d):
        return f - s if d == 0 else f + s

    def z_arrival(arr, s, d):
        b = came(s, d)
        here = spot(arr, b, c)
        return remote(here, here, zs.at[d, s, arr], zr.at[d, s, arr], (c, f, t))

    def y_copy(arr, s, d, k):
        here = spot(arr, came(s, d), c)
        there = (lax.rem(chip + k, chips) * 2 + core, f, t)
        return remote(here, here, ys.at[d, s, k, arr], yr.at[d, s, k, arr], there)

    def k_copy(arr, s, d, k, side):
        p = lax.rem(chip + chips - k, chips) * 2 + side
        here = spot(arr, came(s, d), p)
        return remote(here, here, ks.at[d, s, k, arr], kr.at[d, s, k, arr], (sib, f, t))

    def y_arrival(arr, s, d, k):
        p = lax.rem(chip + chips - k, chips) * 2 + core
        here = spot(arr, came(s, d), p)
        return remote(here, here, ys.at[d, s, k, arr], yr.at[d, s, k, arr], (sib, f, t))

    tabs = [
        remote(tab, ftab.at[f], ts.at[k], tr.at[k], (c, lax.rem(f + k, F), t)) for k in range(1, F)
    ]
    for copy in tabs:
        copy.start()
    for d in range(2):

        @pl.when(z_sends(1, d))
        def _():
            for arr in range(2):
                z_copy(arr, 1, d).start()

    locals_ = [
        pltpu.make_async_copy(tab, ftab.at[f], loc.at[0]),
        pltpu.make_async_copy(wa, fa.at[pl.ds(pl.multiple_of(f * ra, ra), ra)], loc.at[1]),
        pltpu.make_async_copy(wo, fo.at[:, pl.ds(pl.multiple_of(f * co, co), co)], loc.at[2]),
    ]
    for copy in locals_:
        copy.start()

    def pass_on(s, d):
        for arr in range(2):
            for k in range(1, chips):
                y_arrival(arr, s, d, k).wait_recv()
                k_copy(arr, s, d, k, core).start()

    for s in range(1, F):
        for d in range(2):

            @pl.when(z_gets(s, d))
            def _():
                for arr in range(2):
                    z_arrival(arr, s, d).wait_recv()
                    if s + 1 < F:

                        @pl.when(z_sends(s + 1, d))
                        def _():
                            z_copy(arr, s + 1, d).start()

                    for k in range(1, chips):
                        y_copy(arr, s, d, k).start()
                    k_copy(arr, s, d, 0, core).start()

        if s > 1:
            for d in range(2):
                pl.when(z_gets(s - 1, d))(functools.partial(pass_on, s - 1, d))
    for d in range(2):
        pl.when(z_gets(F - 1, d))(functools.partial(pass_on, F - 1, d))
    for copy in tabs:
        copy.wait()
    for copy in locals_:
        copy.wait()
    for s in range(1, F):
        for d in range(2):

            @pl.when(z_sends(s, d))
            def _():
                for arr in range(2):
                    z_copy(arr, s, d).wait_send()

            @pl.when(z_gets(s, d))
            def _():
                for arr in range(2):
                    for k in range(1, chips):
                        y_copy(arr, s, d, k).wait_send()
                    for k in range(chips):
                        k_copy(arr, s, d, k, core).wait_send()
                        k_copy(arr, s, d, k, 1 - core).wait_recv()


def gather_weights(C, F, wa, wo, tab):
    ra, ca = wa.shape
    ro, co = wo.shape
    chips = C // 2
    dma = pltpu.SemaphoreType.DMA
    return pl.pallas_call(
        functools.partial(gather_body, C, F),
        out_shape=(
            jax.ShapeDtypeStruct((F * ra, ca), wa.dtype),
            jax.ShapeDtypeStruct((ro, F * co), wo.dtype),
            jax.ShapeDtypeStruct((F,) + tab.shape, tab.dtype),
        ),
        in_specs=[ANY] * 3,
        out_specs=[ANY] * 3,
        scratch_shapes=[
            dma((3,)), dma((2, F, 2)), dma((2, F, 2)),
            dma((2, F, chips, 2)), dma((2, F, chips, 2)),
            dma((2, F, chips, 2)), dma((2, F, chips, 2)),
            dma((F,)), dma((F,)),
        ],
        compiler_params=params(1, 16),
    )(wa, wo, tab)


def slab_place(C, T):
    c, f, t = place()
    return c, f, t, c * T + t


def slab_device(index, f, T):
    return (lax.div(index, T), f, lax.rem(index, T))


def dispatch_body(C, F, T, tabbed, rows, select, *refs):
    if tabbed:
        tab, out, zbuf, ftab, stage, loc, zs, zr, ss, sr, ts, tr = refs
    else:
        out, zbuf, stage, loc, zs, zr, ss, sr = refs
    c, f, t, me = slab_place(C, T)
    S = C * T
    K = select.shape[2]
    copies = select.shape[3] // rows.shape[0]
    columns = [(c, lax.rem(f + k, F), t) for k in range(1, F)]
    greet(columns + [slab_device(lax.rem(me + j, S), f, T) for j in range(1, S)])
    sends = [
        remote(rows, zbuf.at[f], zs.at[k], zr.at[k], columns[k - 1]) for k in range(1, F)
    ]
    if tabbed:
        tabs = [remote(tab, ftab.at[f], ts.at[k], tr.at[k], columns[k - 1]) for k in range(1, F)]
        for copy in tabs:
            copy.start()
        ftab[f] = tab[...]
    for copy in sends:
        copy.start()
    zbuf[f] = rows[...]

    def slab_copy(k, j):
        b = lax.rem(f + F - k, F)
        e = lax.rem(me + j, S)
        return remote(
            stage.at[e, b], out.at[me, b], ss.at[k, j], sr.at[k, j], slab_device(e, f, T)
        )

    def slab_arrival(k, j):
        b = lax.rem(f + F - k, F)
        e = lax.rem(me + S - j, S)
        return remote(
            stage.at[e, b], out.at[e, b], ss.at[k, j], sr.at[k, j], slab_device(e, f, T)
        )

    def own_copy(k):
        b = lax.rem(f + F - k, F)
        return pltpu.make_async_copy(stage.at[me, b], out.at[me, b], loc.at[k])

    for k in range(F):
        b = lax.rem(f + F - k, F)
        if k > 0:
            remote(rows, zbuf.at[b], zs.at[k], zr.at[k], columns[k - 1]).wait_recv()

        def pick(j):
            e = lax.rem(me + j, S)
            block = zbuf[b]
            if copies > 1:
                block = jnp.concatenate([block] * copies, axis=0)
            stage[e, b] = jnp.dot(
                select[b, e], block, preferred_element_type=FL
            ).astype(BF)

        if S <= 8:
            for j in range(1, S):
                pick(j)
                slab_copy(k, j).start()
        else:

            def step(j, carry):
                pick(j)
                slab_copy(k, j).start()
                return carry

            lax.fori_loop(1, S, step, 0)
        pick(0)
        own_copy(k).start()
    if tabbed:
        for copy in tabs:
            copy.wait()
    for copy in sends:
        copy.wait_send()
    for k in range(F):
        own_copy(k).wait()

        def settle(j, carry):
            slab_copy(k, j).wait_send()
            slab_arrival(k, j).wait_recv()
            return carry

        lax.fori_loop(1, S, settle, 0)


def dispatch(identity, C, F, T, rows, select, tab=None):
    S = C * T
    K = select.shape[2]
    R, W = rows.shape
    dma = pltpu.SemaphoreType.DMA
    tabbed = tab is not None
    outs = [jax.ShapeDtypeStruct((S, F, K, W), BF), jax.ShapeDtypeStruct((F, R, W), BF)]
    out_specs = [ANY, VMEM]
    ins = [rows, select]
    scratch = [
        pltpu.VMEM((S, F, K, W), BF), dma((F,)), dma((F,)), dma((F,)), dma((F, S)), dma((F, S)),
    ]
    if tabbed:
        outs.append(jax.ShapeDtypeStruct((F,) + tab.shape, tab.dtype))
        out_specs.append(VMEM)
        ins.append(tab)
        scratch += [dma((F,)), dma((F,))]
    return pl.pallas_call(
        functools.partial(dispatch_body, C, F, T, tabbed),
        out_shape=tuple(outs),
        in_specs=[VMEM] * len(ins),
        out_specs=out_specs,
        scratch_shapes=scratch,
        compiler_params=params(identity, 32),
    )(*ins)


def combine_body(C, F, T, tabbed, rows, weigh, *refs):
    if tabbed:
        tab, got, part, ftab, stage, loc, zs, zr, ss, sr, ts, tr = refs
    else:
        got, part, stage, loc, zs, zr, ss, sr = refs
    c, f, t, me = slab_place(C, T)
    S = C * T
    K, W = got.shape[2], got.shape[3]
    n = weigh.shape[1]
    columns = [(c, lax.rem(f + k, F), t) for k in range(1, F)]
    greet(columns + [slab_device(lax.rem(me + j, S), f, T) for j in range(1, S)])

    def slab_copy(k, j):
        b = lax.rem(f + k, F)
        e = lax.rem(me + j, S)
        return remote(
            rows.at[e, b], got.at[b, me], ss.at[k, j], sr.at[k, j], slab_device(e, f, T)
        )

    def slab_arrival(k, j):
        b = lax.rem(f + k, F)
        e = lax.rem(me + S - j, S)
        return remote(
            rows.at[e, b], got.at[b, e], ss.at[k, j], sr.at[k, j], slab_device(e, f, T)
        )

    def own_copy(k):
        b = lax.rem(f + k, F)
        return pltpu.make_async_copy(rows.at[me, b], got.at[b, me], loc.at[k])

    order = list(range(1, F)) + [0]
    for k in order:

        def begin(j, carry):
            slab_copy(k, j).start()
            return carry

        lax.fori_loop(1, S, begin, 0)
        own_copy(k).start()
    if tabbed:
        tabs = [
            remote(tab.at[lax.rem(f + k, F)], ftab.at[f], ts.at[k], tr.at[k], columns[k - 1])
            for k in range(1, F)
        ]
        for copy in tabs:
            copy.start()
        ftab[f] = tab[f]

    def z_copy(k):
        b = lax.rem(f + k, F)
        return remote(stage.at[b], part.at[f], zs.at[k], zr.at[k], columns[k - 1])

    def z_arrival(k):
        b = lax.rem(f + F - k, F)
        return remote(stage.at[b], part.at[b], zs.at[k], zr.at[k], columns[k - 1])

    step = min(W, 512)
    for k in order:
        b = lax.rem(f + k, F)
        own_copy(k).wait()

        def settle(j, carry):
            slab_arrival(k, j).wait_recv()
            return carry

        lax.fori_loop(1, S, settle, 0)
        target = part if k == 0 else stage

        def add(i, carry):
            columns_ = pl.ds(pl.multiple_of(i * step, step), step)
            block = got[b, :, :, columns_].reshape(S * K, step)
            total = jnp.dot(weigh[b, 0], block, preferred_element_type=FL)
            for m in range(1, n):
                total += jnp.dot(weigh[b, m], block, preferred_element_type=FL)
            target[b, :, columns_] = total.astype(BF)
            return carry

        lax.fori_loop(0, W // step, add, 0)
        if k > 0:
            z_copy(k).start()
    for k in range(1, F):
        z_copy(k).wait_send()
        z_arrival(k).wait_recv()
    for k in range(F):

        def leave(j, carry):
            slab_copy(k, j).wait_send()
            return carry

        lax.fori_loop(1, S, leave, 0)
    if tabbed:
        for copy in tabs:
            copy.wait()


def combine(identity, C, F, T, rows, weigh, tab=None):
    S, _, K, W = rows.shape
    R = weigh.shape[2]
    dma = pltpu.SemaphoreType.DMA
    tabbed = tab is not None
    outs = [jax.ShapeDtypeStruct((F, S, K, W), BF), jax.ShapeDtypeStruct((F, R, W), BF)]
    ins = [rows, weigh]
    scratch = [
        pltpu.VMEM((F, R, W), BF), dma((F,)), dma((F,)), dma((F,)), dma((F, S)), dma((F, S)),
    ]
    if tabbed:
        outs.append(jax.ShapeDtypeStruct(tab.shape, tab.dtype))
        ins.append(tab)
        scratch += [dma((F,)), dma((F,))]
    return pl.pallas_call(
        functools.partial(combine_body, C, F, T, tabbed),
        out_shape=tuple(outs),
        in_specs=[ANY] + [VMEM] * (len(ins) - 1),
        out_specs=[VMEM] * len(outs),
        scratch_shapes=scratch,
        compiler_params=params(identity, 32),
    )(*ins)


def ctx_sum_body(C, x, out, got, ss, sr):
    c, f, t = place()
    peers = [(lax.rem(c + k, C), f, t) for k in range(1, C)]
    greet(peers)

    def copy(k):
        p = lax.rem(c + k, C)
        return remote(x.at[p], got.at[c], ss.at[k], sr.at[k], (p, f, t))

    def arrival(k):
        p = lax.rem(c + C - k, C)
        return remote(x.at[p], got.at[p], ss.at[k], sr.at[k], (p, f, t))

    for k in range(1, C):
        copy(k).start()
    got[c] = x[c]
    for k in range(1, C):
        arrival(k).wait_recv()
    total = got[0].astype(FL)
    for p in range(1, C):
        total += got[p].astype(FL)
    out[...] = total
    for k in range(1, C):
        copy(k).wait_send()


def ctx_sum(identity, C, x):
    dma = pltpu.SemaphoreType.DMA
    return pl.pallas_call(
        functools.partial(ctx_sum_body, C),
        out_shape=jax.ShapeDtypeStruct(x.shape[1:], FL),
        in_specs=[VMEM],
        out_specs=VMEM,
        scratch_shapes=[pltpu.VMEM(x.shape, x.dtype), dma((C,)), dma((C,))],
        compiler_params=params(identity, 24),
    )(x)


def small_body(C, F, T, x, out, zgot, mid, sgot, zs, zr, ss, sr):
    c, f, t, me = slab_place(C, T)
    S = C * T
    columns = [(c, lax.rem(f + k, F), t) for k in range(1, F)]
    greet(columns + [slab_device(lax.rem(me + j, S), f, T) for j in range(1, S)])

    def z_copy(k):
        return remote(x.at[lax.rem(f + k, F)], zgot.at[f], zs.at[k], zr.at[k], columns[k - 1])

    def z_arrival(k):
        b = lax.rem(f + F - k, F)
        return remote(x.at[b], zgot.at[b], zs.at[k], zr.at[k], columns[k - 1])

    for k in range(1, F):
        z_copy(k).start()
    zgot[f] = x[f]
    for k in range(1, F):
        z_arrival(k).wait_recv()
    total = zgot[0]
    for b in range(1, F):
        total += zgot[b]
    mid[...] = total
    sgot[me] = total

    def s_copy(j):
        return remote(
            mid, sgot.at[me], ss.at[j], sr.at[j], slab_device(lax.rem(me + j, S), f, T)
        )

    def s_arrival(j):
        e = lax.rem(me + S - j, S)
        return remote(mid, sgot.at[e], ss.at[j], sr.at[j], slab_device(e, f, T))

    for j in range(1, S):
        s_copy(j).start()
    for j in range(1, S):
        s_arrival(j).wait_recv()
    total = sgot[0]
    for e in range(1, S):
        total += sgot[e]
    out[...] = total
    for k in range(1, F):
        z_copy(k).wait_send()
    for j in range(1, S):
        s_copy(j).wait_send()


def small_sum(identity, C, F, T, x):
    dma = pltpu.SemaphoreType.DMA
    S = C * T
    one = x.shape[1:]
    return pl.pallas_call(
        functools.partial(small_body, C, F, T),
        out_shape=jax.ShapeDtypeStruct(one, FL),
        in_specs=[VMEM],
        out_specs=VMEM,
        scratch_shapes=[
            pltpu.VMEM((F,) + one, FL), pltpu.VMEM(one, FL), pltpu.VMEM((S,) + one, FL),
            dma((F,)), dma((F,)), dma((S,)), dma((S,)),
        ],
        compiler_params=params(identity, 24),
    )(x)


def far_first(F):
    table = []
    for f in range(F):
        order = []
        for i in range(F):
            ends = [F - 1 - i, i] if f * 2 < F else [i, F - 1 - i]
            for b in ends:
                if ((b > f and b == F - 1 - i) or (b < f and b == i)) and b not in order:
                    order.append(b)
        table.append(order + [f])
    return table


def grads_body(
    C, F, xt, da, ht, dt, outa, outo,
    ska, sko, rka, rko, sya, syo, rya, ryo, rza, rzo, sza, szo,
    k_s, k_r, y_s, y_r, z_s, z_r, g_s, g_r, h_s, h_r,
):
    c, f, t = place()
    core, chip = lax.rem(c, 2), lax.div(c, 2)
    chips = C // 2
    sib = c + 1 - 2 * core
    pa, po, co = outa.shape[1], outo.shape[1], outo.shape[2]
    ra = pa * C
    table = far_first(F)

    def block(q):
        value = jnp.int32(table[0][q])
        for g in range(1, F):
            value = jnp.where(f == g, table[g][q], value)
        return value

    blocks = [block(q) for q in range(F)]
    ends = [(c, lax.rem(f + 1, F), t), (c, lax.rem(f + F - 1, F), t)]
    mates = [(lax.rem(chip + k, chips) * 2 + core, f, t) for k in range(1, chips)]
    greet(ends + mates + [(sib, f, t)])

    def piece_a(b, p):
        rows = pl.ds(pl.multiple_of(b * ra + p * pa, pa), pa)
        return jnp.dot(xt[rows, :], da[...], preferred_element_type=FL)

    def piece_o(b, p):
        rows = pl.ds(pl.multiple_of(p * po, po), po)
        cols = pl.ds(pl.multiple_of(b * co, co), co)
        return jnp.dot(ht[rows, :], dt[:, cols], preferred_element_type=FL)

    def core_copies(q, k):
        b = blocks[q]
        return [
            remote(ska.at[b, k], rka.at[b, k], k_s.at[q, k, 0], k_r.at[q, k, 0], (sib, f, t)),
            remote(sko.at[b, k], rko.at[b, k], k_s.at[q, k, 1], k_r.at[q, k, 1], (sib, f, t)),
        ]

    for q in range(F):
        b = blocks[q]
        for k in [*range(1, chips), 0]:
            p = lax.rem(chip + k, chips) * 2 + 1 - core
            ska[b, k] = piece_a(b, p).astype(BF)
            sko[b, k] = piece_o(b, p).astype(BF)
            for copy in core_copies(q, k):
                copy.start()

    def chip_copies(q, k):
        b = blocks[q]
        there = mates[k - 1]
        return [
            remote(sya.at[b, k - 1], rya.at[b, k - 1], y_s.at[q, k, 0], y_r.at[q, k, 0], there),
            remote(syo.at[b, k - 1], ryo.at[b, k - 1], y_s.at[q, k, 1], y_r.at[q, k, 1], there),
        ]

    for q in range(F):
        b = blocks[q]
        for k in range(1, chips):
            p = lax.rem(chip + k, chips) * 2 + core
            for copy in core_copies(q, k):
                copy.wait_recv()
            sya[b, k - 1] = (piece_a(b, p) + rka[b, k].astype(FL)).astype(BF)
            syo[b, k - 1] = (piece_o(b, p) + rko[b, k].astype(FL)).astype(BF)
            for copy in chip_copies(q, k):
                copy.start()

    def z_copies(q, b, slot, there):
        return [
            remote(sza.at[b], rza.at[slot], z_s.at[q, 0], z_r.at[slot, 0], there),
            remote(szo.at[b], rzo.at[slot], z_s.at[q, 1], z_r.at[slot, 1], there),
        ]

    def z_wait(slot):
        for copy in z_copies(0, 0, slot, ends[0]):
            copy.wait_recv()

    for q in range(F):
        b = blocks[q]
        for copy in core_copies(q, 0):
            copy.wait_recv()
        for k in range(1, chips):
            for copy in chip_copies(q, k):
                copy.wait_recv()
        total_a = piece_a(b, c) + rka[b, 0].astype(FL)
        total_o = piece_o(b, c) + rko[b, 0].astype(FL)
        for k in range(1, chips):
            total_a += rya[b, k - 1].astype(FL)
            total_o += ryo[b, k - 1].astype(FL)
        if q < F - 1:
            up = b > f
            first = jnp.where(up, f == 0, f == F - 1)

            @pl.when(first)
            def _():
                sza[b] = total_a.astype(BF)
                szo[b] = total_o.astype(BF)

            @pl.when(jnp.logical_not(first))
            def _():
                z_wait(b)
                sza[b] = (total_a + rza[b].astype(FL)).astype(BF)
                szo[b] = (total_o + rzo[b].astype(FL)).astype(BF)

            @pl.when(up)
            def _():
                for copy in z_copies(q, b, b, (c, f + 1, t)):
                    copy.start()

            @pl.when(jnp.logical_not(up))
            def _():
                slot = jnp.where(b == f - 1, F, b)
                for copy in z_copies(q, b, slot, (c, f - 1, t)):
                    copy.start()

        else:
            sza[f] = total_a.astype(BF)
            szo[f] = total_o.astype(BF)

            @pl.when(f > 0)
            def _():
                z_wait(f)
                sza[f] = (total_a + rza[f].astype(FL)).astype(BF)
                szo[f] = (total_o + rzo[f].astype(FL)).astype(BF)

            @pl.when(f < F - 1)
            def _():
                z_wait(F)
                outa[c] = (sza[f].astype(FL) + rza[F].astype(FL)).astype(BF)
                outo[c] = (szo[f].astype(FL) + rzo[F].astype(FL)).astype(BF)

            @pl.when(f == F - 1)
            def _():
                outa[c] = sza[f]
                outo[c] = szo[f]

    def spread(k):
        there = mates[k - 1]
        return [
            remote(outa.at[c], outa.at[c], g_s.at[k, 0], g_r.at[k, 0], there),
            remote(outo.at[c], outo.at[c], g_s.at[k, 1], g_r.at[k, 1], there),
        ]

    def hand(k, side):
        p = lax.rem(chip + chips - k, chips) * 2 + side
        return [
            remote(outa.at[p], outa.at[p], h_s.at[k, 0], h_r.at[k, 0], (sib, f, t)),
            remote(outo.at[p], outo.at[p], h_s.at[k, 1], h_r.at[k, 1], (sib, f, t)),
        ]

    def spread_arrival(k):
        p = lax.rem(chip + chips - k, chips) * 2 + core
        return [
            remote(outa.at[p], outa.at[p], g_s.at[k, 0], g_r.at[k, 0], mates[k - 1]),
            remote(outo.at[p], outo.at[p], g_s.at[k, 1], g_r.at[k, 1], mates[k - 1]),
        ]

    for k in range(1, chips):
        for copy in spread(k):
            copy.start()
    for copy in hand(0, core):
        copy.start()
    for k in range(1, chips):
        for copy in spread_arrival(k):
            copy.wait_recv()
        for copy in hand(k, core):
            copy.start()
    for k in range(chips):
        for copy in hand(k, 1 - core):
            copy.wait_recv()
        for copy in hand(k, core):
            copy.wait_send()
    for k in range(1, chips):
        for copy in spread(k):
            copy.wait_send()
    for q in range(F):
        for k in range(chips):
            for copy in core_copies(q, k):
                copy.wait_send()
        for k in range(1, chips):
            for copy in chip_copies(q, k):
                copy.wait_send()
        if q < F - 1:
            for copy in z_copies(q, 0, 0, ends[0]):
                copy.wait_send()


def weight_grads(identity, C, F, xt, da, ht, dt):
    D, R = xt.shape
    pa, na = D // F // C, da.shape[1]
    po, no = ht.shape[0] // C, dt.shape[1] // F
    chips = C // 2
    dma = pltpu.SemaphoreType.DMA

    def pair(*lead):
        return [pltpu.VMEM(lead + (pa, na), BF), pltpu.VMEM(lead + (po, no), BF)]

    return pl.pallas_call(
        functools.partial(grads_body, C, F),
        out_shape=(
            jax.ShapeDtypeStruct((C, pa, na), BF),
            jax.ShapeDtypeStruct((C, po, no), BF),
        ),
        in_specs=[VMEM] * 4,
        out_specs=[VMEM] * 2,
        scratch_shapes=[
            *pair(F, chips), *pair(F, chips), *pair(F, chips - 1), *pair(F, chips - 1),
            *pair(F + 1), *pair(F),
            dma((F, chips, 2)), dma((F, chips, 2)), dma((F, chips, 2)), dma((F, chips, 2)),
            dma((F, 2)), dma((F + 1, 2)), dma((chips, 2)), dma((chips, 2)),
            dma((chips, 2)), dma((chips, 2)),
        ],
        compiler_params=params(identity, 60),
    )(xt, da, ht, dt)


def tail_body(
    C, F, T, KH,
    grad_own, heads, normed, qrot, kv, keys_t, raw, lse, bias, cosf, sins, qgain, kgain, again,
    own_in, resid_in, router, vec_in, fo, fall,
    gin, outa, outo, small,
    wbuf, dall, nall, hq, rq, dheads, draw, dk, dv, ksend, kgot, gains, nsend, ngot, nown,
    sza, szo, rza, rzo, smx, zgot, mid, sgot,
    wsem, xs, xr, as_, ar, hs, hr, ds_, dr, rs, rr, z_s, z_r, ts, tr, us, ur,
):
    c, f, t, me = slab_place(C, T)
    S = C * T
    R, QC = heads.shape
    W = normed.shape[1]
    PC = raw.shape[1]
    L = kv.shape[1]
    HS = qgain.shape[1]
    QH = QC // HS
    G = QH // KH
    Rh = grad_own.shape[0]
    KC = KH * HS
    pa = rq.shape[2]
    po = hq.shape[2]
    rows_a, cols_o = outa.shape[0], outo.shape[1]
    root = HS ** (-0.5)
    core = lax.rem(c, 2)
    sib = c + 1 - 2 * core
    mate = lax.rem(c + 2, C)
    mate_sib = lax.rem(sib + 2, C)
    table = far_first(F)

    def block(q):
        value = jnp.int32(table[0][q])
        for g in range(1, F):
            value = jnp.where(f == g, table[g][q], value)
        return value

    blocks = [block(q) for q in range(F)]
    columns = [(c, lax.rem(f + k, F), t) for k in range(1, F)]
    greet(columns + [slab_device(lax.rem(me + j, S), f, T) for j in range(1, S)])
    at_t = pl.ds(pl.multiple_of(t * Rh, Rh), Rh)
    at_u = pl.ds(pl.multiple_of((1 - t) * Rh, Rh), Rh)
    beside = (c, f, 1 - t)

    load_o = pltpu.make_async_copy(fo, wbuf.at[:, pl.ds(0, W)], wsem.at[0])
    load_o.start()

    swap_d = remote(grad_own, dall.at[c, at_t], xs.at[0], xr.at[0], beside)
    swap_d_in = remote(grad_own, dall.at[c, at_u], xs.at[0], xr.at[0], beside)
    swap_n = remote(nsend, ngot, xs.at[1], xr.at[1], beside)

    def spread(view, n, i):
        here = view(mate) if i == 2 else view(c)
        there = (mate if i == 0 else sib, f, t)
        return remote(here, here, as_.at[n, i], ar.at[n, i], there)

    def spread_in(view, n, i):
        here = view((mate, sib, mate_sib)[i])
        return remote(here, here, as_.at[n, i], ar.at[n, i], (sib, f, t))

    def spread_start(view, n):
        spread(view, n, 0).start()
        spread(view, n, 1).start()

    def spread_pass(view, n):
        spread_in(view, n, 0).wait_recv()
        spread(view, n, 2).start()

    def spread_end(view, n):
        spread_in(view, n, 1).wait_recv()
        spread_in(view, n, 2).wait_recv()

    def spread_sent(view, n):
        for i in range(3):
            spread(view, n, i).wait_send()

    def chunk_copies(source, target, ss, sr):
        out, come = [], []
        for k in range(1, C):
            p, o = lax.rem(c + k, C), lax.rem(c + C - k, C)
            out.append(remote(source(p), target(c), ss.at[k], sr.at[k], (p, f, t)))
            come.append(remote(source(o), target(o), ss.at[k], sr.at[k], (o, f, t)))
        return out, come

    def lane(p, n):
        return pl.ds(pl.multiple_of(p * n, n), n)

    heads_out, heads_come = chunk_copies(
        lambda p: heads.at[:, lane(p, po)], lambda o: hq.at[o], hs, hr
    )
    kv_moves = [
        chunk_copies(lambda p, g=g: ksend.at[g, p], lambda o, g=g: kgot.at[g, o], ds_.at[g], dr.at[g])
        for g in range(KH)
    ]
    def nall_of(p):
        return nall.at[p]

    def outo_of(p):
        return outo.at[lane(p, po)]

    def outa_of(p):
        return outa.at[:, lane(p, pa)]

    dall_of = [
        lambda p, q=q: dall.at[p, :, lane(blocks[q], cols_o)] for q in range(F)
    ]

    swap_d.start()
    for copy in heads_out:
        copy.start()
    dall[c, at_t] = grad_own[...]
    nall[c] = normed[...]
    hq[c] = heads[:, lane(c, po)]
    swap_d_in.wait_recv()
    for q in range(F):
        spread_start(dall_of[q], 3 + q)

    load_o.wait()
    step = min(512, QC)

    def head_grads(i, carry):
        at = lane(i, step)
        dheads[:, at] = outer_cols(dall[c], wbuf[at, pl.ds(0, W)]).astype(BF)
        return carry

    lax.fori_loop(0, QC // step, head_grads, 0)
    load_w = pltpu.make_async_copy(fall.at[:, pl.ds(0, PC)], wbuf, wsem.at[1])
    load_w.start()

    def unturn(values):
        return values * cosf[...] - pltpu.roll(values, HS // 2, 1) * sins[...]

    def norm_grads(values, gain_vec, upstream):
        factor = lax.rsqrt(jnp.mean(values * values, axis=-1, keepdims=True) + EPS)
        out, terms = norm_back(values, factor, gain_vec, upstream)
        return out, jnp.sum(terms, axis=0, keepdims=True)

    gains[...] = jnp.zeros_like(gains)
    def piece_o(b):
        return inner_rows(
            hq[...].reshape(C * R, po), dall[:, :, lane(b, cols_o)].reshape(C * R, cols_o)
        )

    def piece_a(b):
        return inner_rows(
            nall[:, :, lane(b, rows_a)].reshape(C * R, rows_a), rq[...].reshape(C * R, pa)
        )

    pieces = ((piece_o, szo, rzo, outo_of), (piece_a, sza, rza, outa_of))
    end = (f == 0) | (f == F - 1)

    def z_out(n, q):
        b = blocks[q]
        _, send, got, _ = pieces[n]
        return remote(send.at[b], got.at[b], z_s.at[n, q], z_r.at[n, b], (c, f + 1, t))

    def z_down(n, q):
        b = blocks[q]
        slot = jnp.where(b == f - 1, F, b)
        _, send, got, _ = pieces[n]
        return remote(send.at[b], got.at[slot], z_s.at[n, q], z_r.at[n, slot], (c, f - 1, t))

    def z_wait(n, slot):
        _, send, got, _ = pieces[n]
        remote(send.at[0], got.at[slot], z_s.at[n, 0], z_r.at[n, slot], (c, f, t)).wait_recv()

    def z_send(n, q):
        up = blocks[q] > f

        @pl.when(up)
        def _():
            z_out(n, q).start()

        @pl.when(jnp.logical_not(up))
        def _():
            z_down(n, q).start()

    def z_first(n, q):
        fn, send, _, _ = pieces[n]

        @pl.when(end)
        def _():
            send[blocks[q]] = fn(blocks[q]).astype(BF)
            z_send(n, q)

    def o_first(q):
        spread_end(dall_of[q], 3 + q)
        if q < F - 1:
            z_first(0, q)

    def z_relay(n, q):
        fn, send, got, _ = pieces[n]

        @pl.when(jnp.logical_not(end))
        def _():
            b = blocks[q]
            z_wait(n, b)
            send[b] = (fn(b) + got[b].astype(FL)).astype(BF)
            z_send(n, q)

    def z_last(n):
        fn, send, got, out = pieces[n]
        send[f] = fn(f).astype(BF)

        @pl.when(f > 0)
        def _():
            z_wait(n, f)
            send[f] = (send[f].astype(FL) + got[f].astype(FL)).astype(BF)

        @pl.when(f < F - 1)
        def _():
            z_wait(n, F)
            out(c)[...] = (send[f].astype(FL) + got[F].astype(FL)).astype(BF)

        @pl.when(f == F - 1)
        def _():
            out(c)[...] = send[f]


    key_step = min(L, 512)

    def one_head(g, h):
        at = lane(h, HS)
        q_head, o_grad = qrot[:, at], dheads[:, at]
        product = o_grad.astype(FL) * heads[:, at].astype(FL)
        delta = jnp.sum(product.T, axis=0, keepdims=True)
        row = lse[pl.ds(h, 1), :]
        q_grad = jnp.zeros((HS, R), FL)
        for j in range(L // key_step):
            ks = pl.ds(j * key_step, key_step)
            scores = outer_cols(kv[g, ks, :], q_head) * root
            probs = jnp.exp(scores + bias[ks, :] - row)
            d_probs = outer_cols(kv[KH + g, ks, :], o_grad)
            d_scores = (probs * (d_probs - delta)).astype(BF)
            dv[ks, :] += jnp.dot(probs.astype(BF), o_grad, preferred_element_type=FL)
            dk[ks, :] += jnp.dot(d_scores, q_head, preferred_element_type=FL)
            q_grad += jnp.dot(keys_t[g, :, ks], d_scores, preferred_element_type=FL)
        q_back, terms = norm_grads(raw[:, at], qgain[...], unturn(q_grad.T * root))
        draw[:, at] = q_back.astype(BF)
        gains[0:1, :] += terms

    def some_heads(g, first, count):
        def step_(i, carry):
            one_head(g, first + i)
            return carry

        lax.fori_loop(0, count, step_, 0)

    raw_due = [-(-min((p + 1) * pa, QC) // HS) for p in range(C)]
    raw_gone = []

    def raw_sends(done):
        for p in range(C):
            if p not in raw_gone and raw_due[p] <= done and (p + 1) * pa <= QC:
                raw_gone.append(p)
                raw_send(p)

    def raw_copy(p):
        return remote(draw.at[:, p * pa : (p + 1) * pa], rq.at[c], rs.at[p], rr.at[c], (p, f, t))

    def raw_come(o):
        return remote(draw.at[:, 0:pa], rq.at[o], rs.at[0], rr.at[o], (o, f, t))

    def raw_send(p):
        @pl.when(c != p)
        def _():
            raw_copy(p).start()

        @pl.when(c == p)
        def _():
            rq[c] = draw[:, p * pa : (p + 1) * pa]

    halves = 2
    part_heads = G // halves
    beat = 0
    for g in range(KH):
        dk[...] = jnp.zeros_like(dk)
        dv[...] = jnp.zeros_like(dv)
        for half in range(halves):
            some_heads(g, g * G + half * part_heads, part_heads)
            raw_sends(g * G + (half + 1) * part_heads)
            if half == halves - 1:
                for p in range(C):
                    at = pl.ds(p * R, R)
                    ksend[g, p, :, 0:HS] = (dk[at, :] * root).astype(BF)
                    ksend[g, p, :, HS : 2 * HS] = dv[at, :].astype(BF)
                for copy in kv_moves[g][0]:
                    copy.start()
                kgot[g, c] = ksend[g, c]
            if beat < F:
                spread_pass(dall_of[beat], 3 + beat)
            if beat == 0:
                for copy in heads_come:
                    copy.wait_recv()
            elif beat < F:
                o_first(beat - 1)
            beat += 1
    for q in range(beat, F):
        spread_pass(dall_of[q], 3 + q)
        o_first(q - 1)
    spread_start(nall_of, 0)

    o_first(F - 1)
    z_relay(0, 0)

    for g in range(KH):
        for copy in kv_moves[g][1]:
            copy.wait_recv()
        total = kgot[g, 0].astype(FL)
        for p in range(1, C):
            total += kgot[g, p].astype(FL)
        k_cols = slice(QC + g * HS, QC + (g + 1) * HS)
        k_back, terms = norm_grads(raw[:, k_cols], kgain[...], unturn(total[:, :HS]))
        draw[:, k_cols] = k_back.astype(BF)
        draw[:, QC + KC + g * HS : QC + KC + (g + 1) * HS] = total[:, HS:].astype(BF)
        gains[1:2, :] += terms
    for p in range(C):
        if p not in raw_gone:
            raw_send(p)
    z_relay(0, 1)
    load_w.wait()
    width_step = min(512, W)

    def norm_theirs(i, carry):
        at = lane(i, width_step)
        nsend[:, at] = outer_cols(draw[at_u, :], wbuf[at, :]).astype(BF)
        return carry

    lax.fori_loop(0, W // width_step, norm_theirs, 0)
    swap_n.start()

    def norm_ours(i, carry):
        at = lane(i, width_step)
        nown[:, at] = outer_cols(draw[at_t, :], wbuf[at, :])
        return carry

    lax.fori_loop(0, W // width_step, norm_ours, 0)

    spread_pass(nall_of, 0)
    for q in range(2, F - 1):
        z_relay(0, q)
    spread_end(nall_of, 0)
    for k in range(1, C):
        raw_come(lax.rem(c + k, C)).wait_recv()
    for q in range(F - 1):
        z_first(1, q)
    z_relay(1, 0)
    z_last(0)
    spread_start(outo_of, 1)

    swap_n.wait_recv()
    upstream = nown[...] + ngot[...].astype(FL)
    values = own_in[...]
    factor = lax.rsqrt(jnp.mean(values * values, axis=-1, keepdims=True) + EPS)
    back, terms = norm_back(values, factor, again[...], upstream)
    gin[...] = resid_in[...] + back
    for b in range(F):
        smx[b, 0 : router.shape[1]] = router[b]
        at = router.shape[1]
        smx[b, at : at + 8] = vec_in[...]
        smx[b, at : at + 1] = jnp.sum(terms, axis=0, keepdims=True)
        smx[b, at + 2 : at + 3, 0:HS] = gains[0:1, :]
        smx[b, at + 2 : at + 3, HS : 2 * HS] = gains[1:2, :]

    def t_copy(k):
        return remote(smx.at[lax.rem(f + k, F)], zgot.at[f], ts.at[k], tr.at[k], columns[k - 1])

    def t_arrival(k):
        b = lax.rem(f + F - k, F)
        return remote(smx.at[b], zgot.at[b], ts.at[k], tr.at[k], columns[k - 1])

    for k in range(1, F):
        t_copy(k).start()
    zgot[f] = smx[f]
    for q in range(1, F - 1):
        z_relay(1, q)
    spread_pass(outo_of, 1)
    for k in range(1, F):
        t_arrival(k).wait_recv()
    total = zgot[0]
    for b in range(1, F):
        total += zgot[b]
    mid[...] = total
    sgot[me] = total

    def u_copy(j):
        return remote(
            mid, sgot.at[me], us.at[j], ur.at[j], slab_device(lax.rem(me + j, S), f, T)
        )

    def u_arrival(j):
        e = lax.rem(me + S - j, S)
        return remote(mid, sgot.at[e], us.at[j], ur.at[j], slab_device(e, f, T))

    for j in range(1, S):
        u_copy(j).start()
    z_last(1)
    spread_start(outa_of, 2)
    for j in range(1, S):
        u_arrival(j).wait_recv()
    total = sgot[0]
    for e in range(1, S):
        total += sgot[e]
    small[...] = total
    spread_end(outo_of, 1)
    spread_pass(outa_of, 2)
    spread_end(outa_of, 2)

    for view, n in ((nall_of, 0), (outo_of, 1), (outa_of, 2)):
        spread_sent(view, n)
    for q in range(F):
        spread_sent(dall_of[q], 3 + q)
    swap_d.wait_send()
    swap_n.wait_send()
    for copy in heads_out:
        copy.wait_send()
    for p in range(C):

        @pl.when(c != p)
        def _():
            raw_copy(p).wait_send()

    for g in range(KH):
        for copy in kv_moves[g][0]:
            copy.wait_send()
    for n in range(2):
        for q in range(F - 1):
            z_out(n, q).wait_send()
    for k in range(1, F):
        t_copy(k).wait_send()
    for j in range(1, S):
        u_copy(j).wait_send()


def tail(identity, C, F, T, KH, args, D, po):
    grad_own, heads, normed, qrot, kv, keys_t, raw, lse, bias = args[:9]
    qgain = args[11]
    router, fall = args[16], args[19]
    R, QC = heads.shape
    W = normed.shape[1]
    PC = raw.shape[1]
    L = kv.shape[1]
    HS = qgain.shape[1]
    Rh = grad_own.shape[0]
    S = C * T
    pa = PC // C
    rows_a, cols_o = W // F, W // F
    small_shape = (router.shape[1] + 8, W)
    dma = pltpu.SemaphoreType.DMA
    V = pltpu.VMEM
    return pl.pallas_call(
        functools.partial(tail_body, C, F, T, KH),
        out_shape=(
            jax.ShapeDtypeStruct((Rh, W), FL),
            jax.ShapeDtypeStruct((rows_a, C * pa), BF),
            jax.ShapeDtypeStruct((C * po, cols_o), BF),
            jax.ShapeDtypeStruct(small_shape, FL),
        ),
        in_specs=[VMEM] * 18 + [ANY] * 2,
        out_specs=[VMEM] * 4,
        scratch_shapes=[
            V((W, PC), BF), V((C, R, W), BF), V((C, R, W), BF), V((C, R, po), BF),
            V((C, R, pa), BF), V((R, QC), BF), V((R, PC), BF), V((L, HS), FL), V((L, HS), FL),
            V((KH, C, R, 2 * HS), BF), V((KH, C, R, 2 * HS), BF), V((8, HS), FL),
            V((Rh, W), BF), V((Rh, W), BF), V((Rh, W), FL),
            V((F, rows_a, pa), BF), V((F, po, cols_o), BF),
            V((F + 1, rows_a, pa), BF), V((F + 1, po, cols_o), BF),
            V((F,) + small_shape, FL), V((F,) + small_shape, FL), V(small_shape, FL),
            V((S,) + small_shape, FL),
            dma((2,)), dma((2,)), dma((2,)), dma((3 + F, 3)), dma((3 + F, 3)), dma((C,)), dma((C,)),
            dma((KH, C)), dma((KH, C)), dma((C,)), dma((C,)),
            dma((2, F)), dma((2, F + 1)), dma((F,)), dma((F,)), dma((S,)), dma((S,)),
        ],
        compiler_params=params(identity, 62),
    )(*args)


def head_body(
    C, F, T, KH,
    hidden, tab, again, qgain, kgain, fgain, cosf, sins, bias, wa, wo,
    fall, full, ftab, raw, qrot, kv, keys_t, lse, heads, normed, resid, low, gates,
    fa, fo, vals_t, nsend, ngot, nown,
    loc, zs, zr, ys, yr, ks, kr, ts, tr, cs, cr, xs, xr,
):
    c, f, t, me = slab_place(C, T)
    S = C * T
    R, W = hidden.shape
    Rh = tab.shape[0]
    HS = qgain.shape[1]
    PC = raw.shape[1]
    QC = heads.shape[1]
    KC = KH * HS
    L = kv.shape[1]
    G = QC // HS // KH
    root = HS ** (-0.5)
    core = lax.rem(c, 2)
    sib = c + 1 - 2 * core
    mate = lax.rem(c + 2, C)
    mate_sib = lax.rem(sib + 2, C)
    ra, (ro, co) = wa.shape[0], wo.shape
    pa, po = ra // C, ro // C
    ha, ho = pa // 2, po // 2
    columns = [(c, lax.rem(f + k, F), t) for k in range(1, F)]
    greet(columns + [slab_device(lax.rem(me + j, S), f, T) for j in range(1, S)])

    def spot(arr, b, p):
        half = arr % 2
        if arr < 2:
            return fa.at[pl.ds(pl.multiple_of(b * ra + p * pa + half * ha, ha), ha)]
        rows = pl.ds(pl.multiple_of(p * po + half * ho, ho), ho)
        return fo.at[rows, pl.ds(pl.multiple_of(b * co, co), co)]

    def own(arr):
        half = arr % 2
        if arr < 2:
            return wa.at[pl.ds(pl.multiple_of(c * pa + half * ha, ha), ha)]
        return wo.at[pl.ds(pl.multiple_of(c * po + half * ho, ho), ho)]

    def z_copy(arr, s, d):
        b = f - (s - 1) if d == 0 else f + (s - 1)
        source = own(arr) if s == 1 else spot(arr, b, c)
        there = (c, f + 1 if d == 0 else f - 1, t)
        return remote(source, spot(arr, b, c), zs.at[d, s, arr], zr.at[d, s, arr], there)

    def z_sends(s, d):
        b = f - (s - 1) if d == 0 else f + (s - 1)
        return (f + 1 < F) & (b >= 0) if d == 0 else (f > 0) & (b < F)

    def z_gets(s, d):
        return f - s >= 0 if d == 0 else f + s < F

    def came(s, d):
        return f - s if d == 0 else f + s

    def move(arr, s, d, p, sent, got, i, device):
        here = spot(arr, came(s, d), p)
        return remote(here, here, sent.at[d, s, arr, i], got.at[d, s, arr, i], device)

    def z_begin(arr):
        for d in range(2):

            @pl.when(z_sends(1, d))
            def _():
                z_copy(arr, 1, d).start()

    def z_in(arr, s):
        for d in range(2):

            @pl.when(z_gets(s, d))
            def _():
                here = spot(arr, came(s, d), c)
                remote(here, here, zs.at[d, s, arr], zr.at[d, s, arr], (sib, f, t)).wait_recv()
                if s + 1 < F:

                    @pl.when(z_sends(s + 1, d))
                    def _():
                        z_copy(arr, s + 1, d).start()

                move(arr, s, d, c, ys, yr, 0, (mate, f, t)).start()
                move(arr, s, d, c, ks, kr, 0, (sib, f, t)).start()

    def y_in(arr, s):
        for d in range(2):

            @pl.when(z_gets(s, d))
            def _():
                move(arr, s, d, mate, ys, yr, 0, (mate, f, t)).wait_recv()
                move(arr, s, d, mate, ks, kr, 1, (sib, f, t)).start()

    def k_in(arr, s, d):
        move(arr, s, d, sib, ks, kr, 0, (sib, f, t)).wait_recv()
        move(arr, s, d, mate_sib, ks, kr, 1, (sib, f, t)).wait_recv()

    z_begin(0)
    z_begin(1)
    tabs = [
        remote(tab, ftab.at[f], ts.at[k], tr.at[k], columns[k - 1]) for k in range(1, F)
    ]
    for copy in tabs:
        copy.start()
    own_a = pltpu.make_async_copy(wa, fa.at[pl.ds(pl.multiple_of(f * ra, ra), ra)], loc.at[0])
    own_o = pltpu.make_async_copy(
        wo, fo.at[:, pl.ds(pl.multiple_of(f * co, co), co)], loc.at[1]
    )
    own_a.start()
    own_o.start()
    ftab[f] = tab[...]

    inputs = hidden[...].astype(FL)
    normed[...] = norm_rows(inputs, again[...])[0].astype(BF)
    wide = min(512, PC)

    def project(b, first):
        at = pl.ds(pl.multiple_of(b * ra, ra), ra)
        left = normed[:, at]

        def piece(i, carry):
            cols = pl.ds(pl.multiple_of(i * wide, wide), wide)
            part = jnp.dot(left, fa[at, cols], preferred_element_type=FL)
            if first:
                raw[:, cols] = part
            else:
                raw[:, cols] += part
            return carry

        lax.fori_loop(0, PC // wide, piece, 0)

    def project_in(s):
        for d in range(2):

            @pl.when(z_gets(s, d))
            def _():
                k_in(0, s, d)
                k_in(1, s, d)
                project(came(s, d), False)

    own_a.wait()
    project(f, True)
    z_in(0, 1)
    z_in(1, 1)
    for s in range(2, F):
        z_in(0, s)
        y_in(0, s - 1)
        z_in(1, s)
        y_in(1, s - 1)
        if s == F - 2:
            z_begin(2)
            z_begin(3)
        project_in(s - 1)
    y_in(0, F - 1)
    y_in(1, F - 1)
    project_in(F - 1)

    def turn(values):
        return values * cosf[...] + pltpu.roll(values, HS // 2, 1) * sins[...]

    at_c = pl.ds(pl.multiple_of(c * R, R), R)
    for g in range(KH):
        k_raw = raw[:, QC + g * HS : QC + (g + 1) * HS]
        kv[g, at_c, :] = turn(norm_rows(k_raw, kgain[...])[0]).astype(BF)
        kv[KH + g, at_c, :] = raw[:, QC + KC + g * HS : QC + KC + (g + 1) * HS].astype(BF)

    def kv_move(p, i, device):
        here = kv.at[:, pl.ds(pl.multiple_of(p * R, R), R), :]
        return remote(here, here, cs.at[i], cr.at[i], device)

    kv_move(c, 0, (mate, f, t)).start()
    kv_move(c, 1, (sib, f, t)).start()

    def query(i, carry):
        at = pl.ds(pl.multiple_of(i * HS, HS), HS)
        qrot[:, at] = turn(norm_rows(raw[:, at], qgain[...])[0]).astype(BF)
        return carry

    lax.fori_loop(0, QC // HS, query, 0)
    save_a = pltpu.make_async_copy(fa, fall, loc.at[2])
    save_a.start()
    z_in(2, 1)
    z_in(3, 1)
    kv_move(mate, 0, (mate, f, t)).wait_recv()
    kv_move(mate, 2, (sib, f, t)).start()
    kv_move(sib, 1, (sib, f, t)).wait_recv()
    kv_move(mate_sib, 2, (sib, f, t)).wait_recv()
    for g in range(KH):
        keys_t[g] = kv[g].astype(FL).T.astype(BF)
        vals_t[g] = kv[KH + g].astype(FL).T.astype(BF)

    def some_heads(g, first, count):
        def one_head(i, carry):
            h = first + i
            at = pl.ds(pl.multiple_of(h * HS, HS), HS)
            scores = outer_cols(kv[g], qrot[:, at]) * root + bias[...]
            peak = jnp.max(scores, axis=0, keepdims=True)
            weight = jnp.exp(scores - peak)
            total = jnp.sum(weight, axis=0, keepdims=True)
            lse[pl.ds(h, 1), :] = peak + jnp.log(total)
            probs = (weight / total).astype(BF)
            heads[:, at] = jnp.dot(vals_t[g], probs, preferred_element_type=FL).T.astype(BF)
            return carry

        lax.fori_loop(0, count, one_head, 0)

    o_events = []
    for s in range(2, F):
        o_events.append((z_in, 2, s, y_in, 2, s - 1))
        o_events.append((z_in, 3, s, y_in, 3, s - 1))
    half = G // 2
    for i in range(2 * KH):
        some_heads(i // 2, i * half, half)
        if i < len(o_events):
            za, arr_a, sa, ya, arr_b, sb = o_events[i]
            za(arr_a, sa)
            ya(arr_b, sb)
    for za, arr_a, sa, ya, arr_b, sb in o_events[2 * KH :]:
        za(arr_a, sa)
        ya(arr_b, sb)
    y_in(2, F - 1)
    y_in(3, F - 1)
    for s in range(1, F):
        for d in range(2):

            @pl.when(z_gets(s, d))
            def _():
                k_in(2, s, d)
                k_in(3, s, d)

    own_o.wait()
    save_o = pltpu.make_async_copy(fo, full, loc.at[3])
    save_o.start()
    at_t = pl.ds(pl.multiple_of(t * Rh, Rh), Rh)
    at_u = pl.ds(pl.multiple_of((1 - t) * Rh, Rh), Rh)
    step = min(512, W)

    def theirs(i, carry):
        cols = pl.ds(pl.multiple_of(i * step, step), step)
        nsend[:, cols] = jnp.dot(
            heads[at_u, :], fo[:, cols], preferred_element_type=FL
        ).astype(BF)
        return carry

    def ours(i, carry):
        cols = pl.ds(pl.multiple_of(i * step, step), step)
        nown[:, cols] = jnp.dot(heads[at_t, :], fo[:, cols], preferred_element_type=FL)
        return carry

    lax.fori_loop(0, W // step, theirs, 0)
    swap = remote(nsend, ngot, xs.at[0], xr.at[0], (c, f, 1 - t))
    swap.start()
    lax.fori_loop(0, W // step, ours, 0)
    swap.wait_recv()
    total = hidden[at_t, :].astype(FL) + (nown[...] + ngot[...].astype(FL))
    resid[...] = total
    ffn_low = norm_rows(total, fgain[...])[0].astype(BF)
    low[...] = ffn_low
    logits = jnp.dot(ffn_low, fa[:, PC:], preferred_element_type=FL)
    named = tab[...] >= 0.0
    masked = jnp.where(named, logits, MASKED)
    shifted = jnp.where(
        named, jnp.exp(masked - jnp.max(masked, axis=-1, keepdims=True)), 0.0
    )
    gates[...] = shifted / jnp.sum(shifted, axis=-1, keepdims=True)

    save_a.wait()
    save_o.wait()
    swap.wait_send()
    for copy in tabs:
        copy.wait()
    kv_move(c, 0, (mate, f, t)).wait_send()
    kv_move(c, 1, (sib, f, t)).wait_send()
    kv_move(mate, 2, (sib, f, t)).wait_send()
    for s in range(1, F):
        for d in range(2):

            @pl.when(z_sends(s, d))
            def _():
                for arr in range(4):
                    z_copy(arr, s, d).wait_send()

            @pl.when(z_gets(s, d))
            def _():
                for arr in range(4):
                    move(arr, s, d, c, ys, yr, 0, (mate, f, t)).wait_send()
                    move(arr, s, d, c, ks, kr, 0, (sib, f, t)).wait_send()
                    move(arr, s, d, mate, ks, kr, 1, (sib, f, t)).wait_send()


def head(identity, C, F, T, KH, PC, L, args):
    hidden, tab, qgain, wa, wo = args[0], args[1], args[3], args[9], args[10]
    R, W = hidden.shape
    Rh, lanes = tab.shape
    HS = qgain.shape[1]
    ra, ca = wa.shape
    QC, co = wo.shape
    dma = pltpu.SemaphoreType.DMA
    V = pltpu.VMEM
    shape = jax.ShapeDtypeStruct
    return pl.pallas_call(
        functools.partial(head_body, C, F, T, KH),
        out_shape=(
            shape((F * ra, ca), BF), shape((QC, F * co), BF), shape((F, Rh, lanes), FL),
            shape((R, PC), FL), shape((R, QC), BF), shape((2 * KH, L, HS), BF),
            shape((KH, HS, L), BF), shape((QC // HS, R), FL), shape((R, QC), BF),
            shape((R, W), BF), shape((Rh, W), FL), shape((Rh, W), BF), shape((Rh, lanes), FL),
        ),
        in_specs=[VMEM] * 9 + [ANY] * 2,
        out_specs=[ANY] * 2 + [VMEM] * 11,
        scratch_shapes=[
            V((F * ra, ca), BF), V((QC, F * co), BF), V((KH, HS, L), BF),
            V((Rh, W), BF), V((Rh, W), BF), V((Rh, W), FL),
            dma((4,)), dma((2, F, 4)), dma((2, F, 4)), dma((2, F, 4, 1)), dma((2, F, 4, 1)),
            dma((2, F, 4, 2)), dma((2, F, 4, 2)), dma((F,)), dma((F,)), dma((3,)), dma((3,)),
            dma((1,)), dma((1,)),
        ],
        compiler_params=params(identity, 58),
    )(*args)


def moe_place(C, F, T):
    c, f, t, me = slab_place(C, T)
    S = C * T
    columns = [(c, lax.rem(f + k, F), t) for k in range(1, F)]
    slab = [slab_device(lax.rem(me + j, S), f, T) for j in range(S)]

    def block(k):
        return lax.rem(f + F - k, F)

    def to(j):
        return lax.rem(me + j, S)

    def come(j):
        return lax.rem(me + S - j, S)

    return c, f, t, me, columns, slab, block, to, come


def moe_forward_body(
    C, F, T,
    rows, gate_t, select, w_in, w_out,
    xr, got, pre, mixed, part, fgate,
    zbuf, stage, xs, gs, ysend, wi, wo, pstage, zpart,
    loc, zs, zr, ss, sr, rs, rr, ps, pr, ts, tr, xl, gl, pl_,
):
    c, f, t, me, columns, slab, block, to, come = moe_place(C, F, T)
    S = C * T
    K, W = xr.shape[2], xr.shape[3]
    FFW = w_out.shape[0]
    greet(columns + slab[1:])
    load_i = pltpu.make_async_copy(w_in, wi, loc.at[0])
    load_o = pltpu.make_async_copy(w_out, wo, loc.at[1])
    z_out = [remote(rows, zbuf.at[f], zs.at[k], zr.at[k], columns[k - 1]) for k in range(1, F)]
    g_out = [remote(gate_t, fgate.at[f], ts.at[k], tr.at[k], columns[k - 1]) for k in range(1, F)]
    for copy in z_out + g_out:
        copy.start()
    load_i.start()
    load_o.start()
    zbuf[f] = rows[...]
    fgate[f] = gate_t[...]

    def slab_copy(k, j):
        b = block(k)
        return remote(stage.at[to(j), b], xs.at[b, me], ss.at[k, j], sr.at[k, j], slab[j])

    def slab_arrival(k, j):
        b = block(k)
        return remote(stage.at[to(j), b], xs.at[b, come(j)], ss.at[k, j], sr.at[k, j], slab[j])

    def back_copy(k, j):
        b = block(k)
        return remote(ysend.at[b, to(j)], gs.at[b, me], rs.at[k, j], rr.at[k, j], slab[j])

    def back_arrival(k, j):
        b = block(k)
        return remote(ysend.at[b, to(j)], gs.at[b, come(j)], rs.at[k, j], rr.at[k, j], slab[j])

    def part_copy(k):
        b = block(k)
        return remote(pstage.at[b], zpart.at[f], ps.at[k], pr.at[k], (c, b, t))

    def part_arrival(k):
        b = lax.rem(f + k, F)
        return remote(pstage.at[b], zpart.at[b], ps.at[k], pr.at[k], (c, b, t))

    def keep_x(k):
        return pltpu.make_async_copy(xs.at[block(k)], xr.at[block(k)], xl.at[k])

    def keep_got(k):
        return pltpu.make_async_copy(gs.at[block(k)], got.at[block(k)], gl.at[k])

    def send(k):
        b = block(k)
        if k > 0:
            remote(rows, zbuf.at[b], zs.at[k], zr.at[k], columns[k - 1]).wait_recv()
        for j in [*range(1, S), 0]:
            e = to(j)
            picked = jnp.dot(select[b, e], zbuf[b], preferred_element_type=FL).astype(BF)
            if j:
                stage[e, b] = picked
                slab_copy(k, j).start()
            else:
                xs[b, me] = picked

    def expert(k):
        b = block(k)
        for j in range(1, S):
            slab_arrival(k, j).wait_recv()
        if k == 0:
            load_i.wait()
        keep_x(k).start()
        x = xs[b].reshape(S * K, W)
        tile = 256
        for i in range(FFW // tile):
            at = slice(i * tile, (i + 1) * tile)
            up_at = slice(FFW + i * tile, FFW + (i + 1) * tile)
            gate_pre = jnp.dot(x, wi[:, at], preferred_element_type=FL)
            up_pre = jnp.dot(x, wi[:, up_at], preferred_element_type=FL)
            pre[b, :, at] = gate_pre
            pre[b, :, up_at] = up_pre
            mixed[b, :, at] = (gate_pre * jax.nn.sigmoid(gate_pre) * up_pre).astype(BF)
        if k == 0:
            load_o.wait()
        hidden = mixed[b]
        tile = min(512, W)
        for i in range(W // tile):
            at = slice(i * tile, (i + 1) * tile)
            y = jnp.dot(hidden, wo[:, at], preferred_element_type=FL).astype(BF)
            ysend[b, :, :, at] = y.reshape(S, K, tile)
        for j in range(1, S):
            back_copy(k, j).start()
        gs[b, me] = ysend[b, me]

    def gather(k):
        b = block(k)
        for j in range(1, S):
            back_arrival(k, j).wait_recv()
        keep_got(k).start()
        scaled = []
        for s in range(S):
            e = (s // T) * F * T + f * T + s % T
            scaled.append(select[b, s].astype(FL) * fgate[b, pl.ds(e, 1), :])
        scaled = jnp.concatenate(scaled, axis=0)
        high = scaled.astype(BF)
        low = (scaled - high.astype(FL)).astype(BF)
        tile = min(512, W)
        for i in range(W // tile):
            at = slice(i * tile, (i + 1) * tile)
            y = gs[b, :, :, at].reshape(S * K, tile)
            total = inner_rows(high, y) + inner_rows(low, y)
            if k:
                pstage[b, :, at] = total.astype(BF)
            else:
                part[:, at] = total
        if k:
            part_copy(k).start()

    send(0)
    send(1)
    expert(0)
    send(2)
    expert(1)
    for k in range(3, F):
        send(k)
    for k in range(1, F):
        g_out[k - 1].wait_send()
        remote(gate_t, fgate.at[block(k)], ts.at[k], tr.at[k], columns[k - 1]).wait_recv()
    gather(0)
    for k in range(2, F):
        expert(k)
        gather(k - 1)
    gather(F - 1)
    for k in range(1, F):
        part_arrival(k).wait_recv()
        part[...] += zpart[lax.rem(f + k, F)].astype(FL)
    for copy in z_out:
        copy.wait_send()
    for k in range(F):
        keep_x(k).wait()
        keep_got(k).wait()
        if k:
            part_copy(k).wait_send()
        for j in range(1, S):
            slab_copy(k, j).wait_send()
            back_copy(k, j).wait_send()


def moe_forward(identity, C, F, T, rows, gate_t, select, w_in, w_out):
    S = C * T
    K = select.shape[2]
    R, W = rows.shape
    H2, FFW = w_in.shape[1], w_out.shape[0]
    dma = pltpu.SemaphoreType.DMA
    V = pltpu.VMEM
    shape = jax.ShapeDtypeStruct
    return pl.pallas_call(
        functools.partial(moe_forward_body, C, F, T),
        out_shape=(
            shape((F, S, K, W), BF), shape((F, S, K, W), BF), shape((F, S * K, H2), FL),
            shape((F, S * K, FFW), BF), shape((R, W), FL), shape((F,) + gate_t.shape, FL),
        ),
        in_specs=[VMEM] * 3 + [ANY] * 2,
        out_specs=[ANY] * 2 + [VMEM] * 4,
        scratch_shapes=[
            V((F, R, W), BF), V((S, F, K, W), BF), V((F, S, K, W), BF), V((F, S, K, W), BF),
            V((F, S, K, W), BF), V((W, H2), BF), V((FFW, W), BF), V((F, R, W), BF),
            V((F, R, W), BF),
            dma((2,)), dma((F,)), dma((F,)), dma((F, S)), dma((F, S)), dma((F, S)), dma((F, S)),
            dma((F,)), dma((F,)), dma((F,)), dma((F,)), dma((F,)), dma((F,)), dma((F,)),
        ],
        compiler_params=params(identity, 60),
    )(rows, gate_t, select, w_in, w_out)


def moe_backward_body(
    C, F, T,
    rows, fgate, select, mixed, w_in, w_out, xr, got, pre,
    part, grad_in, grad_out, dgate,
    zbuf, stage, gs, ysx, back, wi, wo, pstage, zpart, dpre, prebuf, tiles, dgs, dgr,
    loc, zs, zr, ss, sr, rs, rr, ps, pr, ds_, dr, pl_, tl,
):
    c, f, t, me, columns, slab, block, to, come = moe_place(C, F, T)
    S = C * T
    K, W = xr.shape[2], xr.shape[3]
    FFW = w_out.shape[0]
    R = rows.shape[0]
    greet(columns + slab[1:])
    load_i = pltpu.make_async_copy(w_in, wi, loc.at[0])
    load_o = pltpu.make_async_copy(w_out, wo, loc.at[1])
    load_y = pltpu.make_async_copy(got, ysx, loc.at[2])
    load_x = pltpu.make_async_copy(xr, ysx, loc.at[3])
    z_out = [remote(rows, zbuf.at[f], zs.at[k], zr.at[k], columns[k - 1]) for k in range(1, F)]
    for copy in z_out:
        copy.start()
    load_y.start()
    load_o.start()
    load_i.start()
    zbuf[f] = rows[...]

    def pre_load(k):
        return pltpu.make_async_copy(pre.at[block(k)], prebuf, pl_.at[k])

    def slab_copy(k, j):
        b = block(k)
        return remote(stage.at[to(j), b], gs.at[b, me], ss.at[k, j], sr.at[k, j], slab[j])

    def slab_arrival(k, j):
        b = block(k)
        return remote(stage.at[to(j), b], gs.at[b, come(j)], ss.at[k, j], sr.at[k, j], slab[j])

    def back_copy(k, j):
        b = block(k)
        return remote(stage.at[to(j), b], back.at[b, me], rs.at[k, j], rr.at[k, j], slab[j])

    def back_arrival(k, j):
        b = block(k)
        return remote(stage.at[to(j), b], back.at[b, come(j)], rs.at[k, j], rr.at[k, j], slab[j])

    def part_copy(k):
        b = block(k)
        return remote(pstage.at[b], zpart.at[f], ps.at[k], pr.at[k], (c, b, t))

    def part_arrival(k):
        b = lax.rem(f + k, F)
        return remote(pstage.at[b], zpart.at[b], ps.at[k], pr.at[k], (c, b, t))

    def gate_copy(k):
        b = block(k)
        return remote(dgs.at[b], dgr.at[f], ds_.at[k], dr.at[k], (c, b, t))

    def gate_arrival(k):
        b = lax.rem(f + k, F)
        return remote(dgs.at[b], dgr.at[b], ds_.at[k], dr.at[k], (c, b, t))

    lanes = lax.broadcasted_iota(jnp.int32, (K, R), 1)

    def send(k):
        b = block(k)
        if k > 0:
            remote(rows, zbuf.at[b], zs.at[k], zr.at[k], columns[k - 1]).wait_recv()
        for j in [*range(1, S), 0]:
            s = to(j)
            e = lax.div(s, T) * F * T + f * T + lax.rem(s, T)
            chosen = select[b, s]
            picked = jnp.dot(chosen, zbuf[b], preferred_element_type=FL)
            gate = jnp.sum(
                chosen.astype(FL) * fgate[b, pl.ds(e, 1), :], axis=1, keepdims=True
            )
            scaled = (picked * gate).astype(BF)
            if j:
                stage[s, b] = scaled
                slab_copy(k, j).start()
            else:
                gs[b, me] = scaled

    def gate_grads(k):
        b = block(k)
        total = jnp.zeros((R, R), FL)
        for s in range(S):
            chosen = select[b, s]
            picked = jnp.dot(chosen, zbuf[b], preferred_element_type=FL)
            dots = jnp.sum(picked * ysx[b, s].astype(FL), axis=1, keepdims=True)
            spread = jnp.where(lanes == s, dots, 0.0)
            high = spread.astype(BF)
            low = (spread - high.astype(FL)).astype(BF)
            total += inner_rows(high, chosen) + inner_rows(low, chosen)
        dgs[b] = total[:S, :]
        if k:
            gate_copy(k).start()
        else:
            dgr[f] = total[:S, :]

    def expert(k):
        b = block(k)
        for j in range(1, S):
            slab_arrival(k, j).wait_recv()
        if k == 0:
            load_o.wait()
        g = gs[b].reshape(S * K, W)
        pre_load(k).wait()
        tile = 256
        for i in range(FFW // tile):
            at = slice(i * tile, (i + 1) * tile)
            up_at = slice(FFW + i * tile, FFW + (i + 1) * tile)
            grad_mixed = outer_cols(g, wo[at, :])
            gate_pre = prebuf[:, at]
            up_pre = prebuf[:, up_at]
            sigmoid = jax.nn.sigmoid(gate_pre)
            dpre[b, :, at] = (
                grad_mixed * up_pre * (sigmoid * (1.0 + gate_pre * (1.0 - sigmoid)))
            ).astype(BF)
            dpre[b, :, up_at] = (grad_mixed * (gate_pre * sigmoid)).astype(BF)
        if k + 1 < F:
            pre_load(k + 1).start()
        if k == 0:
            load_i.wait()
        for j in range(1, S):
            slab_copy(k, j).wait_send()
        d = dpre[b]
        tile = min(512, W)
        for i in range(W // tile):
            at = slice(i * tile, (i + 1) * tile)
            x = outer_cols(d, wi[at, :]).astype(BF).reshape(S, K, tile)
            for s in range(S):
                stage[s, b, :, at] = x[s]
        for j in range(1, S):
            back_copy(k, j).start()
        back[b, me] = stage[me, b]

    def gather(k):
        b = block(k)
        for j in range(1, S):
            back_arrival(k, j).wait_recv()
        chosen = select[b].reshape(S * K, R)
        tile = min(512, W)
        for i in range(W // tile):
            at = slice(i * tile, (i + 1) * tile)
            total = inner_rows(chosen, back[b, :, :, at].reshape(S * K, tile))
            if k:
                pstage[b, :, at] = total.astype(BF)
            else:
                part[:, at] = total
        if k:
            part_copy(k).start()

    made = []

    def weight_tile(left, right, target, at):
        n = len(made)
        slot = n % 2
        if n >= 2:
            made[n - 2].wait()
        width = right.shape[1]
        tiles[slot, :, 0:width] = inner_rows(left, right)
        copy = pltpu.make_async_copy(
            tiles.at[slot, :, pl.ds(0, width)], target.at[pl.ds(at, 256)], tl.at[n]
        )
        copy.start()
        made.append(copy)

    def out_grads(first, last):
        g = gs[...].reshape(F * S * K, W)
        for i in range(first, last):
            left = mixed[:, :, i * 256 : (i + 1) * 256].reshape(F * S * K, 256)
            weight_tile(left, g, grad_out, i * 256)

    def in_grads(first, last):
        d = dpre[...].reshape(F * S * K, 2 * FFW)
        for i in range(first, last):
            left = ysx[:, :, :, i * 256 : (i + 1) * 256].reshape(F * S * K, 256)
            weight_tile(left, d, grad_in, i * 256)

    pre_load(0).start()
    send(0)
    load_y.wait()
    gate_grads(0)
    send(1)
    gate_grads(1)
    expert(0)
    send(2)
    gate_grads(2)
    expert(1)
    for k in range(3, F):
        send(k)
        gate_grads(k)
    load_x.start()
    gather(0)
    for k in range(2, F):
        expert(k)
        gather(k - 1)
    out_grads(0, FFW // 256)
    load_x.wait()
    in_grads(0, W // 512)
    gather(F - 1)
    in_grads(W // 512, W // 256)
    for k in range(1, F):
        part_arrival(k).wait_recv()
        part[...] += zpart[lax.rem(f + k, F)].astype(FL)
        gate_arrival(k).wait_recv()
    dgate[...] = dgr[...]
    for copy in made[-2:]:
        copy.wait()
    for copy in z_out:
        copy.wait_send()
    for k in range(F):
        if k:
            part_copy(k).wait_send()
            gate_copy(k).wait_send()
        for j in range(1, S):
            back_copy(k, j).wait_send()


def moe_backward(identity, C, F, T, rows, fgate, select, mixed, w_in, w_out, xr, got, pre):
    S = C * T
    K = select.shape[2]
    R, W = rows.shape
    H2, FFW = w_in.shape[1], w_out.shape[0]
    dma = pltpu.SemaphoreType.DMA
    V = pltpu.VMEM
    shape = jax.ShapeDtypeStruct
    return pl.pallas_call(
        functools.partial(moe_backward_body, C, F, T),
        out_shape=(
            shape((R, W), FL), shape((W, H2), FL), shape((FFW, W), FL), shape((F, S, R), FL),
        ),
        in_specs=[VMEM] * 4 + [ANY] * 5,
        out_specs=[VMEM, ANY, ANY, VMEM],
        scratch_shapes=[
            V((F, R, W), BF), V((S, F, K, W), BF), V((F, S, K, W), BF), V((F, S, K, W), BF),
            V((F, S, K, W), BF), V((W, H2), BF), V((FFW, W), BF), V((F, R, W), BF),
            V((F, R, W), BF), V((F, S * K, H2), BF), V((S * K, H2), FL),
            V((2, 256, max(W, H2)), FL), V((F, S, R), FL), V((F, S, R), FL),
            dma((4,)), dma((F,)), dma((F,)), dma((F, S)), dma((F, S)), dma((F, S)), dma((F, S)),
            dma((F,)), dma((F,)), dma((F,)), dma((F,)), dma((F,)),
            dma((FFW // 256 + W // 256,)),
        ],
        compiler_params=params(identity, 62),
    )(rows, fgate, select, mixed, w_in, w_out, xr, got, pre)


def split_low(values):
    high = lax.reduce_precision(values, 8, 7)
    return high.astype(BF), (values - high).astype(BF)


def local(
    hidden_in,
    teacher,
    lengths,
    routes,
    attn_gain,
    w_query,
    w_key,
    w_value,
    w_output,
    query_gain,
    key_gain,
    ffn_gain,
    w_router,
    w_expert_in,
    w_expert_out,
):
    c, f, t = place()
    C, F, T = (lax.axis_size(axis) for axis in AXES)
    S = C * T
    row_count = hidden_in.shape[1]
    width = hidden_in.shape[2]
    half_rows = row_count // T
    head_size = query_gain.shape[0]
    inv_root = head_size ** (-0.5)
    bf_type = BF
    fl_type = FL

    expert_count = S * F
    lanes = -(-expert_count // 128) * 128
    route_ids = routes[0]
    top_count = route_ids.shape[1]
    capacity = max(2, half_rows * top_count * 3 // (2 * expert_count))
    cap = -(-capacity // 16) * 16
    expert_ids = jnp.arange(lanes, dtype=jnp.int32)
    named = jnp.any(route_ids[:, :, None] == expert_ids[None, None, :], axis=1)
    row_ids = jnp.arange(half_rows, dtype=jnp.int32)
    below = (row_ids[None, :] < row_ids[:, None]).astype(bf_type)
    earlier = jnp.dot(below, named.astype(bf_type), preferred_element_type=fl_type)
    rank_tab = jnp.where(named, earlier, -1.0)

    q_cols, kv_cols = w_query.shape[1], w_key.shape[1]
    w_all = jnp.concatenate(
        [w_query, w_key, w_value, jnp.pad(w_router, ((0, 0), (0, lanes - expert_count)))], axis=1
    )
    proj_cols = q_cols + 2 * kv_cols
    q_heads = q_cols // head_size
    kv_heads = kv_cols // head_size
    group_size = q_heads // kv_heads
    inputs = hidden_in[0].astype(fl_type)
    positions = c * row_count + jnp.arange(row_count, dtype=jnp.int32)
    cosine, sine_tab = rope_tables(positions, head_size)
    length = jnp.take(lengths, f)
    total_len = row_count * C
    row_start = t * half_rows
    other_start = (1 - t) * half_rows
    own_inputs = lax.dynamic_slice_in_dim(inputs, row_start, half_rows, 0)
    own_positions = lax.dynamic_slice_in_dim(positions, row_start, half_rows, 0)
    fused = C == 4 and T == 2
    swap = [(i, 1 - i) for i in range(T)]
    if fused:
        cos_full = jnp.concatenate([cosine, cosine], axis=1)
        sin_signed = jnp.concatenate([-sine_tab, sine_tab], axis=1)
        key_pos = jnp.arange(total_len, dtype=jnp.int32)[:, None]
        bias = jnp.where((key_pos <= positions[None, :]) & (key_pos < length), 0.0, MASKED)
        (
            full_all, full_o, rank_z, raw, q_rot, all_both, keys_t, log_total, heads_low,
            normed_low, residual, ffn_low, gate_tab,
        ) = head(
            1, C, F, T, kv_heads, proj_cols, total_len,
            (
                hidden_in[0], rank_tab, attn_gain[None], query_gain[None], key_gain[None],
                ffn_gain[None], cos_full, sin_signed, bias, w_all, w_output,
            ),
        )
        full_router = full_all[:, proj_cols : proj_cols + expert_count]
        gates = gate_tab[:, :expert_count]
        ffn_factor = lax.rsqrt(jnp.mean(residual * residual, axis=-1, keepdims=True) + EPS)
    else:
        full_all, full_o, rank_z = gather_weights(C, F, w_all, w_output, rank_tab)
        full_qkv = full_all[:, :proj_cols]
        full_router = full_all[:, proj_cols : proj_cols + expert_count]
        normed, norm_factor = norm_rows(inputs, attn_gain)
        normed_low = normed.astype(bf_type)
        raw = jnp.dot(normed_low, full_qkv, preferred_element_type=fl_type)
        q_raw = raw[:, :q_cols].reshape(row_count, q_heads, head_size)
        k_raw = raw[:, q_cols : q_cols + kv_cols].reshape(row_count, kv_heads, head_size)
        values_low = raw[:, q_cols + kv_cols :].astype(bf_type).reshape(row_count, kv_heads, head_size)
        q_normed, q_factor = norm_rows(q_raw, query_gain)
        k_normed, k_factor = norm_rows(k_raw, key_gain)
        q_rot = rotate(q_normed, cosine, sine_tab).astype(bf_type)
        k_rot = rotate(k_normed, cosine, sine_tab).astype(bf_type)
        queries = jnp.transpose(q_rot.reshape(row_count, kv_heads, group_size, head_size), (1, 2, 0, 3))
        both = jnp.transpose(jnp.concatenate([k_rot, values_low], axis=1), (1, 0, 2))
        all_both = lax.all_gather(both, "ctx", axis=1, tiled=True)
        all_keys, all_values = all_both[:kv_heads], all_both[kv_heads:]
        block_len = min(1024, total_len)
        offsets = jnp.arange(total_len // block_len, dtype=jnp.int32) * block_len
        stat_shape = (kv_heads, group_size, row_count)

        def lse_step(carry, offset):
            running_max, running_sum = carry
            key_rows = lax.dynamic_slice_in_dim(all_keys, offset, block_len, 1)
            scores, allowed = block_scores(queries, key_rows, offset, positions, length, inv_root)
            new_max = jnp.maximum(running_max, jnp.max(scores, axis=-1))
            exponent = jnp.where(allowed, jnp.exp(scores - new_max[..., None]), 0.0)
            return (
                (new_max, running_sum * jnp.exp(running_max - new_max) + jnp.sum(exponent, axis=-1)),
                None,
            )

        (row_max, row_sum), _ = lax.scan(
            lse_step, (jnp.full(stat_shape, MASKED, fl_type), jnp.zeros(stat_shape, fl_type)), offsets
        )
        log_total = row_max + jnp.log(row_sum)

        def probs_of(offset):
            key_rows = lax.dynamic_slice_in_dim(all_keys, offset, block_len, 1)
            value_rows = lax.dynamic_slice_in_dim(all_values, offset, block_len, 1)
            scores, allowed = block_scores(queries, key_rows, offset, positions, length, inv_root)
            return (
                jnp.where(allowed, jnp.exp(scores - log_total[..., None]), 0.0),
                key_rows,
                value_rows,
            )

        def out_step(running, offset):
            probabilities, key_rows, value_rows = probs_of(offset)
            return (
                running
                + jnp.einsum(
                    "kgqj,kjd->kgqd",
                    probabilities.astype(bf_type),
                    value_rows,
                    preferred_element_type=fl_type,
                ),
                None,
            )

        attn_acc, _ = lax.scan(
            out_step, jnp.zeros((kv_heads, group_size, row_count, head_size), fl_type), offsets
        )
        heads_low = (
            jnp.transpose(attn_acc, (2, 0, 1, 3))
            .reshape(row_count, q_heads * head_size)
            .astype(bf_type)
        )
        heads_other = lax.dynamic_slice_in_dim(heads_low, other_start, half_rows, 0)
        heads_own = lax.dynamic_slice_in_dim(heads_low, row_start, half_rows, 0)
        theirs = jnp.dot(heads_other, full_o, preferred_element_type=fl_type).astype(bf_type)
        ours = lax.ppermute(theirs, "tp", swap)
        attn_rows = jnp.dot(heads_own, full_o, preferred_element_type=fl_type) + ours.astype(fl_type)
        own_factor = lax.dynamic_slice_in_dim(norm_factor, row_start, half_rows, 0)
        residual = own_inputs + attn_rows
        ffn_in, ffn_factor = norm_rows(residual, ffn_gain)
        ffn_low = ffn_in.astype(bf_type)
        logits = jnp.dot(ffn_low, full_router, preferred_element_type=fl_type)
        is_named = named[:, :expert_count]
        masked = jnp.where(is_named, logits, MASKED)
        shifted = jnp.where(is_named, jnp.exp(masked - jnp.max(masked, axis=-1, keepdims=True)), 0.0)
        gates = shifted / jnp.sum(shifted, axis=-1, keepdims=True)
        gate_tab = jnp.pad(gates, ((0, 0), (0, lanes - expert_count)))

    def of_slab(table):
        picked = table[:, :, :expert_count].reshape(F, half_rows, C, F, T)
        return lax.dynamic_index_in_dim(picked, f, 3, keepdims=False).reshape(F, half_rows, S)

    rank_slab = of_slab(rank_z)
    slot_ids = jnp.arange(cap, dtype=fl_type)
    chosen_rows = rank_slab[:, :, :, None] == slot_ids
    chosen_slots = (
        jnp.transpose(rank_slab, (0, 2, 1))[:, :, None, :] == slot_ids[:, None]
    )

    select = chosen_slots.astype(bf_type)
    if fused:
        gate_t = jnp.swapaxes(gates, 0, 1)
        expert_x, returned, both_pre, mixed_low, mixture, gate_z = moe_forward(
            2, C, F, T, ffn_low, gate_t, select, w_expert_in[0], w_expert_out[0]
        )
    else:
        received, _, gate_z = dispatch(2, C, F, T, ffn_low, select, gate_tab)
        expert_rows = received.reshape(-1, width)
        both_pre = jnp.dot(expert_rows, w_expert_in[0], preferred_element_type=fl_type)
        ff_width = w_expert_out.shape[1]
        gate_pre = both_pre[:, :ff_width]
        up_pre = both_pre[:, ff_width:]
        sigmoid_gate = jax.nn.sigmoid(gate_pre)
        silu_gate = gate_pre * sigmoid_gate
        mixed_low = (silu_gate * up_pre).astype(bf_type)
        expert_out = (
            jnp.dot(mixed_low, w_expert_out[0], preferred_element_type=fl_type)
            .astype(bf_type)
            .reshape(S, F, cap, width)
        )
        gate_slab = of_slab(gate_z)
        weigh = jnp.where(chosen_rows, gate_slab[..., None], 0.0).reshape(F, 1, half_rows, S * cap)
        weigh = jnp.concatenate(split_low(weigh), axis=1)
        returned, parts = combine(3, C, F, T, expert_out, weigh)
        mixture = jnp.sum(parts.astype(fl_type), axis=0)
    output_f = residual + mixture
    count = jnp.sum(lengths).astype(fl_type)
    tokens_total = lengths.shape[0] * row_count * C
    valid = own_positions < length
    error = jnp.where(valid[:, None], output_f - teacher[0].astype(fl_type), 0.0)
    loss_part = jnp.sum(error * error)
    grad_out = error * (tokens_total / count)

    if fused:
        grad_mixture, grad_expert_in, grad_expert_out, gate_back = moe_backward(
            3, C, F, T, grad_out.astype(bf_type), gate_z, select, mixed_low,
            w_expert_in[0], w_expert_out[0], expert_x, returned, both_pre,
        )
        grad_gate = jnp.transpose(
            gate_back.reshape(F, C, T, half_rows), (3, 1, 0, 2)
        ).reshape(half_rows, expert_count)
    else:
        select_gates = jnp.where(
            chosen_slots, jnp.transpose(gate_slab, (0, 2, 1))[:, :, None, :], 0.0
        )
        select_gates = jnp.concatenate(split_low(select_gates), axis=-1)
        grad_recv, grad_out_z = dispatch(4, C, F, T, grad_out.astype(bf_type), select_gates)
        slot_grads = jnp.einsum("zskr,zrd->zskd", select, grad_out_z, preferred_element_type=fl_type)
        slot_gate = jnp.sum(slot_grads * returned.astype(fl_type), axis=-1)
        gate_grads = jnp.sum(jnp.where(chosen_rows, slot_gate[:, None, :, :], 0.0), axis=-1)
        gate_grads = jnp.pad(gate_grads, ((0, 0), (0, 0), (0, -S % 128)))

        grad_recv = grad_recv.reshape(-1, width)
        grad_mixed = outer_cols(grad_recv, w_expert_out[0])
        grad_expert_out = inner_rows(mixed_low, grad_recv)
        grad_gate_pre = grad_mixed * up_pre * (sigmoid_gate * (1.0 + gate_pre * (1.0 - sigmoid_gate)))
        grad_up_pre = grad_mixed * silu_gate
        grad_pre = jnp.concatenate([grad_gate_pre, grad_up_pre], axis=1).astype(bf_type)
        grad_expert_in = inner_rows(expert_rows, grad_pre)
        grad_rows = (
            outer_cols(grad_pre, w_expert_in[0]).astype(bf_type).reshape(S, F, cap, width)
        )
        weigh_one = chosen_rows.astype(bf_type).reshape(F, 1, half_rows, S * cap)
        _, grad_parts, gate_back = combine(5, C, F, T, grad_rows, weigh_one, gate_grads)
        grad_gate = jnp.transpose(
            gate_back[:, :, :S].reshape(F, half_rows, C, T), (1, 2, 0, 3)
        ).reshape(half_rows, expert_count)
        grad_mixture = jnp.sum(grad_parts.astype(fl_type), axis=0)
    grad_logits = (
        gates * (grad_gate - jnp.sum(gates * grad_gate, axis=-1, keepdims=True))
    ).astype(bf_type)
    grad_ffn = grad_mixture + outer_cols(grad_logits, full_router)
    router_part = inner_rows(ffn_low, grad_logits)
    grad_resid_norm, ffn_gain_terms = norm_back(residual, ffn_factor, ffn_gain, grad_ffn)
    grad_residual = grad_out + grad_resid_norm
    grad_own = grad_residual.astype(bf_type)
    if fused:
        vec_in = jnp.zeros((8, width), fl_type)
        vec_in = vec_in.at[1].set(jnp.sum(ffn_gain_terms, axis=0))
        vec_in = vec_in.at[2, 2 * head_size].set(loss_part)
        router_rows = router_part.reshape(F, -1, width)
        grad_input, total_a, total_o, summed = tail(
            9, C, F, T, kv_heads,
            (
                grad_own, heads_low, normed_low, q_rot, all_both, keys_t, raw, log_total, bias,
                cos_full, sin_signed, query_gain[None], key_gain[None], attn_gain[None],
                own_inputs, grad_residual, router_rows, vec_in, full_o, full_all,
            ),
            width, q_cols // C,
        )
        grad_query = total_a[:, :q_cols].astype(fl_type)
        grad_key = total_a[:, q_cols : q_cols + kv_cols].astype(fl_type)
        grad_value = total_a[:, q_cols + kv_cols :].astype(fl_type)
        grad_output_w = total_o.astype(fl_type)
        router_len = router_rows.shape[1]
        grad_router = summed[:router_len].reshape(w_router.shape)
        sum_attn, sum_ffn = summed[router_len], summed[router_len + 1]
        sum_query = summed[router_len + 2, :head_size]
        sum_key = summed[router_len + 2, head_size : 2 * head_size]
        loss_total = summed[router_len + 2, 2 * head_size]
    else:
        grad_other = lax.ppermute(grad_own, "tp", swap)
        grad_attn = jnp.where(
            t == 0,
            jnp.concatenate([grad_own, grad_other], axis=0),
            jnp.concatenate([grad_other, grad_own], axis=0),
        )
        grad_heads = jnp.transpose(
            outer_cols(grad_attn, full_o)
            .astype(bf_type)
            .reshape(row_count, kv_heads, group_size, head_size),
            (1, 2, 0, 3),
        )

        def delta_step(running, offset):
            probabilities, key_rows, value_rows = probs_of(offset)
            grad_weights = jnp.einsum(
                "kgqd,kjd->kgqj", grad_heads, value_rows, preferred_element_type=fl_type
            )
            return (running + jnp.sum(probabilities * grad_weights, axis=-1), None)

        delta, _ = lax.scan(delta_step, jnp.zeros(stat_shape, fl_type), offsets)

        def grad_step(running, offset):
            probabilities, key_rows, value_rows = probs_of(offset)
            grad_weights = jnp.einsum(
                "kgqd,kjd->kgqj", grad_heads, value_rows, preferred_element_type=fl_type
            )
            grad_scores = (probabilities * (grad_weights - delta[..., None])).astype(bf_type)
            running = (
                running
                + jnp.einsum("kgqj,kjd->kgqd", grad_scores, key_rows, preferred_element_type=fl_type)
                * inv_root
            )
            key_part = (
                jnp.einsum("kgqj,kgqd->kjd", grad_scores, queries, preferred_element_type=fl_type)
                * inv_root
            )
            value_part = jnp.einsum(
                "kgqj,kgqd->kjd",
                probabilities.astype(bf_type),
                grad_heads,
                preferred_element_type=fl_type,
            )
            return (running, (key_part, value_part))

        grad_qrot, (key_blocks, value_blocks) = lax.scan(
            grad_step, jnp.zeros((kv_heads, group_size, row_count, head_size), fl_type), offsets
        )
        both_grads = jnp.concatenate([key_blocks, value_blocks], axis=1).astype(bf_type)
        both_grads = jnp.transpose(both_grads, (0, 2, 1, 3)).reshape(C, row_count, 2 * kv_cols)
        both_sum = ctx_sum(6, C, both_grads)
        grad_krot = both_sum[:, :kv_cols].reshape(row_count, kv_heads, head_size)
        grad_values_low = both_sum[:, kv_cols:].astype(bf_type)
        grad_qrot = jnp.transpose(grad_qrot, (2, 0, 1, 3)).reshape(row_count, q_heads, head_size)
        grad_qraw, query_gain_terms = norm_back(
            q_raw, q_factor, query_gain, rotate(grad_qrot, cosine, -sine_tab)
        )
        grad_kraw, key_gain_terms = norm_back(
            k_raw, k_factor, key_gain, rotate(grad_krot, cosine, -sine_tab)
        )
        grad_raw = jnp.concatenate(
            [
                grad_qraw.astype(bf_type).reshape(row_count, -1),
                grad_kraw.astype(bf_type).reshape(row_count, -1),
                grad_values_low,
            ],
            axis=1,
        )
        raw_other = lax.dynamic_slice_in_dim(grad_raw, other_start, half_rows, 0)
        raw_own = lax.dynamic_slice_in_dim(grad_raw, row_start, half_rows, 0)
        norm_theirs = outer_cols(raw_other, full_qkv).astype(bf_type)
        norm_ours = lax.ppermute(norm_theirs, "tp", swap)
        grad_normed = outer_cols(raw_own, full_qkv) + norm_ours.astype(fl_type)
        grad_input_norm, attn_gain_terms = norm_back(own_inputs, own_factor, attn_gain, grad_normed)
        grad_input = grad_residual + grad_input_norm

        total_a, total_o = weight_grads(
            7, C, F, normed_low.T, grad_raw, heads_low.T, grad_attn
        )
        total_a = total_a.reshape(-1, proj_cols).astype(fl_type)
        grad_query = total_a[:, :q_cols]
        grad_key = total_a[:, q_cols : q_cols + kv_cols]
        grad_value = total_a[:, q_cols + kv_cols :]
        grad_output_w = total_o.reshape(w_output.shape).astype(fl_type)

        vector = jnp.concatenate(
            [
                jnp.sum(attn_gain_terms, axis=0),
                jnp.sum(ffn_gain_terms, axis=0),
                jnp.sum(query_gain_terms, axis=(0, 1)),
                jnp.sum(key_gain_terms, axis=(0, 1)),
                loss_part[None],
            ]
        )
        vector = jnp.pad(vector, (0, -vector.shape[0] % 1024)).reshape(-1, 128)
        router_rows = router_part.reshape(F, -1, 128)
        small = jnp.concatenate(
            [router_rows, jnp.broadcast_to(vector[None], (F,) + vector.shape)], axis=1
        )
        summed = small_sum(8, C, F, T, small)
        router_len = router_rows.shape[1]
        grad_router = summed[:router_len].reshape(w_router.shape)
        flat = summed[router_len:].reshape(-1)
        head_at = 2 * width
        sum_attn, sum_ffn = flat[:width], flat[width:head_at]
        sum_query = flat[head_at : head_at + head_size]
        sum_key = flat[head_at + head_size : head_at + 2 * head_size]
        loss_total = flat[head_at + 2 * head_size]
    loss_value = loss_total / (count * width)
    return (
        output_f.astype(bf_type)[None],
        loss_value,
        grad_input[None],
        sum_attn,
        grad_query,
        grad_key,
        grad_value,
        grad_output_w,
        sum_query,
        sum_key,
        sum_ffn,
        grad_router,
        grad_expert_in[None],
        grad_expert_out[None],
    )


def solution(mesh):
    return jax.shard_map(
        local,
        mesh=mesh,
        in_specs=(
            P("fsdp", "ctx", None),
            P("fsdp", ("ctx", "tp"), None),
            P(),
            P("fsdp", ("ctx", "tp"), None),
            P(),
            P("fsdp", "tp"),
            P("fsdp", "tp"),
            P("fsdp", "tp"),
            P("tp", "fsdp"),
            P(),
            P(),
            P(),
            P("fsdp", None),
            P(("ctx", "fsdp", "tp"), None, None),
            P(("ctx", "fsdp", "tp"), None, None),
        ),
        out_specs=(
            P("fsdp", ("ctx", "tp"), None),
            P(),
            P("fsdp", ("ctx", "tp"), None),
            P(),
            P("fsdp", "tp"),
            P("fsdp", "tp"),
            P("fsdp", "tp"),
            P("tp", "fsdp"),
            P(),
            P(),
            P(),
            P("fsdp", None),
            P(("ctx", "fsdp", "tp"), None, None),
            P(("ctx", "fsdp", "tp"), None, None),
        ),
        check_vma=False,
    )
```

```python
import functools

import jax
import jax.numpy as jnp
from jax import lax
from jax.experimental import pallas as pl
from jax.experimental.pallas import tpu as pltpu
from jax.sharding import PartitionSpec as P

EPS = 1e-06
ROPE_BASE = 1000000.0
MASKED = -1e30
LOG2E = 1.4426950408889634
AXES = ("ctx", "fsdp", "tp")
MESH = pl.DeviceIdType.MESH
ANY = pl.BlockSpec(memory_space=pl.ANY)
VMEM = pl.BlockSpec(memory_space=pltpu.VMEM)
BF = jnp.bfloat16
FL = jnp.float32
MIB = 1024 * 1024


def norm_rows(values, gain_vec):
    factor = lax.rsqrt(jnp.mean(values * values, axis=-1, keepdims=True) + EPS)
    return (values * factor * gain_vec, factor)


def norm_back(values, factor, gain_vec, upstream):
    weighted = upstream * gain_vec
    inner_mean = jnp.mean(values * weighted, axis=-1, keepdims=True)
    return (
        factor * weighted - values * (factor * factor * factor) * inner_mean,
        upstream * values * factor,
    )


def rope_tables(positions, head_size):
    half_size = head_size // 2
    frequency = jnp.power(ROPE_BASE, -jnp.arange(half_size, dtype=jnp.float32) * (2.0 / head_size))
    angles = positions.astype(jnp.float32)[:, None] * frequency[None, :]
    return (jnp.cos(angles), jnp.sin(angles))


def rotate(values, cosine, sine_tab):
    half_size = values.shape[-1] // 2
    front_half = values[..., :half_size]
    back_half = values[..., half_size:]
    cos_rows = cosine[:, None, :]
    sin_rows = sine_tab[:, None, :]
    return jnp.concatenate(
        [
            front_half * cos_rows - back_half * sin_rows,
            back_half * cos_rows + front_half * sin_rows,
        ],
        axis=-1,
    )


def inner_rows(left, right):
    return lax.dot_general(
        left, right, (((0,), (0,)), ((), ())), preferred_element_type=jnp.float32
    )


def outer_cols(left, right):
    return lax.dot_general(
        left, right, (((1,), (1,)), ((), ())), preferred_element_type=jnp.float32
    )


def block_scores(queries, key_rows, offset, positions, length, inv_root):
    block_len = key_rows.shape[1]
    raw_scores = (
        jnp.einsum("kgqd,kjd->kgqj", queries, key_rows, preferred_element_type=jnp.float32)
        * inv_root
    )
    key_pos = offset + jnp.arange(block_len, dtype=jnp.int32)
    allowed = (key_pos[None, :] <= positions[:, None]) & (key_pos[None, :] < length)
    return (jnp.where(allowed, raw_scores, MASKED), allowed)


def place():
    return tuple(lax.axis_index(axis) for axis in AXES)


def remote(source, target, sent, got, device):
    return pltpu.make_async_remote_copy(
        src_ref=source, dst_ref=target, send_sem=sent, recv_sem=got,
        device_id=device, device_id_type=MESH,
    )


def greet(devices):
    barrier = pltpu.get_barrier_semaphore()
    for device in devices:
        pl.semaphore_signal(barrier, inc=1, device_id=device, device_id_type=MESH)
    pl.semaphore_wait(barrier, len(devices))


def params(identity, mebibytes):
    return pltpu.CompilerParams(
        collective_id=identity, has_side_effects=True, vmem_limit_bytes=int(mebibytes * MIB)
    )


def gather_body(C, F, wa, wo, tab, fa, fo, ftab, loc, zs, zr, ys, yr, ks, kr, ts, tr):
    c, f, t = place()
    core, chip = lax.rem(c, 2), lax.div(c, 2)
    chips = C // 2
    sib = c + 1 - 2 * core
    ra, (ro, co) = wa.shape[0], wo.shape
    pa, po = ra // C, ro // C

    def spot(arr, b, p):
        if arr == 0:
            return fa.at[pl.ds(pl.multiple_of(b * ra + p * pa, pa), pa)]
        return fo.at[pl.ds(pl.multiple_of(p * po, po), po), pl.ds(pl.multiple_of(b * co, co), co)]

    def own(arr):
        if arr == 0:
            return wa.at[pl.ds(pl.multiple_of(c * pa, pa), pa)]
        return wo.at[pl.ds(pl.multiple_of(c * po, po), po)]

    peers = [(c, lax.rem(f + k, F), t) for k in range(1, F)]
    peers += [(lax.rem(chip + k, chips) * 2 + core, f, t) for k in range(1, chips)]
    peers += [(sib, f, t)]
    greet(peers)

    def z_copy(arr, s, d):
        b = f - (s - 1) if d == 0 else f + (s - 1)
        source = own(arr) if s == 1 else spot(arr, b, c)
        return remote(
            source, spot(arr, b, c), zs.at[d, s, arr], zr.at[d, s, arr],
            (c, f + 1 if d == 0 else f - 1, t),
        )

    def z_sends(s, d):
        b = f - (s - 1) if d == 0 else f + (s - 1)
        return (f + 1 < F) & (b >= 0) if d == 0 else (f > 0) & (b < F)

    def z_gets(s, d):
        return f - s >= 0 if d == 0 else f + s < F

    def came(s, d):
        return f - s if d == 0 else f + s

    def z_arrival(arr, s, d):
        b = came(s, d)
        here = spot(arr, b, c)
        return remote(here, here, zs.at[d, s, arr], zr.at[d, s, arr], (c, f, t))

    def y_copy(arr, s, d, k):
        here = spot(arr, came(s, d), c)
        there = (lax.rem(chip + k, chips) * 2 + core, f, t)
        return remote(here, here, ys.at[d, s, k, arr], yr.at[d, s, k, arr], there)

    def k_copy(arr, s, d, k, side):
        p = lax.rem(chip + chips - k, chips) * 2 + side
        here = spot(arr, came(s, d), p)
        return remote(here, here, ks.at[d, s, k, arr], kr.at[d, s, k, arr], (sib, f, t))

    def y_arrival(arr, s, d, k):
        p = lax.rem(chip + chips - k, chips) * 2 + core
        here = spot(arr, came(s, d), p)
        return remote(here, here, ys.at[d, s, k, arr], yr.at[d, s, k, arr], (sib, f, t))

    tabs = [
        remote(tab, ftab.at[f], ts.at[k], tr.at[k], (c, lax.rem(f + k, F), t)) for k in range(1, F)
    ]
    for copy in tabs:
        copy.start()
    for d in range(2):

        @pl.when(z_sends(1, d))
        def _():
            for arr in range(2):
                z_copy(arr, 1, d).start()

    locals_ = [
        pltpu.make_async_copy(tab, ftab.at[f], loc.at[0]),
        pltpu.make_async_copy(wa, fa.at[pl.ds(pl.multiple_of(f * ra, ra), ra)], loc.at[1]),
        pltpu.make_async_copy(wo, fo.at[:, pl.ds(pl.multiple_of(f * co, co), co)], loc.at[2]),
    ]
    for copy in locals_:
        copy.start()

    def pass_on(s, d):
        for arr in range(2):
            for k in range(1, chips):
                y_arrival(arr, s, d, k).wait_recv()
                k_copy(arr, s, d, k, core).start()

    for s in range(1, F):
        for d in range(2):

            @pl.when(z_gets(s, d))
            def _():
                for arr in range(2):
                    z_arrival(arr, s, d).wait_recv()
                    if s + 1 < F:

                        @pl.when(z_sends(s + 1, d))
                        def _():
                            z_copy(arr, s + 1, d).start()

                    for k in range(1, chips):
                        y_copy(arr, s, d, k).start()
                    k_copy(arr, s, d, 0, core).start()

        if s > 1:
            for d in range(2):
                pl.when(z_gets(s - 1, d))(functools.partial(pass_on, s - 1, d))
    for d in range(2):
        pl.when(z_gets(F - 1, d))(functools.partial(pass_on, F - 1, d))
    for copy in tabs:
        copy.wait()
    for copy in locals_:
        copy.wait()
    for s in range(1, F):
        for d in range(2):

            @pl.when(z_sends(s, d))
            def _():
                for arr in range(2):
                    z_copy(arr, s, d).wait_send()

            @pl.when(z_gets(s, d))
            def _():
                for arr in range(2):
                    for k in range(1, chips):
                        y_copy(arr, s, d, k).wait_send()
                    for k in range(chips):
                        k_copy(arr, s, d, k, core).wait_send()
                        k_copy(arr, s, d, k, 1 - core).wait_recv()


def gather_weights(C, F, wa, wo, tab):
    ra, ca = wa.shape
    ro, co = wo.shape
    chips = C // 2
    dma = pltpu.SemaphoreType.DMA
    return pl.pallas_call(
        functools.partial(gather_body, C, F),
        out_shape=(
            jax.ShapeDtypeStruct((F * ra, ca), wa.dtype),
            jax.ShapeDtypeStruct((ro, F * co), wo.dtype),
            jax.ShapeDtypeStruct((F,) + tab.shape, tab.dtype),
        ),
        in_specs=[ANY] * 3,
        out_specs=[ANY] * 3,
        scratch_shapes=[
            dma((3,)), dma((2, F, 2)), dma((2, F, 2)),
            dma((2, F, chips, 2)), dma((2, F, chips, 2)),
            dma((2, F, chips, 2)), dma((2, F, chips, 2)),
            dma((F,)), dma((F,)),
        ],
        compiler_params=params(1, 16),
    )(wa, wo, tab)


def slab_place(C, T):
    c, f, t = place()
    return c, f, t, c * T + t


def slab_device(index, f, T):
    return (lax.div(index, T), f, lax.rem(index, T))


def dispatch_body(C, F, T, tabbed, rows, select, *refs):
    if tabbed:
        tab, out, zbuf, ftab, stage, loc, zs, zr, ss, sr, ts, tr = refs
    else:
        out, zbuf, stage, loc, zs, zr, ss, sr = refs
    c, f, t, me = slab_place(C, T)
    S = C * T
    K = select.shape[2]
    copies = select.shape[3] // rows.shape[0]
    columns = [(c, lax.rem(f + k, F), t) for k in range(1, F)]
    greet(columns + [slab_device(lax.rem(me + j, S), f, T) for j in range(1, S)])
    sends = [
        remote(rows, zbuf.at[f], zs.at[k], zr.at[k], columns[k - 1]) for k in range(1, F)
    ]
    if tabbed:
        tabs = [remote(tab, ftab.at[f], ts.at[k], tr.at[k], columns[k - 1]) for k in range(1, F)]
        for copy in tabs:
            copy.start()
        ftab[f] = tab[...]
    for copy in sends:
        copy.start()
    zbuf[f] = rows[...]

    def slab_copy(k, j):
        b = lax.rem(f + F - k, F)
        e = lax.rem(me + j, S)
        return remote(
            stage.at[e, b], out.at[me, b], ss.at[k, j], sr.at[k, j], slab_device(e, f, T)
        )

    def slab_arrival(k, j):
        b = lax.rem(f + F - k, F)
        e = lax.rem(me + S - j, S)
        return remote(
            stage.at[e, b], out.at[e, b], ss.at[k, j], sr.at[k, j], slab_device(e, f, T)
        )

    def own_copy(k):
        b = lax.rem(f + F - k, F)
        return pltpu.make_async_copy(stage.at[me, b], out.at[me, b], loc.at[k])

    for k in range(F):
        b = lax.rem(f + F - k, F)
        if k > 0:
            remote(rows, zbuf.at[b], zs.at[k], zr.at[k], columns[k - 1]).wait_recv()

        def pick(j):
            e = lax.rem(me + j, S)
            block = zbuf[b]
            if copies > 1:
                block = jnp.concatenate([block] * copies, axis=0)
            stage[e, b] = jnp.dot(
                select[b, e], block, preferred_element_type=FL
            ).astype(BF)

        if S <= 8:
            for j in range(1, S):
                pick(j)
                slab_copy(k, j).start()
        else:

            def step(j, carry):
                pick(j)
                slab_copy(k, j).start()
                return carry

            lax.fori_loop(1, S, step, 0)
        pick(0)
        own_copy(k).start()
    if tabbed:
        for copy in tabs:
            copy.wait()
    for copy in sends:
        copy.wait_send()
    for k in range(F):
        own_copy(k).wait()

        def settle(j, carry):
            slab_copy(k, j).wait_send()
            slab_arrival(k, j).wait_recv()
            return carry

        lax.fori_loop(1, S, settle, 0)


def dispatch(identity, C, F, T, rows, select, tab=None):
    S = C * T
    K = select.shape[2]
    R, W = rows.shape
    dma = pltpu.SemaphoreType.DMA
    tabbed = tab is not None
    outs = [jax.ShapeDtypeStruct((S, F, K, W), BF), jax.ShapeDtypeStruct((F, R, W), BF)]
    out_specs = [ANY, VMEM]
    ins = [rows, select]
    scratch = [
        pltpu.VMEM((S, F, K, W), BF), dma((F,)), dma((F,)), dma((F,)), dma((F, S)), dma((F, S)),
    ]
    if tabbed:
        outs.append(jax.ShapeDtypeStruct((F,) + tab.shape, tab.dtype))
        out_specs.append(VMEM)
        ins.append(tab)
        scratch += [dma((F,)), dma((F,))]
    return pl.pallas_call(
        functools.partial(dispatch_body, C, F, T, tabbed),
        out_shape=tuple(outs),
        in_specs=[VMEM] * len(ins),
        out_specs=out_specs,
        scratch_shapes=scratch,
        compiler_params=params(identity, 32),
    )(*ins)


def combine_body(C, F, T, tabbed, rows, weigh, *refs):
    if tabbed:
        tab, got, part, ftab, stage, loc, zs, zr, ss, sr, ts, tr = refs
    else:
        got, part, stage, loc, zs, zr, ss, sr = refs
    c, f, t, me = slab_place(C, T)
    S = C * T
    K, W = got.shape[2], got.shape[3]
    n = weigh.shape[1]
    columns = [(c, lax.rem(f + k, F), t) for k in range(1, F)]
    greet(columns + [slab_device(lax.rem(me + j, S), f, T) for j in range(1, S)])

    def slab_copy(k, j):
        b = lax.rem(f + k, F)
        e = lax.rem(me + j, S)
        return remote(
            rows.at[e, b], got.at[b, me], ss.at[k, j], sr.at[k, j], slab_device(e, f, T)
        )

    def slab_arrival(k, j):
        b = lax.rem(f + k, F)
        e = lax.rem(me + S - j, S)
        return remote(
            rows.at[e, b], got.at[b, e], ss.at[k, j], sr.at[k, j], slab_device(e, f, T)
        )

    def own_copy(k):
        b = lax.rem(f + k, F)
        return pltpu.make_async_copy(rows.at[me, b], got.at[b, me], loc.at[k])

    order = list(range(1, F)) + [0]
    for k in order:

        def begin(j, carry):
            slab_copy(k, j).start()
            return carry

        lax.fori_loop(1, S, begin, 0)
        own_copy(k).start()
    if tabbed:
        tabs = [
            remote(tab.at[lax.rem(f + k, F)], ftab.at[f], ts.at[k], tr.at[k], columns[k - 1])
            for k in range(1, F)
        ]
        for copy in tabs:
            copy.start()
        ftab[f] = tab[f]

    def z_copy(k):
        b = lax.rem(f + k, F)
        return remote(stage.at[b], part.at[f], zs.at[k], zr.at[k], columns[k - 1])

    def z_arrival(k):
        b = lax.rem(f + F - k, F)
        return remote(stage.at[b], part.at[b], zs.at[k], zr.at[k], columns[k - 1])

    step = min(W, 512)
    for k in order:
        b = lax.rem(f + k, F)
        own_copy(k).wait()

        def settle(j, carry):
            slab_arrival(k, j).wait_recv()
            return carry

        lax.fori_loop(1, S, settle, 0)
        target = part if k == 0 else stage

        def add(i, carry):
            columns_ = pl.ds(pl.multiple_of(i * step, step), step)
            block = got[b, :, :, columns_].reshape(S * K, step)
            total = jnp.dot(weigh[b, 0], block, preferred_element_type=FL)
            for m in range(1, n):
                total += jnp.dot(weigh[b, m], block, preferred_element_type=FL)
            target[b, :, columns_] = total.astype(BF)
            return carry

        lax.fori_loop(0, W // step, add, 0)
        if k > 0:
            z_copy(k).start()
    for k in range(1, F):
        z_copy(k).wait_send()
        z_arrival(k).wait_recv()
    for k in range(F):

        def leave(j, carry):
            slab_copy(k, j).wait_send()
            return carry

        lax.fori_loop(1, S, leave, 0)
    if tabbed:
        for copy in tabs:
            copy.wait()


def combine(identity, C, F, T, rows, weigh, tab=None):
    S, _, K, W = rows.shape
    R = weigh.shape[2]
    dma = pltpu.SemaphoreType.DMA
    tabbed = tab is not None
    outs = [jax.ShapeDtypeStruct((F, S, K, W), BF), jax.ShapeDtypeStruct((F, R, W), BF)]
    ins = [rows, weigh]
    scratch = [
        pltpu.VMEM((F, R, W), BF), dma((F,)), dma((F,)), dma((F,)), dma((F, S)), dma((F, S)),
    ]
    if tabbed:
        outs.append(jax.ShapeDtypeStruct(tab.shape, tab.dtype))
        ins.append(tab)
        scratch += [dma((F,)), dma((F,))]
    return pl.pallas_call(
        functools.partial(combine_body, C, F, T, tabbed),
        out_shape=tuple(outs),
        in_specs=[ANY] + [VMEM] * (len(ins) - 1),
        out_specs=[VMEM] * len(outs),
        scratch_shapes=scratch,
        compiler_params=params(identity, 32),
    )(*ins)


def ctx_sum_body(C, x, out, got, ss, sr):
    c, f, t = place()
    peers = [(lax.rem(c + k, C), f, t) for k in range(1, C)]
    greet(peers)

    def copy(k):
        p = lax.rem(c + k, C)
        return remote(x.at[p], got.at[c], ss.at[k], sr.at[k], (p, f, t))

    def arrival(k):
        p = lax.rem(c + C - k, C)
        return remote(x.at[p], got.at[p], ss.at[k], sr.at[k], (p, f, t))

    for k in range(1, C):
        copy(k).start()
    got[c] = x[c]
    for k in range(1, C):
        arrival(k).wait_recv()
    total = got[0].astype(FL)
    for p in range(1, C):
        total += got[p].astype(FL)
    out[...] = total
    for k in range(1, C):
        copy(k).wait_send()


def ctx_sum(identity, C, x):
    dma = pltpu.SemaphoreType.DMA
    return pl.pallas_call(
        functools.partial(ctx_sum_body, C),
        out_shape=jax.ShapeDtypeStruct(x.shape[1:], FL),
        in_specs=[VMEM],
        out_specs=VMEM,
        scratch_shapes=[pltpu.VMEM(x.shape, x.dtype), dma((C,)), dma((C,))],
        compiler_params=params(identity, 24),
    )(x)


def small_body(C, F, T, x, out, zgot, mid, sgot, zs, zr, ss, sr):
    c, f, t, me = slab_place(C, T)
    S = C * T
    columns = [(c, lax.rem(f + k, F), t) for k in range(1, F)]
    greet(columns + [slab_device(lax.rem(me + j, S), f, T) for j in range(1, S)])

    def z_copy(k):
        return remote(x.at[lax.rem(f + k, F)], zgot.at[f], zs.at[k], zr.at[k], columns[k - 1])

    def z_arrival(k):
        b = lax.rem(f + F - k, F)
        return remote(x.at[b], zgot.at[b], zs.at[k], zr.at[k], columns[k - 1])

    for k in range(1, F):
        z_copy(k).start()
    zgot[f] = x[f]
    for k in range(1, F):
        z_arrival(k).wait_recv()
    total = zgot[0]
    for b in range(1, F):
        total += zgot[b]
    mid[...] = total
    sgot[me] = total

    def s_copy(j):
        return remote(
            mid, sgot.at[me], ss.at[j], sr.at[j], slab_device(lax.rem(me + j, S), f, T)
        )

    def s_arrival(j):
        e = lax.rem(me + S - j, S)
        return remote(mid, sgot.at[e], ss.at[j], sr.at[j], slab_device(e, f, T))

    for j in range(1, S):
        s_copy(j).start()
    for j in range(1, S):
        s_arrival(j).wait_recv()
    total = sgot[0]
    for e in range(1, S):
        total += sgot[e]
    out[...] = total
    for k in range(1, F):
        z_copy(k).wait_send()
    for j in range(1, S):
        s_copy(j).wait_send()


def small_sum(identity, C, F, T, x):
    dma = pltpu.SemaphoreType.DMA
    S = C * T
    one = x.shape[1:]
    return pl.pallas_call(
        functools.partial(small_body, C, F, T),
        out_shape=jax.ShapeDtypeStruct(one, FL),
        in_specs=[VMEM],
        out_specs=VMEM,
        scratch_shapes=[
            pltpu.VMEM((F,) + one, FL), pltpu.VMEM(one, FL), pltpu.VMEM((S,) + one, FL),
            dma((F,)), dma((F,)), dma((S,)), dma((S,)),
        ],
        compiler_params=params(identity, 24),
    )(x)


def far_first(F):
    table = []
    for f in range(F):
        order = []
        for i in range(F):
            ends = [F - 1 - i, i] if f * 2 < F else [i, F - 1 - i]
            for b in ends:
                if ((b > f and b == F - 1 - i) or (b < f and b == i)) and b not in order:
                    order.append(b)
        table.append(order + [f])
    return table


def grads_body(
    C, F, xt, da, ht, dt, outa, outo,
    ska, sko, rka, rko, sya, syo, rya, ryo, rza, rzo, sza, szo,
    k_s, k_r, y_s, y_r, z_s, z_r, g_s, g_r, h_s, h_r,
):
    c, f, t = place()
    core, chip = lax.rem(c, 2), lax.div(c, 2)
    chips = C // 2
    sib = c + 1 - 2 * core
    pa, po, co = outa.shape[1], outo.shape[1], outo.shape[2]
    ra = pa * C
    table = far_first(F)

    def block(q):
        value = jnp.int32(table[0][q])
        for g in range(1, F):
            value = jnp.where(f == g, table[g][q], value)
        return value

    blocks = [block(q) for q in range(F)]
    ends = [(c, lax.rem(f + 1, F), t), (c, lax.rem(f + F - 1, F), t)]
    mates = [(lax.rem(chip + k, chips) * 2 + core, f, t) for k in range(1, chips)]
    greet(ends + mates + [(sib, f, t)])

    def piece_a(b, p):
        rows = pl.ds(pl.multiple_of(b * ra + p * pa, pa), pa)
        return jnp.dot(xt[rows, :], da[...], preferred_element_type=FL)

    def piece_o(b, p):
        rows = pl.ds(pl.multiple_of(p * po, po), po)
        cols = pl.ds(pl.multiple_of(b * co, co), co)
        return jnp.dot(ht[rows, :], dt[:, cols], preferred_element_type=FL)

    def core_copies(q, k):
        b = blocks[q]
        return [
            remote(ska.at[b, k], rka.at[b, k], k_s.at[q, k, 0], k_r.at[q, k, 0], (sib, f, t)),
            remote(sko.at[b, k], rko.at[b, k], k_s.at[q, k, 1], k_r.at[q, k, 1], (sib, f, t)),
        ]

    for q in range(F):
        b = blocks[q]
        for k in [*range(1, chips), 0]:
            p = lax.rem(chip + k, chips) * 2 + 1 - core
            ska[b, k] = piece_a(b, p).astype(BF)
            sko[b, k] = piece_o(b, p).astype(BF)
            for copy in core_copies(q, k):
                copy.start()

    def chip_copies(q, k):
        b = blocks[q]
        there = mates[k - 1]
        return [
            remote(sya.at[b, k - 1], rya.at[b, k - 1], y_s.at[q, k, 0], y_r.at[q, k, 0], there),
            remote(syo.at[b, k - 1], ryo.at[b, k - 1], y_s.at[q, k, 1], y_r.at[q, k, 1], there),
        ]

    for q in range(F):
        b = blocks[q]
        for k in range(1, chips):
            p = lax.rem(chip + k, chips) * 2 + core
            for copy in core_copies(q, k):
                copy.wait_recv()
            sya[b, k - 1] = (piece_a(b, p) + rka[b, k].astype(FL)).astype(BF)
            syo[b, k - 1] = (piece_o(b, p) + rko[b, k].astype(FL)).astype(BF)
            for copy in chip_copies(q, k):
                copy.start()

    def z_copies(q, b, slot, there):
        return [
            remote(sza.at[b], rza.at[slot], z_s.at[q, 0], z_r.at[slot, 0], there),
            remote(szo.at[b], rzo.at[slot], z_s.at[q, 1], z_r.at[slot, 1], there),
        ]

    def z_wait(slot):
        for copy in z_copies(0, 0, slot, ends[0]):
            copy.wait_recv()

    for q in range(F):
        b = blocks[q]
        for copy in core_copies(q, 0):
            copy.wait_recv()
        for k in range(1, chips):
            for copy in chip_copies(q, k):
                copy.wait_recv()
        total_a = piece_a(b, c) + rka[b, 0].astype(FL)
        total_o = piece_o(b, c) + rko[b, 0].astype(FL)
        for k in range(1, chips):
            total_a += rya[b, k - 1].astype(FL)
            total_o += ryo[b, k - 1].astype(FL)
        if q < F - 1:
            up = b > f
            first = jnp.where(up, f == 0, f == F - 1)

            @pl.when(first)
            def _():
                sza[b] = total_a.astype(BF)
                szo[b] = total_o.astype(BF)

            @pl.when(jnp.logical_not(first))
            def _():
                z_wait(b)
                sza[b] = (total_a + rza[b].astype(FL)).astype(BF)
                szo[b] = (total_o + rzo[b].astype(FL)).astype(BF)

            @pl.when(up)
            def _():
                for copy in z_copies(q, b, b, (c, f + 1, t)):
                    copy.start()

            @pl.when(jnp.logical_not(up))
            def _():
                slot = jnp.where(b == f - 1, F, b)
                for copy in z_copies(q, b, slot, (c, f - 1, t)):
                    copy.start()

        else:
            sza[f] = total_a.astype(BF)
            szo[f] = total_o.astype(BF)

            @pl.when(f > 0)
            def _():
                z_wait(f)
                sza[f] = (total_a + rza[f].astype(FL)).astype(BF)
                szo[f] = (total_o + rzo[f].astype(FL)).astype(BF)

            @pl.when(f < F - 1)
            def _():
                z_wait(F)
                outa[c] = (sza[f].astype(FL) + rza[F].astype(FL)).astype(BF)
                outo[c] = (szo[f].astype(FL) + rzo[F].astype(FL)).astype(BF)

            @pl.when(f == F - 1)
            def _():
                outa[c] = sza[f]
                outo[c] = szo[f]

    def spread(k):
        there = mates[k - 1]
        return [
            remote(outa.at[c], outa.at[c], g_s.at[k, 0], g_r.at[k, 0], there),
            remote(outo.at[c], outo.at[c], g_s.at[k, 1], g_r.at[k, 1], there),
        ]

    def hand(k, side):
        p = lax.rem(chip + chips - k, chips) * 2 + side
        return [
            remote(outa.at[p], outa.at[p], h_s.at[k, 0], h_r.at[k, 0], (sib, f, t)),
            remote(outo.at[p], outo.at[p], h_s.at[k, 1], h_r.at[k, 1], (sib, f, t)),
        ]

    def spread_arrival(k):
        p = lax.rem(chip + chips - k, chips) * 2 + core
        return [
            remote(outa.at[p], outa.at[p], g_s.at[k, 0], g_r.at[k, 0], mates[k - 1]),
            remote(outo.at[p], outo.at[p], g_s.at[k, 1], g_r.at[k, 1], mates[k - 1]),
        ]

    for k in range(1, chips):
        for copy in spread(k):
            copy.start()
    for copy in hand(0, core):
        copy.start()
    for k in range(1, chips):
        for copy in spread_arrival(k):
            copy.wait_recv()
        for copy in hand(k, core):
            copy.start()
    for k in range(chips):
        for copy in hand(k, 1 - core):
            copy.wait_recv()
        for copy in hand(k, core):
            copy.wait_send()
    for k in range(1, chips):
        for copy in spread(k):
            copy.wait_send()
    for q in range(F):
        for k in range(chips):
            for copy in core_copies(q, k):
                copy.wait_send()
        for k in range(1, chips):
            for copy in chip_copies(q, k):
                copy.wait_send()
        if q < F - 1:
            for copy in z_copies(q, 0, 0, ends[0]):
                copy.wait_send()


def weight_grads(identity, C, F, xt, da, ht, dt):
    D, R = xt.shape
    pa, na = D // F // C, da.shape[1]
    po, no = ht.shape[0] // C, dt.shape[1] // F
    chips = C // 2
    dma = pltpu.SemaphoreType.DMA

    def pair(*lead):
        return [pltpu.VMEM(lead + (pa, na), BF), pltpu.VMEM(lead + (po, no), BF)]

    return pl.pallas_call(
        functools.partial(grads_body, C, F),
        out_shape=(
            jax.ShapeDtypeStruct((C, pa, na), BF),
            jax.ShapeDtypeStruct((C, po, no), BF),
        ),
        in_specs=[VMEM] * 4,
        out_specs=[VMEM] * 2,
        scratch_shapes=[
            *pair(F, chips), *pair(F, chips), *pair(F, chips - 1), *pair(F, chips - 1),
            *pair(F + 1), *pair(F),
            dma((F, chips, 2)), dma((F, chips, 2)), dma((F, chips, 2)), dma((F, chips, 2)),
            dma((F, 2)), dma((F + 1, 2)), dma((chips, 2)), dma((chips, 2)),
            dma((chips, 2)), dma((chips, 2)),
        ],
        compiler_params=params(identity, 60),
    )(xt, da, ht, dt)


def tail_body(
    C, F, T, KH,
    grad_own, heads, qrot, kv, keys_t, raw, lse, bias, cosf, sins, qgain, kgain, again,
    own_in, resid_in, router, vec_in, normed, fo, fall,
    gin, outa, outo, small,
    wbuf, dall, nall, hq, rq, dheads, draw, dk, dv, ksend, kgot, gains, nsend, ngot, nown,
    sza, szo, rza, rzo, smx, zgot, sums, sgot,
    wsem, xs, xr, as_, ar, hs, hr, ns, nr, gs_, gr, ds_, dr, rs, rr, z_s, z_r, ts, tr, us, ur,
):
    c, f, t, me = slab_place(C, T)
    S = C * T
    R, QC = heads.shape
    W = grad_own.shape[1]
    PC = raw.shape[1]
    L = kv.shape[1]
    HS = qgain.shape[1]
    QH = QC // HS
    G = QH // KH
    Rh = grad_own.shape[0]
    KC = KH * HS
    pa = rq.shape[2]
    po = hq.shape[2]
    rows_a, cols_o = outa.shape[0], outo.shape[1]
    root = HS ** (-0.5)
    core = lax.rem(c, 2)
    sib = c + 1 - 2 * core
    mate = lax.rem(c + 2, C)
    mate_sib = lax.rem(sib + 2, C)
    table = far_first(F)

    def block(q):
        value = jnp.int32(table[0][q])
        for g in range(1, F):
            value = jnp.where(f == g, table[g][q], value)
        return value

    blocks = [block(q) for q in range(F)]
    columns = [(c, lax.rem(f + k, F), t) for k in range(1, F)]
    greet(columns + [slab_device(lax.rem(me + j, S), f, T) for j in range(1, S)])
    at_t = pl.ds(pl.multiple_of(t * Rh, Rh), Rh)
    at_u = pl.ds(pl.multiple_of((1 - t) * Rh, Rh), Rh)
    beside = (c, f, 1 - t)

    load_o = pltpu.make_async_copy(fo, wbuf.at[:, pl.ds(0, W)], wsem.at[0])
    load_o.start()

    swap_d = remote(grad_own, dall.at[c, at_t], xs.at[0], xr.at[0], beside)
    swap_d_in = remote(grad_own, dall.at[c, at_u], xs.at[0], xr.at[0], beside)
    swap_n = remote(nsend, ngot, xs.at[1], xr.at[1], beside)

    def spread(view, n, i):
        here = view(mate) if i == 2 else view(c)
        there = (mate if i == 0 else sib, f, t)
        return remote(here, here, as_.at[n, i], ar.at[n, i], there)

    def spread_in(view, n, i):
        here = view((mate, sib, mate_sib)[i])
        return remote(here, here, as_.at[n, i], ar.at[n, i], (sib, f, t))

    def spread_start(view, n):
        spread(view, n, 0).start()
        spread(view, n, 1).start()

    def spread_pass(view, n):
        spread_in(view, n, 0).wait_recv()
        spread(view, n, 2).start()

    def spread_end(view, n):
        spread_in(view, n, 1).wait_recv()
        spread_in(view, n, 2).wait_recv()

    def spread_sent(view, n):
        for i in range(3):
            spread(view, n, i).wait_send()

    def chunk_copies(source, target, ss, sr):
        out, come = [], []
        for k in range(1, C):
            p, o = lax.rem(c + k, C), lax.rem(c + C - k, C)
            out.append(remote(source(p), target(c), ss.at[k], sr.at[k], (p, f, t)))
            come.append(remote(source(o), target(o), ss.at[k], sr.at[k], (o, f, t)))
        return out, come

    def lane(p, n):
        return pl.ds(pl.multiple_of(p * n, n), n)

    heads_out, heads_come = chunk_copies(
        lambda p: heads.at[:, lane(p, po)], lambda o: hq.at[o], hs, hr
    )
    kv_moves = [
        chunk_copies(lambda p, g=g: ksend.at[g, p], lambda o, g=g: kgot.at[g, o], ds_.at[g], dr.at[g])
        for g in range(KH)
    ]
    def outo_of(p):
        return outo.at[lane(p, po)]

    def outa_of(p):
        return outa.at[:, lane(p, pa)]

    def dall_of(q):
        def view(p, half):
            at = lane(blocks[q], cols_o)
            if half is None:
                return dall.at[p, :, at]
            return dall.at[p, pl.ds(pl.multiple_of(half * Rh, Rh), Rh), at]

        return view

    d_moves = [
        row_spread(C, dall_of(q), lambda i, q=q: gs_.at[q, i], lambda i, q=q: gr.at[q, i])
        for q in range(F)
    ]

    def nall_of(p, half):
        if half is None:
            return nall.at[p]
        return nall.at[p, pl.ds(pl.multiple_of(half * Rh, Rh), Rh)]

    def normed_of(half):
        if half is None:
            return normed
        return normed.at[pl.ds(pl.multiple_of(half * Rh, Rh), Rh)]

    n_start, n_wait, n_drain = row_spread(
        C, nall_of, lambda i: ns.at[i], lambda i: nr.at[i], normed_of
    )

    swap_d.start()
    dall[c, at_t] = grad_own[...]
    for q in range(F):
        d_moves[q][0](0)
    for copy in heads_out:
        copy.start()
    n_start(0, 1)
    hq[c] = heads[:, lane(c, po)]
    nall[c] = normed[...]
    swap_d_in.wait_recv()
    for q in range(F):
        d_moves[q][0](1)

    load_o.wait()
    step = min(512, QC)

    def head_grads(i, carry):
        at = lane(i, step)
        dheads[:, at] = outer_cols(dall[c], wbuf[at, pl.ds(0, W)]).astype(BF)
        return carry

    lax.fori_loop(0, QC // step, head_grads, 0)
    load_w = pltpu.make_async_copy(fall.at[:, pl.ds(0, PC)], wbuf, wsem.at[1])
    load_w.start()

    def unturn(values):
        return values * cosf[...] - pltpu.roll(values, HS // 2, 1) * sins[...]

    def norm_grads(values, gain_vec, upstream):
        factor = lax.rsqrt(jnp.mean(values * values, axis=-1, keepdims=True) + EPS)
        out, terms = norm_back(values, factor, gain_vec, upstream)
        return out, jnp.sum(terms, axis=0, keepdims=True)

    gains[...] = jnp.zeros_like(gains)
    def piece_o(b):
        return inner_rows(
            hq[...].reshape(C * R, po), dall[:, :, lane(b, cols_o)].reshape(C * R, cols_o)
        )

    def piece_a(b):
        return inner_rows(
            nall[:, :, lane(b, rows_a)].reshape(C * R, rows_a), rq[...].reshape(C * R, pa)
        )

    pieces = ((piece_o, szo, rzo, outo_of), (piece_a, sza, rza, outa_of))
    end = (f == 0) | (f == F - 1)

    def z_out(n, q):
        b = blocks[q]
        _, send, got, _ = pieces[n]
        return remote(send.at[b], got.at[b], z_s.at[n, q], z_r.at[n, b], (c, f + 1, t))

    def z_down(n, q):
        b = blocks[q]
        slot = jnp.where(b == f - 1, F, b)
        _, send, got, _ = pieces[n]
        return remote(send.at[b], got.at[slot], z_s.at[n, q], z_r.at[n, slot], (c, f - 1, t))

    def z_wait(n, slot):
        _, send, got, _ = pieces[n]
        remote(send.at[0], got.at[slot], z_s.at[n, 0], z_r.at[n, slot], (c, f, t)).wait_recv()

    def z_send(n, q):
        up = blocks[q] > f

        @pl.when(up)
        def _():
            z_out(n, q).start()

        @pl.when(jnp.logical_not(up))
        def _():
            z_down(n, q).start()

    def z_first(n, q):
        fn, send, _, _ = pieces[n]

        @pl.when(end)
        def _():
            send[blocks[q]] = fn(blocks[q]).astype(BF)
            z_send(n, q)

    def o_first(q):
        d_moves[q][1](1, 3, 4)
        if q < F - 1:
            z_first(0, q)

    def z_relay(n, q):
        fn, send, got, _ = pieces[n]

        @pl.when(jnp.logical_not(end))
        def _():
            b = blocks[q]
            z_wait(n, b)
            send[b] = (fn(b) + got[b].astype(FL)).astype(BF)
            z_send(n, q)

    def z_last(n):
        fn, send, got, out = pieces[n]
        send[f] = fn(f).astype(BF)

        @pl.when(f > 0)
        def _():
            z_wait(n, f)
            send[f] = (send[f].astype(FL) + got[f].astype(FL)).astype(BF)

        @pl.when(f < F - 1)
        def _():
            z_wait(n, F)
            out(c)[...] = (send[f].astype(FL) + got[F].astype(FL)).astype(BF)

        @pl.when(f == F - 1)
        def _():
            out(c)[...] = send[f]


    key_step = min(L, 512)

    def one_head(g, h):
        at = lane(h, HS)
        q_head, o_grad = qrot[:, at], dheads[:, at]
        product = o_grad.astype(FL) * heads[:, at].astype(FL)
        delta = jnp.sum(product.T, axis=0, keepdims=True)
        row = lse[pl.ds(h, 1), :]
        q_grad = jnp.zeros((HS, R), FL)
        for j in range(L // key_step):
            ks = pl.ds(j * key_step, key_step)
            scores = outer_cols(kv[g, ks, :], q_head) * (root * LOG2E)
            probs = jnp.exp2(scores + bias[ks, :] - row)
            d_probs = outer_cols(kv[KH + g, ks, :], o_grad)
            d_scores = (probs * (d_probs - delta)).astype(BF)
            dv[ks, :] += jnp.dot(probs.astype(BF), o_grad, preferred_element_type=FL)
            dk[ks, :] += jnp.dot(d_scores, q_head, preferred_element_type=FL)
            q_grad += jnp.dot(keys_t[g, :, ks], d_scores, preferred_element_type=FL)
        q_back, terms = norm_grads(raw[:, at], qgain[...], unturn(q_grad.T * root))
        draw[:, at] = q_back.astype(BF)
        gains[0:1, :] += terms

    def some_heads(g, first, count):
        def step_(i, carry):
            one_head(g, first + i)
            return carry

        lax.fori_loop(0, count, step_, 0)

    raw_due = [-(-min((p + 1) * pa, QC) // HS) for p in range(C)]
    raw_gone = []

    def raw_sends(done):
        for p in range(C):
            if p not in raw_gone and raw_due[p] <= done and (p + 1) * pa <= QC:
                raw_gone.append(p)
                raw_send(p)

    def raw_copy(p):
        return remote(draw.at[:, p * pa : (p + 1) * pa], rq.at[c], rs.at[p], rr.at[c], (p, f, t))

    def raw_come(o):
        return remote(draw.at[:, 0:pa], rq.at[o], rs.at[0], rr.at[o], (o, f, t))

    def raw_send(p):
        @pl.when(c != p)
        def _():
            raw_copy(p).start()

        @pl.when(c == p)
        def _():
            rq[c] = draw[:, p * pa : (p + 1) * pa]

    def d_pass(q):
        if q == 0:
            for p in range(F):
                d_moves[p][1](0)
                d_moves[p][0](2, 3)
        d_moves[q][1](2)
        d_moves[q][0](4)

    halves = 2
    part_heads = G // halves
    beat = 0
    for g in range(KH):
        dk[...] = jnp.zeros_like(dk)
        dv[...] = jnp.zeros_like(dv)
        for half in range(halves):
            some_heads(g, g * G + half * part_heads, part_heads)
            raw_sends(g * G + (half + 1) * part_heads)
            if half == halves - 1:
                for p in range(C):
                    at = pl.ds(p * R, R)
                    ksend[g, p, :, 0:HS] = (dk[at, :] * root).astype(BF)
                    ksend[g, p, :, HS : 2 * HS] = dv[at, :].astype(BF)
                for copy in kv_moves[g][0]:
                    copy.start()
                kgot[g, c] = ksend[g, c]
            if beat < F:
                d_pass(beat)
            if beat == 1:
                n_wait(0)
                n_start(2, 3)
            if beat == 2:
                n_wait(2)
                n_start(4)
            if beat == 0:
                for copy in heads_come:
                    copy.wait_recv()
            elif beat < F:
                o_first(beat - 1)
            beat += 1
    for q in range(beat, F):
        d_pass(q)
        o_first(q - 1)

    o_first(F - 1)
    z_relay(0, 0)

    for g in range(KH):
        for copy in kv_moves[g][1]:
            copy.wait_recv()
        total = kgot[g, 0].astype(FL)
        for p in range(1, C):
            total += kgot[g, p].astype(FL)
        k_cols = slice(QC + g * HS, QC + (g + 1) * HS)
        k_back, terms = norm_grads(raw[:, k_cols], kgain[...], unturn(total[:, :HS]))
        draw[:, k_cols] = k_back.astype(BF)
        draw[:, QC + KC + g * HS : QC + KC + (g + 1) * HS] = total[:, HS:].astype(BF)
        gains[1:2, :] += terms
    for p in range(C):
        if p not in raw_gone:
            raw_send(p)
    z_relay(0, 1)
    load_w.wait()
    width_step = min(512, W)

    def norm_theirs(i, carry):
        at = lane(i, width_step)
        nsend[:, at] = outer_cols(draw[at_u, :], wbuf[at, :]).astype(BF)
        return carry

    lax.fori_loop(0, W // width_step, norm_theirs, 0)
    swap_n.start()

    def norm_ours(i, carry):
        at = lane(i, width_step)
        nown[:, at] = outer_cols(draw[at_t, :], wbuf[at, :])
        return carry

    lax.fori_loop(0, W // width_step, norm_ours, 0)

    for q in range(2, F - 1):
        z_relay(0, q)
    n_wait(1, 3, 4)
    for k in range(1, C):
        raw_come(lax.rem(c + k, C)).wait_recv()
    for q in range(F - 1):
        z_first(1, q)
    z_relay(1, 0)
    z_last(0)
    spread_start(outo_of, 0)

    swap_n.wait_recv()
    upstream = nown[...] + ngot[...].astype(FL)
    values = own_in[...]
    factor = lax.rsqrt(jnp.mean(values * values, axis=-1, keepdims=True) + EPS)
    back, terms = norm_back(values, factor, again[...], upstream)
    gin[...] = resid_in[...] + back
    for b in range(F):
        smx[b, 0 : router.shape[1]] = router[b]
        at = router.shape[1]
        smx[b, at : at + 8] = vec_in[...]
        smx[b, at : at + 1] = jnp.sum(terms, axis=0, keepdims=True)
        smx[b, at + 2 : at + 3, 0:HS] = gains[0:1, :]
        smx[b, at + 2 : at + 3, HS : 2 * HS] = gains[1:2, :]

    def t_copy(k):
        return remote(smx.at[lax.rem(f + k, F)], zgot.at[f], ts.at[k], tr.at[k], columns[k - 1])

    def t_arrival(k):
        b = lax.rem(f + F - k, F)
        return remote(smx.at[b], zgot.at[b], ts.at[k], tr.at[k], columns[k - 1])

    for k in range(1, F):
        t_copy(k).start()
    zgot[f] = smx[f]
    for q in range(1, F - 1):
        z_relay(1, q)
    spread_pass(outo_of, 0)
    for k in range(1, F):
        t_arrival(k).wait_recv()
    total = zgot[0]
    for b in range(1, F):
        total += zgot[b]
    sums[0] = total

    def u_copy(i):
        there = ((sib, f, t), beside, (mate, f, t))[i]
        return remote(sums.at[i], sgot.at[i], us.at[i], ur.at[i], there)

    u_copy(0).start()
    z_last(1)
    spread_start(outa_of, 1)
    for i in range(3):
        u_copy(i).wait_recv()
        total = sums[i] + sgot[i]
        if i < 2:
            sums[i + 1] = total
            u_copy(i + 1).start()
        else:
            small[...] = total
    spread_end(outo_of, 0)
    spread_pass(outa_of, 1)
    spread_end(outa_of, 1)

    for view, n in ((outo_of, 0), (outa_of, 1)):
        spread_sent(view, n)
    for q in range(F):
        d_moves[q][2]()
    n_drain()
    for copy in heads_out:
        copy.wait_send()
    swap_d.wait_send()
    swap_n.wait_send()
    for p in range(C):

        @pl.when(c != p)
        def _():
            raw_copy(p).wait_send()

    for g in range(KH):
        for copy in kv_moves[g][0]:
            copy.wait_send()
    for n in range(2):
        for q in range(F - 1):
            z_out(n, q).wait_send()
    for k in range(1, F):
        t_copy(k).wait_send()
    for i in range(3):
        u_copy(i).wait_send()


def tail(identity, C, F, T, KH, args, D, po):
    grad_own, heads, qrot, kv, keys_t, raw, lse, bias = args[:8]
    qgain = args[10]
    router = args[15]
    R, QC = heads.shape
    W = grad_own.shape[1]
    PC = raw.shape[1]
    L = kv.shape[1]
    HS = qgain.shape[1]
    Rh = grad_own.shape[0]
    S = C * T
    pa = PC // C
    rows_a, cols_o = W // F, W // F
    small_shape = (router.shape[1] + 8, W)
    dma = pltpu.SemaphoreType.DMA
    V = pltpu.VMEM
    return pl.pallas_call(
        functools.partial(tail_body, C, F, T, KH),
        out_shape=(
            jax.ShapeDtypeStruct((Rh, W), FL),
            jax.ShapeDtypeStruct((rows_a, C * pa), BF),
            jax.ShapeDtypeStruct((C * po, cols_o), BF),
            jax.ShapeDtypeStruct(small_shape, FL),
        ),
        in_specs=[VMEM] * 18 + [ANY] * 2,
        out_specs=[VMEM] * 4,
        scratch_shapes=[
            V((W, PC), BF), V((C, R, W), BF), V((C, R, W), BF), V((C, R, po), BF),
            V((C, R, pa), BF), V((R, QC), BF), V((R, PC), BF), V((L, HS), FL), V((L, HS), FL),
            V((KH, C, R, 2 * HS), BF), V((KH, C, R, 2 * HS), BF), V((8, HS), FL),
            V((Rh, W), BF), V((Rh, W), BF), V((Rh, W), FL),
            V((F, rows_a, pa), BF), V((F, po, cols_o), BF),
            V((F + 1, rows_a, pa), BF), V((F + 1, po, cols_o), BF),
            V((F,) + small_shape, FL), V((F,) + small_shape, FL), V((3,) + small_shape, FL),
            V((3,) + small_shape, FL),
            dma((4,)), dma((2,)), dma((2,)), dma((2, 3)), dma((2, 3)), dma((C,)), dma((C,)), dma((5,)), dma((5,)),
            dma((F, 5)), dma((F, 5)),
            dma((KH, C)), dma((KH, C)), dma((C,)), dma((C,)),
            dma((2, F)), dma((2, F + 1)), dma((F,)), dma((F,)), dma((3,)), dma((3,)),
        ],
        compiler_params=params(identity, 62),
    )(*args)


def row_spread(C, view, sent, got, own=None):
    c, f, t = place()
    sib = c + 1 - 2 * lax.rem(c, 2)
    mate, mate_sib = lax.rem(c + 2, C), lax.rem(sib + 2, C)
    to_mate, to_sib, to_side = (mate, f, t), (sib, f, t), (c, f, 1 - t)
    here = (view(c, t), view(c, None))
    if own is not None:
        here = (own(t), own(None))
    leave = (
        (here[0], view(c, t), to_mate), (here[1], view(c, None), to_sib),
        (view(mate, t), view(mate, t), to_side), (view(mate, t), view(mate, t), to_sib),
        (view(mate, 1 - t), view(mate, 1 - t), to_sib),
    )
    arrive = (
        view(mate, t), view(sib, None), view(mate, 1 - t), view(mate_sib, t),
        view(mate_sib, 1 - t),
    )

    def start(*which):
        for i in which:
            remote(leave[i][0], leave[i][1], sent(i), got(i), leave[i][2]).start()

    def wait(*which):
        for i in which:
            remote(arrive[i], arrive[i], sent(i), got(i), to_sib).wait_recv()

    def drain():
        for i in range(5):
            remote(leave[i][0], leave[i][1], sent(i), got(i), leave[i][2]).wait_send()

    return start, wait, drain


def head_body(
    C, F, T, KH,
    hidden, tab, tab_t, again, qgain, kgain, fgain, cosf, sins, bias, wa, wo,
    fall, full, ftab, raw, qrot, kv, keys_t, lse, heads, normed, resid, low, gates,
    fa, fo, vals_t, nsend, ngot, nown,
    loc, zs, zr, ys, yr, ks, kr, ts, tr, cs, cr, xs, xr,
):
    c, f, t = place()
    R, W = hidden.shape
    Rh = tab.shape[0]
    HS = qgain.shape[1]
    PC = raw.shape[1]
    QC = heads.shape[1]
    KC = KH * HS
    L = kv.shape[1]
    G = QC // HS // KH
    root = HS ** (-0.5)
    core = lax.rem(c, 2)
    sib = c + 1 - 2 * core
    mate = lax.rem(c + 2, C)
    mate_sib = lax.rem(sib + 2, C)
    ra, (ro, co) = wa.shape[0], wo.shape
    pa, po = ra // C, ro // C
    ha, ho = pa // 2, po // 2
    x = Exchange(C, F, T)
    x.greet()

    def spot(arr, b, p):
        half = arr % 2
        if arr < 2:
            return fa.at[pl.ds(pl.multiple_of(b * ra + p * pa + half * ha, ha), ha)]
        rows = pl.ds(pl.multiple_of(p * po + half * ho, ho), ho)
        return fo.at[rows, pl.ds(pl.multiple_of(b * co, co), co)]

    def own(arr):
        half = arr % 2
        if arr < 2:
            return wa.at[pl.ds(pl.multiple_of(c * pa + half * ha, ha), ha)]
        return wo.at[pl.ds(pl.multiple_of(c * po + half * ho, ho), ho)]

    def z_copy(arr, s, d):
        b = f - (s - 1) if d == 0 else f + (s - 1)
        source = own(arr) if s == 1 else spot(arr, b, c)
        there = (c, f + 1 if d == 0 else f - 1, t)
        return remote(source, spot(arr, b, c), zs.at[d, s, arr], zr.at[d, s, arr], there)

    def z_sends(s, d):
        b = f - (s - 1) if d == 0 else f + (s - 1)
        return (f + 1 < F) & (b >= 0) if d == 0 else (f > 0) & (b < F)

    def z_gets(s, d):
        return f - s >= 0 if d == 0 else f + s < F

    def came(s, d):
        return f - s if d == 0 else f + s

    def move(arr, s, d, p, sent, got, i, device):
        here = spot(arr, came(s, d), p)
        return remote(here, here, sent.at[d, s, arr, i], got.at[d, s, arr, i], device)

    def z_begin(arr):
        for d in range(2):

            @pl.when(z_sends(1, d))
            def _():
                z_copy(arr, 1, d).start()

    def z_in(arr, s):
        for d in range(2):

            @pl.when(z_gets(s, d))
            def _():
                here = spot(arr, came(s, d), c)
                remote(here, here, zs.at[d, s, arr], zr.at[d, s, arr], (sib, f, t)).wait_recv()
                if s + 1 < F:

                    @pl.when(z_sends(s + 1, d))
                    def _():
                        z_copy(arr, s + 1, d).start()

                move(arr, s, d, c, ys, yr, 0, (mate, f, t)).start()
                move(arr, s, d, c, ks, kr, 0, (sib, f, t)).start()

    def y_in(arr, s):
        for d in range(2):

            @pl.when(z_gets(s, d))
            def _():
                move(arr, s, d, mate, ys, yr, 0, (mate, f, t)).wait_recv()
                move(arr, s, d, mate, ks, kr, 1, (sib, f, t)).start()

    def k_in(arr, s, d):
        move(arr, s, d, sib, ks, kr, 0, (sib, f, t)).wait_recv()
        move(arr, s, d, mate_sib, ks, kr, 1, (sib, f, t)).wait_recv()

    z_begin(0)
    z_begin(1)
    tabs, tabs_come = x.table_copies(tab_t, ftab, ts, tr)
    for copy in tabs:
        copy.start()
    own_a = pltpu.make_async_copy(wa, fa.at[pl.ds(pl.multiple_of(f * ra, ra), ra)], loc.at[0])
    own_o = pltpu.make_async_copy(
        wo, fo.at[:, pl.ds(pl.multiple_of(f * co, co), co)], loc.at[1]
    )
    own_a.start()
    own_o.start()
    ftab[0, f] = tab_t[...]

    inputs = hidden[...].astype(FL)
    normed[...] = norm_rows(inputs, again[...])[0].astype(BF)
    wide = min(512, PC)

    def project(b, first):
        at = pl.ds(pl.multiple_of(b * ra, ra), ra)
        left = normed[:, at]

        def piece(i, carry):
            cols = pl.ds(pl.multiple_of(i * wide, wide), wide)
            part = jnp.dot(left, fa[at, cols], preferred_element_type=FL)
            if first:
                raw[:, cols] = part
            else:
                raw[:, cols] += part
            return carry

        lax.fori_loop(0, PC // wide, piece, 0)

    def project_in(s):
        for d in range(2):

            @pl.when(z_gets(s, d))
            def _():
                k_in(0, s, d)
                k_in(1, s, d)
                project(came(s, d), False)

    own_a.wait()
    project(f, True)
    z_in(0, 1)
    z_in(1, 1)
    for s in range(2, F):
        z_in(0, s)
        y_in(0, s - 1)
        z_in(1, s)
        y_in(1, s - 1)
        if s == F - 2:
            z_begin(2)
            z_begin(3)
        project_in(s - 1)
    y_in(0, F - 1)
    y_in(1, F - 1)
    z_in(2, 1)
    z_in(3, 1)
    project_in(F - 1)

    def turn(values):
        return values * cosf[...] + pltpu.roll(values, HS // 2, 1) * sins[...]

    at_c = pl.ds(pl.multiple_of(c * R, R), R)
    for g in range(KH):
        k_raw = raw[:, QC + g * HS : QC + (g + 1) * HS]
        kv[g, at_c, :] = turn(norm_rows(k_raw, kgain[...])[0]).astype(BF)
        kv[KH + g, at_c, :] = raw[:, QC + KC + g * HS : QC + KC + (g + 1) * HS].astype(BF)

    def kv_move(p, i, device):
        here = kv.at[:, pl.ds(pl.multiple_of(p * R, R), R), :]
        return remote(here, here, cs.at[i], cr.at[i], device)

    kv_move(c, 0, (mate, f, t)).start()
    kv_move(c, 1, (sib, f, t)).start()

    def query(i, carry):
        at = pl.ds(pl.multiple_of(i * HS, HS), HS)
        qrot[:, at] = turn(norm_rows(raw[:, at], qgain[...])[0]).astype(BF)
        return carry

    lax.fori_loop(0, QC // HS, query, 0)
    save_a = pltpu.make_async_copy(fa, fall, loc.at[2])
    save_a.start()
    y_in(2, 1)
    y_in(3, 1)
    z_in(2, 2)
    kv_move(mate, 0, (mate, f, t)).wait_recv()
    kv_move(mate, 2, (sib, f, t)).start()
    kv_move(sib, 1, (sib, f, t)).wait_recv()
    kv_move(mate_sib, 2, (sib, f, t)).wait_recv()
    for g in range(KH):
        keys_t[g] = kv[g].astype(FL).T.astype(BF)
        vals_t[g] = kv[KH + g].astype(FL).T.astype(BF)

    def some_heads(g, first, count):
        def one_head(i, carry):
            h = first + i
            at = pl.ds(pl.multiple_of(h * HS, HS), HS)
            weight = jnp.exp2(outer_cols(kv[g], qrot[:, at]) * (root * LOG2E) + bias[...])
            total = jnp.sum(weight, axis=0, keepdims=True)
            lse[pl.ds(h, 1), :] = jnp.log2(total)
            probs = (weight * (1.0 / total)).astype(BF)
            heads[:, at] = jnp.dot(vals_t[g], probs, preferred_element_type=FL).T.astype(BF)
            return carry

        lax.fori_loop(0, count, one_head, 0)

    at_t = pl.ds(pl.multiple_of(t * Rh, Rh), Rh)
    at_u = pl.ds(pl.multiple_of((1 - t) * Rh, Rh), Rh)

    def swap(b):
        cols = pl.ds(pl.multiple_of(b * co, co), co)
        return remote(nsend.at[:, cols], ngot.at[:, cols], xs.at[b], xr.at[b], (c, f, 1 - t))

    def output(b):
        cols = pl.ds(pl.multiple_of(b * co, co), co)
        nsend[:, cols] = jnp.dot(
            heads[at_u, :], fo[:, cols], preferred_element_type=FL
        ).astype(BF)
        swap(b).start()
        nown[:, cols] = jnp.dot(heads[at_t, :], fo[:, cols], preferred_element_type=FL)

    def output_in(s):
        for d in range(2):

            @pl.when(z_gets(s, d))
            def _():
                k_in(2, s, d)
                k_in(3, s, d)
                output(came(s, d))

    events = [[(z_in, 3, 2)], [(y_in, 2, 2)], [(y_in, 3, 2)]]
    half = G // 2
    for i in range(2 * KH):
        some_heads(i // 2, i * half, half)
        for event, arr, s in events[i] if i < len(events) else ():
            event(arr, s)
    own_o.wait()
    output(f)
    output_in(1)
    for s in range(3, F):
        z_in(2, s)
        z_in(3, s)
        output_in(s - 1)
        y_in(2, s)
        y_in(3, s)
    save_o = pltpu.make_async_copy(fo, full, loc.at[3])
    output_in(F - 1)
    save_o.start()
    for b in range(F):
        swap(b).wait_recv()
    total = hidden[at_t, :].astype(FL) + (nown[...] + ngot[...].astype(FL))
    resid[...] = total
    ffn_low = norm_rows(total, fgain[...])[0].astype(BF)
    low[...] = ffn_low
    logits = jnp.dot(ffn_low, fa[:, PC:], preferred_element_type=FL)
    named = tab[...] >= 0.0
    masked = jnp.where(named, logits, MASKED)
    shifted = jnp.where(
        named, jnp.exp(masked - jnp.max(masked, axis=-1, keepdims=True)), 0.0
    )
    gates[...] = shifted / jnp.sum(shifted, axis=-1, keepdims=True)

    save_a.wait()
    save_o.wait()
    for b in range(F):
        swap(b).wait_send()
    for copy in tabs:
        copy.wait_send()
    for copy in tabs_come:
        copy.wait_recv()
    kv_move(c, 0, (mate, f, t)).wait_send()
    kv_move(c, 1, (sib, f, t)).wait_send()
    kv_move(mate, 2, (sib, f, t)).wait_send()
    for s in range(1, F):
        for d in range(2):

            @pl.when(z_sends(s, d))
            def _():
                for arr in range(4):
                    z_copy(arr, s, d).wait_send()

            @pl.when(z_gets(s, d))
            def _():
                for arr in range(4):
                    move(arr, s, d, c, ys, yr, 0, (mate, f, t)).wait_send()
                    move(arr, s, d, c, ks, kr, 0, (sib, f, t)).wait_send()
                    move(arr, s, d, mate, ks, kr, 1, (sib, f, t)).wait_send()


def head(identity, C, F, T, KH, PC, L, args):
    hidden, tab, tab_t, qgain, wa, wo = args[0], args[1], args[2], args[4], args[10], args[11]
    R, W = hidden.shape
    Rh, lanes = tab.shape
    HS = qgain.shape[1]
    ra, ca = wa.shape
    QC, co = wo.shape
    dma = pltpu.SemaphoreType.DMA
    V = pltpu.VMEM
    shape = jax.ShapeDtypeStruct
    return pl.pallas_call(
        functools.partial(head_body, C, F, T, KH),
        out_shape=(
            shape((F * ra, ca), BF), shape((QC, F * co), BF), shape((3, F) + tab_t.shape, FL),
            shape((R, PC), FL), shape((R, QC), BF), shape((2 * KH, L, HS), BF),
            shape((KH, HS, L), BF), shape((QC // HS, R), FL), shape((R, QC), BF),
            shape((R, W), BF), shape((Rh, W), FL), shape((Rh, W), BF),
            shape((Rh, lanes), FL),
        ),
        in_specs=[VMEM] * 10 + [ANY] * 2,
        out_specs=[ANY] * 2 + [VMEM] * 11,
        scratch_shapes=[
            V((F * ra, ca), BF), V((QC, F * co), BF), V((KH, HS, L), BF),
            V((Rh, W), BF), V((Rh, W), BF), V((Rh, W), FL),
            dma((4,)), dma((2, F, 4)), dma((2, F, 4)), dma((2, F, 4, 1)), dma((2, F, 4, 1)),
            dma((2, F, 4, 2)), dma((2, F, 4, 2)), dma((3, F)), dma((3, F)), dma((3,)),
            dma((3,)),
            dma((F,)), dma((F,)),
        ],
        compiler_params=params(identity, 60),
    )(*args)


def block_order(F):
    if F == 4:
        return [[0, 1, 3, 2], [1, 2, 3, 0], [2, 1, 0, 3], [3, 2, 0, 1]]
    return [[(f + k) % F for k in range(F)] for f in range(F)]


class Exchange:
    def __init__(self, C, F, T):
        c, f, t = place()
        self.C, self.F, self.T, self.c, self.f, self.t = C, F, T, c, f, t
        self.chip, self.core = lax.div(c, 2), lax.rem(c, 2)
        self.mate = lax.rem(c + 2, C)
        self.unit = self.core * T + t
        table = block_order(F)
        self.blocks = []
        for k in range(F):
            value = jnp.int32(table[0][k])
            for g in range(1, F):
                value = jnp.where(f == g, table[g][k], value)
            self.blocks.append(value)
        self.side = ((c, f, 1 - t), (self.mate, f, t))
        self.own_at = (t, self.chip)
        self.self_at = (c, self.unit)

    def columns(self):
        c, f, t, F = self.c, self.f, self.t, self.F
        own = [(c, lax.rem(f + k, F), t) for k in range(1, F)]
        beside = [(c, lax.rem(f + k, F), 1 - t) for k in range(F)]
        across = [(self.mate, lax.rem(f + k, F), t) for k in range(F)]
        return own, beside, across

    def greet(self):
        c, f, t, C = self.c, self.f, self.t, self.C
        own, beside, across = self.columns()
        rest = [(lax.rem(c + j, C), f, 1 - t) for j in range(1, C)]
        rest += [(lax.rem(c + j, C), f, t) for j in (1, 3)]
        greet(own + beside + across + rest)

    def table_copies(self, source, tables, sent, got):
        out, come = [], []
        for i, column in enumerate(self.columns()):
            for n, device in enumerate(column):
                k = n + 1 if i == 0 else n
                out.append(remote(source, tables.at[i, self.f], sent.at[i, k], got.at[i, k], device))
                origin = lax.rem(self.f + self.F - k, self.F)
                come.append(
                    remote(source, tables.at[i, origin], sent.at[i, k], got.at[i, k], device)
                )
        return out, come

    def target(self, group, j):
        if group == 0:
            p = lax.rem(self.c + j, 4)
            return p, (p, self.f, self.t)
        p = lax.rem(self.unit + j, 4)
        return p, (self.chip * 2 + lax.div(p, self.T), self.f, lax.rem(p, self.T))

    def expert_id(self, group, p):
        if group == 0:
            return (p * self.F + self.f) * self.T + self.t
        chip_core = self.chip * 2 + lax.div(p, self.T)
        return (chip_core * self.F + self.f) * self.T + lax.rem(p, self.T)

    def origin_view(self, buf, group, b, p, H):
        if group == 0:
            first = pl.multiple_of(lax.rem(p, 2) * self.T, self.T)
            return buf.at[b, lax.div(p, 2), pl.ds(first, self.T), :, pl.ds(0, H)]
        return buf.at[b, :, p, :, pl.ds(H, H)]

    def table_of(self, group, q):
        own = q == self.own_at[group]
        return jnp.where(own, 0, 1 + group)

    def one_hot(self, ranks, group, b, q, p, K):
        row = ranks[self.table_of(group, q), b, pl.ds(self.expert_id(group, p), 1), :]
        slots = lax.broadcasted_iota(jnp.int32, (K, row.shape[1]), 0).astype(FL)
        return slots == row

    def gate_row(self, gates, group, b, q, p):
        return gates[self.table_of(group, q), b, pl.ds(self.expert_id(group, p), 1), :]

    def z_sends(self, s, d):
        b = self.f - (s - 1) if d == 0 else self.f + (s - 1)
        if d == 0:
            return (self.f + 1 < self.F) & (b >= 0)
        return (self.f > 0) & (b < self.F)

    def z_gets(self, s, d):
        return self.f - s >= 0 if d == 0 else self.f + s < self.F

    def z_copy(self, zbuf, zs, zr, s, d):
        b = self.f - (s - 1) if d == 0 else self.f + (s - 1)
        there = (self.c, self.f + 1 if d == 0 else self.f - 1, self.t)
        return remote(zbuf.at[b], zbuf.at[b], zs.at[d, s], zr.at[d, s], there)

    def z_begin(self, zbuf, zs, zr):
        for d in range(2):

            @pl.when(self.z_sends(1, d))
            def _():
                self.z_copy(zbuf, zs, zr, 1, d).start()

    def z_relay(self, zbuf, zs, zr, s):
        for d in range(2):

            @pl.when(self.z_gets(s, d))
            def _():
                b = self.f - s if d == 0 else self.f + s
                remote(
                    zbuf.at[b], zbuf.at[b], zs.at[d, s], zr.at[d, s], self.side[0]
                ).wait_recv()
                if s + 1 < self.F:

                    @pl.when(self.z_sends(s + 1, d))
                    def _():
                        self.z_copy(zbuf, zs, zr, s + 1, d).start()

    def z_drain(self, zbuf, zs, zr):
        for s in range(1, self.F):
            for d in range(2):

                @pl.when(self.z_sends(s, d))
                def _():
                    self.z_copy(zbuf, zs, zr, s, d).wait_send()


def moe_forward_body(
    C, F, T,
    rows, gate_t, ranks, w_in, w_out,
    xr, got0, got1, pre, mixed, part, gates,
    zbuf, dense, st0, st1, xs, gt0, gt1, wi, wo, prebuf, own_part, cross, pstage, zpart,
    loc, zs, zr, es, er, ss, sr, rs, rr, cs, cr, ps, pr, ts, tr, xl, gl, pl_,
):
    x = Exchange(C, F, T)
    c, f, t = x.c, x.f, x.t
    K, W = xr.shape[3], xr.shape[4]
    S, H = C * T, W // 2
    FFW = w_out.shape[0]
    stages, gots, keeps = (st0, st1), (gt0, gt1), (got0, got1)
    x.greet()
    zbuf[f] = rows[...]
    x.z_begin(zbuf, zs, zr)

    def dense_copy(k, g):
        b = x.blocks[k]
        return remote(
            zbuf.at[b, :, pl.ds(g * H, H)], dense.at[g, b], es.at[g, k], er.at[g, k], x.side[g]
        )

    def send_dense(k):
        for g in range(2):
            dense_copy(k, g).start()

    send_dense(0)
    load_i = pltpu.make_async_copy(w_in, wi, loc.at[0])
    load_o = pltpu.make_async_copy(w_out, wo, loc.at[1])
    load_i.start()
    load_o.start()
    g_out, g_come = x.table_copies(gate_t, gates, ts, tr)
    for copy in g_out:
        copy.start()
    gates[0, f] = gate_t[...]

    def sparse(k, g, j, arriving):
        b = x.blocks[k]
        p, device = x.target(g, 4 - j if arriving else j)
        index = p if arriving else x.self_at[g]
        return remote(
            stages[g].at[b, p], x.origin_view(xs, g, b, index, H),
            ss.at[g, k, j], sr.at[g, k, j], device,
        )

    def back(k, g, j, arriving):
        b = x.blocks[k]
        p, device = x.target(g, 4 - j if arriving else j)
        index = p if arriving else x.self_at[g]
        return remote(
            stages[g].at[b, p], gots[g].at[b, :, index], rs.at[g, k, j], rr.at[g, k, j], device
        )

    def source(k, g, q):
        b = x.blocks[k]
        own = zbuf[b, :, g * H : (g + 1) * H]
        return jnp.where(q == x.own_at[g], own, dense[g, b])

    def dispatch_rows(k):
        b = x.blocks[k]
        for g in range(2):
            dense_copy(k, g).wait_recv()
        for j in (2, 1, 3, 0):
            for g in range(2):
                p, _ = x.target(g, j)
                for q in range(2):
                    hot = x.one_hot(ranks, g, b, q, p, K).astype(BF)
                    stages[g][b, p, q] = jnp.dot(
                        hot, source(k, g, q), preferred_element_type=FL
                    ).astype(BF)
                if j:
                    sparse(k, g, j, False).start()
                else:
                    x.origin_view(xs, g, b, p, H)[...] = stages[g][b, p]

    def keep_x(k):
        return pltpu.make_async_copy(xs.at[x.blocks[k]], xr.at[x.blocks[k]], xl.at[k])

    def keep_got(k, g):
        b = x.blocks[k]
        return pltpu.make_async_copy(gots[g].at[b], keeps[g].at[b], gl.at[g, k])

    def keep_pre(k):
        return pltpu.make_async_copy(prebuf, pre.at[x.blocks[k]], pl_.at[k])

    def expert(k):
        b = x.blocks[k]
        for j in range(1, 4):
            for g in range(2):
                sparse(k, g, j, True).wait_recv()
        if k == 0:
            load_i.wait()
        else:
            keep_pre(k - 1).wait()
        keep_x(k).start()
        left = xs[b].reshape(S * K, W)
        tile = 256
        for i in range(FFW // tile):
            at = slice(i * tile, (i + 1) * tile)
            up_at = slice(FFW + i * tile, FFW + (i + 1) * tile)
            gate_pre = jnp.dot(left, wi[:, at], preferred_element_type=FL)
            up_pre = jnp.dot(left, wi[:, up_at], preferred_element_type=FL)
            prebuf[:, at] = gate_pre
            prebuf[:, up_at] = up_pre
            mixed[b, :, at] = (gate_pre * jax.nn.sigmoid(gate_pre) * up_pre).astype(BF)
        keep_pre(k).start()
        if k == 0:
            load_o.wait()
        for j in range(1, 4):
            for g in range(2):
                sparse(k, g, j, False).wait_send()
        send_back(k, mixed[b], lambda at: wo[:, at], False)

    def send_back(k, left, right, turned):
        b = x.blocks[k]
        tile = min(512, H)
        for i in range(W // tile):
            at = slice(i * tile, (i + 1) * tile)
            y = jnp.dot(left, right(at), preferred_element_type=FL).astype(BF)
            y = y.reshape(2, 4, K, tile)
            for chip in range(2):
                for unit in range(4):
                    if i * tile < H:
                        st0[b, chip * 2 + unit // T, unit % T, :, at] = y[chip, unit]
                    else:
                        cols = slice(i * tile - H, (i + 1) * tile - H)
                        st1[b, unit, chip, :, cols] = y[chip, unit]
            if (i + 1) * tile in (H, W):
                g = 0 if (i + 1) * tile == H else 1
                for j in (2, 1, 3):
                    back(k, g, j, False).start()
                me = x.self_at[g]
                for q in range(2):
                    gots[g][b, q, me] = stages[g][b, me, q]

    def cross_copy(k, g):
        b = x.blocks[k]
        return remote(pstage.at[b, :, pl.ds(g * H, H)], cross.at[g, b], cs.at[g, k], cr.at[g, k], x.side[g])

    def gather(k):
        b = x.blocks[k]
        for g in range(2):
            for j in range(1, 4):
                back(k, g, j, True).wait_recv()
            keep_got(k, g).start()
            for near in range(2):
                q = x.own_at[g] if near else 1 - x.own_at[g]
                scaled = []
                for p in range(4):
                    hot = x.one_hot(ranks, g, b, q, p, K)
                    scaled.append(jnp.where(hot, x.gate_row(gates, g, b, q, p), 0.0))
                scaled = jnp.concatenate(scaled, axis=0)
                high = scaled.astype(BF)
                low = (scaled - high.astype(FL)).astype(BF)
                tile = min(512, H)
                for i in range(H // tile):
                    at = slice(i * tile, (i + 1) * tile)
                    out_at = slice(g * H + i * tile, g * H + (i + 1) * tile)
                    y = gots[g][b, q, :, :, at].reshape(4 * K, tile)
                    total = inner_rows(high, y) + inner_rows(low, y)
                    if near:
                        own_part[k % 2, :, out_at] = total
                    else:
                        pstage[b, :, out_at] = total.astype(BF)
                if not near:
                    cross_copy(k, g).start()

    def part_copy(k):
        b = x.blocks[k]
        return remote(pstage.at[b], zpart.at[f], ps.at[b], pr.at[f], (c, b, t))

    def part_arrival(k):
        b = x.blocks[k]
        return remote(pstage.at[b], zpart.at[b], ps.at[b], pr.at[b], (c, b, t))

    def finish(k):
        b = x.blocks[k]
        for g in range(2):
            cross_copy(k, g).wait_recv()
            cross_copy(k, g).wait_send()
            at = slice(g * H, (g + 1) * H)
            total = own_part[k % 2, :, at] + cross[g, b].astype(FL)
            if k:
                pstage[b, :, at] = total.astype(BF)
            else:
                part[:, at] = total
        if k:
            part_copy(k).start()

    dispatch_rows(0)
    x.z_relay(zbuf, zs, zr, 1)
    send_dense(1)
    expert(0)
    dispatch_rows(1)
    for s in range(2, F):
        x.z_relay(zbuf, zs, zr, s)
    for k in range(2, F):
        send_dense(k)
    for copy in g_out:
        copy.wait_send()
    for copy in g_come:
        copy.wait_recv()
    expert(1)
    dispatch_rows(2)
    gather(0)
    dispatch_rows(3)
    expert(2)
    gather(1)
    finish(0)
    expert(3)
    finish(1)
    gather(2)
    gather(3)
    finish(2)
    finish(3)
    for k in range(1, F):
        part_arrival(k).wait_recv()
        part[...] += zpart[x.blocks[k]].astype(FL)
    x.z_drain(zbuf, zs, zr)
    keep_pre(F - 1).wait()
    for k in range(F):
        keep_x(k).wait()
        if k:
            part_copy(k).wait_send()
        for g in range(2):
            keep_got(k, g).wait()
            dense_copy(k, g).wait_send()
            for j in range(1, 4):
                back(k, g, j, False).wait_send()


def moe_forward(identity, C, F, T, K, rows, gate_t, ranks, w_in, w_out):
    S = C * T
    R, W = rows.shape
    H = W // 2
    H2, FFW = w_in.shape[1], w_out.shape[0]
    dma = pltpu.SemaphoreType.DMA
    V = pltpu.VMEM
    shape = jax.ShapeDtypeStruct
    return pl.pallas_call(
        functools.partial(moe_forward_body, C, F, T),
        out_shape=(
            shape((F, 2, 4, K, W), BF), shape((F, 2, 4, K, H), BF), shape((F, 2, 4, K, H), BF),
            shape((F, S * K, H2), FL), shape((F, S * K, FFW), BF), shape((R, W), FL),
            shape((3, F) + gate_t.shape, FL),
        ),
        in_specs=[VMEM] * 3 + [ANY] * 2,
        out_specs=[ANY] * 4 + [VMEM] * 3,
        scratch_shapes=[
            V((F, R, W), BF), V((2, F, R, H), BF), V((F, 4, 2, K, H), BF), V((F, 4, 2, K, H), BF),
            V((F, 2, 4, K, W), BF), V((F, 2, 4, K, H), BF), V((F, 2, 4, K, H), BF),
            V((W, H2), BF), V((FFW, W), BF), V((S * K, H2), FL), V((2, R, W), FL),
            V((2, F, R, H), BF), V((F, R, W), BF), V((F, R, W), BF),
            dma((2,)), dma((2, F)), dma((2, F)), dma((2, F)), dma((2, F)), dma((2, F, 4)),
            dma((2, F, 4)), dma((2, F, 4)), dma((2, F, 4)), dma((2, F)), dma((2, F)), dma((F,)),
            dma((F,)), dma((3, F)), dma((3, F)), dma((F,)), dma((2, F)), dma((F,)),
        ],
        compiler_params=params(identity, 61),
    )(rows, gate_t, ranks, w_in, w_out)


def moe_backward_body(
    C, F, T,
    gates, ranks, mixed, rows, w_in, w_out, xr, got0, got1, pre,
    part, grad_in, grad_out, dgr0, dgr1,
    zbuf, dense, st0, st1, xs, gt0, gt1, ysx, wi, wo, dpre, prebuf, tiles, own_part, cross,
    pstage, zpart, dgs,
    loc, zs, zr, es, er, ss, sr, rs, rr, cs, cr, ps, pr, ds_, dr, pl_, tl,
):
    x = Exchange(C, F, T)
    c, f, t = x.c, x.f, x.t
    K, W = xr.shape[3], xr.shape[4]
    S, H = C * T, W // 2
    FFW = w_out.shape[0]
    R = rows.shape[0]
    stages, gots, gate_in = (st0, st1), (gt0, gt1), (dgr0, dgr1)
    load_r = pltpu.make_async_copy(rows, zbuf.at[f], loc.at[5])
    load_r.start()
    x.greet()
    load_r.wait()
    x.z_begin(zbuf, zs, zr)

    def dense_copy(k, g):
        b = x.blocks[k]
        return remote(
            zbuf.at[b, :, pl.ds(g * H, H)], dense.at[g, b], es.at[g, k], er.at[g, k], x.side[g]
        )

    def send_dense(k):
        for g in range(2):
            dense_copy(k, g).start()

    send_dense(0)
    load_y = [
        pltpu.make_async_copy(got, ysx.at[:, :, :, :, pl.ds(g * H, H)], loc.at[g])
        for g, got in enumerate((got0, got1))
    ]
    load_o = pltpu.make_async_copy(w_out, wo, loc.at[2])
    load_i = pltpu.make_async_copy(w_in, wi, loc.at[3])
    load_x = pltpu.make_async_copy(xr, ysx, loc.at[4])
    for copy in load_y:
        copy.start()
    load_o.start()
    load_i.start()

    def pre_load(k):
        return pltpu.make_async_copy(pre.at[x.blocks[k]], prebuf, pl_.at[k])

    pre_load(0).start()

    def sparse(k, g, j, arriving):
        b = x.blocks[k]
        p, device = x.target(g, 4 - j if arriving else j)
        index = p if arriving else x.self_at[g]
        return remote(
            stages[g].at[b, p], x.origin_view(xs, g, b, index, H),
            ss.at[g, k, j], sr.at[g, k, j], device,
        )

    def back(k, g, j, arriving):
        b = x.blocks[k]
        p, device = x.target(g, 4 - j if arriving else j)
        index = p if arriving else x.self_at[g]
        return remote(
            stages[g].at[b, p], gots[g].at[b, :, index], rs.at[g, k, j], rr.at[g, k, j], device
        )

    def source(k, g, q):
        b = x.blocks[k]
        own = zbuf[b, :, g * H : (g + 1) * H]
        return jnp.where(q == x.own_at[g], own, dense[g, b])

    def dispatch_rows(k):
        b = x.blocks[k]
        for g in range(2):
            dense_copy(k, g).wait_recv()
        for j in (2, 1, 3, 0):
            for g in range(2):
                p, _ = x.target(g, j)
                for q in range(2):
                    hot = x.one_hot(ranks, g, b, q, p, K)
                    gate = jnp.sum(
                        jnp.where(hot, x.gate_row(gates, g, b, q, p), 0.0), axis=1, keepdims=True
                    )
                    picked = jnp.dot(
                        hot.astype(BF), source(k, g, q), preferred_element_type=FL
                    )
                    stages[g][b, p, q] = (picked * gate).astype(BF)
                if j:
                    sparse(k, g, j, False).start()
                else:
                    x.origin_view(xs, g, b, p, H)[...] = stages[g][b, p]

    lanes = lax.broadcasted_iota(jnp.int32, (K, R), 1)

    def gate_copy(k, g, near):
        b = x.blocks[k]
        q = x.own_at[g] if near else 1 - x.own_at[g]
        side = (c, b, 1 - t) if g == 0 else (x.mate, b, t)
        device = (c, b, t) if near else side
        return remote(
            dgs.at[g, q, b], gate_in[g].at[x.own_at[g], f],
            ds_.at[g, 1 - near, b], dr.at[g, 1 - near, f], device,
        )

    def gate_arrival(k, g, near):
        b = x.blocks[k]
        q = x.own_at[g] if near else 1 - x.own_at[g]
        return remote(
            dgs.at[g, q, b], gate_in[g].at[q, b],
            ds_.at[g, 1 - near, b], dr.at[g, 1 - near, b], x.side[g],
        )

    def gate_grads(k):
        b = x.blocks[k]
        for g in range(2):
            for near in range(2):
                q = x.own_at[g] if near else 1 - x.own_at[g]
                total = jnp.zeros((R, R), FL)
                rows_q = zbuf[b, :, g * H : (g + 1) * H] if near else dense[g, b]
                for p in range(4):
                    hot = x.one_hot(ranks, g, b, q, p, K).astype(BF)
                    picked = jnp.dot(hot, rows_q, preferred_element_type=FL)
                    y = ysx[b, q, p, :, g * H : (g + 1) * H].astype(FL)
                    dots = jnp.sum(picked * y, axis=1, keepdims=True)
                    spread = jnp.where(lanes == p, dots, 0.0)
                    high = spread.astype(BF)
                    low = (spread - high.astype(FL)).astype(BF)
                    total += inner_rows(high, hot) + inner_rows(low, hot)
                if near and k == 0:
                    gate_in[g][q, b] = total[:8, :]
                else:
                    dgs[g, q, b] = total[:8, :]
                    gate_copy(k, g, near).start()

    def expert(k):
        b = x.blocks[k]
        for j in range(1, 4):
            for g in range(2):
                sparse(k, g, j, True).wait_recv()
        if k == 0:
            load_o.wait()
        left = xs[b].reshape(S * K, W)
        pre_load(k).wait()
        tile = 256
        for i in range(FFW // tile):
            at = slice(i * tile, (i + 1) * tile)
            up_at = slice(FFW + i * tile, FFW + (i + 1) * tile)
            grad_mixed = outer_cols(left, wo[at, :])
            gate_pre = prebuf[:, at]
            up_pre = prebuf[:, up_at]
            sigmoid = jax.nn.sigmoid(gate_pre)
            dpre[b, :, at] = (
                grad_mixed * up_pre * (sigmoid * (1.0 + gate_pre * (1.0 - sigmoid)))
            ).astype(BF)
            dpre[b, :, up_at] = (grad_mixed * (gate_pre * sigmoid)).astype(BF)
        if k + 1 < F:
            pre_load(k + 1).start()
        if k == 0:
            load_i.wait()
        for j in range(1, 4):
            for g in range(2):
                sparse(k, g, j, False).wait_send()
        d = dpre[b]
        tile = min(512, H)
        for i in range(W // tile):
            at = slice(i * tile, (i + 1) * tile)
            y = outer_cols(d, wi[at, :]).astype(BF).reshape(2, 4, K, tile)
            for chip in range(2):
                for unit in range(4):
                    if i * tile < H:
                        st0[b, chip * 2 + unit // T, unit % T, :, at] = y[chip, unit]
                    else:
                        cols = slice(i * tile - H, (i + 1) * tile - H)
                        st1[b, unit, chip, :, cols] = y[chip, unit]
            if (i + 1) * tile in (H, W):
                g = 0 if (i + 1) * tile == H else 1
                for j in (2, 1, 3):
                    back(k, g, j, False).start()
                me = x.self_at[g]
                for q in range(2):
                    gots[g][b, q, me] = stages[g][b, me, q]

    def cross_copy(k, g):
        b = x.blocks[k]
        return remote(pstage.at[b, :, pl.ds(g * H, H)], cross.at[g, b], cs.at[g, k], cr.at[g, k], x.side[g])

    def gather(k):
        b = x.blocks[k]
        for g in range(2):
            for j in range(1, 4):
                back(k, g, j, True).wait_recv()
            for near in range(2):
                q = x.own_at[g] if near else 1 - x.own_at[g]
                hot = jnp.concatenate(
                    [x.one_hot(ranks, g, b, q, p, K).astype(FL) for p in range(4)], axis=0
                ).astype(BF)
                tile = min(512, H)
                for i in range(H // tile):
                    at = slice(i * tile, (i + 1) * tile)
                    out_at = slice(g * H + i * tile, g * H + (i + 1) * tile)
                    total = inner_rows(hot, gots[g][b, q, :, :, at].reshape(4 * K, tile))
                    if near:
                        own_part[:, out_at] = total
                    else:
                        pstage[b, :, out_at] = total.astype(BF)
                if not near:
                    cross_copy(k, g).start()

    def part_copy(k):
        b = x.blocks[k]
        return remote(pstage.at[b], zpart.at[f], ps.at[b], pr.at[f], (c, b, t))

    def part_arrival(k):
        b = x.blocks[k]
        return remote(pstage.at[b], zpart.at[b], ps.at[b], pr.at[b], (c, b, t))

    def finish(k):
        b = x.blocks[k]
        for g in range(2):
            cross_copy(k, g).wait_recv()
            cross_copy(k, g).wait_send()
            at = slice(g * H, (g + 1) * H)
            total = own_part[:, at] + cross[g, b].astype(FL)
            if k:
                pstage[b, :, at] = total.astype(BF)
            else:
                part[:, at] = total
        if k:
            part_copy(k).start()

    made = []

    def weight_tile(left, right, target, at):
        width = right.shape[1] // 2
        for half in range(2):
            n = len(made)
            if n >= 2:
                made[n - 2].wait()
            cols = slice(half * width, (half + 1) * width)
            tiles[n % 2, :, 0:width] = inner_rows(left, right[:, cols]).astype(BF)
            copy = pltpu.make_async_copy(
                tiles.at[n % 2, :, pl.ds(0, width)],
                target.at[pl.ds(at, 256), pl.ds(half * width, width)],
                tl.at[n],
            )
            copy.start()
            made.append(copy)

    def out_grads(first, last):
        g = xs[...].reshape(F * S * K, W)
        for i in range(first, last):
            left = mixed[:, :, i * 256 : (i + 1) * 256].reshape(F * S * K, 256)
            weight_tile(left, g, grad_out, i * 256)

    def in_grads(first, last):
        d = dpre[...].reshape(F * S * K, 2 * FFW)
        for i in range(first, last):
            left = ysx[:, :, :, :, i * 256 : (i + 1) * 256].reshape(F * S * K, 256)
            weight_tile(left, d, grad_in, i * 256)

    dispatch_rows(0)
    x.z_relay(zbuf, zs, zr, 1)
    send_dense(1)
    for copy in load_y:
        copy.wait()
    gate_grads(0)
    expert(0)
    dispatch_rows(1)
    for s in range(2, F):
        x.z_relay(zbuf, zs, zr, s)
    for k in range(2, F):
        send_dense(k)
    gate_grads(1)
    expert(1)
    dispatch_rows(2)
    gather(0)
    dispatch_rows(3)
    gate_grads(2)
    expert(2)
    finish(0)
    gather(1)
    gate_grads(3)
    load_x.start()
    expert(3)
    finish(1)
    gather(2)
    out_grads(0, FFW // 256)
    finish(2)
    gather(3)
    load_x.wait()
    in_grads(0, 1)
    finish(3)
    in_grads(1, W // 256)
    for k in range(1, F):
        part_arrival(k).wait_recv()
        part[...] += zpart[x.blocks[k]].astype(FL)
    for k in range(F):
        for g in range(2):
            for near in range(2):
                if k or not near:
                    gate_arrival(k, g, near).wait_recv()
                    gate_copy(k, g, near).wait_send()
    for copy in made[-2:]:
        copy.wait()
    x.z_drain(zbuf, zs, zr)
    for k in range(F):
        if k:
            part_copy(k).wait_send()
        for g in range(2):
            dense_copy(k, g).wait_send()
            for j in range(1, 4):
                back(k, g, j, False).wait_send()


def moe_backward(identity, C, F, T, rows, gates, ranks, mixed, w_in, w_out, xr, got0, got1, pre):
    S = C * T
    K = xr.shape[3]
    R, W = rows.shape
    H = W // 2
    H2, FFW = w_in.shape[1], w_out.shape[0]
    dma = pltpu.SemaphoreType.DMA
    V = pltpu.VMEM
    shape = jax.ShapeDtypeStruct
    return pl.pallas_call(
        functools.partial(moe_backward_body, C, F, T),
        out_shape=(
            shape((R, W), FL), shape((W, H2), BF), shape((FFW, W), BF),
            shape((2, F, 8, R), FL), shape((2, F, 8, R), FL),
        ),
        in_specs=[VMEM] * 3 + [ANY] * 7,
        out_specs=[VMEM, ANY, ANY, VMEM, VMEM],
        scratch_shapes=[
            V((F, R, W), BF), V((2, F, R, H), BF), V((F, 4, 2, K, H), BF), V((F, 4, 2, K, H), BF),
            V((F, 2, 4, K, W), BF), V((F, 2, 4, K, H), BF), V((F, 2, 4, K, H), BF),
            V((F, 2, 4, K, W), BF), V((W, H2), BF), V((FFW, W), BF), V((F, S * K, H2), BF),
            V((S * K, H2), FL), V((2, 256, max(W, H2) // 2), BF), V((R, W), FL),
            V((2, F, R, H), BF), V((F, R, W), BF), V((F, R, W), BF), V((2, 2, F, 8, R), FL),
            dma((6,)), dma((2, F)), dma((2, F)), dma((2, F)), dma((2, F)), dma((2, F, 4)),
            dma((2, F, 4)), dma((2, F, 4)), dma((2, F, 4)), dma((2, F)), dma((2, F)), dma((F,)),
            dma((F,)), dma((2, 2, F)), dma((2, 2, F)), dma((F,)),
            dma((2 * (FFW // 256 + W // 256),)),
        ],
        compiler_params=params(identity, 63.5),
    )(gates, ranks, mixed, rows, w_in, w_out, xr, got0, got1, pre)


def split_low(values):
    high = lax.reduce_precision(values, 8, 7)
    return high.astype(BF), (values - high).astype(BF)


def local(
    hidden_in,
    teacher,
    lengths,
    routes,
    attn_gain,
    w_query,
    w_key,
    w_value,
    w_output,
    query_gain,
    key_gain,
    ffn_gain,
    w_router,
    w_expert_in,
    w_expert_out,
):
    c, f, t = place()
    C, F, T = (lax.axis_size(axis) for axis in AXES)
    S = C * T
    row_count = hidden_in.shape[1]
    width = hidden_in.shape[2]
    half_rows = row_count // T
    head_size = query_gain.shape[0]
    inv_root = head_size ** (-0.5)
    bf_type = BF
    fl_type = FL

    expert_count = S * F
    lanes = -(-expert_count // 128) * 128
    route_ids = routes[0]
    top_count = route_ids.shape[1]
    capacity = max(2, half_rows * top_count * 3 // (2 * expert_count))
    cap = -(-capacity // 16) * 16
    expert_ids = jnp.arange(lanes, dtype=jnp.int32)
    named = jnp.any(route_ids[:, :, None] == expert_ids[None, None, :], axis=1)
    row_ids = jnp.arange(half_rows, dtype=jnp.int32)
    below = (row_ids[None, :] < row_ids[:, None]).astype(bf_type)
    earlier = jnp.dot(below, named.astype(bf_type), preferred_element_type=fl_type)
    rank_tab = jnp.where(named, earlier, -1.0)

    q_cols, kv_cols = w_query.shape[1], w_key.shape[1]
    w_all = jnp.concatenate(
        [w_query, w_key, w_value, jnp.pad(w_router, ((0, 0), (0, lanes - expert_count)))], axis=1
    )
    proj_cols = q_cols + 2 * kv_cols
    q_heads = q_cols // head_size
    kv_heads = kv_cols // head_size
    group_size = q_heads // kv_heads
    inputs = hidden_in[0].astype(fl_type)
    positions = c * row_count + jnp.arange(row_count, dtype=jnp.int32)
    cosine, sine_tab = rope_tables(positions, head_size)
    length = jnp.take(lengths, f)
    total_len = row_count * C
    row_start = t * half_rows
    other_start = (1 - t) * half_rows
    own_inputs = lax.dynamic_slice_in_dim(inputs, row_start, half_rows, 0)
    own_positions = lax.dynamic_slice_in_dim(positions, row_start, half_rows, 0)
    fused = C == 4 and T == 2
    swap = [(i, 1 - i) for i in range(T)]
    if fused:
        cos_full = jnp.concatenate([cosine, cosine], axis=1)
        sin_signed = jnp.concatenate([-sine_tab, sine_tab], axis=1)
        key_pos = jnp.arange(total_len, dtype=jnp.int32)[:, None]
        bias = jnp.where((key_pos <= positions[None, :]) & (key_pos < length), 0.0, MASKED)
        (
            full_all, full_o, rank_z, raw, q_rot, all_both, keys_t, log_total, heads_low,
            normed_low, residual, ffn_low, gate_tab,
        ) = head(
            1, C, F, T, kv_heads, proj_cols, total_len,
            (
                hidden_in[0], rank_tab, rank_tab[:, :expert_count].T, attn_gain[None], query_gain[None], key_gain[None],
                ffn_gain[None], cos_full, sin_signed, bias, w_all, w_output,
            ),
        )
        full_router = full_all[:, proj_cols : proj_cols + expert_count]
        gates = gate_tab[:, :expert_count]
        ffn_factor = lax.rsqrt(jnp.mean(residual * residual, axis=-1, keepdims=True) + EPS)
    else:
        full_all, full_o, rank_z = gather_weights(C, F, w_all, w_output, rank_tab)
        full_qkv = full_all[:, :proj_cols]
        full_router = full_all[:, proj_cols : proj_cols + expert_count]
        normed, norm_factor = norm_rows(inputs, attn_gain)
        normed_low = normed.astype(bf_type)
        raw = jnp.dot(normed_low, full_qkv, preferred_element_type=fl_type)
        q_raw = raw[:, :q_cols].reshape(row_count, q_heads, head_size)
        k_raw = raw[:, q_cols : q_cols + kv_cols].reshape(row_count, kv_heads, head_size)
        values_low = raw[:, q_cols + kv_cols :].astype(bf_type).reshape(row_count, kv_heads, head_size)
        q_normed, q_factor = norm_rows(q_raw, query_gain)
        k_normed, k_factor = norm_rows(k_raw, key_gain)
        q_rot = rotate(q_normed, cosine, sine_tab).astype(bf_type)
        k_rot = rotate(k_normed, cosine, sine_tab).astype(bf_type)
        queries = jnp.transpose(q_rot.reshape(row_count, kv_heads, group_size, head_size), (1, 2, 0, 3))
        both = jnp.transpose(jnp.concatenate([k_rot, values_low], axis=1), (1, 0, 2))
        all_both = lax.all_gather(both, "ctx", axis=1, tiled=True)
        all_keys, all_values = all_both[:kv_heads], all_both[kv_heads:]
        block_len = min(1024, total_len)
        offsets = jnp.arange(total_len // block_len, dtype=jnp.int32) * block_len
        stat_shape = (kv_heads, group_size, row_count)

        def lse_step(carry, offset):
            running_max, running_sum = carry
            key_rows = lax.dynamic_slice_in_dim(all_keys, offset, block_len, 1)
            scores, allowed = block_scores(queries, key_rows, offset, positions, length, inv_root)
            new_max = jnp.maximum(running_max, jnp.max(scores, axis=-1))
            exponent = jnp.where(allowed, jnp.exp(scores - new_max[..., None]), 0.0)
            return (
                (new_max, running_sum * jnp.exp(running_max - new_max) + jnp.sum(exponent, axis=-1)),
                None,
            )

        (row_max, row_sum), _ = lax.scan(
            lse_step, (jnp.full(stat_shape, MASKED, fl_type), jnp.zeros(stat_shape, fl_type)), offsets
        )
        log_total = row_max + jnp.log(row_sum)

        def probs_of(offset):
            key_rows = lax.dynamic_slice_in_dim(all_keys, offset, block_len, 1)
            value_rows = lax.dynamic_slice_in_dim(all_values, offset, block_len, 1)
            scores, allowed = block_scores(queries, key_rows, offset, positions, length, inv_root)
            return (
                jnp.where(allowed, jnp.exp(scores - log_total[..., None]), 0.0),
                key_rows,
                value_rows,
            )

        def out_step(running, offset):
            probabilities, key_rows, value_rows = probs_of(offset)
            return (
                running
                + jnp.einsum(
                    "kgqj,kjd->kgqd",
                    probabilities.astype(bf_type),
                    value_rows,
                    preferred_element_type=fl_type,
                ),
                None,
            )

        attn_acc, _ = lax.scan(
            out_step, jnp.zeros((kv_heads, group_size, row_count, head_size), fl_type), offsets
        )
        heads_low = (
            jnp.transpose(attn_acc, (2, 0, 1, 3))
            .reshape(row_count, q_heads * head_size)
            .astype(bf_type)
        )
        heads_other = lax.dynamic_slice_in_dim(heads_low, other_start, half_rows, 0)
        heads_own = lax.dynamic_slice_in_dim(heads_low, row_start, half_rows, 0)
        theirs = jnp.dot(heads_other, full_o, preferred_element_type=fl_type).astype(bf_type)
        ours = lax.ppermute(theirs, "tp", swap)
        attn_rows = jnp.dot(heads_own, full_o, preferred_element_type=fl_type) + ours.astype(fl_type)
        own_factor = lax.dynamic_slice_in_dim(norm_factor, row_start, half_rows, 0)
        residual = own_inputs + attn_rows
        ffn_in, ffn_factor = norm_rows(residual, ffn_gain)
        ffn_low = ffn_in.astype(bf_type)
        logits = jnp.dot(ffn_low, full_router, preferred_element_type=fl_type)
        is_named = named[:, :expert_count]
        masked = jnp.where(is_named, logits, MASKED)
        shifted = jnp.where(is_named, jnp.exp(masked - jnp.max(masked, axis=-1, keepdims=True)), 0.0)
        gates = shifted / jnp.sum(shifted, axis=-1, keepdims=True)
        gate_tab = jnp.pad(gates, ((0, 0), (0, lanes - expert_count)))

    if fused:
        gate_t = jnp.swapaxes(gates, 0, 1)
        expert_x, got_0, got_1, both_pre, mixed_low, mixture, gate_z = moe_forward(
            2, C, F, T, cap, ffn_low, gate_t, rank_z, w_expert_in[0], w_expert_out[0]
        )
    else:
        def of_slab(table):
            picked = table[:, :, :expert_count].reshape(F, half_rows, C, F, T)
            return lax.dynamic_index_in_dim(picked, f, 3, keepdims=False).reshape(F, half_rows, S)

        rank_slab = of_slab(rank_z)
        slot_ids = jnp.arange(cap, dtype=fl_type)
        chosen_rows = rank_slab[:, :, :, None] == slot_ids
        chosen_slots = (
            jnp.transpose(rank_slab, (0, 2, 1))[:, :, None, :] == slot_ids[:, None]
        )

        select = chosen_slots.astype(bf_type)
        received, _, gate_z = dispatch(2, C, F, T, ffn_low, select, gate_tab)
        expert_rows = received.reshape(-1, width)
        both_pre = jnp.dot(expert_rows, w_expert_in[0], preferred_element_type=fl_type)
        ff_width = w_expert_out.shape[1]
        gate_pre = both_pre[:, :ff_width]
        up_pre = both_pre[:, ff_width:]
        sigmoid_gate = jax.nn.sigmoid(gate_pre)
        silu_gate = gate_pre * sigmoid_gate
        mixed_low = (silu_gate * up_pre).astype(bf_type)
        expert_out = (
            jnp.dot(mixed_low, w_expert_out[0], preferred_element_type=fl_type)
            .astype(bf_type)
            .reshape(S, F, cap, width)
        )
        gate_slab = of_slab(gate_z)
        weigh = jnp.where(chosen_rows, gate_slab[..., None], 0.0).reshape(F, 1, half_rows, S * cap)
        weigh = jnp.concatenate(split_low(weigh), axis=1)
        returned, parts = combine(3, C, F, T, expert_out, weigh)
        mixture = jnp.sum(parts.astype(fl_type), axis=0)
    output_f = residual + mixture
    count = jnp.sum(lengths).astype(fl_type)
    tokens_total = lengths.shape[0] * row_count * C
    valid = own_positions < length
    error = jnp.where(valid[:, None], output_f - teacher[0].astype(fl_type), 0.0)
    loss_part = jnp.sum(error * error)
    grad_out = error * (tokens_total / count)

    if fused:
        grad_mixture, grad_expert_in, grad_expert_out, back_0, back_1 = moe_backward(
            3, C, F, T, grad_out.astype(bf_type), gate_z, rank_z, mixed_low,
            w_expert_in[0], w_expert_out[0], expert_x, got_0, got_1, both_pre,
        )
        back_0 = jnp.transpose(back_0[:, :, :C], (3, 2, 1, 0))
        back_1 = back_1[:, :, : 2 * T].reshape(2, F, 2, T, half_rows)
        back_1 = jnp.transpose(back_1, (4, 0, 2, 1, 3)).reshape(half_rows, C, F, T)
        grad_gate = (back_0 + back_1).reshape(half_rows, expert_count)
    else:
        select_gates = jnp.where(
            chosen_slots, jnp.transpose(gate_slab, (0, 2, 1))[:, :, None, :], 0.0
        )
        select_gates = jnp.concatenate(split_low(select_gates), axis=-1)
        grad_recv, grad_out_z = dispatch(4, C, F, T, grad_out.astype(bf_type), select_gates)
        slot_grads = jnp.einsum("zskr,zrd->zskd", select, grad_out_z, preferred_element_type=fl_type)
        slot_gate = jnp.sum(slot_grads * returned.astype(fl_type), axis=-1)
        gate_grads = jnp.sum(jnp.where(chosen_rows, slot_gate[:, None, :, :], 0.0), axis=-1)
        gate_grads = jnp.pad(gate_grads, ((0, 0), (0, 0), (0, -S % 128)))

        grad_recv = grad_recv.reshape(-1, width)
        grad_mixed = outer_cols(grad_recv, w_expert_out[0])
        grad_expert_out = inner_rows(mixed_low, grad_recv)
        grad_gate_pre = grad_mixed * up_pre * (sigmoid_gate * (1.0 + gate_pre * (1.0 - sigmoid_gate)))
        grad_up_pre = grad_mixed * silu_gate
        grad_pre = jnp.concatenate([grad_gate_pre, grad_up_pre], axis=1).astype(bf_type)
        grad_expert_in = inner_rows(expert_rows, grad_pre)
        grad_rows = (
            outer_cols(grad_pre, w_expert_in[0]).astype(bf_type).reshape(S, F, cap, width)
        )
        weigh_one = chosen_rows.astype(bf_type).reshape(F, 1, half_rows, S * cap)
        _, grad_parts, gate_back = combine(5, C, F, T, grad_rows, weigh_one, gate_grads)
        grad_gate = jnp.transpose(
            gate_back[:, :, :S].reshape(F, half_rows, C, T), (1, 2, 0, 3)
        ).reshape(half_rows, expert_count)
        grad_mixture = jnp.sum(grad_parts.astype(fl_type), axis=0)
    grad_logits = (
        gates * (grad_gate - jnp.sum(gates * grad_gate, axis=-1, keepdims=True))
    ).astype(bf_type)
    grad_ffn = grad_mixture + outer_cols(grad_logits, full_router)
    router_part = inner_rows(ffn_low, grad_logits)
    grad_resid_norm, ffn_gain_terms = norm_back(residual, ffn_factor, ffn_gain, grad_ffn)
    grad_residual = grad_out + grad_resid_norm
    grad_own = grad_residual.astype(bf_type)
    if fused:
        vec_in = jnp.zeros((8, width), fl_type)
        vec_in = vec_in.at[1].set(jnp.sum(ffn_gain_terms, axis=0))
        vec_in = vec_in.at[2, 2 * head_size].set(loss_part)
        router_rows = router_part.reshape(F, -1, width)
        grad_input, total_a, total_o, summed = tail(
            9, C, F, T, kv_heads,
            (
                grad_own, heads_low, q_rot, all_both, keys_t, raw, log_total, bias,
                cos_full, sin_signed, query_gain[None], key_gain[None], attn_gain[None],
                own_inputs, grad_residual, router_rows, vec_in, normed_low, full_o, full_all,
            ),
            width, q_cols // C,
        )
        grad_query = total_a[:, :q_cols].astype(fl_type)
        grad_key = total_a[:, q_cols : q_cols + kv_cols].astype(fl_type)
        grad_value = total_a[:, q_cols + kv_cols :].astype(fl_type)
        grad_output_w = total_o.astype(fl_type)
        router_len = router_rows.shape[1]
        grad_router = summed[:router_len].reshape(w_router.shape)
        sum_attn, sum_ffn = summed[router_len], summed[router_len + 1]
        sum_query = summed[router_len + 2, :head_size]
        sum_key = summed[router_len + 2, head_size : 2 * head_size]
        loss_total = summed[router_len + 2, 2 * head_size]
    else:
        grad_other = lax.ppermute(grad_own, "tp", swap)
        grad_attn = jnp.where(
            t == 0,
            jnp.concatenate([grad_own, grad_other], axis=0),
            jnp.concatenate([grad_other, grad_own], axis=0),
        )
        grad_heads = jnp.transpose(
            outer_cols(grad_attn, full_o)
            .astype(bf_type)
            .reshape(row_count, kv_heads, group_size, head_size),
            (1, 2, 0, 3),
        )

        def delta_step(running, offset):
            probabilities, key_rows, value_rows = probs_of(offset)
            grad_weights = jnp.einsum(
                "kgqd,kjd->kgqj", grad_heads, value_rows, preferred_element_type=fl_type
            )
            return (running + jnp.sum(probabilities * grad_weights, axis=-1), None)

        delta, _ = lax.scan(delta_step, jnp.zeros(stat_shape, fl_type), offsets)

        def grad_step(running, offset):
            probabilities, key_rows, value_rows = probs_of(offset)
            grad_weights = jnp.einsum(
                "kgqd,kjd->kgqj", grad_heads, value_rows, preferred_element_type=fl_type
            )
            grad_scores = (probabilities * (grad_weights - delta[..., None])).astype(bf_type)
            running = (
                running
                + jnp.einsum("kgqj,kjd->kgqd", grad_scores, key_rows, preferred_element_type=fl_type)
                * inv_root
            )
            key_part = (
                jnp.einsum("kgqj,kgqd->kjd", grad_scores, queries, preferred_element_type=fl_type)
                * inv_root
            )
            value_part = jnp.einsum(
                "kgqj,kgqd->kjd",
                probabilities.astype(bf_type),
                grad_heads,
                preferred_element_type=fl_type,
            )
            return (running, (key_part, value_part))

        grad_qrot, (key_blocks, value_blocks) = lax.scan(
            grad_step, jnp.zeros((kv_heads, group_size, row_count, head_size), fl_type), offsets
        )
        both_grads = jnp.concatenate([key_blocks, value_blocks], axis=1).astype(bf_type)
        both_grads = jnp.transpose(both_grads, (0, 2, 1, 3)).reshape(C, row_count, 2 * kv_cols)
        both_sum = ctx_sum(6, C, both_grads)
        grad_krot = both_sum[:, :kv_cols].reshape(row_count, kv_heads, head_size)
        grad_values_low = both_sum[:, kv_cols:].astype(bf_type)
        grad_qrot = jnp.transpose(grad_qrot, (2, 0, 1, 3)).reshape(row_count, q_heads, head_size)
        grad_qraw, query_gain_terms = norm_back(
            q_raw, q_factor, query_gain, rotate(grad_qrot, cosine, -sine_tab)
        )
        grad_kraw, key_gain_terms = norm_back(
            k_raw, k_factor, key_gain, rotate(grad_krot, cosine, -sine_tab)
        )
        grad_raw = jnp.concatenate(
            [
                grad_qraw.astype(bf_type).reshape(row_count, -1),
                grad_kraw.astype(bf_type).reshape(row_count, -1),
                grad_values_low,
            ],
            axis=1,
        )
        raw_other = lax.dynamic_slice_in_dim(grad_raw, other_start, half_rows, 0)
        raw_own = lax.dynamic_slice_in_dim(grad_raw, row_start, half_rows, 0)
        norm_theirs = outer_cols(raw_other, full_qkv).astype(bf_type)
        norm_ours = lax.ppermute(norm_theirs, "tp", swap)
        grad_normed = outer_cols(raw_own, full_qkv) + norm_ours.astype(fl_type)
        grad_input_norm, attn_gain_terms = norm_back(own_inputs, own_factor, attn_gain, grad_normed)
        grad_input = grad_residual + grad_input_norm

        total_a, total_o = weight_grads(
            7, C, F, normed_low.T, grad_raw, heads_low.T, grad_attn
        )
        total_a = total_a.reshape(-1, proj_cols).astype(fl_type)
        grad_query = total_a[:, :q_cols]
        grad_key = total_a[:, q_cols : q_cols + kv_cols]
        grad_value = total_a[:, q_cols + kv_cols :]
        grad_output_w = total_o.reshape(w_output.shape).astype(fl_type)

        vector = jnp.concatenate(
            [
                jnp.sum(attn_gain_terms, axis=0),
                jnp.sum(ffn_gain_terms, axis=0),
                jnp.sum(query_gain_terms, axis=(0, 1)),
                jnp.sum(key_gain_terms, axis=(0, 1)),
                loss_part[None],
            ]
        )
        vector = jnp.pad(vector, (0, -vector.shape[0] % 1024)).reshape(-1, 128)
        router_rows = router_part.reshape(F, -1, 128)
        small = jnp.concatenate(
            [router_rows, jnp.broadcast_to(vector[None], (F,) + vector.shape)], axis=1
        )
        summed = small_sum(8, C, F, T, small)
        router_len = router_rows.shape[1]
        grad_router = summed[:router_len].reshape(w_router.shape)
        flat = summed[router_len:].reshape(-1)
        head_at = 2 * width
        sum_attn, sum_ffn = flat[:width], flat[width:head_at]
        sum_query = flat[head_at : head_at + head_size]
        sum_key = flat[head_at + head_size : head_at + 2 * head_size]
        loss_total = flat[head_at + 2 * head_size]
    loss_value = loss_total / (count * width)
    return (
        output_f.astype(bf_type)[None],
        loss_value,
        grad_input[None],
        sum_attn,
        grad_query,
        grad_key,
        grad_value,
        grad_output_w,
        sum_query,
        sum_key,
        sum_ffn,
        grad_router,
        grad_expert_in.astype(fl_type)[None],
        grad_expert_out.astype(fl_type)[None],
    )


def solution(mesh):
    return jax.shard_map(
        local,
        mesh=mesh,
        in_specs=(
            P("fsdp", "ctx", None),
            P("fsdp", ("ctx", "tp"), None),
            P(),
            P("fsdp", ("ctx", "tp"), None),
            P(),
            P("fsdp", "tp"),
            P("fsdp", "tp"),
            P("fsdp", "tp"),
            P("tp", "fsdp"),
            P(),
            P(),
            P(),
            P("fsdp", None),
            P(("ctx", "fsdp", "tp"), None, None),
            P(("ctx", "fsdp", "tp"), None, None),
        ),
        out_specs=(
            P("fsdp", ("ctx", "tp"), None),
            P(),
            P("fsdp", ("ctx", "tp"), None),
            P(),
            P("fsdp", "tp"),
            P("fsdp", "tp"),
            P("fsdp", "tp"),
            P("tp", "fsdp"),
            P(),
            P(),
            P(),
            P("fsdp", None),
            P(("ctx", "fsdp", "tp"), None, None),
            P(("ctx", "fsdp", "tp"), None, None),
        ),
        check_vma=False,
    )
```

```python
import functools

import jax
import jax.numpy as jnp
from jax import lax
from jax.experimental import pallas as pl
from jax.experimental.pallas import tpu as pltpu
from jax.sharding import PartitionSpec as P

EPS = 1e-06
ROPE_BASE = 1000000.0
MASKED = -1e30
LOG2E = 1.4426950408889634
AXES = ("ctx", "fsdp", "tp")
MESH = pl.DeviceIdType.MESH
ANY = pl.BlockSpec(memory_space=pl.ANY)
VMEM = pl.BlockSpec(memory_space=pltpu.VMEM)
BF = jnp.bfloat16
FL = jnp.float32
MIB = 1024 * 1024


def norm_rows(values, gain_vec):
    factor = lax.rsqrt(jnp.mean(values * values, axis=-1, keepdims=True) + EPS)
    return (values * factor * gain_vec, factor)


def norm_back(values, factor, gain_vec, upstream):
    weighted = upstream * gain_vec
    inner_mean = jnp.mean(values * weighted, axis=-1, keepdims=True)
    return (
        factor * weighted - values * (factor * factor * factor) * inner_mean,
        upstream * values * factor,
    )


def rope_tables(positions, head_size):
    half_size = head_size // 2
    frequency = jnp.power(ROPE_BASE, -jnp.arange(half_size, dtype=jnp.float32) * (2.0 / head_size))
    angles = positions.astype(jnp.float32)[:, None] * frequency[None, :]
    return (jnp.cos(angles), jnp.sin(angles))


def rotate(values, cosine, sine_tab):
    half_size = values.shape[-1] // 2
    front_half = values[..., :half_size]
    back_half = values[..., half_size:]
    cos_rows = cosine[:, None, :]
    sin_rows = sine_tab[:, None, :]
    return jnp.concatenate(
        [
            front_half * cos_rows - back_half * sin_rows,
            back_half * cos_rows + front_half * sin_rows,
        ],
        axis=-1,
    )


def inner_rows(left, right):
    return lax.dot_general(
        left, right, (((0,), (0,)), ((), ())), preferred_element_type=jnp.float32
    )


def outer_cols(left, right):
    return lax.dot_general(
        left, right, (((1,), (1,)), ((), ())), preferred_element_type=jnp.float32
    )


def block_scores(queries, key_rows, offset, positions, length, inv_root):
    block_len = key_rows.shape[1]
    raw_scores = (
        jnp.einsum("kgqd,kjd->kgqj", queries, key_rows, preferred_element_type=jnp.float32)
        * inv_root
    )
    key_pos = offset + jnp.arange(block_len, dtype=jnp.int32)
    allowed = (key_pos[None, :] <= positions[:, None]) & (key_pos[None, :] < length)
    return (jnp.where(allowed, raw_scores, MASKED), allowed)


def place():
    return tuple(lax.axis_index(axis) for axis in AXES)


def remote(source, target, sent, got, device):
    return pltpu.make_async_remote_copy(
        src_ref=source, dst_ref=target, send_sem=sent, recv_sem=got,
        device_id=device, device_id_type=MESH,
    )


def greet(devices):
    barrier = pltpu.get_barrier_semaphore()
    for device in devices:
        pl.semaphore_signal(barrier, inc=1, device_id=device, device_id_type=MESH)
    pl.semaphore_wait(barrier, len(devices))


def params(identity, mebibytes):
    return pltpu.CompilerParams(
        collective_id=identity, has_side_effects=True, vmem_limit_bytes=int(mebibytes * MIB)
    )


def gather_body(C, F, wa, wo, tab, fa, fo, ftab, loc, zs, zr, ys, yr, ks, kr, ts, tr):
    c, f, t = place()
    core, chip = lax.rem(c, 2), lax.div(c, 2)
    chips = C // 2
    sib = c + 1 - 2 * core
    ra, (ro, co) = wa.shape[0], wo.shape
    pa, po = ra // C, ro // C

    def spot(arr, b, p):
        if arr == 0:
            return fa.at[pl.ds(pl.multiple_of(b * ra + p * pa, pa), pa)]
        return fo.at[pl.ds(pl.multiple_of(p * po, po), po), pl.ds(pl.multiple_of(b * co, co), co)]

    def own(arr):
        if arr == 0:
            return wa.at[pl.ds(pl.multiple_of(c * pa, pa), pa)]
        return wo.at[pl.ds(pl.multiple_of(c * po, po), po)]

    peers = [(c, lax.rem(f + k, F), t) for k in range(1, F)]
    peers += [(lax.rem(chip + k, chips) * 2 + core, f, t) for k in range(1, chips)]
    peers += [(sib, f, t)]
    greet(peers)

    def z_copy(arr, s, d):
        b = f - (s - 1) if d == 0 else f + (s - 1)
        source = own(arr) if s == 1 else spot(arr, b, c)
        return remote(
            source, spot(arr, b, c), zs.at[d, s, arr], zr.at[d, s, arr],
            (c, f + 1 if d == 0 else f - 1, t),
        )

    def z_sends(s, d):
        b = f - (s - 1) if d == 0 else f + (s - 1)
        return (f + 1 < F) & (b >= 0) if d == 0 else (f > 0) & (b < F)

    def z_gets(s, d):
        return f - s >= 0 if d == 0 else f + s < F

    def came(s, d):
        return f - s if d == 0 else f + s

    def z_arrival(arr, s, d):
        b = came(s, d)
        here = spot(arr, b, c)
        return remote(here, here, zs.at[d, s, arr], zr.at[d, s, arr], (c, f, t))

    def y_copy(arr, s, d, k):
        here = spot(arr, came(s, d), c)
        there = (lax.rem(chip + k, chips) * 2 + core, f, t)
        return remote(here, here, ys.at[d, s, k, arr], yr.at[d, s, k, arr], there)

    def k_copy(arr, s, d, k, side):
        p = lax.rem(chip + chips - k, chips) * 2 + side
        here = spot(arr, came(s, d), p)
        return remote(here, here, ks.at[d, s, k, arr], kr.at[d, s, k, arr], (sib, f, t))

    def y_arrival(arr, s, d, k):
        p = lax.rem(chip + chips - k, chips) * 2 + core
        here = spot(arr, came(s, d), p)
        return remote(here, here, ys.at[d, s, k, arr], yr.at[d, s, k, arr], (sib, f, t))

    tabs = [
        remote(tab, ftab.at[f], ts.at[k], tr.at[k], (c, lax.rem(f + k, F), t)) for k in range(1, F)
    ]
    for copy in tabs:
        copy.start()
    for d in range(2):

        @pl.when(z_sends(1, d))
        def _():
            for arr in range(2):
                z_copy(arr, 1, d).start()

    locals_ = [
        pltpu.make_async_copy(tab, ftab.at[f], loc.at[0]),
        pltpu.make_async_copy(wa, fa.at[pl.ds(pl.multiple_of(f * ra, ra), ra)], loc.at[1]),
        pltpu.make_async_copy(wo, fo.at[:, pl.ds(pl.multiple_of(f * co, co), co)], loc.at[2]),
    ]
    for copy in locals_:
        copy.start()

    def pass_on(s, d):
        for arr in range(2):
            for k in range(1, chips):
                y_arrival(arr, s, d, k).wait_recv()
                k_copy(arr, s, d, k, core).start()

    for s in range(1, F):
        for d in range(2):

            @pl.when(z_gets(s, d))
            def _():
                for arr in range(2):
                    z_arrival(arr, s, d).wait_recv()
                    if s + 1 < F:

                        @pl.when(z_sends(s + 1, d))
                        def _():
                            z_copy(arr, s + 1, d).start()

                    for k in range(1, chips):
                        y_copy(arr, s, d, k).start()
                    k_copy(arr, s, d, 0, core).start()

        if s > 1:
            for d in range(2):
                pl.when(z_gets(s - 1, d))(functools.partial(pass_on, s - 1, d))
    for d in range(2):
        pl.when(z_gets(F - 1, d))(functools.partial(pass_on, F - 1, d))
    for copy in tabs:
        copy.wait()
    for copy in locals_:
        copy.wait()
    for s in range(1, F):
        for d in range(2):

            @pl.when(z_sends(s, d))
            def _():
                for arr in range(2):
                    z_copy(arr, s, d).wait_send()

            @pl.when(z_gets(s, d))
            def _():
                for arr in range(2):
                    for k in range(1, chips):
                        y_copy(arr, s, d, k).wait_send()
                    for k in range(chips):
                        k_copy(arr, s, d, k, core).wait_send()
                        k_copy(arr, s, d, k, 1 - core).wait_recv()


def gather_weights(C, F, wa, wo, tab):
    ra, ca = wa.shape
    ro, co = wo.shape
    chips = C // 2
    dma = pltpu.SemaphoreType.DMA
    return pl.pallas_call(
        functools.partial(gather_body, C, F),
        out_shape=(
            jax.ShapeDtypeStruct((F * ra, ca), wa.dtype),
            jax.ShapeDtypeStruct((ro, F * co), wo.dtype),
            jax.ShapeDtypeStruct((F,) + tab.shape, tab.dtype),
        ),
        in_specs=[ANY] * 3,
        out_specs=[ANY] * 3,
        scratch_shapes=[
            dma((3,)), dma((2, F, 2)), dma((2, F, 2)),
            dma((2, F, chips, 2)), dma((2, F, chips, 2)),
            dma((2, F, chips, 2)), dma((2, F, chips, 2)),
            dma((F,)), dma((F,)),
        ],
        compiler_params=params(1, 16),
    )(wa, wo, tab)


def slab_place(C, T):
    c, f, t = place()
    return c, f, t, c * T + t


def slab_device(index, f, T):
    return (lax.div(index, T), f, lax.rem(index, T))


def dispatch_body(C, F, T, tabbed, rows, select, *refs):
    if tabbed:
        tab, out, zbuf, ftab, stage, loc, zs, zr, ss, sr, ts, tr = refs
    else:
        out, zbuf, stage, loc, zs, zr, ss, sr = refs
    c, f, t, me = slab_place(C, T)
    S = C * T
    K = select.shape[2]
    copies = select.shape[3] // rows.shape[0]
    columns = [(c, lax.rem(f + k, F), t) for k in range(1, F)]
    greet(columns + [slab_device(lax.rem(me + j, S), f, T) for j in range(1, S)])
    sends = [
        remote(rows, zbuf.at[f], zs.at[k], zr.at[k], columns[k - 1]) for k in range(1, F)
    ]
    if tabbed:
        tabs = [remote(tab, ftab.at[f], ts.at[k], tr.at[k], columns[k - 1]) for k in range(1, F)]
        for copy in tabs:
            copy.start()
        ftab[f] = tab[...]
    for copy in sends:
        copy.start()
    zbuf[f] = rows[...]

    def slab_copy(k, j):
        b = lax.rem(f + F - k, F)
        e = lax.rem(me + j, S)
        return remote(
            stage.at[e, b], out.at[me, b], ss.at[k, j], sr.at[k, j], slab_device(e, f, T)
        )

    def slab_arrival(k, j):
        b = lax.rem(f + F - k, F)
        e = lax.rem(me + S - j, S)
        return remote(
            stage.at[e, b], out.at[e, b], ss.at[k, j], sr.at[k, j], slab_device(e, f, T)
        )

    def own_copy(k):
        b = lax.rem(f + F - k, F)
        return pltpu.make_async_copy(stage.at[me, b], out.at[me, b], loc.at[k])

    for k in range(F):
        b = lax.rem(f + F - k, F)
        if k > 0:
            remote(rows, zbuf.at[b], zs.at[k], zr.at[k], columns[k - 1]).wait_recv()

        def pick(j):
            e = lax.rem(me + j, S)
            block = zbuf[b]
            if copies > 1:
                block = jnp.concatenate([block] * copies, axis=0)
            stage[e, b] = jnp.dot(
                select[b, e], block, preferred_element_type=FL
            ).astype(BF)

        if S <= 8:
            for j in range(1, S):
                pick(j)
                slab_copy(k, j).start()
        else:

            def step(j, carry):
                pick(j)
                slab_copy(k, j).start()
                return carry

            lax.fori_loop(1, S, step, 0)
        pick(0)
        own_copy(k).start()
    if tabbed:
        for copy in tabs:
            copy.wait()
    for copy in sends:
        copy.wait_send()
    for k in range(F):
        own_copy(k).wait()

        def settle(j, carry):
            slab_copy(k, j).wait_send()
            slab_arrival(k, j).wait_recv()
            return carry

        lax.fori_loop(1, S, settle, 0)


def dispatch(identity, C, F, T, rows, select, tab=None):
    S = C * T
    K = select.shape[2]
    R, W = rows.shape
    dma = pltpu.SemaphoreType.DMA
    tabbed = tab is not None
    outs = [jax.ShapeDtypeStruct((S, F, K, W), BF), jax.ShapeDtypeStruct((F, R, W), BF)]
    out_specs = [ANY, VMEM]
    ins = [rows, select]
    scratch = [
        pltpu.VMEM((S, F, K, W), BF), dma((F,)), dma((F,)), dma((F,)), dma((F, S)), dma((F, S)),
    ]
    if tabbed:
        outs.append(jax.ShapeDtypeStruct((F,) + tab.shape, tab.dtype))
        out_specs.append(VMEM)
        ins.append(tab)
        scratch += [dma((F,)), dma((F,))]
    return pl.pallas_call(
        functools.partial(dispatch_body, C, F, T, tabbed),
        out_shape=tuple(outs),
        in_specs=[VMEM] * len(ins),
        out_specs=out_specs,
        scratch_shapes=scratch,
        compiler_params=params(identity, 32),
    )(*ins)


def combine_body(C, F, T, tabbed, rows, weigh, *refs):
    if tabbed:
        tab, got, part, ftab, stage, loc, zs, zr, ss, sr, ts, tr = refs
    else:
        got, part, stage, loc, zs, zr, ss, sr = refs
    c, f, t, me = slab_place(C, T)
    S = C * T
    K, W = got.shape[2], got.shape[3]
    n = weigh.shape[1]
    columns = [(c, lax.rem(f + k, F), t) for k in range(1, F)]
    greet(columns + [slab_device(lax.rem(me + j, S), f, T) for j in range(1, S)])

    def slab_copy(k, j):
        b = lax.rem(f + k, F)
        e = lax.rem(me + j, S)
        return remote(
            rows.at[e, b], got.at[b, me], ss.at[k, j], sr.at[k, j], slab_device(e, f, T)
        )

    def slab_arrival(k, j):
        b = lax.rem(f + k, F)
        e = lax.rem(me + S - j, S)
        return remote(
            rows.at[e, b], got.at[b, e], ss.at[k, j], sr.at[k, j], slab_device(e, f, T)
        )

    def own_copy(k):
        b = lax.rem(f + k, F)
        return pltpu.make_async_copy(rows.at[me, b], got.at[b, me], loc.at[k])

    order = list(range(1, F)) + [0]
    for k in order:

        def begin(j, carry):
            slab_copy(k, j).start()
            return carry

        lax.fori_loop(1, S, begin, 0)
        own_copy(k).start()
    if tabbed:
        tabs = [
            remote(tab.at[lax.rem(f + k, F)], ftab.at[f], ts.at[k], tr.at[k], columns[k - 1])
            for k in range(1, F)
        ]
        for copy in tabs:
            copy.start()
        ftab[f] = tab[f]

    def z_copy(k):
        b = lax.rem(f + k, F)
        return remote(stage.at[b], part.at[f], zs.at[k], zr.at[k], columns[k - 1])

    def z_arrival(k):
        b = lax.rem(f + F - k, F)
        return remote(stage.at[b], part.at[b], zs.at[k], zr.at[k], columns[k - 1])

    step = min(W, 512)
    for k in order:
        b = lax.rem(f + k, F)
        own_copy(k).wait()

        def settle(j, carry):
            slab_arrival(k, j).wait_recv()
            return carry

        lax.fori_loop(1, S, settle, 0)
        target = part if k == 0 else stage

        def add(i, carry):
            columns_ = pl.ds(pl.multiple_of(i * step, step), step)
            block = got[b, :, :, columns_].reshape(S * K, step)
            total = jnp.dot(weigh[b, 0], block, preferred_element_type=FL)
            for m in range(1, n):
                total += jnp.dot(weigh[b, m], block, preferred_element_type=FL)
            target[b, :, columns_] = total.astype(BF)
            return carry

        lax.fori_loop(0, W // step, add, 0)
        if k > 0:
            z_copy(k).start()
    for k in range(1, F):
        z_copy(k).wait_send()
        z_arrival(k).wait_recv()
    for k in range(F):

        def leave(j, carry):
            slab_copy(k, j).wait_send()
            return carry

        lax.fori_loop(1, S, leave, 0)
    if tabbed:
        for copy in tabs:
            copy.wait()


def combine(identity, C, F, T, rows, weigh, tab=None):
    S, _, K, W = rows.shape
    R = weigh.shape[2]
    dma = pltpu.SemaphoreType.DMA
    tabbed = tab is not None
    outs = [jax.ShapeDtypeStruct((F, S, K, W), BF), jax.ShapeDtypeStruct((F, R, W), BF)]
    ins = [rows, weigh]
    scratch = [
        pltpu.VMEM((F, R, W), BF), dma((F,)), dma((F,)), dma((F,)), dma((F, S)), dma((F, S)),
    ]
    if tabbed:
        outs.append(jax.ShapeDtypeStruct(tab.shape, tab.dtype))
        ins.append(tab)
        scratch += [dma((F,)), dma((F,))]
    return pl.pallas_call(
        functools.partial(combine_body, C, F, T, tabbed),
        out_shape=tuple(outs),
        in_specs=[ANY] + [VMEM] * (len(ins) - 1),
        out_specs=[VMEM] * len(outs),
        scratch_shapes=scratch,
        compiler_params=params(identity, 32),
    )(*ins)


def ctx_sum_body(C, x, out, got, ss, sr):
    c, f, t = place()
    peers = [(lax.rem(c + k, C), f, t) for k in range(1, C)]
    greet(peers)

    def copy(k):
        p = lax.rem(c + k, C)
        return remote(x.at[p], got.at[c], ss.at[k], sr.at[k], (p, f, t))

    def arrival(k):
        p = lax.rem(c + C - k, C)
        return remote(x.at[p], got.at[p], ss.at[k], sr.at[k], (p, f, t))

    for k in range(1, C):
        copy(k).start()
    got[c] = x[c]
    for k in range(1, C):
        arrival(k).wait_recv()
    total = got[0].astype(FL)
    for p in range(1, C):
        total += got[p].astype(FL)
    out[...] = total
    for k in range(1, C):
        copy(k).wait_send()


def ctx_sum(identity, C, x):
    dma = pltpu.SemaphoreType.DMA
    return pl.pallas_call(
        functools.partial(ctx_sum_body, C),
        out_shape=jax.ShapeDtypeStruct(x.shape[1:], FL),
        in_specs=[VMEM],
        out_specs=VMEM,
        scratch_shapes=[pltpu.VMEM(x.shape, x.dtype), dma((C,)), dma((C,))],
        compiler_params=params(identity, 24),
    )(x)


def small_body(C, F, T, x, out, zgot, mid, sgot, zs, zr, ss, sr):
    c, f, t, me = slab_place(C, T)
    S = C * T
    columns = [(c, lax.rem(f + k, F), t) for k in range(1, F)]
    greet(columns + [slab_device(lax.rem(me + j, S), f, T) for j in range(1, S)])

    def z_copy(k):
        return remote(x.at[lax.rem(f + k, F)], zgot.at[f], zs.at[k], zr.at[k], columns[k - 1])

    def z_arrival(k):
        b = lax.rem(f + F - k, F)
        return remote(x.at[b], zgot.at[b], zs.at[k], zr.at[k], columns[k - 1])

    for k in range(1, F):
        z_copy(k).start()
    zgot[f] = x[f]
    for k in range(1, F):
        z_arrival(k).wait_recv()
    total = zgot[0]
    for b in range(1, F):
        total += zgot[b]
    mid[...] = total
    sgot[me] = total

    def s_copy(j):
        return remote(
            mid, sgot.at[me], ss.at[j], sr.at[j], slab_device(lax.rem(me + j, S), f, T)
        )

    def s_arrival(j):
        e = lax.rem(me + S - j, S)
        return remote(mid, sgot.at[e], ss.at[j], sr.at[j], slab_device(e, f, T))

    for j in range(1, S):
        s_copy(j).start()
    for j in range(1, S):
        s_arrival(j).wait_recv()
    total = sgot[0]
    for e in range(1, S):
        total += sgot[e]
    out[...] = total
    for k in range(1, F):
        z_copy(k).wait_send()
    for j in range(1, S):
        s_copy(j).wait_send()


def small_sum(identity, C, F, T, x):
    dma = pltpu.SemaphoreType.DMA
    S = C * T
    one = x.shape[1:]
    return pl.pallas_call(
        functools.partial(small_body, C, F, T),
        out_shape=jax.ShapeDtypeStruct(one, FL),
        in_specs=[VMEM],
        out_specs=VMEM,
        scratch_shapes=[
            pltpu.VMEM((F,) + one, FL), pltpu.VMEM(one, FL), pltpu.VMEM((S,) + one, FL),
            dma((F,)), dma((F,)), dma((S,)), dma((S,)),
        ],
        compiler_params=params(identity, 24),
    )(x)


def far_first(F):
    table = []
    for f in range(F):
        order = []
        for i in range(F):
            ends = [F - 1 - i, i] if f * 2 < F else [i, F - 1 - i]
            for b in ends:
                if ((b > f and b == F - 1 - i) or (b < f and b == i)) and b not in order:
                    order.append(b)
        table.append(order + [f])
    return table


def grads_body(
    C, F, xt, da, ht, dt, outa, outo,
    ska, sko, rka, rko, sya, syo, rya, ryo, rza, rzo, sza, szo,
    k_s, k_r, y_s, y_r, z_s, z_r, g_s, g_r, h_s, h_r,
):
    c, f, t = place()
    core, chip = lax.rem(c, 2), lax.div(c, 2)
    chips = C // 2
    sib = c + 1 - 2 * core
    pa, po, co = outa.shape[1], outo.shape[1], outo.shape[2]
    ra = pa * C
    table = far_first(F)

    def block(q):
        value = jnp.int32(table[0][q])
        for g in range(1, F):
            value = jnp.where(f == g, table[g][q], value)
        return value

    blocks = [block(q) for q in range(F)]
    ends = [(c, lax.rem(f + 1, F), t), (c, lax.rem(f + F - 1, F), t)]
    mates = [(lax.rem(chip + k, chips) * 2 + core, f, t) for k in range(1, chips)]
    greet(ends + mates + [(sib, f, t)])

    def piece_a(b, p):
        rows = pl.ds(pl.multiple_of(b * ra + p * pa, pa), pa)
        return jnp.dot(xt[rows, :], da[...], preferred_element_type=FL)

    def piece_o(b, p):
        rows = pl.ds(pl.multiple_of(p * po, po), po)
        cols = pl.ds(pl.multiple_of(b * co, co), co)
        return jnp.dot(ht[rows, :], dt[:, cols], preferred_element_type=FL)

    def core_copies(q, k):
        b = blocks[q]
        return [
            remote(ska.at[b, k], rka.at[b, k], k_s.at[q, k, 0], k_r.at[q, k, 0], (sib, f, t)),
            remote(sko.at[b, k], rko.at[b, k], k_s.at[q, k, 1], k_r.at[q, k, 1], (sib, f, t)),
        ]

    for q in range(F):
        b = blocks[q]
        for k in [*range(1, chips), 0]:
            p = lax.rem(chip + k, chips) * 2 + 1 - core
            ska[b, k] = piece_a(b, p).astype(BF)
            sko[b, k] = piece_o(b, p).astype(BF)
            for copy in core_copies(q, k):
                copy.start()

    def chip_copies(q, k):
        b = blocks[q]
        there = mates[k - 1]
        return [
            remote(sya.at[b, k - 1], rya.at[b, k - 1], y_s.at[q, k, 0], y_r.at[q, k, 0], there),
            remote(syo.at[b, k - 1], ryo.at[b, k - 1], y_s.at[q, k, 1], y_r.at[q, k, 1], there),
        ]

    for q in range(F):
        b = blocks[q]
        for k in range(1, chips):
            p = lax.rem(chip + k, chips) * 2 + core
            for copy in core_copies(q, k):
                copy.wait_recv()
            sya[b, k - 1] = (piece_a(b, p) + rka[b, k].astype(FL)).astype(BF)
            syo[b, k - 1] = (piece_o(b, p) + rko[b, k].astype(FL)).astype(BF)
            for copy in chip_copies(q, k):
                copy.start()

    def z_copies(q, b, slot, there):
        return [
            remote(sza.at[b], rza.at[slot], z_s.at[q, 0], z_r.at[slot, 0], there),
            remote(szo.at[b], rzo.at[slot], z_s.at[q, 1], z_r.at[slot, 1], there),
        ]

    def z_wait(slot):
        for copy in z_copies(0, 0, slot, ends[0]):
            copy.wait_recv()

    for q in range(F):
        b = blocks[q]
        for copy in core_copies(q, 0):
            copy.wait_recv()
        for k in range(1, chips):
            for copy in chip_copies(q, k):
                copy.wait_recv()
        total_a = piece_a(b, c) + rka[b, 0].astype(FL)
        total_o = piece_o(b, c) + rko[b, 0].astype(FL)
        for k in range(1, chips):
            total_a += rya[b, k - 1].astype(FL)
            total_o += ryo[b, k - 1].astype(FL)
        if q < F - 1:
            up = b > f
            first = jnp.where(up, f == 0, f == F - 1)

            @pl.when(first)
            def _():
                sza[b] = total_a.astype(BF)
                szo[b] = total_o.astype(BF)

            @pl.when(jnp.logical_not(first))
            def _():
                z_wait(b)
                sza[b] = (total_a + rza[b].astype(FL)).astype(BF)
                szo[b] = (total_o + rzo[b].astype(FL)).astype(BF)

            @pl.when(up)
            def _():
                for copy in z_copies(q, b, b, (c, f + 1, t)):
                    copy.start()

            @pl.when(jnp.logical_not(up))
            def _():
                slot = jnp.where(b == f - 1, F, b)
                for copy in z_copies(q, b, slot, (c, f - 1, t)):
                    copy.start()

        else:
            sza[f] = total_a.astype(BF)
            szo[f] = total_o.astype(BF)

            @pl.when(f > 0)
            def _():
                z_wait(f)
                sza[f] = (total_a + rza[f].astype(FL)).astype(BF)
                szo[f] = (total_o + rzo[f].astype(FL)).astype(BF)

            @pl.when(f < F - 1)
            def _():
                z_wait(F)
                outa[c] = (sza[f].astype(FL) + rza[F].astype(FL)).astype(BF)
                outo[c] = (szo[f].astype(FL) + rzo[F].astype(FL)).astype(BF)

            @pl.when(f == F - 1)
            def _():
                outa[c] = sza[f]
                outo[c] = szo[f]

    def spread(k):
        there = mates[k - 1]
        return [
            remote(outa.at[c], outa.at[c], g_s.at[k, 0], g_r.at[k, 0], there),
            remote(outo.at[c], outo.at[c], g_s.at[k, 1], g_r.at[k, 1], there),
        ]

    def hand(k, side):
        p = lax.rem(chip + chips - k, chips) * 2 + side
        return [
            remote(outa.at[p], outa.at[p], h_s.at[k, 0], h_r.at[k, 0], (sib, f, t)),
            remote(outo.at[p], outo.at[p], h_s.at[k, 1], h_r.at[k, 1], (sib, f, t)),
        ]

    def spread_arrival(k):
        p = lax.rem(chip + chips - k, chips) * 2 + core
        return [
            remote(outa.at[p], outa.at[p], g_s.at[k, 0], g_r.at[k, 0], mates[k - 1]),
            remote(outo.at[p], outo.at[p], g_s.at[k, 1], g_r.at[k, 1], mates[k - 1]),
        ]

    for k in range(1, chips):
        for copy in spread(k):
            copy.start()
    for copy in hand(0, core):
        copy.start()
    for k in range(1, chips):
        for copy in spread_arrival(k):
            copy.wait_recv()
        for copy in hand(k, core):
            copy.start()
    for k in range(chips):
        for copy in hand(k, 1 - core):
            copy.wait_recv()
        for copy in hand(k, core):
            copy.wait_send()
    for k in range(1, chips):
        for copy in spread(k):
            copy.wait_send()
    for q in range(F):
        for k in range(chips):
            for copy in core_copies(q, k):
                copy.wait_send()
        for k in range(1, chips):
            for copy in chip_copies(q, k):
                copy.wait_send()
        if q < F - 1:
            for copy in z_copies(q, 0, 0, ends[0]):
                copy.wait_send()


def weight_grads(identity, C, F, xt, da, ht, dt):
    D, R = xt.shape
    pa, na = D // F // C, da.shape[1]
    po, no = ht.shape[0] // C, dt.shape[1] // F
    chips = C // 2
    dma = pltpu.SemaphoreType.DMA

    def pair(*lead):
        return [pltpu.VMEM(lead + (pa, na), BF), pltpu.VMEM(lead + (po, no), BF)]

    return pl.pallas_call(
        functools.partial(grads_body, C, F),
        out_shape=(
            jax.ShapeDtypeStruct((C, pa, na), BF),
            jax.ShapeDtypeStruct((C, po, no), BF),
        ),
        in_specs=[VMEM] * 4,
        out_specs=[VMEM] * 2,
        scratch_shapes=[
            *pair(F, chips), *pair(F, chips), *pair(F, chips - 1), *pair(F, chips - 1),
            *pair(F + 1), *pair(F),
            dma((F, chips, 2)), dma((F, chips, 2)), dma((F, chips, 2)), dma((F, chips, 2)),
            dma((F, 2)), dma((F + 1, 2)), dma((chips, 2)), dma((chips, 2)),
            dma((chips, 2)), dma((chips, 2)),
        ],
        compiler_params=params(identity, 60),
    )(xt, da, ht, dt)


def tail_body(
    C, F, T, KH,
    grad_own, heads, qrot, kv, keys_t, raw, lse, bias, cosf, sins, qgain, kgain, again,
    hidden, resid_in, router, vec_in, normed, fo, fall,
    gin, outa, outo, small,
    wbuf, dall, nall, hq, rq, dheads, draw, dk, dv, ksend, kgot, gains, nsend, ngot, nown,
    sza, szo, rza, rzo, smx, zgot, sums, sgot,
    wsem, xs, xr, as_, ar, hs, hr, ns, nr, gs_, gr, ds_, dr, rs, rr, z_s, z_r, ts, tr, us, ur,
):
    c, f, t, me = slab_place(C, T)
    S = C * T
    R, QC = heads.shape
    W = grad_own.shape[1]
    PC = raw.shape[1]
    L = kv.shape[1]
    HS = qgain.shape[1]
    QH = QC // HS
    G = QH // KH
    Rh = grad_own.shape[0]
    KC = KH * HS
    pa = rq.shape[2]
    po = hq.shape[2]
    rows_a, cols_o = outa.shape[0], outo.shape[1]
    root = HS ** (-0.5)
    core = lax.rem(c, 2)
    sib = c + 1 - 2 * core
    mate = lax.rem(c + 2, C)
    mate_sib = lax.rem(sib + 2, C)
    table = far_first(F)

    def block(q):
        value = jnp.int32(table[0][q])
        for g in range(1, F):
            value = jnp.where(f == g, table[g][q], value)
        return value

    blocks = [block(q) for q in range(F)]
    columns = [(c, lax.rem(f + k, F), t) for k in range(1, F)]
    greet(columns + [slab_device(lax.rem(me + j, S), f, T) for j in range(1, S)])
    at_t = pl.ds(pl.multiple_of(t * Rh, Rh), Rh)
    at_u = pl.ds(pl.multiple_of((1 - t) * Rh, Rh), Rh)
    beside = (c, f, 1 - t)

    load_o = pltpu.make_async_copy(fo, wbuf.at[:, pl.ds(0, W)], wsem.at[0])
    load_o.start()

    swap_d = remote(grad_own, dall.at[c, at_t], xs.at[0], xr.at[0], beside)
    swap_d_in = remote(grad_own, dall.at[c, at_u], xs.at[0], xr.at[0], beside)
    swap_n = remote(nsend, ngot, xs.at[1], xr.at[1], beside)

    def spread(view, n, i):
        here = view(mate) if i == 2 else view(c)
        there = (mate if i == 0 else sib, f, t)
        return remote(here, here, as_.at[n, i], ar.at[n, i], there)

    def spread_in(view, n, i):
        here = view((mate, sib, mate_sib)[i])
        return remote(here, here, as_.at[n, i], ar.at[n, i], (sib, f, t))

    def spread_start(view, n):
        spread(view, n, 0).start()
        spread(view, n, 1).start()

    def spread_pass(view, n):
        spread_in(view, n, 0).wait_recv()
        spread(view, n, 2).start()

    def spread_end(view, n):
        spread_in(view, n, 1).wait_recv()
        spread_in(view, n, 2).wait_recv()

    def spread_sent(view, n):
        for i in range(3):
            spread(view, n, i).wait_send()

    def chunk_copies(source, target, ss, sr):
        out, come = [], []
        for k in range(1, C):
            p, o = lax.rem(c + k, C), lax.rem(c + C - k, C)
            out.append(remote(source(p), target(c), ss.at[k], sr.at[k], (p, f, t)))
            come.append(remote(source(o), target(o), ss.at[k], sr.at[k], (o, f, t)))
        return out, come

    def lane(p, n):
        return pl.ds(pl.multiple_of(p * n, n), n)

    heads_out, heads_come = chunk_copies(
        lambda p: heads.at[:, lane(p, po)], lambda o: hq.at[o], hs, hr
    )
    kv_moves = [
        chunk_copies(lambda p, g=g: ksend.at[g, p], lambda o, g=g: kgot.at[g, o], ds_.at[g], dr.at[g])
        for g in range(KH)
    ]
    def outo_of(p):
        return outo.at[lane(p, po)]

    def dall_of(q):
        def view(p, half):
            at = lane(blocks[q], cols_o)
            if half is None:
                return dall.at[p, :, at]
            return dall.at[p, pl.ds(pl.multiple_of(half * Rh, Rh), Rh), at]

        return view

    d_moves = [
        row_spread(C, dall_of(q), lambda i, q=q: gs_.at[q, i], lambda i, q=q: gr.at[q, i])
        for q in range(F)
    ]

    def nall_of(p, half):
        if half is None:
            return nall.at[p]
        return nall.at[p, pl.ds(pl.multiple_of(half * Rh, Rh), Rh)]

    def normed_of(half):
        if half is None:
            return normed
        return normed.at[pl.ds(pl.multiple_of(half * Rh, Rh), Rh)]

    n_start, n_wait, n_drain = row_spread(
        C, nall_of, lambda i: ns.at[i], lambda i: nr.at[i], normed_of
    )

    swap_d.start()
    dall[c, at_t] = grad_own[...]
    for q in range(F):
        d_moves[q][0](0)
    for copy in heads_out:
        copy.start()
    n_start(0, 1)
    hq[c] = heads[:, lane(c, po)]
    nall[c] = normed[...]
    swap_d_in.wait_recv()
    for q in range(F):
        d_moves[q][0](1)

    load_o.wait()
    step = min(512, QC)

    def head_grads(i, carry):
        at = lane(i, step)
        dheads[:, at] = outer_cols(dall[c], wbuf[at, pl.ds(0, W)]).astype(BF)
        return carry

    lax.fori_loop(0, QC // step, head_grads, 0)
    load_w = pltpu.make_async_copy(fall.at[:, pl.ds(0, PC)], wbuf, wsem.at[1])
    load_w.start()

    def unturn(values):
        return values * cosf[...] - pltpu.roll(values, HS // 2, 1) * sins[...]

    def norm_grads(values, gain_vec, upstream):
        factor = lax.rsqrt(jnp.mean(values * values, axis=-1, keepdims=True) + EPS)
        out, terms = norm_back(values, factor, gain_vec, upstream)
        return out, jnp.sum(terms, axis=0, keepdims=True)

    gains[...] = jnp.zeros_like(gains)
    def piece_o(b):
        return inner_rows(
            hq[...].reshape(C * R, po), dall[:, :, lane(b, cols_o)].reshape(C * R, cols_o)
        )

    cut = pa // 256 * 128
    cuts = (slice(0, cut), slice(cut, pa))

    def piece_a(b, cols):
        return inner_rows(
            nall[:, :, lane(b, rows_a)].reshape(C * R, rows_a),
            rq[:, :, cols].reshape(C * R, cols.stop - cols.start),
        )

    def part_of(buf, cols):
        return lambda b: buf.at[b, :, cols]

    def outa_part(p, cols):
        start = pl.multiple_of(p * pa + cols.start, 128)
        return outa.at[:, pl.ds(start, cols.stop - cols.start)]

    pieces = [(piece_o, lambda b: szo.at[b], lambda b: rzo.at[b], outo_of)]
    for cols in cuts:
        pieces.append(
            (
                functools.partial(piece_a, cols=cols), part_of(sza, cols), part_of(rza, cols),
                functools.partial(outa_part, cols=cols),
            )
        )
    end = (f == 0) | (f == F - 1)

    def z_out(n, q):
        b = blocks[q]
        _, send, got, _ = pieces[n]
        return remote(send(b), got(b), z_s.at[n, q], z_r.at[n, b], (c, f + 1, t))

    def z_down(n, q):
        b = blocks[q]
        slot = jnp.where(b == f - 1, F, b)
        _, send, got, _ = pieces[n]
        return remote(send(b), got(slot), z_s.at[n, q], z_r.at[n, slot], (c, f - 1, t))

    def z_wait(n, slot):
        _, send, got, _ = pieces[n]
        remote(send(0), got(slot), z_s.at[n, 0], z_r.at[n, slot], (c, f, t)).wait_recv()

    def z_send(n, q):
        up = blocks[q] > f

        @pl.when(up)
        def _():
            z_out(n, q).start()

        @pl.when(jnp.logical_not(up))
        def _():
            z_down(n, q).start()

    def z_first(n, q):
        fn, send, _, _ = pieces[n]

        @pl.when(end)
        def _():
            send(blocks[q])[...] = fn(blocks[q]).astype(BF)
            z_send(n, q)

    def o_first(q):
        d_moves[q][1](1, 3, 4)
        if q < F - 1:
            z_first(0, q)

    def z_relay(n, q):
        fn, send, got, _ = pieces[n]

        @pl.when(jnp.logical_not(end))
        def _():
            b = blocks[q]
            z_wait(n, b)
            send(b)[...] = (fn(b) + got(b)[...].astype(FL)).astype(BF)
            z_send(n, q)

    def z_last(n):
        fn, send, got, out = pieces[n]
        send(f)[...] = fn(f).astype(BF)

        @pl.when(f > 0)
        def _():
            z_wait(n, f)
            send(f)[...] = (send(f)[...].astype(FL) + got(f)[...].astype(FL)).astype(BF)

        @pl.when(f < F - 1)
        def _():
            z_wait(n, F)
            out(c)[...] = (send(f)[...].astype(FL) + got(F)[...].astype(FL)).astype(BF)

        @pl.when(f == F - 1)
        def _():
            out(c)[...] = send(f)[...]


    key_step = min(L, 512)

    def one_head(g, h):
        at = lane(h, HS)
        q_head, o_grad = qrot[:, at], dheads[:, at]
        product = o_grad.astype(FL) * heads[:, at].astype(FL)
        delta = jnp.sum(product.T, axis=0, keepdims=True)
        row = lse[pl.ds(h, 1), :]
        q_grad = jnp.zeros((HS, R), FL)
        for j in range(L // key_step):
            ks = pl.ds(j * key_step, key_step)
            scores = outer_cols(kv[g, ks, :], q_head) * (root * LOG2E)
            probs = jnp.exp2(scores + bias[ks, :] - row)
            d_probs = outer_cols(kv[KH + g, ks, :], o_grad)
            d_scores = (probs * (d_probs - delta)).astype(BF)
            dv[ks, :] += jnp.dot(probs.astype(BF), o_grad, preferred_element_type=FL)
            dk[ks, :] += jnp.dot(d_scores, q_head, preferred_element_type=FL)
            q_grad += jnp.dot(keys_t[g, :, ks], d_scores, preferred_element_type=FL)
        q_back, terms = norm_grads(raw[:, at], qgain[...], unturn(q_grad.T * root))
        draw[:, at] = q_back.astype(BF)
        gains[0:1, :] += terms

    def some_heads(g, first, count):
        def step_(i, carry):
            one_head(g, first + i)
            return carry

        lax.fori_loop(0, count, step_, 0)

    raw_due = [-(-min((p + 1) * pa, QC) // HS) for p in range(C)]
    raw_gone = []

    def raw_sends(done):
        for p in range(C):
            if p not in raw_gone and raw_due[p] <= done and (p + 1) * pa <= QC:
                raw_gone.append(p)
                raw_send(p)

    def raw_copy(p):
        return remote(draw.at[:, p * pa : (p + 1) * pa], rq.at[c], rs.at[p], rr.at[c], (p, f, t))

    def raw_come(o):
        return remote(draw.at[:, 0:pa], rq.at[o], rs.at[0], rr.at[o], (o, f, t))

    def raw_send(p):
        @pl.when(c != p)
        def _():
            raw_copy(p).start()

        @pl.when(c == p)
        def _():
            rq[c] = draw[:, p * pa : (p + 1) * pa]

    def d_pass(q):
        if q == 0:
            for p in range(F):
                d_moves[p][1](0)
                d_moves[p][0](2, 3)
        d_moves[q][1](2)
        d_moves[q][0](4)

    halves = 2
    part_heads = G // halves
    beat = 0
    for g in range(KH):
        dk[...] = jnp.zeros_like(dk)
        dv[...] = jnp.zeros_like(dv)
        for half in range(halves):
            some_heads(g, g * G + half * part_heads, part_heads)
            raw_sends(g * G + (half + 1) * part_heads)
            if half == halves - 1:
                for p in range(C):
                    at = pl.ds(p * R, R)
                    ksend[g, p, :, 0:HS] = (dk[at, :] * root).astype(BF)
                    ksend[g, p, :, HS : 2 * HS] = dv[at, :].astype(BF)
                for copy in kv_moves[g][0]:
                    copy.start()
                kgot[g, c] = ksend[g, c]
            if beat < F:
                d_pass(beat)
            if beat == 1:
                n_wait(0)
                n_start(2, 3)
            if beat == 2:
                n_wait(2)
                n_start(4)
            if beat == 0:
                for copy in heads_come:
                    copy.wait_recv()
            elif beat < F:
                o_first(beat - 1)
            beat += 1
    for q in range(beat, F):
        d_pass(q)
        o_first(q - 1)

    o_first(F - 1)
    z_relay(0, 0)

    for g in range(KH):
        for copy in kv_moves[g][1]:
            copy.wait_recv()
        total = kgot[g, 0].astype(FL)
        for p in range(1, C):
            total += kgot[g, p].astype(FL)
        k_cols = slice(QC + g * HS, QC + (g + 1) * HS)
        k_back, terms = norm_grads(raw[:, k_cols], kgain[...], unturn(total[:, :HS]))
        draw[:, k_cols] = k_back.astype(BF)
        draw[:, QC + KC + g * HS : QC + KC + (g + 1) * HS] = total[:, HS:].astype(BF)
        gains[1:2, :] += terms
    for p in range(C):
        if p not in raw_gone:
            raw_send(p)
    z_relay(0, 1)
    load_w.wait()
    width_step = min(512, W)

    def norm_theirs(i, carry):
        at = lane(i, width_step)
        nsend[:, at] = outer_cols(draw[at_u, :], wbuf[at, :]).astype(BF)
        return carry

    lax.fori_loop(0, W // width_step, norm_theirs, 0)
    swap_n.start()

    def norm_ours(i, carry):
        at = lane(i, width_step)
        nown[:, at] = outer_cols(draw[at_t, :], wbuf[at, :])
        return carry

    lax.fori_loop(0, W // width_step, norm_ours, 0)

    for q in range(2, F - 1):
        z_relay(0, q)
    n_wait(1, 3, 4)
    for k in range(1, C):
        raw_come(lax.rem(c + k, C)).wait_recv()
    for q in range(F - 1):
        z_first(1, q)
    for q in range(F - 1):
        z_first(2, q)
    z_relay(1, 0)
    z_last(0)
    spread_start(outo_of, 0)

    swap_n.wait_recv()
    upstream = nown[...] + ngot[...].astype(FL)
    values = hidden[at_t, :].astype(FL)
    factor = lax.rsqrt(jnp.mean(values * values, axis=-1, keepdims=True) + EPS)
    back, terms = norm_back(values, factor, again[...], upstream)
    gin[...] = resid_in[...] + back
    E, wide = router.shape[0], W // F
    gain_sum = jnp.sum(terms, axis=0, keepdims=True)
    for b in range(F):
        smx[b, 0:E] = router[:, b * wide : (b + 1) * wide]
        smx[b, E : E + 16] = vec_in[...]
        for i in range(F):
            smx[b, E + i : E + i + 1] = gain_sum[:, i * wide : (i + 1) * wide]
        smx[b, E + 8 : E + 9, 0:HS] = gains[0:1, :]
        smx[b, E + 8 : E + 9, HS : 2 * HS] = gains[1:2, :]

    def t_copy(k):
        return remote(smx.at[lax.rem(f + k, F)], zgot.at[f], ts.at[k], tr.at[k], columns[k - 1])

    def t_arrival(k):
        b = lax.rem(f + F - k, F)
        return remote(smx.at[b], zgot.at[b], ts.at[k], tr.at[k], columns[k - 1])

    for k in range(1, F):
        t_copy(k).start()
    zgot[f] = smx[f]
    for q in range(1, F - 1):
        z_relay(1, q)
    for q in range(F - 1):
        z_relay(2, q)
    spread_pass(outo_of, 0)
    for k in range(1, F):
        t_arrival(k).wait_recv()
    total = zgot[0]
    for b in range(1, F):
        total += zgot[b]
    sums[0] = total

    def u_copy(i):
        there = ((sib, f, t), beside, (mate, f, t))[i]
        return remote(sums.at[i], sgot.at[i], us.at[i], ur.at[i], there)

    u_copy(0).start()
    z_last(1)
    spread_start(pieces[1][3], 1)
    for i in range(3):
        u_copy(i).wait_recv()
        total = sums[i] + sgot[i]
        if i < 2:
            sums[i + 1] = total
            u_copy(i + 1).start()
        else:
            small[...] = total
    spread_end(outo_of, 0)
    z_last(2)
    spread_start(pieces[2][3], 2)
    for n in (1, 2):
        spread_pass(pieces[n][3], n)
    for n in (1, 2):
        spread_end(pieces[n][3], n)

    for n in range(3):
        spread_sent(pieces[n][3], n)
    for q in range(F):
        d_moves[q][2]()
    n_drain()
    for copy in heads_out:
        copy.wait_send()
    swap_d.wait_send()
    swap_n.wait_send()
    for p in range(C):

        @pl.when(c != p)
        def _():
            raw_copy(p).wait_send()

    for g in range(KH):
        for copy in kv_moves[g][0]:
            copy.wait_send()
    for n in range(3):
        for q in range(F - 1):
            z_out(n, q).wait_send()
    for k in range(1, F):
        t_copy(k).wait_send()
    for i in range(3):
        u_copy(i).wait_send()


def tail(identity, C, F, T, KH, args, D, po):
    grad_own, heads, qrot, kv, keys_t, raw, lse, bias = args[:8]
    qgain = args[10]
    router = args[15]
    R, QC = heads.shape
    W = grad_own.shape[1]
    PC = raw.shape[1]
    L = kv.shape[1]
    HS = qgain.shape[1]
    Rh = grad_own.shape[0]
    S = C * T
    pa = PC // C
    rows_a, cols_o = W // F, W // F
    small_shape = (router.shape[0] + 16, W // F)
    dma = pltpu.SemaphoreType.DMA
    V = pltpu.VMEM
    return pl.pallas_call(
        functools.partial(tail_body, C, F, T, KH),
        out_shape=(
            jax.ShapeDtypeStruct((Rh, W), FL),
            jax.ShapeDtypeStruct((rows_a, C * pa), BF),
            jax.ShapeDtypeStruct((C * po, cols_o), BF),
            jax.ShapeDtypeStruct(small_shape, FL),
        ),
        in_specs=[VMEM] * 18 + [ANY] * 2,
        out_specs=[VMEM] * 4,
        scratch_shapes=[
            V((W, PC), BF), V((C, R, W), BF), V((C, R, W), BF), V((C, R, po), BF),
            V((C, R, pa), BF), V((R, QC), BF), V((R, PC), BF), V((L, HS), FL), V((L, HS), FL),
            V((KH, C, R, 2 * HS), BF), V((KH, C, R, 2 * HS), BF), V((8, HS), FL),
            V((Rh, W), BF), V((Rh, W), BF), V((Rh, W), FL),
            V((F, rows_a, pa), BF), V((F, po, cols_o), BF),
            V((F + 1, rows_a, pa), BF), V((F + 1, po, cols_o), BF),
            V((F,) + small_shape, FL), V((F,) + small_shape, FL), V((3,) + small_shape, FL),
            V((3,) + small_shape, FL),
            dma((4,)), dma((2,)), dma((2,)), dma((3, 3)), dma((3, 3)), dma((C,)), dma((C,)), dma((5,)), dma((5,)),
            dma((F, 5)), dma((F, 5)),
            dma((KH, C)), dma((KH, C)), dma((C,)), dma((C,)),
            dma((3, F)), dma((3, F + 1)), dma((F,)), dma((F,)), dma((3,)), dma((3,)),
        ],
        compiler_params=params(identity, 62),
    )(*args)


def row_spread(C, view, sent, got, own=None):
    c, f, t = place()
    sib = c + 1 - 2 * lax.rem(c, 2)
    mate, mate_sib = lax.rem(c + 2, C), lax.rem(sib + 2, C)
    to_mate, to_sib, to_side = (mate, f, t), (sib, f, t), (c, f, 1 - t)
    here = (view(c, t), view(c, None))
    if own is not None:
        here = (own(t), own(None))
    leave = (
        (here[0], view(c, t), to_mate), (here[1], view(c, None), to_sib),
        (view(mate, t), view(mate, t), to_side), (view(mate, t), view(mate, t), to_sib),
        (view(mate, 1 - t), view(mate, 1 - t), to_sib),
    )
    arrive = (
        view(mate, t), view(sib, None), view(mate, 1 - t), view(mate_sib, t),
        view(mate_sib, 1 - t),
    )

    def start(*which):
        for i in which:
            remote(leave[i][0], leave[i][1], sent(i), got(i), leave[i][2]).start()

    def wait(*which):
        for i in which:
            remote(arrive[i], arrive[i], sent(i), got(i), to_sib).wait_recv()

    def drain():
        for i in range(5):
            remote(leave[i][0], leave[i][1], sent(i), got(i), leave[i][2]).wait_send()

    return start, wait, drain


def head_body(
    C, F, T, KH,
    hidden, tab, tab_t, again, qgain, kgain, fgain, cosf, sins, bias, wa, wo,
    fall, full, ftab, raw, qrot, kv, keys_t, lse, heads, normed, resid, low, gates,
    fa, fo, vals_t, nsend, ngot, nown,
    loc, zs, zr, ys, yr, ks, kr, ts, tr, cs, cr, xs, xr,
):
    c, f, t = place()
    R, W = hidden.shape
    Rh = tab.shape[0]
    HS = qgain.shape[1]
    PC = raw.shape[1]
    QC = heads.shape[1]
    KC = KH * HS
    L = kv.shape[1]
    G = QC // HS // KH
    root = HS ** (-0.5)
    core = lax.rem(c, 2)
    sib = c + 1 - 2 * core
    mate = lax.rem(c + 2, C)
    mate_sib = lax.rem(sib + 2, C)
    ra, (ro, co) = wa.shape[0], wo.shape
    pa, po = ra // C, ro // C
    ha, ho = pa // 2, po // 2
    x = Exchange(C, F, T)
    x.greet()

    def spot(arr, b, p):
        half = arr % 2
        if arr < 2:
            return fa.at[pl.ds(pl.multiple_of(b * ra + p * pa + half * ha, ha), ha)]
        rows = pl.ds(pl.multiple_of(p * po + half * ho, ho), ho)
        return fo.at[rows, pl.ds(pl.multiple_of(b * co, co), co)]

    def own(arr):
        half = arr % 2
        if arr < 2:
            return wa.at[pl.ds(pl.multiple_of(c * pa + half * ha, ha), ha)]
        return wo.at[pl.ds(pl.multiple_of(c * po + half * ho, ho), ho)]

    def z_copy(arr, s, d):
        b = f - (s - 1) if d == 0 else f + (s - 1)
        source = own(arr) if s == 1 else spot(arr, b, c)
        there = (c, f + 1 if d == 0 else f - 1, t)
        return remote(source, spot(arr, b, c), zs.at[d, s, arr], zr.at[d, s, arr], there)

    def z_sends(s, d):
        b = f - (s - 1) if d == 0 else f + (s - 1)
        return (f + 1 < F) & (b >= 0) if d == 0 else (f > 0) & (b < F)

    def z_gets(s, d):
        return f - s >= 0 if d == 0 else f + s < F

    def came(s, d):
        return f - s if d == 0 else f + s

    def move(arr, s, d, p, sent, got, i, device):
        here = spot(arr, came(s, d), p)
        return remote(here, here, sent.at[d, s, arr, i], got.at[d, s, arr, i], device)

    def z_begin(arr):
        for d in range(2):

            @pl.when(z_sends(1, d))
            def _():
                z_copy(arr, 1, d).start()

    def z_in(arr, s):
        for d in range(2):

            @pl.when(z_gets(s, d))
            def _():
                here = spot(arr, came(s, d), c)
                remote(here, here, zs.at[d, s, arr], zr.at[d, s, arr], (sib, f, t)).wait_recv()
                if s + 1 < F:

                    @pl.when(z_sends(s + 1, d))
                    def _():
                        z_copy(arr, s + 1, d).start()

                move(arr, s, d, c, ys, yr, 0, (mate, f, t)).start()
                move(arr, s, d, c, ks, kr, 0, (sib, f, t)).start()

    def y_in(arr, s):
        for d in range(2):

            @pl.when(z_gets(s, d))
            def _():
                move(arr, s, d, mate, ys, yr, 0, (mate, f, t)).wait_recv()
                move(arr, s, d, mate, ks, kr, 1, (sib, f, t)).start()

    def k_in(arr, s, d):
        move(arr, s, d, sib, ks, kr, 0, (sib, f, t)).wait_recv()
        move(arr, s, d, mate_sib, ks, kr, 1, (sib, f, t)).wait_recv()

    z_begin(0)
    z_begin(1)
    tabs, tabs_come = x.table_copies(tab_t, ftab, ts, tr)
    for copy in tabs:
        copy.start()
    own_a = pltpu.make_async_copy(wa, fa.at[pl.ds(pl.multiple_of(f * ra, ra), ra)], loc.at[0])
    own_o = pltpu.make_async_copy(
        wo, fo.at[:, pl.ds(pl.multiple_of(f * co, co), co)], loc.at[1]
    )
    own_a.start()
    own_o.start()
    ftab[0, f] = tab_t[...]

    inputs = hidden[...].astype(FL)
    normed[...] = norm_rows(inputs, again[...])[0].astype(BF)
    wide = min(512, PC)

    def project(b, first):
        at = pl.ds(pl.multiple_of(b * ra, ra), ra)
        left = normed[:, at]

        def piece(i, carry):
            cols = pl.ds(pl.multiple_of(i * wide, wide), wide)
            part = jnp.dot(left, fa[at, cols], preferred_element_type=FL)
            if first:
                raw[:, cols] = part
            else:
                raw[:, cols] += part
            return carry

        lax.fori_loop(0, PC // wide, piece, 0)

    def project_in(s):
        for d in range(2):

            @pl.when(z_gets(s, d))
            def _():
                k_in(0, s, d)
                k_in(1, s, d)
                project(came(s, d), False)

    own_a.wait()
    project(f, True)
    z_in(0, 1)
    z_in(1, 1)
    for s in range(2, F):
        z_in(0, s)
        y_in(0, s - 1)
        z_in(1, s)
        y_in(1, s - 1)
        if s == F - 2:
            z_begin(2)
            z_begin(3)
        project_in(s - 1)
    y_in(0, F - 1)
    y_in(1, F - 1)
    z_in(2, 1)
    z_in(3, 1)
    project_in(F - 1)

    def turn(values):
        return values * cosf[...] + pltpu.roll(values, HS // 2, 1) * sins[...]

    at_c = pl.ds(pl.multiple_of(c * R, R), R)
    for g in range(KH):
        k_raw = raw[:, QC + g * HS : QC + (g + 1) * HS]
        kv[g, at_c, :] = turn(norm_rows(k_raw, kgain[...])[0]).astype(BF)
        kv[KH + g, at_c, :] = raw[:, QC + KC + g * HS : QC + KC + (g + 1) * HS].astype(BF)

    def kv_move(p, i, device):
        here = kv.at[:, pl.ds(pl.multiple_of(p * R, R), R), :]
        return remote(here, here, cs.at[i], cr.at[i], device)

    kv_move(c, 0, (mate, f, t)).start()
    kv_move(c, 1, (sib, f, t)).start()

    def query(i, carry):
        at = pl.ds(pl.multiple_of(i * HS, HS), HS)
        qrot[:, at] = turn(norm_rows(raw[:, at], qgain[...])[0]).astype(BF)
        return carry

    lax.fori_loop(0, QC // HS, query, 0)
    save_a = pltpu.make_async_copy(fa, fall, loc.at[2])
    save_a.start()
    y_in(2, 1)
    y_in(3, 1)
    z_in(2, 2)
    kv_move(mate, 0, (mate, f, t)).wait_recv()
    kv_move(mate, 2, (sib, f, t)).start()
    kv_move(sib, 1, (sib, f, t)).wait_recv()
    kv_move(mate_sib, 2, (sib, f, t)).wait_recv()
    for g in range(KH):
        keys_t[g] = kv[g].astype(FL).T.astype(BF)
        vals_t[g] = kv[KH + g].astype(FL).T.astype(BF)

    def some_heads(g, first, count):
        def one_head(i, carry):
            h = first + i
            at = pl.ds(pl.multiple_of(h * HS, HS), HS)
            weight = jnp.exp2(outer_cols(kv[g], qrot[:, at]) * (root * LOG2E) + bias[...])
            total = jnp.sum(weight, axis=0, keepdims=True)
            lse[pl.ds(h, 1), :] = jnp.log2(total)
            probs = (weight * (1.0 / total)).astype(BF)
            heads[:, at] = jnp.dot(vals_t[g], probs, preferred_element_type=FL).T.astype(BF)
            return carry

        lax.fori_loop(0, count, one_head, 0)

    at_t = pl.ds(pl.multiple_of(t * Rh, Rh), Rh)
    at_u = pl.ds(pl.multiple_of((1 - t) * Rh, Rh), Rh)

    def swap(b):
        cols = pl.ds(pl.multiple_of(b * co, co), co)
        return remote(nsend.at[:, cols], ngot.at[:, cols], xs.at[b], xr.at[b], (c, f, 1 - t))

    def output(b):
        cols = pl.ds(pl.multiple_of(b * co, co), co)
        nsend[:, cols] = jnp.dot(
            heads[at_u, :], fo[:, cols], preferred_element_type=FL
        ).astype(BF)
        swap(b).start()
        nown[:, cols] = jnp.dot(heads[at_t, :], fo[:, cols], preferred_element_type=FL)

    def output_in(s):
        for d in range(2):

            @pl.when(z_gets(s, d))
            def _():
                k_in(2, s, d)
                k_in(3, s, d)
                output(came(s, d))

    events = [[(z_in, 3, 2)], [(y_in, 2, 2)], [(y_in, 3, 2)]]
    half = G // 2
    for i in range(2 * KH):
        some_heads(i // 2, i * half, half)
        for event, arr, s in events[i] if i < len(events) else ():
            event(arr, s)
    own_o.wait()
    output(f)
    output_in(1)
    for s in range(3, F):
        z_in(2, s)
        z_in(3, s)
        output_in(s - 1)
        y_in(2, s)
        y_in(3, s)
    save_o = pltpu.make_async_copy(fo, full, loc.at[3])
    output_in(F - 1)
    save_o.start()
    for b in range(F):
        swap(b).wait_recv()
    total = hidden[at_t, :].astype(FL) + (nown[...] + ngot[...].astype(FL))
    resid[...] = total
    ffn_low = norm_rows(total, fgain[...])[0].astype(BF)
    low[...] = ffn_low
    logits = jnp.dot(ffn_low, fa[:, PC:], preferred_element_type=FL)
    named = tab[...] >= 0.0
    masked = jnp.where(named, logits, MASKED)
    shifted = jnp.where(
        named, jnp.exp(masked - jnp.max(masked, axis=-1, keepdims=True)), 0.0
    )
    gates[...] = shifted / jnp.sum(shifted, axis=-1, keepdims=True)

    save_a.wait()
    save_o.wait()
    for b in range(F):
        swap(b).wait_send()
    for copy in tabs:
        copy.wait_send()
    for copy in tabs_come:
        copy.wait_recv()
    kv_move(c, 0, (mate, f, t)).wait_send()
    kv_move(c, 1, (sib, f, t)).wait_send()
    kv_move(mate, 2, (sib, f, t)).wait_send()
    for s in range(1, F):
        for d in range(2):

            @pl.when(z_sends(s, d))
            def _():
                for arr in range(4):
                    z_copy(arr, s, d).wait_send()

            @pl.when(z_gets(s, d))
            def _():
                for arr in range(4):
                    move(arr, s, d, c, ys, yr, 0, (mate, f, t)).wait_send()
                    move(arr, s, d, c, ks, kr, 0, (sib, f, t)).wait_send()
                    move(arr, s, d, mate, ks, kr, 1, (sib, f, t)).wait_send()


def head(identity, C, F, T, KH, PC, L, args):
    hidden, tab, tab_t, qgain, wa, wo = args[0], args[1], args[2], args[4], args[10], args[11]
    R, W = hidden.shape
    Rh, lanes = tab.shape
    HS = qgain.shape[1]
    ra, ca = wa.shape
    QC, co = wo.shape
    dma = pltpu.SemaphoreType.DMA
    V = pltpu.VMEM
    shape = jax.ShapeDtypeStruct
    return pl.pallas_call(
        functools.partial(head_body, C, F, T, KH),
        out_shape=(
            shape((F * ra, ca), BF), shape((QC, F * co), BF), shape((3, F) + tab_t.shape, FL),
            shape((R, PC), FL), shape((R, QC), BF), shape((2 * KH, L, HS), BF),
            shape((KH, HS, L), BF), shape((QC // HS, R), FL), shape((R, QC), BF),
            shape((R, W), BF), shape((Rh, W), FL), shape((Rh, W), BF),
            shape((Rh, lanes), FL),
        ),
        in_specs=[VMEM] * 10 + [ANY] * 2,
        out_specs=[ANY] * 2 + [VMEM] * 11,
        scratch_shapes=[
            V((F * ra, ca), BF), V((QC, F * co), BF), V((KH, HS, L), BF),
            V((Rh, W), BF), V((Rh, W), BF), V((Rh, W), FL),
            dma((4,)), dma((2, F, 4)), dma((2, F, 4)), dma((2, F, 4, 1)), dma((2, F, 4, 1)),
            dma((2, F, 4, 2)), dma((2, F, 4, 2)), dma((3, F)), dma((3, F)), dma((3,)),
            dma((3,)),
            dma((F,)), dma((F,)),
        ],
        compiler_params=params(identity, 60),
    )(*args)


def block_order(F):
    if F == 4:
        return [[0, 1, 3, 2], [1, 2, 3, 0], [2, 1, 0, 3], [3, 2, 0, 1]]
    return [[(f + k) % F for k in range(F)] for f in range(F)]


class Exchange:
    def __init__(self, C, F, T):
        c, f, t = place()
        self.C, self.F, self.T, self.c, self.f, self.t = C, F, T, c, f, t
        self.chip, self.core = lax.div(c, 2), lax.rem(c, 2)
        self.mate = lax.rem(c + 2, C)
        self.unit = self.core * T + t
        table = block_order(F)
        self.blocks = []
        for k in range(F):
            value = jnp.int32(table[0][k])
            for g in range(1, F):
                value = jnp.where(f == g, table[g][k], value)
            self.blocks.append(value)
        self.side = ((c, f, 1 - t), (self.mate, f, t))
        self.own_at = (t, self.chip)
        self.self_at = (c, self.unit)

    def columns(self):
        c, f, t, F = self.c, self.f, self.t, self.F
        own = [(c, lax.rem(f + k, F), t) for k in range(1, F)]
        beside = [(c, lax.rem(f + k, F), 1 - t) for k in range(F)]
        across = [(self.mate, lax.rem(f + k, F), t) for k in range(F)]
        return own, beside, across

    def greet(self):
        c, f, t, C = self.c, self.f, self.t, self.C
        own, beside, across = self.columns()
        rest = [(lax.rem(c + j, C), f, 1 - t) for j in range(1, C)]
        rest += [(lax.rem(c + j, C), f, t) for j in (1, 3)]
        greet(own + beside + across + rest)

    def table_copies(self, source, tables, sent, got):
        out, come = [], []
        for i, column in enumerate(self.columns()):
            for n, device in enumerate(column):
                k = n + 1 if i == 0 else n
                out.append(remote(source, tables.at[i, self.f], sent.at[i, k], got.at[i, k], device))
                origin = lax.rem(self.f + self.F - k, self.F)
                come.append(
                    remote(source, tables.at[i, origin], sent.at[i, k], got.at[i, k], device)
                )
        return out, come

    def target(self, group, j):
        if group == 0:
            p = lax.rem(self.c + j, 4)
            return p, (p, self.f, self.t)
        p = lax.rem(self.unit + j, 4)
        return p, (self.chip * 2 + lax.div(p, self.T), self.f, lax.rem(p, self.T))

    def expert_id(self, group, p):
        if group == 0:
            return (p * self.F + self.f) * self.T + self.t
        chip_core = self.chip * 2 + lax.div(p, self.T)
        return (chip_core * self.F + self.f) * self.T + lax.rem(p, self.T)

    def origin_view(self, buf, group, b, p, H):
        if group == 0:
            first = pl.multiple_of(lax.rem(p, 2) * self.T, self.T)
            return buf.at[b, lax.div(p, 2), pl.ds(first, self.T), :, pl.ds(0, H)]
        return buf.at[b, :, p, :, pl.ds(H, H)]

    def table_of(self, group, q):
        own = q == self.own_at[group]
        return jnp.where(own, 0, 1 + group)

    def one_hot(self, ranks, group, b, q, p, K):
        row = ranks[self.table_of(group, q), b, pl.ds(self.expert_id(group, p), 1), :]
        slots = lax.broadcasted_iota(jnp.int32, (K, row.shape[1]), 0).astype(FL)
        return slots == row

    def gate_row(self, gates, group, b, q, p):
        return gates[self.table_of(group, q), b, pl.ds(self.expert_id(group, p), 1), :]

    def z_sends(self, s, d):
        b = self.f - (s - 1) if d == 0 else self.f + (s - 1)
        if d == 0:
            return (self.f + 1 < self.F) & (b >= 0)
        return (self.f > 0) & (b < self.F)

    def z_gets(self, s, d):
        return self.f - s >= 0 if d == 0 else self.f + s < self.F

    def z_copy(self, zbuf, zs, zr, s, d):
        b = self.f - (s - 1) if d == 0 else self.f + (s - 1)
        there = (self.c, self.f + 1 if d == 0 else self.f - 1, self.t)
        return remote(zbuf.at[b], zbuf.at[b], zs.at[d, s], zr.at[d, s], there)

    def z_begin(self, zbuf, zs, zr):
        for d in range(2):

            @pl.when(self.z_sends(1, d))
            def _():
                self.z_copy(zbuf, zs, zr, 1, d).start()

    def z_relay(self, zbuf, zs, zr, s):
        for d in range(2):

            @pl.when(self.z_gets(s, d))
            def _():
                b = self.f - s if d == 0 else self.f + s
                remote(
                    zbuf.at[b], zbuf.at[b], zs.at[d, s], zr.at[d, s], self.side[0]
                ).wait_recv()
                if s + 1 < self.F:

                    @pl.when(self.z_sends(s + 1, d))
                    def _():
                        self.z_copy(zbuf, zs, zr, s + 1, d).start()

    def z_drain(self, zbuf, zs, zr):
        for s in range(1, self.F):
            for d in range(2):

                @pl.when(self.z_sends(s, d))
                def _():
                    self.z_copy(zbuf, zs, zr, s, d).wait_send()


def moe_forward_body(
    C, F, T,
    rows, gate_t, ranks, w_in, w_out,
    xr, got0, got1, pre, mixed, part, gates,
    zbuf, dense, st0, st1, xs, gt0, gt1, wi, wo, prebuf, own_part, cross, pstage, zpart,
    loc, zs, zr, es, er, ss, sr, rs, rr, cs, cr, ps, pr, ts, tr, xl, gl, pl_,
):
    x = Exchange(C, F, T)
    c, f, t = x.c, x.f, x.t
    K, W = xr.shape[3], xr.shape[4]
    S, H = C * T, W // 2
    FFW = w_out.shape[0]
    stages, gots, keeps = (st0, st1), (gt0, gt1), (got0, got1)
    x.greet()
    zbuf[f] = rows[...]
    x.z_begin(zbuf, zs, zr)

    def dense_copy(k, g):
        b = x.blocks[k]
        return remote(
            zbuf.at[b, :, pl.ds(g * H, H)], dense.at[g, b], es.at[g, k], er.at[g, k], x.side[g]
        )

    def send_dense(k):
        for g in range(2):
            dense_copy(k, g).start()

    send_dense(0)
    load_i = pltpu.make_async_copy(w_in, wi, loc.at[0])
    load_o = pltpu.make_async_copy(w_out, wo, loc.at[1])
    load_i.start()
    load_o.start()
    g_out, g_come = x.table_copies(gate_t, gates, ts, tr)
    for copy in g_out:
        copy.start()
    gates[0, f] = gate_t[...]

    def sparse(k, g, j, arriving):
        b = x.blocks[k]
        p, device = x.target(g, 4 - j if arriving else j)
        index = p if arriving else x.self_at[g]
        return remote(
            stages[g].at[b, p], x.origin_view(xs, g, b, index, H),
            ss.at[g, k, j], sr.at[g, k, j], device,
        )

    def back(k, g, j, arriving):
        b = x.blocks[k]
        p, device = x.target(g, 4 - j if arriving else j)
        index = p if arriving else x.self_at[g]
        return remote(
            stages[g].at[b, p], gots[g].at[b, :, index], rs.at[g, k, j], rr.at[g, k, j], device
        )

    def source(k, g, q):
        b = x.blocks[k]
        own = zbuf[b, :, g * H : (g + 1) * H]
        return jnp.where(q == x.own_at[g], own, dense[g, b])

    def dispatch_rows(k):
        b = x.blocks[k]
        for g in range(2):
            dense_copy(k, g).wait_recv()
        for j in (2, 1, 3, 0):
            for g in range(2):
                p, _ = x.target(g, j)
                for q in range(2):
                    hot = x.one_hot(ranks, g, b, q, p, K).astype(BF)
                    stages[g][b, p, q] = jnp.dot(
                        hot, source(k, g, q), preferred_element_type=FL
                    ).astype(BF)
                if j:
                    sparse(k, g, j, False).start()
                else:
                    x.origin_view(xs, g, b, p, H)[...] = stages[g][b, p]

    def keep_x(k):
        return pltpu.make_async_copy(xs.at[x.blocks[k]], xr.at[x.blocks[k]], xl.at[k])

    def keep_got(k, g):
        b = x.blocks[k]
        return pltpu.make_async_copy(gots[g].at[b], keeps[g].at[b], gl.at[g, k])

    def keep_pre(k):
        return pltpu.make_async_copy(prebuf, pre.at[x.blocks[k]], pl_.at[k])

    def expert(k):
        b = x.blocks[k]
        for j in range(1, 4):
            for g in range(2):
                sparse(k, g, j, True).wait_recv()
        if k == 0:
            load_i.wait()
        else:
            keep_pre(k - 1).wait()
        keep_x(k).start()
        left = xs[b].reshape(S * K, W)
        tile = 256
        for i in range(FFW // tile):
            at = slice(i * tile, (i + 1) * tile)
            up_at = slice(FFW + i * tile, FFW + (i + 1) * tile)
            gate_pre = jnp.dot(left, wi[:, at], preferred_element_type=FL)
            up_pre = jnp.dot(left, wi[:, up_at], preferred_element_type=FL)
            prebuf[:, at] = gate_pre
            prebuf[:, up_at] = up_pre
            mixed[b, :, at] = (gate_pre * jax.nn.sigmoid(gate_pre) * up_pre).astype(BF)
        keep_pre(k).start()
        if k == 0:
            load_o.wait()
        for j in range(1, 4):
            for g in range(2):
                sparse(k, g, j, False).wait_send()
        send_back(k, mixed[b], lambda at: wo[:, at], False)

    def send_back(k, left, right, turned):
        b = x.blocks[k]
        tile = min(512, H)
        for i in range(W // tile):
            at = slice(i * tile, (i + 1) * tile)
            y = jnp.dot(left, right(at), preferred_element_type=FL).astype(BF)
            y = y.reshape(2, 4, K, tile)
            for chip in range(2):
                for unit in range(4):
                    if i * tile < H:
                        st0[b, chip * 2 + unit // T, unit % T, :, at] = y[chip, unit]
                    else:
                        cols = slice(i * tile - H, (i + 1) * tile - H)
                        st1[b, unit, chip, :, cols] = y[chip, unit]
            if (i + 1) * tile in (H, W):
                g = 0 if (i + 1) * tile == H else 1
                for j in (2, 1, 3):
                    back(k, g, j, False).start()
                me = x.self_at[g]
                for q in range(2):
                    gots[g][b, q, me] = stages[g][b, me, q]

    def cross_copy(k, g):
        b = x.blocks[k]
        return remote(pstage.at[b, :, pl.ds(g * H, H)], cross.at[g, b], cs.at[g, k], cr.at[g, k], x.side[g])

    def gather(k):
        b = x.blocks[k]
        for g in range(2):
            for j in range(1, 4):
                back(k, g, j, True).wait_recv()
            keep_got(k, g).start()
            for near in range(2):
                q = x.own_at[g] if near else 1 - x.own_at[g]
                scaled = []
                for p in range(4):
                    hot = x.one_hot(ranks, g, b, q, p, K)
                    scaled.append(jnp.where(hot, x.gate_row(gates, g, b, q, p), 0.0))
                scaled = jnp.concatenate(scaled, axis=0)
                high = scaled.astype(BF)
                low = (scaled - high.astype(FL)).astype(BF)
                tile = min(512, H)
                for i in range(H // tile):
                    at = slice(i * tile, (i + 1) * tile)
                    out_at = slice(g * H + i * tile, g * H + (i + 1) * tile)
                    y = gots[g][b, q, :, :, at].reshape(4 * K, tile)
                    total = inner_rows(high, y) + inner_rows(low, y)
                    if near:
                        own_part[k % 2, :, out_at] = total
                    else:
                        pstage[b, :, out_at] = total.astype(BF)
                if not near:
                    cross_copy(k, g).start()

    def part_copy(k, g):
        b = x.blocks[k]
        at = pl.ds(g * H, H)
        return remote(
            pstage.at[b, :, at], zpart.at[f, :, at], ps.at[g, b], pr.at[g, f], (c, b, t)
        )

    def part_arrival(k, g):
        b = x.blocks[k]
        at = pl.ds(g * H, H)
        return remote(
            pstage.at[b, :, at], zpart.at[b, :, at], ps.at[g, b], pr.at[g, b], (c, b, t)
        )

    def finish(k):
        b = x.blocks[k]
        for g in range(2):
            cross_copy(k, g).wait_recv()
            cross_copy(k, g).wait_send()
            at = slice(g * H, (g + 1) * H)
            total = own_part[k % 2, :, at] + cross[g, b].astype(FL)
            if k:
                pstage[b, :, at] = total.astype(BF)
                part_copy(k, g).start()
            else:
                part[:, at] = total

    dispatch_rows(0)
    x.z_relay(zbuf, zs, zr, 1)
    send_dense(1)
    expert(0)
    dispatch_rows(1)
    for s in range(2, F):
        x.z_relay(zbuf, zs, zr, s)
    for k in range(2, F):
        send_dense(k)
    for copy in g_out:
        copy.wait_send()
    for copy in g_come:
        copy.wait_recv()
    expert(1)
    dispatch_rows(2)
    gather(0)
    dispatch_rows(3)
    expert(2)
    gather(1)
    finish(0)
    expert(3)
    finish(1)
    gather(2)
    finish(2)
    gather(3)
    finish(3)
    for k in range(1, F):
        for g in range(2):
            part_arrival(k, g).wait_recv()
        part[...] += zpart[x.blocks[k]].astype(FL)
    x.z_drain(zbuf, zs, zr)
    keep_pre(F - 1).wait()
    for k in range(F):
        keep_x(k).wait()
        for g in range(2):
            if k:
                part_copy(k, g).wait_send()
            keep_got(k, g).wait()
            dense_copy(k, g).wait_send()
            for j in range(1, 4):
                back(k, g, j, False).wait_send()


def moe_forward(identity, C, F, T, K, rows, gate_t, ranks, w_in, w_out):
    S = C * T
    R, W = rows.shape
    H = W // 2
    H2, FFW = w_in.shape[1], w_out.shape[0]
    dma = pltpu.SemaphoreType.DMA
    V = pltpu.VMEM
    shape = jax.ShapeDtypeStruct
    return pl.pallas_call(
        functools.partial(moe_forward_body, C, F, T),
        out_shape=(
            shape((F, 2, 4, K, W), BF), shape((F, 2, 4, K, H), BF), shape((F, 2, 4, K, H), BF),
            shape((F, S * K, H2), FL), shape((F, S * K, FFW), BF), shape((R, W), FL),
            shape((3, F) + gate_t.shape, FL),
        ),
        in_specs=[VMEM] * 3 + [ANY] * 2,
        out_specs=[ANY] * 4 + [VMEM] * 3,
        scratch_shapes=[
            V((F, R, W), BF), V((2, F, R, H), BF), V((F, 4, 2, K, H), BF), V((F, 4, 2, K, H), BF),
            V((F, 2, 4, K, W), BF), V((F, 2, 4, K, H), BF), V((F, 2, 4, K, H), BF),
            V((W, H2), BF), V((FFW, W), BF), V((S * K, H2), FL), V((2, R, W), FL),
            V((2, F, R, H), BF), V((F, R, W), BF), V((F, R, W), BF),
            dma((2,)), dma((2, F)), dma((2, F)), dma((2, F)), dma((2, F)), dma((2, F, 4)),
            dma((2, F, 4)), dma((2, F, 4)), dma((2, F, 4)), dma((2, F)), dma((2, F)), dma((2, F)),
            dma((2, F)), dma((3, F)), dma((3, F)), dma((F,)), dma((2, F)), dma((F,)),
        ],
        compiler_params=params(identity, 61),
    )(rows, gate_t, ranks, w_in, w_out)


def moe_backward_body(
    C, F, T,
    gates, ranks, mixed, rows, w_in, w_out, xr, got0, got1, pre,
    part, grad_in, grad_out, dgr0, dgr1,
    zbuf, dense, st0, st1, xs, gt0, gt1, ysx, wi, wo, dpre, prebuf, tiles, own_part, cross,
    pstage, zpart, dgs,
    loc, zs, zr, es, er, ss, sr, rs, rr, cs, cr, ps, pr, ds_, dr, pl_, tl,
):
    x = Exchange(C, F, T)
    c, f, t = x.c, x.f, x.t
    K, W = xr.shape[3], xr.shape[4]
    S, H = C * T, W // 2
    FFW = w_out.shape[0]
    R = rows.shape[0]
    stages, gots, gate_in = (st0, st1), (gt0, gt1), (dgr0, dgr1)
    load_r = pltpu.make_async_copy(rows, zbuf.at[f], loc.at[5])
    load_r.start()
    x.greet()
    load_r.wait()
    x.z_begin(zbuf, zs, zr)

    def dense_copy(k, g):
        b = x.blocks[k]
        return remote(
            zbuf.at[b, :, pl.ds(g * H, H)], dense.at[g, b], es.at[g, k], er.at[g, k], x.side[g]
        )

    def send_dense(k):
        for g in range(2):
            dense_copy(k, g).start()

    send_dense(0)
    load_y = [
        pltpu.make_async_copy(got, ysx.at[:, :, :, :, pl.ds(g * H, H)], loc.at[g])
        for g, got in enumerate((got0, got1))
    ]
    load_o = pltpu.make_async_copy(w_out, wo, loc.at[2])
    load_i = pltpu.make_async_copy(w_in, wi, loc.at[3])
    load_x = pltpu.make_async_copy(xr, ysx, loc.at[4])
    for copy in load_y:
        copy.start()
    load_o.start()
    load_i.start()

    def pre_load(k):
        return pltpu.make_async_copy(pre.at[x.blocks[k]], prebuf, pl_.at[k])

    pre_load(0).start()

    def sparse(k, g, j, arriving):
        b = x.blocks[k]
        p, device = x.target(g, 4 - j if arriving else j)
        index = p if arriving else x.self_at[g]
        return remote(
            stages[g].at[b, p], x.origin_view(xs, g, b, index, H),
            ss.at[g, k, j], sr.at[g, k, j], device,
        )

    def back(k, g, j, arriving):
        b = x.blocks[k]
        p, device = x.target(g, 4 - j if arriving else j)
        index = p if arriving else x.self_at[g]
        return remote(
            stages[g].at[b, p], gots[g].at[b, :, index], rs.at[g, k, j], rr.at[g, k, j], device
        )

    def source(k, g, q):
        b = x.blocks[k]
        own = zbuf[b, :, g * H : (g + 1) * H]
        return jnp.where(q == x.own_at[g], own, dense[g, b])

    def dispatch_rows(k):
        b = x.blocks[k]
        for g in range(2):
            dense_copy(k, g).wait_recv()
        for j in (2, 1, 3, 0):
            for g in range(2):
                p, _ = x.target(g, j)
                for q in range(2):
                    hot = x.one_hot(ranks, g, b, q, p, K)
                    gate = jnp.sum(
                        jnp.where(hot, x.gate_row(gates, g, b, q, p), 0.0), axis=1, keepdims=True
                    )
                    picked = jnp.dot(
                        hot.astype(BF), source(k, g, q), preferred_element_type=FL
                    )
                    stages[g][b, p, q] = (picked * gate).astype(BF)
                if j:
                    sparse(k, g, j, False).start()
                else:
                    x.origin_view(xs, g, b, p, H)[...] = stages[g][b, p]

    lanes = lax.broadcasted_iota(jnp.int32, (K, R), 1)

    def gate_copy(k, g, near):
        b = x.blocks[k]
        q = x.own_at[g] if near else 1 - x.own_at[g]
        side = (c, b, 1 - t) if g == 0 else (x.mate, b, t)
        device = (c, b, t) if near else side
        return remote(
            dgs.at[g, q, b], gate_in[g].at[x.own_at[g], f],
            ds_.at[g, 1 - near, b], dr.at[g, 1 - near, f], device,
        )

    def gate_arrival(k, g, near):
        b = x.blocks[k]
        q = x.own_at[g] if near else 1 - x.own_at[g]
        return remote(
            dgs.at[g, q, b], gate_in[g].at[q, b],
            ds_.at[g, 1 - near, b], dr.at[g, 1 - near, b], x.side[g],
        )

    def gate_grads(k):
        b = x.blocks[k]
        for g in range(2):
            for near in range(2):
                q = x.own_at[g] if near else 1 - x.own_at[g]
                total = jnp.zeros((R, R), FL)
                rows_q = zbuf[b, :, g * H : (g + 1) * H] if near else dense[g, b]
                for p in range(4):
                    hot = x.one_hot(ranks, g, b, q, p, K).astype(BF)
                    picked = jnp.dot(hot, rows_q, preferred_element_type=FL)
                    y = ysx[b, q, p, :, g * H : (g + 1) * H].astype(FL)
                    dots = jnp.sum(picked * y, axis=1, keepdims=True)
                    spread = jnp.where(lanes == p, dots, 0.0)
                    high = spread.astype(BF)
                    low = (spread - high.astype(FL)).astype(BF)
                    total += inner_rows(high, hot) + inner_rows(low, hot)
                if near and k == 0:
                    gate_in[g][q, b] = total[:8, :]
                else:
                    dgs[g, q, b] = total[:8, :]
                    gate_copy(k, g, near).start()

    def expert(k):
        b = x.blocks[k]
        for j in range(1, 4):
            for g in range(2):
                sparse(k, g, j, True).wait_recv()
        if k == 0:
            load_o.wait()
        left = xs[b].reshape(S * K, W)
        pre_load(k).wait()
        tile = 256
        for i in range(FFW // tile):
            at = slice(i * tile, (i + 1) * tile)
            up_at = slice(FFW + i * tile, FFW + (i + 1) * tile)
            grad_mixed = outer_cols(left, wo[at, :])
            gate_pre = prebuf[:, at]
            up_pre = prebuf[:, up_at]
            sigmoid = jax.nn.sigmoid(gate_pre)
            dpre[b, :, at] = (
                grad_mixed * up_pre * (sigmoid * (1.0 + gate_pre * (1.0 - sigmoid)))
            ).astype(BF)
            dpre[b, :, up_at] = (grad_mixed * (gate_pre * sigmoid)).astype(BF)
        if k + 1 < F:
            pre_load(k + 1).start()
        if k == 0:
            load_i.wait()
        for j in range(1, 4):
            for g in range(2):
                sparse(k, g, j, False).wait_send()
        d = dpre[b]
        tile = min(512, H)
        for i in range(W // tile):
            at = slice(i * tile, (i + 1) * tile)
            y = outer_cols(d, wi[at, :]).astype(BF).reshape(2, 4, K, tile)
            for chip in range(2):
                for unit in range(4):
                    if i * tile < H:
                        st0[b, chip * 2 + unit // T, unit % T, :, at] = y[chip, unit]
                    else:
                        cols = slice(i * tile - H, (i + 1) * tile - H)
                        st1[b, unit, chip, :, cols] = y[chip, unit]
            if (i + 1) * tile in (H, W):
                g = 0 if (i + 1) * tile == H else 1
                for j in (2, 1, 3):
                    back(k, g, j, False).start()
                me = x.self_at[g]
                for q in range(2):
                    gots[g][b, q, me] = stages[g][b, me, q]

    def cross_copy(k, g):
        b = x.blocks[k]
        return remote(pstage.at[b, :, pl.ds(g * H, H)], cross.at[g, b], cs.at[g, k], cr.at[g, k], x.side[g])

    def gather(k):
        b = x.blocks[k]
        for g in range(2):
            for j in range(1, 4):
                back(k, g, j, True).wait_recv()
            for near in range(2):
                q = x.own_at[g] if near else 1 - x.own_at[g]
                hot = jnp.concatenate(
                    [x.one_hot(ranks, g, b, q, p, K).astype(FL) for p in range(4)], axis=0
                ).astype(BF)
                tile = min(512, H)
                for i in range(H // tile):
                    at = slice(i * tile, (i + 1) * tile)
                    out_at = slice(g * H + i * tile, g * H + (i + 1) * tile)
                    total = inner_rows(hot, gots[g][b, q, :, :, at].reshape(4 * K, tile))
                    if near:
                        own_part[:, out_at] = total
                    else:
                        pstage[b, :, out_at] = total.astype(BF)
                if not near:
                    cross_copy(k, g).start()

    def part_copy(k, g):
        b = x.blocks[k]
        at = pl.ds(g * H, H)
        return remote(
            pstage.at[b, :, at], zpart.at[f, :, at], ps.at[g, b], pr.at[g, f], (c, b, t)
        )

    def part_arrival(k, g):
        b = x.blocks[k]
        at = pl.ds(g * H, H)
        return remote(
            pstage.at[b, :, at], zpart.at[b, :, at], ps.at[g, b], pr.at[g, b], (c, b, t)
        )

    def finish(k):
        b = x.blocks[k]
        for g in range(2):
            cross_copy(k, g).wait_recv()
            cross_copy(k, g).wait_send()
            at = slice(g * H, (g + 1) * H)
            total = own_part[:, at] + cross[g, b].astype(FL)
            if k:
                pstage[b, :, at] = total.astype(BF)
                part_copy(k, g).start()
            else:
                part[:, at] = total

    made = []

    def weight_tile(left, right, target, at):
        width = right.shape[1] // 2
        for half in range(2):
            n = len(made)
            if n >= 2:
                made[n - 2].wait()
            cols = slice(half * width, (half + 1) * width)
            tiles[n % 2, :, 0:width] = inner_rows(left, right[:, cols]).astype(BF)
            copy = pltpu.make_async_copy(
                tiles.at[n % 2, :, pl.ds(0, width)],
                target.at[pl.ds(at, 256), pl.ds(half * width, width)],
                tl.at[n],
            )
            copy.start()
            made.append(copy)

    def out_grads(first, last):
        g = xs[...].reshape(F * S * K, W)
        for i in range(first, last):
            left = mixed[:, :, i * 256 : (i + 1) * 256].reshape(F * S * K, 256)
            weight_tile(left, g, grad_out, i * 256)

    def in_grads(first, last):
        d = dpre[...].reshape(F * S * K, 2 * FFW)
        for i in range(first, last):
            left = ysx[:, :, :, :, i * 256 : (i + 1) * 256].reshape(F * S * K, 256)
            weight_tile(left, d, grad_in, i * 256)

    dispatch_rows(0)
    x.z_relay(zbuf, zs, zr, 1)
    send_dense(1)
    for copy in load_y:
        copy.wait()
    gate_grads(0)
    expert(0)
    dispatch_rows(1)
    for s in range(2, F):
        x.z_relay(zbuf, zs, zr, s)
    for k in range(2, F):
        send_dense(k)
    gate_grads(1)
    expert(1)
    dispatch_rows(2)
    gather(0)
    dispatch_rows(3)
    gate_grads(2)
    expert(2)
    finish(0)
    gather(1)
    gate_grads(3)
    load_x.start()
    expert(3)
    finish(1)
    gather(2)
    out_grads(0, 1)
    finish(2)
    out_grads(1, FFW // 256)
    gather(3)
    load_x.wait()
    in_grads(0, 1)
    finish(3)
    in_grads(1, W // 256)
    for k in range(1, F):
        for g in range(2):
            part_arrival(k, g).wait_recv()
        part[...] += zpart[x.blocks[k]].astype(FL)
    for k in range(F):
        for g in range(2):
            for near in range(2):
                if k or not near:
                    gate_arrival(k, g, near).wait_recv()
                    gate_copy(k, g, near).wait_send()
    for copy in made[-2:]:
        copy.wait()
    x.z_drain(zbuf, zs, zr)
    for k in range(F):
        for g in range(2):
            if k:
                part_copy(k, g).wait_send()
            dense_copy(k, g).wait_send()
            for j in range(1, 4):
                back(k, g, j, False).wait_send()


def moe_backward(identity, C, F, T, rows, gates, ranks, mixed, w_in, w_out, xr, got0, got1, pre):
    S = C * T
    K = xr.shape[3]
    R, W = rows.shape
    H = W // 2
    H2, FFW = w_in.shape[1], w_out.shape[0]
    dma = pltpu.SemaphoreType.DMA
    V = pltpu.VMEM
    shape = jax.ShapeDtypeStruct
    return pl.pallas_call(
        functools.partial(moe_backward_body, C, F, T),
        out_shape=(
            shape((R, W), FL), shape((W, H2), BF), shape((FFW, W), BF),
            shape((2, F, 8, R), FL), shape((2, F, 8, R), FL),
        ),
        in_specs=[VMEM] * 3 + [ANY] * 7,
        out_specs=[VMEM, ANY, ANY, VMEM, VMEM],
        scratch_shapes=[
            V((F, R, W), BF), V((2, F, R, H), BF), V((F, 4, 2, K, H), BF), V((F, 4, 2, K, H), BF),
            V((F, 2, 4, K, W), BF), V((F, 2, 4, K, H), BF), V((F, 2, 4, K, H), BF),
            V((F, 2, 4, K, W), BF), V((W, H2), BF), V((FFW, W), BF), V((F, S * K, H2), BF),
            V((S * K, H2), FL), V((2, 256, max(W, H2) // 2), BF), V((R, W), FL),
            V((2, F, R, H), BF), V((F, R, W), BF), V((F, R, W), BF), V((2, 2, F, 8, R), FL),
            dma((6,)), dma((2, F)), dma((2, F)), dma((2, F)), dma((2, F)), dma((2, F, 4)),
            dma((2, F, 4)), dma((2, F, 4)), dma((2, F, 4)), dma((2, F)), dma((2, F)), dma((2, F)),
            dma((2, F)), dma((2, 2, F)), dma((2, 2, F)), dma((F,)),
            dma((2 * (FFW // 256 + W // 256),)),
        ],
        compiler_params=params(identity, 63.5),
    )(gates, ranks, mixed, rows, w_in, w_out, xr, got0, got1, pre)


def split_low(values):
    high = lax.reduce_precision(values, 8, 7)
    return high.astype(BF), (values - high).astype(BF)


def local(
    hidden_in,
    teacher,
    lengths,
    routes,
    attn_gain,
    w_query,
    w_key,
    w_value,
    w_output,
    query_gain,
    key_gain,
    ffn_gain,
    w_router,
    w_expert_in,
    w_expert_out,
):
    c, f, t = place()
    C, F, T = (lax.axis_size(axis) for axis in AXES)
    S = C * T
    row_count = hidden_in.shape[1]
    width = hidden_in.shape[2]
    half_rows = row_count // T
    head_size = query_gain.shape[0]
    inv_root = head_size ** (-0.5)
    bf_type = BF
    fl_type = FL

    expert_count = S * F
    lanes = -(-expert_count // 128) * 128
    route_ids = routes[0]
    top_count = route_ids.shape[1]
    capacity = max(2, half_rows * top_count * 3 // (2 * expert_count))
    cap = -(-capacity // 16) * 16
    expert_ids = jnp.arange(lanes, dtype=jnp.int32)
    named = jnp.any(route_ids[:, :, None] == expert_ids[None, None, :], axis=1)
    row_ids = jnp.arange(half_rows, dtype=jnp.int32)
    below = (row_ids[None, :] < row_ids[:, None]).astype(bf_type)
    earlier = jnp.dot(below, named.astype(bf_type), preferred_element_type=fl_type)
    rank_tab = jnp.where(named, earlier, -1.0)

    q_cols, kv_cols = w_query.shape[1], w_key.shape[1]
    w_all = jnp.concatenate(
        [w_query, w_key, w_value, jnp.pad(w_router, ((0, 0), (0, lanes - expert_count)))], axis=1
    )
    proj_cols = q_cols + 2 * kv_cols
    q_heads = q_cols // head_size
    kv_heads = kv_cols // head_size
    group_size = q_heads // kv_heads
    inputs = hidden_in[0].astype(fl_type)
    positions = c * row_count + jnp.arange(row_count, dtype=jnp.int32)
    cosine, sine_tab = rope_tables(positions, head_size)
    length = jnp.take(lengths, f)
    total_len = row_count * C
    row_start = t * half_rows
    other_start = (1 - t) * half_rows
    own_inputs = lax.dynamic_slice_in_dim(inputs, row_start, half_rows, 0)
    own_positions = lax.dynamic_slice_in_dim(positions, row_start, half_rows, 0)
    fused = C == 4 and T == 2
    swap = [(i, 1 - i) for i in range(T)]
    if fused:
        cos_full = jnp.concatenate([cosine, cosine], axis=1)
        sin_signed = jnp.concatenate([-sine_tab, sine_tab], axis=1)
        key_pos = jnp.arange(total_len, dtype=jnp.int32)[:, None]
        bias = jnp.where((key_pos <= positions[None, :]) & (key_pos < length), 0.0, MASKED)
        (
            full_all, full_o, rank_z, raw, q_rot, all_both, keys_t, log_total, heads_low,
            normed_low, residual, ffn_low, gate_tab,
        ) = head(
            1, C, F, T, kv_heads, proj_cols, total_len,
            (
                hidden_in[0], rank_tab, rank_tab[:, :expert_count].T, attn_gain[None], query_gain[None], key_gain[None],
                ffn_gain[None], cos_full, sin_signed, bias, w_all, w_output,
            ),
        )
        full_router = full_all[:, proj_cols : proj_cols + expert_count]
        gates = gate_tab[:, :expert_count]
        ffn_factor = lax.rsqrt(jnp.mean(residual * residual, axis=-1, keepdims=True) + EPS)
    else:
        full_all, full_o, rank_z = gather_weights(C, F, w_all, w_output, rank_tab)
        full_qkv = full_all[:, :proj_cols]
        full_router = full_all[:, proj_cols : proj_cols + expert_count]
        normed, norm_factor = norm_rows(inputs, attn_gain)
        normed_low = normed.astype(bf_type)
        raw = jnp.dot(normed_low, full_qkv, preferred_element_type=fl_type)
        q_raw = raw[:, :q_cols].reshape(row_count, q_heads, head_size)
        k_raw = raw[:, q_cols : q_cols + kv_cols].reshape(row_count, kv_heads, head_size)
        values_low = raw[:, q_cols + kv_cols :].astype(bf_type).reshape(row_count, kv_heads, head_size)
        q_normed, q_factor = norm_rows(q_raw, query_gain)
        k_normed, k_factor = norm_rows(k_raw, key_gain)
        q_rot = rotate(q_normed, cosine, sine_tab).astype(bf_type)
        k_rot = rotate(k_normed, cosine, sine_tab).astype(bf_type)
        queries = jnp.transpose(q_rot.reshape(row_count, kv_heads, group_size, head_size), (1, 2, 0, 3))
        both = jnp.transpose(jnp.concatenate([k_rot, values_low], axis=1), (1, 0, 2))
        all_both = lax.all_gather(both, "ctx", axis=1, tiled=True)
        all_keys, all_values = all_both[:kv_heads], all_both[kv_heads:]
        block_len = min(1024, total_len)
        offsets = jnp.arange(total_len // block_len, dtype=jnp.int32) * block_len
        stat_shape = (kv_heads, group_size, row_count)

        def lse_step(carry, offset):
            running_max, running_sum = carry
            key_rows = lax.dynamic_slice_in_dim(all_keys, offset, block_len, 1)
            scores, allowed = block_scores(queries, key_rows, offset, positions, length, inv_root)
            new_max = jnp.maximum(running_max, jnp.max(scores, axis=-1))
            exponent = jnp.where(allowed, jnp.exp(scores - new_max[..., None]), 0.0)
            return (
                (new_max, running_sum * jnp.exp(running_max - new_max) + jnp.sum(exponent, axis=-1)),
                None,
            )

        (row_max, row_sum), _ = lax.scan(
            lse_step, (jnp.full(stat_shape, MASKED, fl_type), jnp.zeros(stat_shape, fl_type)), offsets
        )
        log_total = row_max + jnp.log(row_sum)

        def probs_of(offset):
            key_rows = lax.dynamic_slice_in_dim(all_keys, offset, block_len, 1)
            value_rows = lax.dynamic_slice_in_dim(all_values, offset, block_len, 1)
            scores, allowed = block_scores(queries, key_rows, offset, positions, length, inv_root)
            return (
                jnp.where(allowed, jnp.exp(scores - log_total[..., None]), 0.0),
                key_rows,
                value_rows,
            )

        def out_step(running, offset):
            probabilities, key_rows, value_rows = probs_of(offset)
            return (
                running
                + jnp.einsum(
                    "kgqj,kjd->kgqd",
                    probabilities.astype(bf_type),
                    value_rows,
                    preferred_element_type=fl_type,
                ),
                None,
            )

        attn_acc, _ = lax.scan(
            out_step, jnp.zeros((kv_heads, group_size, row_count, head_size), fl_type), offsets
        )
        heads_low = (
            jnp.transpose(attn_acc, (2, 0, 1, 3))
            .reshape(row_count, q_heads * head_size)
            .astype(bf_type)
        )
        heads_other = lax.dynamic_slice_in_dim(heads_low, other_start, half_rows, 0)
        heads_own = lax.dynamic_slice_in_dim(heads_low, row_start, half_rows, 0)
        theirs = jnp.dot(heads_other, full_o, preferred_element_type=fl_type).astype(bf_type)
        ours = lax.ppermute(theirs, "tp", swap)
        attn_rows = jnp.dot(heads_own, full_o, preferred_element_type=fl_type) + ours.astype(fl_type)
        own_factor = lax.dynamic_slice_in_dim(norm_factor, row_start, half_rows, 0)
        residual = own_inputs + attn_rows
        ffn_in, ffn_factor = norm_rows(residual, ffn_gain)
        ffn_low = ffn_in.astype(bf_type)
        logits = jnp.dot(ffn_low, full_router, preferred_element_type=fl_type)
        is_named = named[:, :expert_count]
        masked = jnp.where(is_named, logits, MASKED)
        shifted = jnp.where(is_named, jnp.exp(masked - jnp.max(masked, axis=-1, keepdims=True)), 0.0)
        gates = shifted / jnp.sum(shifted, axis=-1, keepdims=True)
        gate_tab = jnp.pad(gates, ((0, 0), (0, lanes - expert_count)))

    if fused:
        gate_t = jnp.swapaxes(gates, 0, 1)
        expert_x, got_0, got_1, both_pre, mixed_low, mixture, gate_z = moe_forward(
            2, C, F, T, cap, ffn_low, gate_t, rank_z, w_expert_in[0], w_expert_out[0]
        )
    else:
        def of_slab(table):
            picked = table[:, :, :expert_count].reshape(F, half_rows, C, F, T)
            return lax.dynamic_index_in_dim(picked, f, 3, keepdims=False).reshape(F, half_rows, S)

        rank_slab = of_slab(rank_z)
        slot_ids = jnp.arange(cap, dtype=fl_type)
        chosen_rows = rank_slab[:, :, :, None] == slot_ids
        chosen_slots = (
            jnp.transpose(rank_slab, (0, 2, 1))[:, :, None, :] == slot_ids[:, None]
        )

        select = chosen_slots.astype(bf_type)
        received, _, gate_z = dispatch(2, C, F, T, ffn_low, select, gate_tab)
        expert_rows = received.reshape(-1, width)
        both_pre = jnp.dot(expert_rows, w_expert_in[0], preferred_element_type=fl_type)
        ff_width = w_expert_out.shape[1]
        gate_pre = both_pre[:, :ff_width]
        up_pre = both_pre[:, ff_width:]
        sigmoid_gate = jax.nn.sigmoid(gate_pre)
        silu_gate = gate_pre * sigmoid_gate
        mixed_low = (silu_gate * up_pre).astype(bf_type)
        expert_out = (
            jnp.dot(mixed_low, w_expert_out[0], preferred_element_type=fl_type)
            .astype(bf_type)
            .reshape(S, F, cap, width)
        )
        gate_slab = of_slab(gate_z)
        weigh = jnp.where(chosen_rows, gate_slab[..., None], 0.0).reshape(F, 1, half_rows, S * cap)
        weigh = jnp.concatenate(split_low(weigh), axis=1)
        returned, parts = combine(3, C, F, T, expert_out, weigh)
        mixture = jnp.sum(parts.astype(fl_type), axis=0)
    output_f = residual + mixture
    count = jnp.sum(lengths).astype(fl_type)
    tokens_total = lengths.shape[0] * row_count * C
    valid = own_positions < length
    error = jnp.where(valid[:, None], output_f - teacher[0].astype(fl_type), 0.0)
    loss_part = jnp.sum(error * error)
    grad_out = error * (tokens_total / count)

    if fused:
        grad_mixture, grad_expert_in, grad_expert_out, back_0, back_1 = moe_backward(
            3, C, F, T, grad_out.astype(bf_type), gate_z, rank_z, mixed_low,
            w_expert_in[0], w_expert_out[0], expert_x, got_0, got_1, both_pre,
        )
        back_0 = jnp.transpose(back_0[:, :, :C], (3, 2, 1, 0))
        back_1 = back_1[:, :, : 2 * T].reshape(2, F, 2, T, half_rows)
        back_1 = jnp.transpose(back_1, (4, 0, 2, 1, 3)).reshape(half_rows, C, F, T)
        grad_gate = (back_0 + back_1).reshape(half_rows, expert_count)
    else:
        select_gates = jnp.where(
            chosen_slots, jnp.transpose(gate_slab, (0, 2, 1))[:, :, None, :], 0.0
        )
        select_gates = jnp.concatenate(split_low(select_gates), axis=-1)
        grad_recv, grad_out_z = dispatch(4, C, F, T, grad_out.astype(bf_type), select_gates)
        slot_grads = jnp.einsum("zskr,zrd->zskd", select, grad_out_z, preferred_element_type=fl_type)
        slot_gate = jnp.sum(slot_grads * returned.astype(fl_type), axis=-1)
        gate_grads = jnp.sum(jnp.where(chosen_rows, slot_gate[:, None, :, :], 0.0), axis=-1)
        gate_grads = jnp.pad(gate_grads, ((0, 0), (0, 0), (0, -S % 128)))

        grad_recv = grad_recv.reshape(-1, width)
        grad_mixed = outer_cols(grad_recv, w_expert_out[0])
        grad_expert_out = inner_rows(mixed_low, grad_recv)
        grad_gate_pre = grad_mixed * up_pre * (sigmoid_gate * (1.0 + gate_pre * (1.0 - sigmoid_gate)))
        grad_up_pre = grad_mixed * silu_gate
        grad_pre = jnp.concatenate([grad_gate_pre, grad_up_pre], axis=1).astype(bf_type)
        grad_expert_in = inner_rows(expert_rows, grad_pre)
        grad_rows = (
            outer_cols(grad_pre, w_expert_in[0]).astype(bf_type).reshape(S, F, cap, width)
        )
        weigh_one = chosen_rows.astype(bf_type).reshape(F, 1, half_rows, S * cap)
        _, grad_parts, gate_back = combine(5, C, F, T, grad_rows, weigh_one, gate_grads)
        grad_gate = jnp.transpose(
            gate_back[:, :, :S].reshape(F, half_rows, C, T), (1, 2, 0, 3)
        ).reshape(half_rows, expert_count)
        grad_mixture = jnp.sum(grad_parts.astype(fl_type), axis=0)
    grad_logits = (
        gates * (grad_gate - jnp.sum(gates * grad_gate, axis=-1, keepdims=True))
    ).astype(bf_type)
    grad_ffn = grad_mixture + outer_cols(grad_logits, full_router)
    router_part = inner_rows(ffn_low, grad_logits)
    grad_resid_norm, ffn_gain_terms = norm_back(residual, ffn_factor, ffn_gain, grad_ffn)
    grad_residual = grad_out + grad_resid_norm
    grad_own = grad_residual.astype(bf_type)
    if fused:
        wide = width // F
        vec_in = jnp.zeros((16, wide), fl_type)
        vec_in = vec_in.at[F : 2 * F].set(jnp.sum(ffn_gain_terms, axis=0).reshape(F, wide))
        vec_in = vec_in.at[8, 2 * head_size].set(loss_part)
        router_rows = inner_rows(grad_logits, ffn_low)
        grad_input, total_a, total_o, summed = tail(
            9, C, F, T, kv_heads,
            (
                grad_own, heads_low, q_rot, all_both, keys_t, raw, log_total, bias,
                cos_full, sin_signed, query_gain[None], key_gain[None], attn_gain[None],
                hidden_in[0], grad_residual, router_rows, vec_in, normed_low, full_o, full_all,
            ),
            width, q_cols // C,
        )
        grad_query = total_a[:, :q_cols].astype(fl_type)
        grad_key = total_a[:, q_cols : q_cols + kv_cols].astype(fl_type)
        grad_value = total_a[:, q_cols + kv_cols :].astype(fl_type)
        grad_output_w = total_o.astype(fl_type)
        router_len = router_rows.shape[0]
        grad_router = summed[:router_len].T
        sum_attn = summed[router_len : router_len + F].reshape(width)
        sum_ffn = summed[router_len + F : router_len + 2 * F].reshape(width)
        sum_query = summed[router_len + 8, :head_size]
        sum_key = summed[router_len + 8, head_size : 2 * head_size]
        loss_total = summed[router_len + 8, 2 * head_size]
    else:
        grad_other = lax.ppermute(grad_own, "tp", swap)
        grad_attn = jnp.where(
            t == 0,
            jnp.concatenate([grad_own, grad_other], axis=0),
            jnp.concatenate([grad_other, grad_own], axis=0),
        )
        grad_heads = jnp.transpose(
            outer_cols(grad_attn, full_o)
            .astype(bf_type)
            .reshape(row_count, kv_heads, group_size, head_size),
            (1, 2, 0, 3),
        )

        def delta_step(running, offset):
            probabilities, key_rows, value_rows = probs_of(offset)
            grad_weights = jnp.einsum(
                "kgqd,kjd->kgqj", grad_heads, value_rows, preferred_element_type=fl_type
            )
            return (running + jnp.sum(probabilities * grad_weights, axis=-1), None)

        delta, _ = lax.scan(delta_step, jnp.zeros(stat_shape, fl_type), offsets)

        def grad_step(running, offset):
            probabilities, key_rows, value_rows = probs_of(offset)
            grad_weights = jnp.einsum(
                "kgqd,kjd->kgqj", grad_heads, value_rows, preferred_element_type=fl_type
            )
            grad_scores = (probabilities * (grad_weights - delta[..., None])).astype(bf_type)
            running = (
                running
                + jnp.einsum("kgqj,kjd->kgqd", grad_scores, key_rows, preferred_element_type=fl_type)
                * inv_root
            )
            key_part = (
                jnp.einsum("kgqj,kgqd->kjd", grad_scores, queries, preferred_element_type=fl_type)
                * inv_root
            )
            value_part = jnp.einsum(
                "kgqj,kgqd->kjd",
                probabilities.astype(bf_type),
                grad_heads,
                preferred_element_type=fl_type,
            )
            return (running, (key_part, value_part))

        grad_qrot, (key_blocks, value_blocks) = lax.scan(
            grad_step, jnp.zeros((kv_heads, group_size, row_count, head_size), fl_type), offsets
        )
        both_grads = jnp.concatenate([key_blocks, value_blocks], axis=1).astype(bf_type)
        both_grads = jnp.transpose(both_grads, (0, 2, 1, 3)).reshape(C, row_count, 2 * kv_cols)
        both_sum = ctx_sum(6, C, both_grads)
        grad_krot = both_sum[:, :kv_cols].reshape(row_count, kv_heads, head_size)
        grad_values_low = both_sum[:, kv_cols:].astype(bf_type)
        grad_qrot = jnp.transpose(grad_qrot, (2, 0, 1, 3)).reshape(row_count, q_heads, head_size)
        grad_qraw, query_gain_terms = norm_back(
            q_raw, q_factor, query_gain, rotate(grad_qrot, cosine, -sine_tab)
        )
        grad_kraw, key_gain_terms = norm_back(
            k_raw, k_factor, key_gain, rotate(grad_krot, cosine, -sine_tab)
        )
        grad_raw = jnp.concatenate(
            [
                grad_qraw.astype(bf_type).reshape(row_count, -1),
                grad_kraw.astype(bf_type).reshape(row_count, -1),
                grad_values_low,
            ],
            axis=1,
        )
        raw_other = lax.dynamic_slice_in_dim(grad_raw, other_start, half_rows, 0)
        raw_own = lax.dynamic_slice_in_dim(grad_raw, row_start, half_rows, 0)
        norm_theirs = outer_cols(raw_other, full_qkv).astype(bf_type)
        norm_ours = lax.ppermute(norm_theirs, "tp", swap)
        grad_normed = outer_cols(raw_own, full_qkv) + norm_ours.astype(fl_type)
        grad_input_norm, attn_gain_terms = norm_back(own_inputs, own_factor, attn_gain, grad_normed)
        grad_input = grad_residual + grad_input_norm

        total_a, total_o = weight_grads(
            7, C, F, normed_low.T, grad_raw, heads_low.T, grad_attn
        )
        total_a = total_a.reshape(-1, proj_cols).astype(fl_type)
        grad_query = total_a[:, :q_cols]
        grad_key = total_a[:, q_cols : q_cols + kv_cols]
        grad_value = total_a[:, q_cols + kv_cols :]
        grad_output_w = total_o.reshape(w_output.shape).astype(fl_type)

        vector = jnp.concatenate(
            [
                jnp.sum(attn_gain_terms, axis=0),
                jnp.sum(ffn_gain_terms, axis=0),
                jnp.sum(query_gain_terms, axis=(0, 1)),
                jnp.sum(key_gain_terms, axis=(0, 1)),
                loss_part[None],
            ]
        )
        vector = jnp.pad(vector, (0, -vector.shape[0] % 1024)).reshape(-1, 128)
        router_rows = router_part.reshape(F, -1, 128)
        small = jnp.concatenate(
            [router_rows, jnp.broadcast_to(vector[None], (F,) + vector.shape)], axis=1
        )
        summed = small_sum(8, C, F, T, small)
        router_len = router_rows.shape[1]
        grad_router = summed[:router_len].reshape(w_router.shape)
        flat = summed[router_len:].reshape(-1)
        head_at = 2 * width
        sum_attn, sum_ffn = flat[:width], flat[width:head_at]
        sum_query = flat[head_at : head_at + head_size]
        sum_key = flat[head_at + head_size : head_at + 2 * head_size]
        loss_total = flat[head_at + 2 * head_size]
    loss_value = loss_total / (count * width)
    return (
        output_f.astype(bf_type)[None],
        loss_value,
        grad_input[None],
        sum_attn,
        grad_query,
        grad_key,
        grad_value,
        grad_output_w,
        sum_query,
        sum_key,
        sum_ffn,
        grad_router,
        grad_expert_in.astype(fl_type)[None],
        grad_expert_out.astype(fl_type)[None],
    )


def solution(mesh):
    return jax.shard_map(
        local,
        mesh=mesh,
        in_specs=(
            P("fsdp", "ctx", None),
            P("fsdp", ("ctx", "tp"), None),
            P(),
            P("fsdp", ("ctx", "tp"), None),
            P(),
            P("fsdp", "tp"),
            P("fsdp", "tp"),
            P("fsdp", "tp"),
            P("tp", "fsdp"),
            P(),
            P(),
            P(),
            P("fsdp", None),
            P(("ctx", "fsdp", "tp"), None, None),
            P(("ctx", "fsdp", "tp"), None, None),
        ),
        out_specs=(
            P("fsdp", ("ctx", "tp"), None),
            P(),
            P("fsdp", ("ctx", "tp"), None),
            P(),
            P("fsdp", "tp"),
            P("fsdp", "tp"),
            P("fsdp", "tp"),
            P("tp", "fsdp"),
            P(),
            P(),
            P(),
            P("fsdp", None),
            P(("ctx", "fsdp", "tp"), None, None),
            P(("ctx", "fsdp", "tp"), None, None),
        ),
        check_vma=False,
    )
```
